32 devices in a mesh: row: 2 (over y), col: 16 (over z, x, core).
Axes of the slice: x: 2, y: 2, z: 4, core: 2. Of those that a mesh axis runs over, the one named last changes fastest.
Arguments:
- features: bfloat16 [16, 14, 224, 256], P(None, 'row', 'col'), may hold values from -6 to 6
- heights: int32 [16], replicated, may hold values from 4 to 14, as said below
- widths: int32 [16], replicated, may hold values from 57 to 224, as said below
- norm1_gain: float32 [256], replicated, may hold values from 0.5 to 1.5
- norm1_shift: float32 [256], replicated, may hold values from -1.25 to 1.25
- qkv_weight: bfloat16 [256, 768], replicated, may hold values from -0.375 to 0.375
- query_bias: float32 [256], replicated, may hold values from -1.25 to 1.25
- value_bias: float32 [256], replicated, may hold values from -1.25 to 1.25
- lepe_weight: float32 [9, 256], replicated, may hold values from -0.1875 to 0.1875
- lepe_bias: float32 [256], replicated, may hold values from -0.3125 to 0.3125
- proj_weight: bfloat16 [256, 256], replicated, may hold values from -3 to 3
- proj_bias: float32 [256], replicated, may hold values from -1.25 to 1.25
- norm2_gain: float32 [256], replicated, may hold values from 0.5 to 1.5
- norm2_shift: float32 [256], replicated, may hold values from -1.25 to 1.25
- fc1_weight: bfloat16 [256, 1024], replicated, may hold values from -0.375 to 0.375
- fc1_bias: float32 [1024], replicated, may hold values from -1.25 to 1.25
- fc2_weight: bfloat16 [1024, 256], replicated, may hold values from -0.1875 to 0.1875
- fc2_bias: float32 [256], replicated, may hold values from -1.25 to 1.25
- cotangent: bfloat16 [16, 14, 224, 256], P(None, 'row', 'col'), may hold values from -6 to 6
Outputs:
- block_out: bfloat16 [16, 14, 224, 256], P(None, 'row', 'col')
- grad_in: float32 [16, 14, 224, 256], P(None, 'row', 'col')
- grad_norm1_gain: float32 [256], replicated
- grad_norm1_shift: float32 [256], replicated
- grad_qkv_weight: float32 [256, 768], replicated
- grad_query_bias: float32 [256], replicated
- grad_value_bias: float32 [256], replicated
- grad_lepe_weight: float32 [9, 256], replicated
- grad_lepe_bias: float32 [256], replicated
- grad_proj_weight: float32 [256, 256], replicated
- grad_proj_bias: float32 [256], replicated
- grad_norm2_gain: float32 [256], replicated
- grad_norm2_shift: float32 [256], replicated
- grad_fc1_weight: float32 [256, 1024], replicated
- grad_fc1_bias: float32 [1024], replicated
- grad_fc2_weight: float32 [1024, 256], replicated
- grad_fc2_bias: float32 [256], replicated
The draws below stay inside these ranges and needn't reach their ends.
Inputs may be any that keep to these rules, and one draw needn't show every extreme that they name: Valid image heights; in every draw exactly one image has the full height 14, the others less. Valid image widths; in every draw exactly one image has the full width 224, the others less.
All inputs are finite; a program needn't handle non-finite values.
Results may differ from the reference program's by a relative error of at most 0.0094.
The reference program's roundings to bfloat16 on the way count: a program that leaves them out, or rounds other values in their place, can miss the bound.
Values may be sent and summed in bfloat16 or wider, within the bound.
A program may use at most 320 MiB of HBM per device.

```python
import jax
import jax.numpy as jnp
from jax import lax

D = 256
FF = 1024
HEADS = 8
SW = 7
IMGS = 16
IH = 14
IW = 224


def full_one(key, upper_bound):
    first_key, second_key = jax.random.split(key)
    drawn_sizes = jax.random.randint(first_key, (IMGS,), upper_bound // 4 + 1, upper_bound)
    chosen = jax.random.randint(second_key, (), 0, IMGS)
    return jnp.where(jnp.arange(IMGS) == chosen, upper_bound, drawn_sizes).astype(jnp.int32)


def draw_heights(key, part):
    key = jax.random.fold_in(key, 11)
    return full_one(key, IH)


def draw_widths(key, part):
    key = jax.random.fold_in(key, 23)
    return full_one(key, IW)


def steps_of(rng, shape, shards, low, high):
    level = 1.0
    for dim, parts in shards:
        steps = jax.random.uniform(jax.random.fold_in(jax.random.fold_in(rng, 6), dim), (parts,), jnp.float32, low / len(shards), high / len(shards))
        level = level * jnp.repeat(jnp.exp(steps), shape[dim] // parts).reshape((-1,) + (1,) * (len(shape) - 1 - dim))
    return level


def scatter_about(own_key, dims, scale, bound, cuts=(), held_as=jnp.bfloat16):
    values = scale * jax.random.normal(own_key, dims, jnp.float32)
    if cuts:
        values = values * steps_of(own_key, dims, cuts, -0.22, 0.18)
    return jnp.clip(values, -bound, bound).astype(held_as)


def setup_inputs(seed: int = 0) -> dict:
    key_of = jax.random.split(jax.random.key(seed), 20)
    return {
        "features": scatter_about(key_of[0], (IMGS, IH, IW, D), 1.0, 6.0, ((1, 2), (2, 16))),
        "heights": draw_heights(jax.random.fold_in(key_of[19], 71), 0),
        "widths": draw_widths(jax.random.fold_in(key_of[19], 71), 0),
        "norm1_gain": jnp.clip(1.0 + 0.1 * jax.random.normal(key_of[3], (D,), jnp.float32), 0.5, 1.5),
        "norm1_shift": scatter_about(key_of[4], (D,), 0.2, 1.25, (), jnp.float32),
        "qkv_weight": scatter_about(key_of[5], (D, 3 * D), D ** -0.5, 0.375),
        "query_bias": scatter_about(key_of[6], (D,), 0.2, 1.25, (), jnp.float32),
        "value_bias": scatter_about(key_of[7], (D,), 0.2, 1.25, (), jnp.float32),
        "lepe_weight": scatter_about(key_of[8], (9, D), 0.03, 0.1875, (), jnp.float32),
        "lepe_bias": scatter_about(key_of[9], (D,), 0.05, 0.3125, (), jnp.float32),
        "proj_weight": scatter_about(key_of[10], (D, D), (max(D // 64, 1)) ** -0.5, 3.0),
        "proj_bias": scatter_about(key_of[11], (D,), 0.2, 1.25, (), jnp.float32),
        "norm2_gain": jnp.clip(1.0 + 0.1 * jax.random.normal(key_of[12], (D,), jnp.float32), 0.5, 1.5),
        "norm2_shift": scatter_about(key_of[13], (D,), 0.2, 1.25, (), jnp.float32),
        "fc1_weight": scatter_about(key_of[14], (D, FF), D ** -0.5, 0.375),
        "fc1_bias": scatter_about(key_of[15], (FF,), 0.2, 1.25, (), jnp.float32),
        "fc2_weight": scatter_about(key_of[16], (FF, D), FF ** -0.5, 0.1875),
        "fc2_bias": scatter_about(key_of[17], (D,), 0.2, 1.25, (), jnp.float32),
        "cotangent": scatter_about(key_of[18], (IMGS, IH, IW, D), 1.0, 6.0, ((1, 2), (2, 16))),
    }


MASKED_SCORE = -1e+30
NORM_EPSILON = 1e-05
PRECISE = lax.Precision.HIGHEST

@jax.custom_vjp
def low(v):
    return lax.optimization_barrier(v.astype(jnp.bfloat16)).astype(jnp.float32)

@jax.custom_vjp
def low_back(v):
    return v

def low_keep(v):
    return (low(v), None)

def low_pass(kept, grad):
    return (grad,)

def back_keep(v):
    return (v, None)

def back_low(kept, grad):
    return (low(grad),)
low.defvjp(low_keep, low_pass)
low_back.defvjp(back_keep, back_low)

def layer_norm(values, ln_gain, ln_shift):
    average = lax.optimization_barrier(jnp.mean(values, -1, keepdims=True))
    centred = values - average
    spread = lax.optimization_barrier(jnp.mean(centred * centred, -1, keepdims=True))
    return centred * lax.rsqrt(spread + NORM_EPSILON) * ln_gain + ln_shift

def gelu_exact(values):
    return jax.nn.gelu(values, approximate=False)

def turned(array):
    return jnp.swapaxes(array, 1, 2)

def conv_padded(padded, kernels):
    images, across, padded_len, channels = padded.shape
    lengthwise = padded_len - 2
    blocks = padded.reshape(images, across // SW, SW, padded_len, channels)
    blocks = jnp.pad(blocks, ((0, 0), (0, 0), (1, 1), (0, 0), (0, 0)))
    summed = jnp.zeros((images, across // SW, SW, lengthwise, channels), blocks.dtype)
    for shift_a in range(3):
        for shift_l in range(3):
            summed = summed + kernels[shift_a, shift_l] * blocks[:, :, shift_a:shift_a + SW, shift_l:shift_l + lengthwise]
    return summed.reshape(images, across, lengthwise, channels)

def pad_length(values):
    return jnp.pad(values, ((0, 0), (0, 0), (1, 1), (0, 0)))

def stripe_attend(members):
    queries, keys_in, values_in, allowed = members
    heads = HEADS // 2
    lengthwise = queries.shape[1]
    q_flat = queries.reshape(SW * lengthwise, heads, -1)
    k_flat = keys_in.reshape(SW * lengthwise, heads, -1)
    v_flat = values_in.reshape(SW * lengthwise, heads, -1)
    score_scale = q_flat.shape[-1] ** (-0.5)
    logits = jnp.einsum('qhe,khe->hqk', q_flat, k_flat, precision=PRECISE) * score_scale
    logits = low_back(jnp.where(allowed.reshape(1, 1, -1), logits, MASKED_SCORE))
    weights = low(jax.nn.softmax(logits, -1))
    merged = jnp.einsum('hqk,khe->qhe', weights, v_flat, precision=PRECISE)
    return merged.reshape(SW, lengthwise, -1)

def branch(queries, keys_in, values_in, allowed):
    count = queries.shape[0] * queries.shape[1] // SW

    def shaped(array):
        return array.reshape((count, SW) + array.shape[2:])
    merged = lax.map(jax.checkpoint(stripe_attend), (shaped(queries), shaped(keys_in), shaped(values_in), shaped(allowed)))
    return merged.reshape(queries.shape)

def forward(inside, source, norm1_gain, norm1_shift, qkv_weight, query_bias, value_bias, lepe_weight, lepe_bias, proj_weight, proj_bias, norm2_gain, norm2_shift, fc1_weight, fc1_bias, fc2_weight, fc2_bias):
    model_dim = source.shape[-1]
    half_dim = model_dim // 2
    normed_low = low(layer_norm(source, norm1_gain, norm1_shift))
    qkv_bias = jnp.concatenate([query_bias, jnp.zeros_like(query_bias), value_bias])
    projected = low(low_back(jnp.einsum('bijd,de->bije', normed_low, qkv_weight, precision=PRECISE) + qkv_bias))
    queries = projected[..., :model_dim]
    keys_all = projected[..., model_dim:2 * model_dim]
    values_all = projected[..., 2 * model_dim:]
    wide_out = branch(queries[..., :half_dim], keys_all[..., :half_dim], values_all[..., :half_dim], inside)
    tall_out = turned(branch(turned(queries[..., half_dim:]), turned(keys_all[..., half_dim:]), turned(values_all[..., half_dim:]), turned(inside)))
    masked = values_all * inside[..., None]
    kernels = lepe_weight.reshape(3, 3, model_dim)
    wide_lepe = conv_padded(pad_length(masked[..., :half_dim]), kernels[..., :half_dim])
    tall_lepe = turned(conv_padded(pad_length(turned(masked[..., half_dim:])), jnp.swapaxes(kernels[..., half_dim:], 0, 1)))
    mixture = low(low_back(jnp.concatenate([wide_out + wide_lepe, tall_out + tall_lepe], -1) + lepe_bias))
    attn_out = low_back(jnp.einsum('bijd,de->bije', mixture, proj_weight, precision=PRECISE) + proj_bias)
    residual = source + attn_out
    act_two = low(layer_norm(residual, norm2_gain, norm2_shift))
    pre_act = low_back(jnp.einsum('bijd,df->bijf', act_two, fc1_weight, precision=PRECISE) + fc1_bias)
    hidden = low(gelu_exact(pre_act))
    mlp_out = low_back(jnp.einsum('bijf,fd->bijd', hidden, fc2_weight, precision=PRECISE) + fc2_bias)
    return residual + mlp_out

def reference(features, heights, widths, norm1_gain, norm1_shift, qkv_weight, query_bias, value_bias, lepe_weight, lepe_bias, proj_weight, proj_bias, norm2_gain, norm2_shift, fc1_weight, fc1_bias, fc2_weight, fc2_bias, cotangent):
    rows_all = jnp.arange(IH)
    cols_all = jnp.arange(IW)
    inside = (rows_all[None, :, None] < heights[:, None, None]) & (cols_all[None, None, :] < widths[:, None, None])
    params = (features, norm1_gain, norm1_shift, qkv_weight, query_bias, value_bias, lepe_weight, lepe_bias, proj_weight, proj_bias, norm2_gain, norm2_shift, fc1_weight, fc1_bias, fc2_weight, fc2_bias)
    floats = tuple((member.astype(jnp.float32) for member in params))

    def closed(*members):
        return forward(inside, *members)
    output, backward = jax.vjp(closed, *floats)
    grads = backward(jnp.where(inside[..., None], cotangent.astype(jnp.float32), 0.0))
    return (output.astype(jnp.bfloat16), grads[0], grads[1], grads[2], grads[3], grads[4], grads[5], grads[6], grads[7], grads[8], grads[9], grads[10], grads[11], grads[12], grads[13], grads[14], grads[15])
```

```python
import functools
import math

import jax
import jax.numpy as jnp
from jax import lax
from jax.experimental import pallas as pl
from jax.experimental.pallas import tpu as pltpu
from jax.sharding import PartitionSpec as P

HEADS = 8
SW = 7
BRANCH_HEADS = HEADS // 2
HALF = 128
HEAD_DIM = 32
NORM_EPSILON = 1e-05
MASKED = -1e30
LOG2E = math.log2(math.e)
VMEM_LIMIT = 56 * 1024 * 1024
MESH = pl.DeviceIdType.MESH
F32 = jnp.float32
BF16 = jnp.bfloat16
NT = (((1,), (1,)), ((), ()))
TN = (((0,), (0,)), ((), ()))


def up(value, unit):
    return -(-value // unit) * unit


def mm(a, b):
    return jnp.dot(a, b, preferred_element_type=F32)


def mm_nt(a, b):
    return lax.dot_general(a, b, NT, preferred_element_type=F32)


def mm_tn(a, b):
    return lax.dot_general(a, b, TN, preferred_element_type=F32)


class Sizes:
    def __init__(self, mesh, shape):
        self.images, self.rows, self.cols, self.dim = shape
        self.R = mesh.shape["row"]
        self.C = mesh.shape["col"]
        self.pix = self.rows * self.cols
        self.tokens = self.pix * self.images
        self.stripes = self.cols // SW
        self.G = self.C // self.images
        self.wide_heads = BRANCH_HEADS // self.G
        self.hc = HALF // self.G
        self.tall_images = self.images // self.R
        self.wide_len = self.C * self.pix
        self.tall_own = self.rows * SW
        self.tall_len = self.R * self.tall_own
        self.tall_pad = up(self.tall_own, 8)
        self.wide_rows3 = up(3 * self.pix, 16)
        self.wide_rows1 = up(self.pix, 16)
        self.tall_slots = self.tall_images * self.stripes
        self.tall_rows1 = self.tall_slots * self.tall_pad
        self.tall_rows3 = 3 * self.tall_rows1


def norm_parts(values):
    average = jnp.mean(values, -1, keepdims=True)
    centred = values - average
    spread = jnp.mean(centred * centred, -1, keepdims=True)
    inverse = lax.rsqrt(spread + NORM_EPSILON)
    return centred * inverse, inverse


def dense_in_kernel(z, x_ref, gain_ref, shift_ref, w_ref, b_ref, sw_ref, st_ref, pw, pt, gw, gt):
    B, D, TC, TR = z.images, z.dim, z.cols, z.rows

    def one_row(i, carry):
        x = x_ref[i].astype(F32).reshape(TC * B, D)
        normed, _ = norm_parts(x)
        low = (normed * gain_ref[...] + shift_ref[...]).astype(BF16)
        proj = (mm(low, w_ref[...]) + b_ref[...]).reshape(TC, B, 3 * D)
        for j in range(TC):
            s, jj = divmod(j, SW)
            wide_at = pl.multiple_of((j * TR + i) * B, B)
            tall_at = pl.multiple_of(((s * TR + i) * SW + jj) * B, B)
            for n in range(3):
                pw[n, pl.ds(wide_at, B), :] = proj[j, :, n * D : n * D + HALF]
                pt[n, pl.ds(tall_at, B), :] = proj[j, :, n * D + HALF : (n + 1) * D]
        return carry

    lax.fori_loop(0, TR, one_row, 0)
    gw[...] = jnp.zeros_like(gw)
    gt[...] = jnp.zeros_like(gt)
    for b in range(B):
        for n in range(3):
            part = pw[n, pl.ds(b, z.pix, stride=B), :]
            for g in range(z.G):
                gw[b * z.G + g, n * z.pix : (n + 1) * z.pix, :] = part[:, g * z.hc : (g + 1) * z.hc]
            for s in range(z.stripes):
                part = pt[n, pl.ds(s * z.tall_own * B + b, z.tall_own, stride=B), :]
                at = (((b % z.tall_images) * z.stripes + s) * 3 + n) * z.tall_pad
                gt[b // z.tall_images, at : at + z.tall_own, :] = part
    sw_ref[...] = gw[...].astype(BF16)
    st_ref[...] = gt[...].astype(BF16)


def erf_parts(values):
    cdf = 0.5 * (1.0 + lax.erf(values * (0.5**0.5)))
    density = jnp.exp(-0.5 * values * values) * (1.0 / math.sqrt(2.0 * math.pi))
    return cdf, density


def dense_mid_kernel(
    z,
    off_ref,
    rw_ref,
    rt_ref,
    x_ref,
    ct_ref,
    hw_ref,
    pw_ref,
    pb_ref,
    gain_ref,
    shift_ref,
    w1_ref,
    b1_ref,
    w2_ref,
    b2_ref,
    y_ref,
    gres_ref,
    gw_ref,
    gt_ref,
    dpw_ref,
    dw1_ref,
    dw2_ref,
    vec_ref,
    db1_ref,
    mw,
    mt,
    gmw,
    gmt,
    gts,
):
    B, D, TC, TR = z.images, z.dim, z.cols, z.rows
    T = TC * B
    for b in range(B):
        parts = [
            rw_ref[b * z.G + g].astype(F32)[: z.pix] for g in range(z.G)
        ]
        mw[pl.ds(b, z.pix, stride=B), :] = parts[0] if z.G == 1 else jnp.concatenate(parts, -1)
    gts[...] = rt_ref[...].astype(F32)
    for b in range(B):
        for s in range(z.stripes):
            at = ((b % z.tall_images) * z.stripes + s) * z.tall_pad
            mt[pl.ds(s * z.tall_own * B + b, z.tall_own, stride=B), :] = gts[
                b // z.tall_images, at : at + z.tall_own, :
            ]
    dpw_ref[...] = jnp.zeros_like(dpw_ref)
    dw1_ref[...] = jnp.zeros_like(dw1_ref)
    dw2_ref[...] = jnp.zeros_like(dw2_ref)
    vec_ref[...] = jnp.zeros_like(vec_ref)
    db1_ref[...] = jnp.zeros_like(db1_ref)
    gmw[...] = jnp.zeros_like(gmw)
    row_start = off_ref[0]
    col_start = off_ref[1]
    below_cols = (lax.broadcasted_iota(jnp.int32, (TC, B, D), 0) + col_start) < hw_ref[1][None]

    def one_row(i, carry):
        x = x_ref[i].astype(F32).reshape(T, D)
        wide = []
        tall = []
        for j in range(TC):
            s, jj = divmod(j, SW)
            wide_at = pl.multiple_of((j * TR + i) * B, B)
            tall_at = pl.multiple_of(((s * TR + i) * SW + jj) * B, B)
            wide.append(mw[pl.ds(wide_at, B), :])
            tall.append(mt[pl.ds(tall_at, B), :])
        mixture = jnp.concatenate(
            [jnp.concatenate(wide, 0), jnp.concatenate(tall, 0)], -1
        ).astype(BF16)
        residual = x + (mm(mixture, pw_ref[...]) + pb_ref[...])
        n2, r2 = norm_parts(residual)
        act = (n2 * gain_ref[...] + shift_ref[...]).astype(BF16)
        pre = mm(act, w1_ref[...]) + b1_ref[...]
        cdf, density = erf_parts(pre)
        hidden = (pre * cdf).astype(BF16)
        slope = cdf + pre * density
        out = residual + (mm(hidden, w2_ref[...]) + b2_ref[...])
        y_ref[i] = out.astype(BF16).reshape(TC, B, D)
        below_rows = (i + row_start) < hw_ref[0][None]
        inside = jnp.logical_and(below_cols, below_rows)
        gy = jnp.where(inside, ct_ref[i].astype(F32), 0.0).reshape(T, D)
        gy_low = gy.astype(BF16)
        dw2_ref[...] += mm_tn(hidden, gy_low)
        gpre = (mm_nt(gy_low, w2_ref[...]) * slope).astype(BF16)
        dw1_ref[...] += mm_tn(act, gpre)
        db1 = jnp.sum(gpre.astype(F32), 0, keepdims=True)
        for k in range(db1.shape[1] // D):
            db1_ref[k : k + 1, :] += db1[:, k * D : (k + 1) * D]
        gact = mm_nt(gpre, w1_ref[...])
        g = gact * gain_ref[...]
        gres = gy + r2 * (
            g - jnp.mean(g, -1, keepdims=True) - n2 * jnp.mean(g * n2, -1, keepdims=True)
        )
        gres_ref[i] = gres.reshape(TC, B, D)
        gattn = gres.astype(BF16)
        dpw_ref[...] += mm_tn(mixture, gattn)
        gmix = mm_nt(gattn, pw_ref[...]).astype(BF16).astype(F32)
        vec_ref[0:1, :] += jnp.sum(gact * n2, 0, keepdims=True)
        vec_ref[1:2, :] += jnp.sum(gact, 0, keepdims=True)
        vec_ref[2:3, :] += jnp.sum(gattn.astype(F32), 0, keepdims=True)
        vec_ref[3:4, :] += jnp.sum(gy, 0, keepdims=True)
        vec_ref[4:5, :] += jnp.sum(gmix, 0, keepdims=True)
        gm3 = gmix.reshape(TC, B, D)
        for j in range(TC):
            s, jj = divmod(j, SW)
            wide_at = pl.multiple_of((j * TR + i) * B, B)
            tall_at = pl.multiple_of(((s * TR + i) * SW + jj) * B, B)
            gmw[pl.ds(wide_at, B), :] = gm3[j, :, :HALF]
            gmt[pl.ds(tall_at, B), :] = gm3[j, :, HALF:]
        return carry

    lax.fori_loop(0, TR, one_row, 0)
    gts[...] = jnp.zeros_like(gts)
    for b in range(B):
        part = gmw[pl.ds(b, z.wide_rows1, stride=B), :].astype(BF16)
        for g in range(z.G):
            gw_ref[b * z.G + g] = part[:, g * z.hc : (g + 1) * z.hc]
        for s in range(z.stripes):
            at = ((b % z.tall_images) * z.stripes + s) * z.tall_pad
            gts[b // z.tall_images, at : at + z.tall_own, :] = gmt[
                pl.ds(s * z.tall_own * B + b, z.tall_own, stride=B), :
            ]
    gt_ref[...] = gts[...].astype(BF16)


def dense_out_kernel(
    z, rw_ref, rt_ref, x_ref, gres_ref, gain_ref, shift_ref, w_ref, gin_ref, dw_ref, vec_ref, pw, pt, gw, gt
):
    B, D, TC, TR = z.images, z.dim, z.cols, z.rows
    T = TC * B
    gw[...] = rw_ref[...].astype(F32)
    gt[...] = rt_ref[...].astype(F32)
    for b in range(B):
        for n in range(3):
            parts = [
                gw[b * z.G + g, n * z.pix : (n + 1) * z.pix, :] for g in range(z.G)
            ]
            pw[n, pl.ds(b, z.pix, stride=B), :] = (
                parts[0] if z.G == 1 else jnp.concatenate(parts, -1)
            )
            for s in range(z.stripes):
                at = (((b % z.tall_images) * z.stripes + s) * 3 + n) * z.tall_pad
                pt[n, pl.ds(s * z.tall_own * B + b, z.tall_own, stride=B), :] = gt[
                    b // z.tall_images, at : at + z.tall_own, :
                ]
    dw_ref[...] = jnp.zeros_like(dw_ref)
    vec_ref[...] = jnp.zeros_like(vec_ref)

    def one_row(i, carry):
        x = x_ref[i].astype(F32).reshape(T, D)
        n1, r1 = norm_parts(x)
        low = (n1 * gain_ref[...] + shift_ref[...]).astype(BF16)
        lanes = []
        for n in range(3):
            wide = []
            tall = []
            for j in range(TC):
                s, jj = divmod(j, SW)
                wide_at = pl.multiple_of((j * TR + i) * B, B)
                tall_at = pl.multiple_of(((s * TR + i) * SW + jj) * B, B)
                wide.append(pw[n, pl.ds(wide_at, B), :])
                tall.append(pt[n, pl.ds(tall_at, B), :])
            lanes.append(jnp.concatenate(wide, 0))
            lanes.append(jnp.concatenate(tall, 0))
        gproj = jnp.concatenate(lanes, -1)
        vec_ref[2:3, :] += jnp.sum(gproj[:, :D], 0, keepdims=True)
        vec_ref[3:4, :] += jnp.sum(gproj[:, 2 * D :], 0, keepdims=True)
        gproj = gproj.astype(BF16)
        dw_ref[...] += mm_tn(low, gproj)
        gn = mm_nt(gproj, w_ref[...])
        vec_ref[0:1, :] += jnp.sum(gn * n1, 0, keepdims=True)
        vec_ref[1:2, :] += jnp.sum(gn, 0, keepdims=True)
        g = gn * gain_ref[...]
        gin = gres_ref[i].reshape(T, D) + r1 * (
            g - jnp.mean(g, -1, keepdims=True) - n1 * jnp.mean(g * n1, -1, keepdims=True)
        )
        gin_ref[i] = gin.reshape(TC, B, D)
        return carry

    lax.fori_loop(0, TR, one_row, 0)


def key_tiles(length, tile):
    return [(at, min(tile, length - at)) for at in range(0, length, tile)]


def token_places(start, count, lanes):
    token = (lax.broadcasted_iota(jnp.int32, (count, lanes), 0) + start).astype(F32)
    along = jnp.floor((token + 0.5) * (1.0 / SW))
    across = token - along * SW
    return along, across


def conv_forward(vpad, base, count, kernels, across):
    total = None
    for a in (-1, 0, 1):
        inner = None
        for l in (-1, 0, 1):
            term = kernels(a, l) * vpad[base + SW * l + a : base + SW * l + a + count, :]
            inner = term if inner is None else inner + term
        if a == -1:
            inner = jnp.where(across >= 1, inner, 0.0)
        if a == 1:
            inner = jnp.where(across <= SW - 2, inner, 0.0)
        total = inner if total is None else total + inner
    return total


def conv_backward(gpad, base, count, kernels, across):
    total = None
    for a in (-1, 0, 1):
        inner = None
        for l in (-1, 0, 1):
            at = base - SW * l - a
            term = kernels(a, l) * gpad[at : at + count, :]
            inner = term if inner is None else inner + term
        if a == -1:
            inner = jnp.where(across <= SW - 2, inner, 0.0)
        if a == 1:
            inner = jnp.where(across >= 1, inner, 0.0)
        total = inner if total is None else total + inner
    return total


def wide_tap(a, l):
    return 3 * (a + 1) + (l + 1)


def tall_tap(a, l):
    return 3 * (l + 1) + (a + 1)


def head_lanes(h, rows):
    lane = lax.broadcasted_iota(jnp.int32, (rows, HALF), 1)
    return jnp.logical_and(lane >= h * HEAD_DIM, lane < (h + 1) * HEAD_DIM)


def wide_assemble(z, recv_ref, stage, targets):
    for c in range(z.C):
        stage[:, : z.hc] = recv_ref[c].astype(F32)
        for n, target in enumerate(targets):
            target[c * z.pix : (c + 1) * z.pix, :] = stage[n * z.pix : (n + 1) * z.pix, :]


def wide_forward_kernel(
    z,
    lim_ref,
    recv_ref,
    lw_ref,
    lb_ref,
    out_ref,
    q_ref,
    k_ref,
    v_ref,
    bias_ref,
    qt_ref,
    ot_ref,
    lse_ref,
    qs,
    ks,
    vpad,
    stage,
    kcat,
    vt,
    ss,
    osum,
):
    L = z.wide_len
    LQ = qs.shape[0]
    QB = 256
    PAD = 8
    tiles = key_tiles(L, 256)
    across_limit = lim_ref[0]
    along_limit = lim_ref[1]
    empty = across_limit * along_limit == 0
    scale = jnp.where(empty, 1e-20, LOG2E * HEAD_DIM**-0.5)
    qs[...] = jnp.zeros_like(qs)
    ks[...] = jnp.zeros_like(ks)
    vpad[...] = jnp.zeros_like(vpad)
    if z.hc < HALF:
        stage[...] = jnp.zeros_like(stage)
    wide_assemble(z, recv_ref, stage, (qs, ks, vpad.at[PAD : PAD + L]))

    def flip(n, carry):
        at = pl.multiple_of(n * QB, QB)
        q = qs[pl.ds(at, QB), :]
        q_ref[pl.ds(at, QB), :] = q.astype(BF16)
        k_ref[pl.ds(at, QB), :] = ks[pl.ds(at, QB), :].astype(BF16)
        v = vpad[pl.ds(pl.multiple_of(at + PAD, 8), QB), :]
        v_ref[pl.ds(at, QB), :] = v.astype(BF16)
        qt_ref[:HALF, pl.ds(at, QB)] = q.T.astype(BF16)
        first = lax.broadcasted_iota(jnp.int32, (HALF, QB), 0) == 0
        qt_ref[HALF:, pl.ds(at, QB)] = jnp.where(first, 1.0, 0.0).astype(BF16)
        vt_full = v.T
        tail = lax.broadcasted_iota(jnp.int32, (16, QB), 0) == 0
        tail = jnp.where(tail, 1.0, 0.0)
        for h in range(z.wide_heads):
            vt[h, :, pl.ds(at, QB)] = jnp.concatenate(
                [vt_full[h * HEAD_DIM : (h + 1) * HEAD_DIM], tail], 0
            ).astype(BF16)
        along, across = token_places(at, QB, HALF)
        inside = jnp.logical_and(across < across_limit, along < along_limit)
        allowed = jnp.logical_or(inside, empty)
        lane = lax.broadcasted_iota(jnp.int32, (QB, HALF), 1) == 0
        bias = jnp.where(jnp.logical_and(lane, jnp.logical_not(allowed)), MASKED, 0.0).astype(BF16)
        bias_ref[pl.ds(at, QB), :] = bias
        kcat[pl.ds(at, QB), HALF:] = bias
        return carry

    lax.fori_loop(0, LQ // QB, flip, 0)

    def one_head(h, carry):
        lse_h = lse_ref.at[pl.ds(h, 1)]
        for at, size in tiles:
            kcat[at : at + size, :HALF] = jnp.where(
                head_lanes(h, size), ks[at : at + size, :], 0.0
            ).astype(BF16)

        def one_block(n, carry):
            at_q = pl.multiple_of(n * QB, QB)
            rhs = qt_ref[:, pl.ds(at_q, QB)]
            top = None
            for at, size in tiles:
                s = mm(kcat[at : at + size, :], rhs)
                ss[at : at + size, :] = s
                high = jnp.max(s.reshape(size // 8, 8, QB), 0)
                top = high if top is None else jnp.maximum(top, high)
            top = jnp.max(top, 0, keepdims=True)
            acc = None
            for at, size in tiles:
                p = jnp.exp2((ss[at : at + size, :] - top) * scale).astype(BF16)
                part = mm(vt[h, :, at : at + size], p)
                acc = part if acc is None else acc + part
            total = acc[HEAD_DIM : HEAD_DIM + 1]
            ot_ref[pl.ds(pl.multiple_of(h * HEAD_DIM, HEAD_DIM), HEAD_DIM), pl.ds(at_q, QB)] = acc[
                :HEAD_DIM
            ] * (1.0 / total)
            lse_h[:, pl.ds(at_q, QB)] = top * scale + jnp.log2(total)
            return carry

        lax.fori_loop(0, LQ // QB, one_block, 0)
        return carry

    lax.fori_loop(0, z.wide_heads, one_head, 0)

    def mask_values(n, carry):
        at = pl.multiple_of(n * QB, QB)
        along, across = token_places(at, QB, HALF)
        inside = jnp.logical_and(across < across_limit, along < along_limit)
        rows = pl.ds(pl.multiple_of(at + PAD, 8), QB)
        vpad[rows, :] = jnp.where(inside, vpad[rows, :], 0.0)
        return carry

    lax.fori_loop(0, LQ // QB, mask_values, 0)

    def finish(n, carry):
        at = pl.multiple_of(n * QB, QB)
        along, across = token_places(at, QB, HALF)
        osum[pl.ds(at, QB), :] = ot_ref[:, pl.ds(at, QB)].T if z.hc == HALF else jnp.concatenate(
            [ot_ref[:, pl.ds(at, QB)].T, jnp.zeros((QB, HALF - z.hc), F32)], -1
        )
        return carry

    lax.fori_loop(0, LQ // QB, finish, 0)

    def taps(a, l):
        t = wide_tap(a, l)
        return lw_ref[t : t + 1, :]

    for at, size in key_tiles(L, 224):
        along, across = token_places(at, size, HALF)
        lepe = conv_forward(vpad, at + PAD, size, taps, across)
        osum[at : at + size, :] = osum[at : at + size, :] + lepe + lb_ref[...]
    for c in range(z.C):
        out_ref[c] = osum[c * z.pix : c * z.pix + z.wide_rows1, : z.hc].astype(BF16)


def wide_backward_kernel(
    z,
    lim_ref,
    recv_ref,
    lw_ref,
    q_ref,
    k_ref,
    v_ref,
    bias_ref,
    qt_ref,
    ot_ref,
    lse_ref,
    out_ref,
    dlw_ref,
    gpad,
    vpad,
    dot,
    delta,
    kcat,
    vh,
    qh,
    gh,
    kt,
    dq,
    dqt,
    dk,
    dv,
    stage,
):
    L = z.wide_len
    LQ = q_ref.shape[0]
    QB = 256
    PAD = 8
    tiles = key_tiles(L, 256)
    across_limit = lim_ref[0]
    along_limit = lim_ref[1]
    empty = across_limit * along_limit == 0
    scale = jnp.where(empty, 1e-20, LOG2E * HEAD_DIM**-0.5)
    gpad[...] = jnp.zeros_like(gpad)
    vpad[...] = jnp.zeros_like(vpad)
    dk[...] = jnp.zeros_like(dk)
    dv[...] = jnp.zeros_like(dv)
    stage[...] = jnp.zeros_like(stage)
    for c in range(z.C):
        stage[: z.wide_rows1, : z.hc] = recv_ref[c].astype(F32)
        gpad[PAD + c * z.pix : PAD + (c + 1) * z.pix, :] = stage[: z.pix, :]

    def flip(n, carry):
        at = pl.multiple_of(n * QB, QB)
        rows = pl.ds(pl.multiple_of(at + PAD, 8), QB)
        g = gpad[rows, :].T
        dot[:, pl.ds(at, QB)] = g.astype(BF16)
        prod = g[: z.hc] * ot_ref[:, pl.ds(at, QB)]
        for h in range(z.wide_heads):
            delta[h : h + 1, pl.ds(at, QB)] = jnp.sum(
                prod[h * HEAD_DIM : (h + 1) * HEAD_DIM], 0, keepdims=True
            )
        k = k_ref[pl.ds(at, QB), :].astype(F32)
        kt[:, pl.ds(at, QB)] = k.T.astype(BF16)
        kcat[pl.ds(at, QB), HALF:] = bias_ref[pl.ds(at, QB), :]
        along, across = token_places(at, QB, HALF)
        inside = jnp.logical_and(across < across_limit, along < along_limit)
        vpad[rows, :] = jnp.where(inside, v_ref[pl.ds(at, QB), :].astype(F32), 0.0)
        return carry

    lax.fori_loop(0, LQ // QB, flip, 0)

    def one_head(h, carry):
        def split(n, carry):
            at = pl.multiple_of(n * QB, QB)
            keep = head_lanes(h, QB)
            rows = pl.ds(at, QB)
            kcat[rows, :HALF] = jnp.where(keep, k_ref[rows, :].astype(F32), 0.0).astype(BF16)
            vh[rows, :] = jnp.where(keep, v_ref[rows, :].astype(F32), 0.0).astype(BF16)
            qh[rows, :] = jnp.where(keep, q_ref[rows, :].astype(F32), 0.0).astype(BF16)
            gh[rows, :] = jnp.where(
                keep, gpad[pl.ds(pl.multiple_of(at + PAD, 8), QB), :], 0.0
            ).astype(BF16)
            return carry

        lax.fori_loop(0, LQ // QB, split, 0)
        head_rows = pl.ds(pl.multiple_of(h * HEAD_DIM, HEAD_DIM), HEAD_DIM)

        def one_block(n, carry):
            at_q = pl.multiple_of(n * QB, QB)
            cols = pl.ds(at_q, QB)
            q_rhs = qt_ref[:, cols]
            g_rhs = dot[:, cols]
            lse = lse_ref[pl.ds(h, 1), cols]
            dlt = delta[pl.ds(h, 1), cols]
            q_low = qh[cols, :]
            g_low = gh[cols, :]
            acc = None
            for at, size in tiles:
                s = mm(kcat[at : at + size, :], q_rhs)
                p = jnp.exp2(s * scale - lse)
                dp = mm(vh[at : at + size, :], g_rhs)
                ds = (p * (dp - dlt)).astype(BF16)
                dv[at : at + size, :] += mm(p.astype(BF16), g_low)
                dk[at : at + size, :] += mm(ds, q_low)
                part = mm(kt[head_rows, at : at + size], ds)
                acc = part if acc is None else acc + part
            dqt[head_rows, cols] = acc
            return carry

        lax.fori_loop(0, LQ // QB, one_block, 0)
        return carry

    lax.fori_loop(0, z.wide_heads, one_head, 0)
    norm = HEAD_DIM**-0.5

    def finish(n, carry):
        at = pl.multiple_of(n * QB, QB)
        dq[pl.ds(at, QB), :] = dqt[:, pl.ds(at, QB)].T * norm
        return carry

    lax.fori_loop(0, LQ // QB, finish, 0)

    def taps(a, l):
        t = wide_tap(a, l)
        return lw_ref[t : t + 1, :]

    sums = {}
    for at, size in key_tiles(L, 224):
        along, across = token_places(at, size, HALF)
        inside = jnp.logical_and(across < across_limit, along < along_limit)
        lepe = conv_backward(gpad, at + PAD, size, taps, across)
        dv[at : at + size, :] += jnp.where(inside, lepe, 0.0)
        dk[at : at + size, :] = dk[at : at + size, :] * norm
        add_kernel_sums(sums, gpad, vpad, at + PAD, size, across, wide_tap)
    dlw_ref[...] = jnp.zeros_like(dlw_ref)
    for t, value in sums.items():
        dlw_ref[t : t + 1, :] = jnp.sum(value, 0, keepdims=True)
    stage[...] = jnp.zeros_like(stage)
    for c in range(z.C):
        own = slice(c * z.pix, (c + 1) * z.pix)
        stage[: z.pix, :] = dq[own, :]
        stage[z.pix : 2 * z.pix, :] = dk[own, :]
        stage[2 * z.pix : 3 * z.pix, :] = dv[own, :]
        out_ref[c] = stage[:, : z.hc].astype(BF16)


def add_kernel_sums(sums, gpad, vpad, base, size, across, tap):
    g = gpad[base : base + size, :]
    for a in (-1, 0, 1):
        ga = g
        if a == -1:
            ga = jnp.where(across >= 1, g, 0.0)
        if a == 1:
            ga = jnp.where(across <= SW - 2, g, 0.0)
        for l in (-1, 0, 1):
            at = base + SW * l + a
            term = (ga * vpad[at : at + size, :]).reshape(size // 8, 8, HALF).sum(0)
            t = tap(a, l)
            sums[t] = sums[t] + term if t in sums else term


def tall_prepare(z, p, lim_ref, kstack, L):
    across_limit = lim_ref[0, p]
    along_limit = lim_ref[1, p]
    empty = across_limit * along_limit == 0
    scale = jnp.where(empty, 1e-20, LOG2E * HEAD_DIM**-0.5)
    along, across = token_places(0, L, HALF)
    inside = jnp.logical_and(across < across_limit, along < along_limit)
    allowed = jnp.logical_or(inside, empty)
    token = lax.broadcasted_iota(jnp.int32, (L, HALF), 0)
    allowed = jnp.logical_and(allowed, token < z.tall_len)
    lane = lax.broadcasted_iota(jnp.int32, (L, HALF), 1) == 0
    bias = jnp.where(jnp.logical_and(lane, jnp.logical_not(allowed)), MASKED, 0.0).astype(BF16)
    return inside, across, scale, bias


def tall_pull(z, source, p, per, n, target, base):
    for r in range(z.R):
        at = pl.multiple_of((p * per + n) * z.tall_pad, 8)
        block = source[r, pl.ds(at, z.tall_pad), :]
        target[base + r * z.tall_own : base + (r + 1) * z.tall_own, :] = block[: z.tall_own]


def tall_push(z, source, p, per, n, target, base=0):
    for r in range(z.R):
        at = pl.multiple_of((p * per + n) * z.tall_pad, 8)
        target[r, pl.ds(at, z.tall_pad), :] = source[
            base + r * z.tall_own : base + r * z.tall_own + z.tall_pad, :
        ]


def tall_scores(z, k, q, bias, kstack, L):
    for h in range(BRANCH_HEADS):
        kstack[h * L : (h + 1) * L, :HALF] = jnp.where(head_lanes(h, L), k, 0.0).astype(BF16)
        kstack[h * L : (h + 1) * L, HALF:] = bias
    first = lax.broadcasted_iota(jnp.int32, (HALF, L), 0) == 0
    qt = jnp.concatenate([q.T, jnp.where(first, 1.0, 0.0)], 0).astype(BF16)
    return mm(kstack[...], qt)


def tall_forward_kernel(
    z, lim_ref, recv_ref, lw_ref, lb_ref, out_ref, ot_ref, lse_ref, src, dst, qs, ks, vs, vpad, osum, kstack
):
    L = qs.shape[0]
    PAD = 8
    src[...] = recv_ref[...].astype(F32)
    qs[...] = jnp.zeros_like(qs)
    ks[...] = jnp.zeros_like(ks)
    vs[...] = jnp.zeros_like(vs)
    vpad[...] = jnp.zeros_like(vpad)
    osum[...] = jnp.zeros_like(osum)

    def taps(a, l):
        t = tall_tap(a, l)
        return lw_ref[t : t + 1, :]

    def one_stripe(p, carry):
        for n, target in enumerate((qs, ks, vs)):
            tall_pull(z, src, p, 3, n, target, 0)
        inside, across, scale, bias = tall_prepare(z, p, lim_ref, kstack, L)
        v = vs[...]
        vt_full = v.T
        tail = lax.broadcasted_iota(jnp.int32, (16, L), 0) == 0
        tail = jnp.where(tail, 1.0, 0.0)
        s = tall_scores(z, ks[...], qs[...], bias, kstack, L)
        outs = []
        for h in range(BRANCH_HEADS):
            sh = s[h * L : (h + 1) * L]
            top = jnp.max(sh, 0, keepdims=True)
            e = jnp.exp2((sh - top) * scale).astype(BF16)
            vt = jnp.concatenate([vt_full[h * HEAD_DIM : (h + 1) * HEAD_DIM], tail], 0).astype(BF16)
            acc = mm(vt, e)
            total = acc[HEAD_DIM : HEAD_DIM + 1]
            outs.append(acc[:HEAD_DIM] * (1.0 / total))
            lse_ref[p, h : h + 1, :] = top * scale + jnp.log2(total)
        ot = jnp.concatenate(outs, 0)
        ot_ref[p] = ot
        vpad[PAD : PAD + L, :] = jnp.where(inside, v, 0.0)
        lepe = conv_forward(vpad, PAD, L, taps, across)
        osum[:L, :] = ot.T + lepe + lb_ref[...]
        tall_push(z, osum, p, 1, 0, dst)
        return carry

    lax.fori_loop(0, z.tall_slots, one_stripe, 0)
    out_ref[...] = dst[...].astype(BF16)


def tall_backward_kernel(
    z,
    lim_ref,
    recv_ref,
    grad_ref,
    lw_ref,
    ot_ref,
    lse_ref,
    out_ref,
    dlw_ref,
    src,
    gsrc,
    dst,
    qs,
    ks,
    vs,
    gpad,
    vpad,
    stage,
    kstack,
):
    L = qs.shape[0]
    PAD = 8
    src[...] = recv_ref[...].astype(F32)
    gsrc[...] = grad_ref[...].astype(F32)
    for ref in (qs, ks, vs, gpad, vpad, stage):
        ref[...] = jnp.zeros_like(ref)
    dlw_ref[...] = jnp.zeros_like(dlw_ref)
    norm = HEAD_DIM**-0.5

    def taps(a, l):
        t = tall_tap(a, l)
        return lw_ref[t : t + 1, :]

    def one_stripe(p, carry):
        for n, target in enumerate((qs, ks, vs)):
            tall_pull(z, src, p, 3, n, target, 0)
        tall_pull(z, gsrc, p, 1, 0, gpad, PAD)
        inside, across, scale, bias = tall_prepare(z, p, lim_ref, kstack, L)
        q, k, v, g = qs[...], ks[...], vs[...], gpad[PAD : PAD + L, :]
        s = tall_scores(z, k, q, bias, kstack, L)
        gt = g.T
        gt_low = gt.astype(BF16)
        prod = gt * ot_ref[p]
        kt = k.T.astype(BF16)
        lse = lse_ref[p]
        vstack = jnp.concatenate(
            [jnp.where(head_lanes(h, L), v, 0.0) for h in range(BRANCH_HEADS)], 0
        ).astype(BF16)
        dp = mm(vstack, gt_low)
        dv = None
        dk = None
        dqs = []
        for h in range(BRANCH_HEADS):
            keep = head_lanes(h, L)
            own = slice(h * HEAD_DIM, (h + 1) * HEAD_DIM)
            rows = slice(h * L, (h + 1) * L)
            delta = jnp.sum(prod[own], 0, keepdims=True)
            w = jnp.exp2(s[rows] * scale - lse[h : h + 1])
            ds = (w * (dp[rows] - delta)).astype(BF16)
            dv_h = mm(w.astype(BF16), jnp.where(keep, g, 0.0).astype(BF16))
            dk_h = mm(ds, jnp.where(keep, q, 0.0).astype(BF16))
            dv = dv_h if dv is None else dv + dv_h
            dk = dk_h if dk is None else dk + dk_h
            dqs.append(mm(kt[own], ds))
        dq = jnp.concatenate(dqs, 0).T * norm
        vpad[PAD : PAD + L, :] = jnp.where(inside, v, 0.0)
        lepe = conv_backward(gpad, PAD, L, taps, across)
        sums = {}
        add_kernel_sums(sums, gpad, vpad, PAD, L, across, tall_tap)
        for t, value in sums.items():
            dlw_ref[t : t + 1, :] += jnp.sum(value, 0, keepdims=True)
        for n, value in enumerate((dq, dk * norm, dv + jnp.where(inside, lepe, 0.0))):
            stage[n, :L, :] = value
            tall_push(z, stage.at[n], p, 3, n, dst)
        return carry

    lax.fori_loop(0, z.tall_slots, one_stripe, 0)
    out_ref[...] = dst[...].astype(BF16)


def exchange_kernel(z, wide_ref, tall_ref, wide_out, tall_out, wsend, wrecv, tsend, trecv, local):
    C, R = z.C, z.R
    col = lax.axis_index("col")
    row = lax.axis_index("row")
    barrier = pltpu.get_barrier_semaphore()
    for k in range(1, C):
        pl.semaphore_signal(
            barrier, inc=1, device_id=(row, lax.rem(col + k, C)), device_id_type=MESH
        )
    for k in range(1, R):
        pl.semaphore_signal(
            barrier, inc=1, device_id=(lax.rem(row + k, R), col), device_id_type=MESH
        )
    pl.semaphore_wait(barrier, C - 1 + R - 1)
    copies = []
    for k in range(1, R):
        target = lax.rem(row + k, R)
        copies.append(
            pltpu.make_async_remote_copy(
                src_ref=tall_ref.at[target],
                dst_ref=tall_out.at[row],
                send_sem=tsend.at[k],
                recv_sem=trecv.at[k],
                device_id=(target, col),
                device_id_type=MESH,
            )
        )
    for k in range(1, C):
        target = lax.rem(col + k, C)
        copies.append(
            pltpu.make_async_remote_copy(
                src_ref=wide_ref.at[target],
                dst_ref=wide_out.at[col],
                send_sem=wsend.at[k],
                recv_sem=wrecv.at[k],
                device_id=(row, target),
                device_id_type=MESH,
            )
        )
    for copy in copies:
        copy.start()
    own = [
        pltpu.make_async_copy(wide_ref.at[col], wide_out.at[col], local.at[0]),
        pltpu.make_async_copy(tall_ref.at[row], tall_out.at[row], local.at[1]),
    ]
    for copy in own:
        copy.start()
    for copy in own:
        copy.wait()
    for copy in copies:
        copy.wait()


def exchange(z, wide, tall, collective_id):
    spec = pl.BlockSpec(memory_space=pl.ANY)
    dma = pltpu.SemaphoreType.DMA
    return pl.pallas_call(
        functools.partial(exchange_kernel, z),
        out_shape=(
            jax.ShapeDtypeStruct(wide.shape, wide.dtype),
            jax.ShapeDtypeStruct(tall.shape, tall.dtype),
        ),
        in_specs=[spec, spec],
        out_specs=(spec, spec),
        scratch_shapes=[dma((z.C,)), dma((z.C,)), dma((z.R,)), dma((z.R,)), dma((2,))],
        compiler_params=pltpu.CompilerParams(collective_id=collective_id, has_side_effects=True),
        name=f"exchange_{collective_id}",
    )(wide, tall)


def split_of(rows, lanes, parts):
    for by_rows in range(parts, 0, -1):
        if parts % by_rows == 0:
            by_lanes = parts // by_rows
            if rows % (16 * by_rows) == 0 and lanes % (128 * by_lanes) == 0:
                return by_rows, by_lanes
    raise ValueError("no split")


def reduce_stages(z):
    return [(2, 1), (2, 2), (z.R, None), (z.C // 4, 4)]


def reduce_plan(z, lanes):
    rows = z.dim
    plan = []
    for members, stride in reduce_stages(z):
        a, b = split_of(rows, lanes, members)
        rows, lanes = rows // a, lanes // b
        plan.append((members, stride, a, b, rows, lanes))
    return plan


def reduce_width(z, lanes):
    while True:
        try:
            reduce_plan(z, lanes)
            return lanes
        except ValueError:
            lanes += 128


def reduce_kernel(z, plan, dqkv_ref, dproj_ref, dfc1_ref, dfc2_ref, small_ref, *refs):
    D = z.dim
    n = len(plan)
    outs, refs = refs[:5], refs[5:]
    oqkv, oproj, ofc1, ofc2, osmall = outs
    full, refs = refs[0], refs[1:]
    recvs, refs = refs[:n], refs[n:]
    held, refs = refs[:n], refs[n:]
    gathers, refs = refs[:n], refs[n:]
    smalls, refs = refs[:n], refs[n:]
    ssem, rsem, gsem, hsem, vsem, wsem = refs
    col = lax.axis_index("col")
    row = lax.axis_index("row")

    def place(stage):
        members, stride = plan[stage][:2]
        if stride is None:
            return row
        return lax.rem(col // stride, members)

    def peer(stage, k):
        members, stride = plan[stage][:2]
        at = lax.rem(place(stage) + k, members)
        if stride is None:
            return at, (at, col)
        return at, (row, col + (at - place(stage)) * stride)

    barrier = pltpu.get_barrier_semaphore()
    count = 0
    for stage in range(n):
        for k in range(1, plan[stage][0]):
            pl.semaphore_signal(barrier, inc=1, device_id=peer(stage, k)[1], device_id_type=MESH)
            count += 1
    pl.semaphore_wait(barrier, count)
    lanes = full.shape[1]
    at = 0
    for ref in (dqkv_ref, dproj_ref, dfc1_ref):
        width = ref.shape[1]
        full[:, at : at + width] = ref[...].astype(BF16)
        at += width
    for k in range(dfc2_ref.shape[0] // D):
        full[:, at : at + D] = dfc2_ref[k * D : (k + 1) * D, :].astype(BF16)
        at += D
    if at < lanes:
        full[:, at:] = jnp.zeros((D, lanes - at), BF16)

    def window(ref, stage, index):
        members, stride, a, b, rows, width = plan[stage]
        r0 = pl.multiple_of((index // b) * rows, 16)
        l0 = pl.multiple_of(lax.rem(index, b) * width, 128)
        return ref.at[pl.ds(r0, rows), pl.ds(l0, width)]

    current = full
    small_now = small_ref
    for stage in range(n):
        members = plan[stage][0]
        me = place(stage)
        copies = []
        for k in range(1, members):
            index, device = peer(stage, k)
            copies.append(
                pltpu.make_async_remote_copy(
                    src_ref=window(current, stage, index),
                    dst_ref=recvs[stage].at[me],
                    send_sem=ssem.at[stage, k],
                    recv_sem=rsem.at[stage, k],
                    device_id=device,
                    device_id_type=MESH,
                )
            )
            copies.append(
                pltpu.make_async_remote_copy(
                    src_ref=small_now,
                    dst_ref=smalls[stage].at[me],
                    send_sem=vsem.at[stage, k],
                    recv_sem=wsem.at[stage, k],
                    device_id=device,
                    device_id_type=MESH,
                )
            )
        for copy in copies:
            copy.start()
        smalls[stage][me] = small_now[...]
        recvs[stage][me] = window(current, stage, me)[...]
        for copy in copies:
            copy.wait()
        total = recvs[stage][0].astype(F32)
        small = smalls[stage][0]
        for k in range(1, members):
            total = total + recvs[stage][k].astype(F32)
            small = small + smalls[stage][k]
        held[stage][...] = total.astype(BF16)
        osmall[...] = small
        current = held[stage]
        if stage + 1 < n:
            smalls[stage][0] = small
            small_now = smalls[stage].at[0]
    for stage in range(n - 1, -1, -1):
        members = plan[stage][0]
        me = place(stage)
        copies = []
        for k in range(1, members):
            index, device = peer(stage, k)
            copies.append(
                pltpu.make_async_remote_copy(
                    src_ref=current,
                    dst_ref=window(gathers[stage], stage, me),
                    send_sem=gsem.at[stage, k],
                    recv_sem=hsem.at[stage, k],
                    device_id=device,
                    device_id_type=MESH,
                )
            )
        for copy in copies:
            copy.start()
        window(gathers[stage], stage, me)[...] = current[...]
        for copy in copies:
            copy.wait()
        current = gathers[stage]
    at = 0
    for ref in (oqkv, oproj, ofc1):
        width = ref.shape[1]
        ref[...] = current[:, at : at + width].astype(F32)
        at += width
    for k in range(ofc2.shape[0] // D):
        ofc2[k * D : (k + 1) * D, :] = current[:, at : at + D].astype(F32)
        at += D


def reduce_all(z, dqkv, dproj, dfc1, dfc2, small, collective_id):
    arrays = (dqkv, dproj, dfc1, dfc2, small)
    lanes = reduce_width(z, sum(a.size for a in arrays[:4]) // z.dim)
    plan = reduce_plan(z, lanes)
    vmem = pl.BlockSpec(memory_space=pltpu.VMEM)
    dma = pltpu.SemaphoreType.DMA
    most = max(step[0] for step in plan)
    gathers = [pltpu.VMEM((z.dim, lanes), BF16)]
    gathers += [pltpu.VMEM((step[4], step[5]), BF16) for step in plan[:-1]]
    return pl.pallas_call(
        functools.partial(reduce_kernel, z, plan),
        out_shape=tuple(jax.ShapeDtypeStruct(a.shape, F32) for a in arrays),
        in_specs=[vmem] * 5,
        out_specs=(vmem,) * 5,
        scratch_shapes=[pltpu.VMEM((z.dim, lanes), BF16)]
        + [pltpu.VMEM((step[0], step[4], step[5]), BF16) for step in plan]
        + [pltpu.VMEM((step[4], step[5]), BF16) for step in plan]
        + gathers
        + [pltpu.VMEM((step[0],) + small.shape, F32) for step in plan]
        + [dma((len(plan), most)) for _ in range(6)],
        compiler_params=pltpu.CompilerParams(
            collective_id=collective_id, has_side_effects=True, vmem_limit_bytes=VMEM_LIMIT
        ),
        name="reduce_all",
    )(*arrays)


def local_call(kernel, z, name, outs, scratch, scalars, arrays):
    vmem = pl.BlockSpec(memory_space=pltpu.VMEM)
    smem = pl.BlockSpec(memory_space=pltpu.SMEM)
    return pl.pallas_call(
        functools.partial(kernel, z),
        out_shape=tuple(jax.ShapeDtypeStruct(shape, kind) for shape, kind in outs),
        in_specs=[smem] * len(scalars) + [vmem] * len(arrays),
        out_specs=(vmem,) * len(outs),
        scratch_shapes=[pltpu.VMEM(shape, kind) for shape, kind in scratch],
        compiler_params=pltpu.CompilerParams(vmem_limit_bytes=VMEM_LIMIT),
        name=name,
    )(*scalars, *arrays)


def per_device(
    mesh,
    features,
    heights,
    widths,
    norm1_gain,
    norm1_shift,
    qkv_weight,
    query_bias,
    value_bias,
    lepe_weight,
    lepe_bias,
    proj_weight,
    proj_bias,
    norm2_gain,
    norm2_shift,
    fc1_weight,
    fc1_bias,
    fc2_weight,
    fc2_bias,
    cotangent,
):
    z = Sizes(mesh, features.shape)
    B, D, TC, TR = z.images, z.dim, z.cols, z.rows
    col = lax.axis_index("col")
    row = lax.axis_index("row")
    row_start = row * TR
    col_start = col * TC
    x = features.transpose(1, 2, 0, 3)
    ct = cotangent.transpose(1, 2, 0, 3)
    qkv_bias = jnp.concatenate([query_bias, jnp.zeros_like(query_bias), value_bias])
    line = lambda v: v.reshape(1, -1)
    FF = fc1_weight.shape[1]

    image = col // z.G
    wide_lim = jnp.stack(
        [jnp.clip(heights[image] - row_start, 0, TR), jnp.clip(widths[image], 0, z.C * TC)]
    )
    own_images = row * z.tall_images + jnp.arange(z.tall_images)
    stripe_start = col_start + SW * jnp.arange(z.stripes)
    tall_across = jnp.clip(widths[own_images][:, None] - stripe_start[None], 0, SW)
    tall_along = jnp.broadcast_to(
        jnp.clip(heights[own_images], 0, z.R * TR)[:, None], tall_across.shape
    )
    tall_lim = jnp.stack([tall_across.reshape(-1), tall_along.reshape(-1)])
    part = lax.rem(col, z.G)
    pad_taps = lambda w: jnp.pad(w, ((0, 16 - w.shape[0]), (0, HALF - w.shape[1])))
    wide_taps = pad_taps(lax.dynamic_slice_in_dim(lepe_weight[:, :HALF], part * z.hc, z.hc, 1))
    wide_tap_bias = jnp.pad(
        lax.dynamic_slice_in_dim(lepe_bias[:HALF], part * z.hc, z.hc, 0), (0, HALF - z.hc)
    )
    tall_taps = pad_taps(lepe_weight[:, HALF:])
    tall_tap_bias = lepe_bias[HALF:]

    wide3 = (z.C, z.wide_rows3, z.hc)
    wide1 = (z.C, z.wide_rows1, z.hc)
    tall3 = (z.R, z.tall_rows3, HALF)
    tall1 = (z.R, z.tall_rows1, HALF)
    flat = up(z.tokens, 16 * B) + 16 * B

    send_wide, send_tall = local_call(
        dense_in_kernel,
        z,
        "dense_in",
        [(wide3, BF16), (tall3, BF16)],
        [((3, flat, HALF), F32), ((3, flat, HALF), F32), (wide3, F32), (tall3, F32)],
        [],
        [x, line(norm1_gain), line(norm1_shift), qkv_weight, line(qkv_bias)],
    )
    wide_qkv, tall_qkv = exchange(z, send_wide, send_tall, 0)

    LT = up(z.tall_len, 128)
    tall_out, tall_ot, tall_lse = local_call(
        tall_forward_kernel,
        z,
        "tall_forward",
        [(tall1, BF16), ((z.tall_slots, HALF, LT), F32), ((z.tall_slots, 8, LT), F32)],
        [
            (tall3, F32),
            (tall1, F32),
            ((LT, HALF), F32),
            ((LT, HALF), F32),
            ((LT, HALF), F32),
            ((LT + 16, HALF), F32),
            ((LT + 16, HALF), F32),
            ((BRANCH_HEADS * LT, 2 * HALF), BF16),
        ],
        [tall_lim],
        [tall_qkv, tall_taps, line(tall_tap_bias)],
    )
    L = z.wide_len
    LQ = up(L, 256)
    wide_out, q, k, v, bias, qt, ot, lse = local_call(
        wide_forward_kernel,
        z,
        "wide_forward",
        [
            (wide1, BF16),
            ((LQ, HALF), BF16),
            ((LQ, HALF), BF16),
            ((LQ, HALF), BF16),
            ((LQ, HALF), BF16),
            ((2 * HALF, LQ), BF16),
            ((z.hc, LQ), F32),
            ((8, LQ), F32),
        ],
        [
            ((LQ, HALF), F32),
            ((LQ, HALF), F32),
            ((LQ + 16, HALF), F32),
            ((z.wide_rows3, HALF), F32),
            ((LQ, 2 * HALF), BF16),
            ((z.wide_heads, HEAD_DIM + 16, LQ), BF16),
            ((LQ, 256), F32),
            ((LQ, HALF), F32),
        ],
        [wide_lim],
        [wide_qkv, wide_taps, line(wide_tap_bias)],
    )
    back_wide, back_tall = exchange(z, wide_out, tall_out, 1)

    limits = jnp.broadcast_to(jnp.stack([heights, widths])[:, :, None], (2, B, D))
    y, gres, gmix_wide, gmix_tall, dproj, dfc1, dfc2, vec_mid, db1 = local_call(
        dense_mid_kernel,
        z,
        "dense_mid",
        [
            ((TR, TC, B, D), BF16),
            ((TR, TC, B, D), F32),
            (wide1, BF16),
            (tall1, BF16),
            ((D, D), F32),
            ((D, FF), F32),
            ((FF, D), F32),
            ((8, D), F32),
            ((8, D), F32),
        ],
        [((flat, HALF), F32)] * 4 + [(tall1, F32)],
        [jnp.stack([row_start, col_start])],
        [
            back_wide,
            back_tall,
            x,
            ct,
            limits,
            proj_weight,
            line(proj_bias),
            line(norm2_gain),
            line(norm2_shift),
            fc1_weight,
            line(fc1_bias),
            fc2_weight,
            line(fc2_bias),
        ],
    )
    grad_wide, grad_tall = exchange(z, gmix_wide, gmix_tall, 2)

    dtall, dtall_taps = local_call(
        tall_backward_kernel,
        z,
        "tall_backward",
        [(tall3, BF16), ((16, HALF), F32)],
        [
            (tall3, F32),
            (tall1, F32),
            (tall3, F32),
            ((LT, HALF), F32),
            ((LT, HALF), F32),
            ((LT, HALF), F32),
            ((LT + 16, HALF), F32),
            ((LT + 16, HALF), F32),
            ((3, LT + 16, HALF), F32),
            ((BRANCH_HEADS * LT, 2 * HALF), BF16),
        ],
        [tall_lim],
        [tall_qkv, grad_tall, tall_taps, tall_ot, tall_lse],
    )
    dwide, dwide_taps = local_call(
        wide_backward_kernel,
        z,
        "wide_backward",
        [(wide3, BF16), ((16, HALF), F32)],
        [
            ((LQ + 16, HALF), F32),
            ((LQ + 16, HALF), F32),
            ((HALF, LQ), BF16),
            ((8, LQ), F32),
            ((LQ, 2 * HALF), BF16),
            ((LQ, HALF), BF16),
            ((LQ, HALF), BF16),
            ((LQ, HALF), BF16),
            ((HALF, LQ), BF16),
            ((LQ, HALF), F32),
            ((HALF, LQ), F32),
            ((LQ, HALF), F32),
            ((LQ, HALF), F32),
            ((z.wide_rows3, HALF), F32),
        ],
        [wide_lim],
        [grad_wide, wide_taps, q, k, v, bias, qt, ot, lse],
    )
    got_wide, got_tall = exchange(z, dwide, dtall, 3)

    grad_in, dqkv, vec_out = local_call(
        dense_out_kernel,
        z,
        "dense_out",
        [((TR, TC, B, D), F32), ((D, 3 * D), F32), ((8, D), F32)],
        [((3, flat, HALF), F32), ((3, flat, HALF), F32), (wide3, F32), (tall3, F32)],
        [],
        [got_wide, got_tall, x, gres, line(norm1_gain), line(norm1_shift), qkv_weight],
    )
    own_taps = dwide_taps[:, : z.hc]
    if z.G > 1:
        own_taps = lax.dynamic_update_slice(
            jnp.zeros((16, HALF), F32), own_taps, (0, part * z.hc)
        )
    small = jnp.concatenate(
        [vec_mid, vec_out, jnp.concatenate([own_taps, dtall_taps], -1), db1], 0
    )
    dqkv, dproj, dfc1, dfc2, small = reduce_all(z, dqkv, dproj, dfc1, dfc2, small, 4)
    return (
        y.transpose(2, 0, 1, 3),
        grad_in.transpose(2, 0, 1, 3),
        small[8],
        small[9],
        dqkv,
        small[10],
        small[11],
        small[16:25],
        small[4],
        dproj,
        small[2],
        small[0],
        small[1],
        dfc1,
        small[32 : 32 + FF // D].reshape(-1),
        dfc2,
        small[3],
    )


def solution(mesh):
    image = P(None, "row", "col", None)
    return jax.shard_map(
        functools.partial(per_device, mesh),
        mesh=mesh,
        in_specs=(image,) + (P(),) * 17 + (image,),
        out_specs=(image, image) + (P(),) * 15,
        check_vma=False,
    )
```

```python
import functools
import math

import jax
import jax.numpy as jnp
from jax import lax
from jax.experimental import pallas as pl
from jax.experimental.pallas import tpu as pltpu
from jax.sharding import PartitionSpec as P

HEADS = 8
SW = 7
BRANCH_HEADS = HEADS // 2
HALF = 128
HEAD_DIM = 32
NORM_EPSILON = 1e-05
MASKED = -1e30
LOG2E = math.log2(math.e)
QB = 256
PAD = 8
VMEM_LIMIT = 56 * 1024 * 1024
MESH = pl.DeviceIdType.MESH
F32 = jnp.float32
BF16 = jnp.bfloat16
NT = (((1,), (1,)), ((), ()))
TN = (((0,), (0,)), ((), ()))


def up(value, unit):
    return -(-value // unit) * unit


def mm(a, b):
    return jnp.dot(a, b, preferred_element_type=F32)


def mm_nt(a, b):
    return lax.dot_general(a, b, NT, preferred_element_type=F32)


def mm_tn(a, b):
    return lax.dot_general(a, b, TN, preferred_element_type=F32)


class Sizes:
    def __init__(self, mesh, shape):
        self.images, self.rows, self.cols, self.dim = shape
        self.R = mesh.shape["row"]
        self.C = mesh.shape["col"]
        self.pix = self.rows * self.cols
        self.tokens = self.pix * self.images
        self.stripes = self.cols // SW
        self.G = self.C // self.images
        self.wide_heads = BRANCH_HEADS // self.G
        self.hc = HALF // self.G
        self.tall_images = self.images // self.R
        self.wide_len = self.C * self.pix
        self.tall_own = self.rows * SW
        self.tall_len = self.R * self.tall_own
        self.tall_pad = up(self.tall_own, 8)
        self.wide_rows3 = up(3 * self.pix, 16)
        self.wide_rows1 = up(self.pix, 16)
        self.tall_slots = self.tall_images * self.stripes
        self.tall_rows1 = self.tall_slots * self.tall_pad
        self.tall_rows3 = 3 * self.tall_rows1


def norm_parts(values):
    average = jnp.mean(values, -1, keepdims=True)
    centred = values - average
    spread = jnp.mean(centred * centred, -1, keepdims=True)
    inverse = lax.rsqrt(spread + NORM_EPSILON)
    return centred * inverse, inverse


def dense_in_kernel(z, x_ref, gain_ref, shift_ref, w_ref, b_ref, sw_ref, st_ref, pw, pt, gw, gt):
    B, D, TC, TR = z.images, z.dim, z.cols, z.rows

    def one_row(i, carry):
        x = x_ref[i].astype(F32).reshape(TC * B, D)
        normed, _ = norm_parts(x)
        low = (normed * gain_ref[...] + shift_ref[...]).astype(BF16)
        proj = (mm(low, w_ref[...]) + b_ref[...]).reshape(TC, B, 3 * D)
        for j in range(TC):
            s, jj = divmod(j, SW)
            wide_at = pl.multiple_of((j * TR + i) * B, B)
            tall_at = pl.multiple_of(((s * TR + i) * SW + jj) * B, B)
            for n in range(3):
                pw[n, pl.ds(wide_at, B), :] = proj[j, :, n * D : n * D + HALF]
                pt[n, pl.ds(tall_at, B), :] = proj[j, :, n * D + HALF : (n + 1) * D]
        return carry

    lax.fori_loop(0, TR, one_row, 0)
    gw[...] = jnp.zeros_like(gw)
    gt[...] = jnp.zeros_like(gt)
    for b in range(B):
        for n in range(3):
            part = pw[n, pl.ds(b, z.pix, stride=B), :]
            for g in range(z.G):
                gw[b * z.G + g, n * z.pix : (n + 1) * z.pix, :] = part[:, g * z.hc : (g + 1) * z.hc]
            for s in range(z.stripes):
                part = pt[n, pl.ds(s * z.tall_own * B + b, z.tall_own, stride=B), :]
                at = (((b % z.tall_images) * z.stripes + s) * 3 + n) * z.tall_pad
                gt[b // z.tall_images, at : at + z.tall_own, :] = part
    sw_ref[...] = gw[...].astype(BF16)
    st_ref[...] = gt[...].astype(BF16)


def erf_parts(values):
    cdf = 0.5 * (1.0 + lax.erf(values * (0.5**0.5)))
    density = jnp.exp(-0.5 * values * values) * (1.0 / math.sqrt(2.0 * math.pi))
    return cdf, density


def dense_mid_kernel(
    z,
    off_ref,
    rw_ref,
    rt_ref,
    x_ref,
    ct_ref,
    hw_ref,
    pw_ref,
    pb_ref,
    gain_ref,
    shift_ref,
    w1_ref,
    b1_ref,
    w2_ref,
    b2_ref,
    y_ref,
    gres_ref,
    gw_ref,
    gt_ref,
    dpw_ref,
    dw1_ref,
    dw2_ref,
    vec_ref,
    db1_ref,
    mw,
    mt,
    gmw,
    gmt,
    gts,
):
    B, D, TC, TR = z.images, z.dim, z.cols, z.rows
    T = TC * B
    for b in range(B):
        parts = [
            rw_ref[b * z.G + g].astype(F32)[: z.pix] for g in range(z.G)
        ]
        mw[pl.ds(b, z.pix, stride=B), :] = parts[0] if z.G == 1 else jnp.concatenate(parts, -1)
    gts[...] = rt_ref[...].astype(F32)
    for b in range(B):
        for s in range(z.stripes):
            at = ((b % z.tall_images) * z.stripes + s) * z.tall_pad
            mt[pl.ds(s * z.tall_own * B + b, z.tall_own, stride=B), :] = gts[
                b // z.tall_images, at : at + z.tall_own, :
            ]
    dpw_ref[...] = jnp.zeros_like(dpw_ref)
    dw1_ref[...] = jnp.zeros_like(dw1_ref)
    dw2_ref[...] = jnp.zeros_like(dw2_ref)
    vec_ref[...] = jnp.zeros_like(vec_ref)
    db1_ref[...] = jnp.zeros_like(db1_ref)
    gmw[...] = jnp.zeros_like(gmw)
    row_start = off_ref[0]
    col_start = off_ref[1]
    below_cols = (lax.broadcasted_iota(jnp.int32, (TC, B, D), 0) + col_start) < hw_ref[1][None]

    def one_row(i, carry):
        x = x_ref[i].astype(F32).reshape(T, D)
        wide = []
        tall = []
        for j in range(TC):
            s, jj = divmod(j, SW)
            wide_at = pl.multiple_of((j * TR + i) * B, B)
            tall_at = pl.multiple_of(((s * TR + i) * SW + jj) * B, B)
            wide.append(mw[pl.ds(wide_at, B), :])
            tall.append(mt[pl.ds(tall_at, B), :])
        mixture = jnp.concatenate(
            [jnp.concatenate(wide, 0), jnp.concatenate(tall, 0)], -1
        ).astype(BF16)
        residual = x + (mm(mixture, pw_ref[...]) + pb_ref[...])
        n2, r2 = norm_parts(residual)
        act = (n2 * gain_ref[...] + shift_ref[...]).astype(BF16)
        pre = mm(act, w1_ref[...]) + b1_ref[...]
        cdf, density = erf_parts(pre)
        hidden = (pre * cdf).astype(BF16)
        slope = cdf + pre * density
        out = residual + (mm(hidden, w2_ref[...]) + b2_ref[...])
        y_ref[i] = out.astype(BF16).reshape(TC, B, D)
        below_rows = (i + row_start) < hw_ref[0][None]
        inside = jnp.logical_and(below_cols, below_rows)
        gy = jnp.where(inside, ct_ref[i].astype(F32), 0.0).reshape(T, D)
        gy_low = gy.astype(BF16)
        dw2_ref[...] += mm_tn(hidden, gy_low)
        gpre = (mm_nt(gy_low, w2_ref[...]) * slope).astype(BF16)
        dw1_ref[...] += mm_tn(act, gpre)
        db1 = jnp.sum(gpre.astype(F32), 0, keepdims=True)
        for k in range(db1.shape[1] // D):
            db1_ref[k : k + 1, :] += db1[:, k * D : (k + 1) * D]
        gact = mm_nt(gpre, w1_ref[...])
        g = gact * gain_ref[...]
        gres = gy + r2 * (
            g - jnp.mean(g, -1, keepdims=True) - n2 * jnp.mean(g * n2, -1, keepdims=True)
        )
        gres_ref[i] = gres.reshape(TC, B, D)
        gattn = gres.astype(BF16)
        dpw_ref[...] += mm_tn(mixture, gattn)
        gmix = mm_nt(gattn, pw_ref[...]).astype(BF16).astype(F32)
        vec_ref[0:1, :] += jnp.sum(gact * n2, 0, keepdims=True)
        vec_ref[1:2, :] += jnp.sum(gact, 0, keepdims=True)
        vec_ref[2:3, :] += jnp.sum(gattn.astype(F32), 0, keepdims=True)
        vec_ref[3:4, :] += jnp.sum(gy, 0, keepdims=True)
        vec_ref[4:5, :] += jnp.sum(gmix, 0, keepdims=True)
        gm3 = gmix.reshape(TC, B, D)
        for j in range(TC):
            s, jj = divmod(j, SW)
            wide_at = pl.multiple_of((j * TR + i) * B, B)
            tall_at = pl.multiple_of(((s * TR + i) * SW + jj) * B, B)
            gmw[pl.ds(wide_at, B), :] = gm3[j, :, :HALF]
            gmt[pl.ds(tall_at, B), :] = gm3[j, :, HALF:]
        return carry

    lax.fori_loop(0, TR, one_row, 0)
    gts[...] = jnp.zeros_like(gts)
    for b in range(B):
        part = gmw[pl.ds(b, z.wide_rows1, stride=B), :].astype(BF16)
        for g in range(z.G):
            gw_ref[b * z.G + g] = part[:, g * z.hc : (g + 1) * z.hc]
        for s in range(z.stripes):
            at = ((b % z.tall_images) * z.stripes + s) * z.tall_pad
            gts[b // z.tall_images, at : at + z.tall_own, :] = gmt[
                pl.ds(s * z.tall_own * B + b, z.tall_own, stride=B), :
            ]
    gt_ref[...] = gts[...].astype(BF16)


def dense_out_kernel(
    z, rw_ref, rt_ref, x_ref, gres_ref, gain_ref, shift_ref, w_ref, gin_ref, dw_ref, vec_ref, pw, pt, gw, gt
):
    B, D, TC, TR = z.images, z.dim, z.cols, z.rows
    T = TC * B
    gw[...] = rw_ref[...].astype(F32)
    gt[...] = rt_ref[...].astype(F32)
    for b in range(B):
        for n in range(3):
            parts = [
                gw[b * z.G + g, n * z.pix : (n + 1) * z.pix, :] for g in range(z.G)
            ]
            pw[n, pl.ds(b, z.pix, stride=B), :] = (
                parts[0] if z.G == 1 else jnp.concatenate(parts, -1)
            )
            for s in range(z.stripes):
                at = (((b % z.tall_images) * z.stripes + s) * 3 + n) * z.tall_pad
                pt[n, pl.ds(s * z.tall_own * B + b, z.tall_own, stride=B), :] = gt[
                    b // z.tall_images, at : at + z.tall_own, :
                ]
    dw_ref[...] = jnp.zeros_like(dw_ref)
    vec_ref[...] = jnp.zeros_like(vec_ref)

    def one_row(i, carry):
        x = x_ref[i].astype(F32).reshape(T, D)
        n1, r1 = norm_parts(x)
        low = (n1 * gain_ref[...] + shift_ref[...]).astype(BF16)
        lanes = []
        for n in range(3):
            wide = []
            tall = []
            for j in range(TC):
                s, jj = divmod(j, SW)
                wide_at = pl.multiple_of((j * TR + i) * B, B)
                tall_at = pl.multiple_of(((s * TR + i) * SW + jj) * B, B)
                wide.append(pw[n, pl.ds(wide_at, B), :])
                tall.append(pt[n, pl.ds(tall_at, B), :])
            lanes.append(jnp.concatenate(wide, 0))
            lanes.append(jnp.concatenate(tall, 0))
        gproj = jnp.concatenate(lanes, -1)
        vec_ref[2:3, :] += jnp.sum(gproj[:, :D], 0, keepdims=True)
        vec_ref[3:4, :] += jnp.sum(gproj[:, 2 * D :], 0, keepdims=True)
        gproj = gproj.astype(BF16)
        dw_ref[...] += mm_tn(low, gproj)
        gn = mm_nt(gproj, w_ref[...])
        vec_ref[0:1, :] += jnp.sum(gn * n1, 0, keepdims=True)
        vec_ref[1:2, :] += jnp.sum(gn, 0, keepdims=True)
        g = gn * gain_ref[...]
        gin = gres_ref[i].reshape(T, D) + r1 * (
            g - jnp.mean(g, -1, keepdims=True) - n1 * jnp.mean(g * n1, -1, keepdims=True)
        )
        gin_ref[i] = gin.reshape(TC, B, D)
        return carry

    lax.fori_loop(0, TR, one_row, 0)


def key_tiles(length, tile):
    return [(at, min(tile, length - at)) for at in range(0, length, tile)]


def token_places(start, count, lanes):
    token = (lax.broadcasted_iota(jnp.int32, (count, lanes), 0) + start).astype(F32)
    along = jnp.floor((token + 0.5) * (1.0 / SW))
    across = token - along * SW
    return along, across


def conv_forward(vpad, base, count, kernels, across):
    total = None
    for a in (-1, 0, 1):
        inner = None
        for l in (-1, 0, 1):
            term = kernels(a, l) * vpad[base + SW * l + a : base + SW * l + a + count, :]
            inner = term if inner is None else inner + term
        if a == -1:
            inner = jnp.where(across >= 1, inner, 0.0)
        if a == 1:
            inner = jnp.where(across <= SW - 2, inner, 0.0)
        total = inner if total is None else total + inner
    return total


def conv_backward(gpad, base, count, kernels, across):
    total = None
    for a in (-1, 0, 1):
        inner = None
        for l in (-1, 0, 1):
            at = base - SW * l - a
            term = kernels(a, l) * gpad[at : at + count, :]
            inner = term if inner is None else inner + term
        if a == -1:
            inner = jnp.where(across <= SW - 2, inner, 0.0)
        if a == 1:
            inner = jnp.where(across >= 1, inner, 0.0)
        total = inner if total is None else total + inner
    return total


def wide_tap(a, l):
    return 3 * (a + 1) + (l + 1)


def tall_tap(a, l):
    return 3 * (l + 1) + (a + 1)


def head_lanes(h, rows):
    lane = lax.broadcasted_iota(jnp.int32, (rows, HALF), 1)
    return jnp.logical_and(lane >= h * HEAD_DIM, lane < (h + 1) * HEAD_DIM)


def wide_assemble(z, recv_ref, stage, targets):
    for c in range(z.C):
        stage[:, : z.hc] = recv_ref[c].astype(F32)
        for n, target in enumerate(targets):
            target[c * z.pix : (c + 1) * z.pix, :] = stage[n * z.pix : (n + 1) * z.pix, :]


def wide_plan(z):
    per_head = z.wide_len // QB
    tail = z.wide_len - per_head * QB
    blocks = per_head * z.wide_heads
    lanes = up(tail * z.wide_heads, 128)
    return per_head, tail, blocks, lanes


def diagonal(tail, heads, lanes):
    channel = lax.broadcasted_iota(jnp.int32, (HALF, lanes), 0)
    query = lax.broadcasted_iota(jnp.int32, (HALF, lanes), 1)
    keep = channel < 0
    for h in range(heads):
        keep = jnp.logical_or(
            keep,
            jnp.logical_and(
                jnp.logical_and(channel >= h * HEAD_DIM, channel < (h + 1) * HEAD_DIM),
                jnp.logical_and(query >= h * tail, query < (h + 1) * tail),
            ),
        )
    return keep


def tail_columns(rows, tail, heads, lanes):
    copies = [rows] * heads
    if lanes > tail * heads:
        copies.append(jnp.zeros((lanes - tail * heads, HALF), F32))
    return jnp.where(diagonal(tail, heads, lanes), jnp.concatenate(copies, 0).T, 0.0)


def tail_rows(columns, tail, heads):
    flat = columns.T
    total = flat[:tail]
    for h in range(1, heads):
        total = total + flat[h * tail : (h + 1) * tail]
    return total


def head_rows_mask(h, value):
    row = lax.broadcasted_iota(jnp.int32, value.shape, 0)
    keep = jnp.logical_and(row >= h * HEAD_DIM, row < (h + 1) * HEAD_DIM)
    return jnp.where(keep, value, 0.0)


def wide_forward_kernel(
    z,
    lim_ref,
    recv_ref,
    lw_ref,
    lb_ref,
    out_ref,
    q_ref,
    v_ref,
    kcat,
    qtb,
    ot_ref,
    lse_ref,
    qs,
    ks,
    vpad,
    stage,
    vt,
    vt_all,
    ss0,
    ss1,
    osum,
):
    L = z.wide_len
    per_head, tail, blocks, tail_lanes = wide_plan(z)
    full = per_head * QB
    heads = z.wide_heads
    across_limit = lim_ref[0]
    along_limit = lim_ref[1]
    empty = across_limit * along_limit == 0
    scale = jnp.where(empty, 1e-20, LOG2E * HEAD_DIM**-0.5)
    vpad[...] = jnp.zeros_like(vpad)
    if z.hc < HALF:
        stage[...] = jnp.zeros_like(stage)
    wide_assemble(z, recv_ref, stage, (qs, ks, vpad.at[PAD : PAD + L]))
    ones = jnp.where(lax.broadcasted_iota(jnp.int32, (HALF, QB), 0) == 0, 1.0, 0.0).astype(BF16)

    def prepare(at, size):
        rows = pl.ds(at, size)
        q = qs[rows, :]
        q_ref[rows, :] = q.astype(BF16)
        v = vpad[pl.ds(pl.multiple_of(at + PAD, 8), size), :]
        v_ref[rows, :] = v.astype(BF16)
        kcat[rows, :HALF] = ks[rows, :].astype(BF16)
        along, across = token_places(at, size, HALF)
        inside = jnp.logical_and(across < across_limit, along < along_limit)
        allowed = jnp.logical_or(inside, empty)
        lane = lax.broadcasted_iota(jnp.int32, (size, HALF), 1) == 0
        bias = jnp.where(jnp.logical_and(lane, jnp.logical_not(allowed)), MASKED, 0.0)
        kcat[rows, HALF:] = bias.astype(BF16)
        vt_full = v.T
        first = lax.broadcasted_iota(jnp.int32, (16, size), 0) == 0
        first = jnp.where(first, 1.0, 0.0)
        vt_all[:, pl.ds(at, size)] = jnp.concatenate([vt_full, first], 0).astype(BF16)
        for h in range(heads):
            own = vt_full[h * HEAD_DIM : (h + 1) * HEAD_DIM]
            vt[h, :, pl.ds(at, size)] = jnp.concatenate([own, first], 0).astype(BF16)
        return q

    def flip(n, carry):
        at = pl.multiple_of(n * QB, QB)
        qt = prepare(at, QB).T
        for h in range(heads):
            cols = pl.ds(pl.multiple_of((h * per_head + n) * QB, QB), QB)
            qtb[:HALF, cols] = head_rows_mask(h, qt).astype(BF16)
            qtb[HALF:, cols] = ones
        return carry

    lax.fori_loop(0, per_head, flip, 0)
    tail_cols = slice(blocks * QB, blocks * QB + tail_lanes)
    tail_q = prepare(full, tail)
    qtb[:HALF, tail_cols] = tail_columns(tail_q, tail, heads, tail_lanes).astype(BF16)
    qtb[HALF:, tail_cols] = ones[:, :tail_lanes]

    def scores(rhs, slot):
        s = mm(kcat[...], rhs)
        slot[...] = s
        return jnp.max(jnp.max(s.reshape(L // 8, 8, s.shape[1]), 0), 0, keepdims=True)

    def block_scores(n, slot):
        return scores(qtb[:, pl.ds(pl.multiple_of(n * QB, QB), QB)], slot)

    def weigh(values, slot, top):
        p = jnp.exp2((slot[...] - top) * scale).astype(BF16)
        acc = mm(values, p)
        at = acc.shape[0] - 16
        total = acc[at : at + 1]
        return acc[:at] * (1.0 / total), top * scale + jnp.log2(total)

    def block_rest(n, slot, top):
        h = n // per_head
        out, lse = weigh(vt[h], slot, top)
        rows = pl.ds(pl.multiple_of(h * HEAD_DIM, HEAD_DIM), HEAD_DIM)
        ot_ref[rows, pl.ds(pl.multiple_of((n - h * per_head) * QB, QB), QB)] = out
        lse_ref[0:1, pl.ds(pl.multiple_of(n * QB, QB), QB)] = lse

    def pair(m, top):
        n = 2 * m
        top_next = block_scores(n + 1, ss1)
        block_rest(n, ss0, top)
        top = block_scores(n + 2, ss0)
        block_rest(n + 1, ss1, top_next)
        return top

    top = lax.fori_loop(0, blocks // 2 - 1, pair, block_scores(0, ss0))
    top_next = block_scores(blocks - 1, ss1)
    block_rest(blocks - 2, ss0, top)
    tail_slot = ss0.at[:, :tail_lanes]
    top = scores(qtb[:, tail_cols], tail_slot)
    block_rest(blocks - 1, ss1, top_next)
    out, lse = weigh(vt_all[...], tail_slot, top)
    lse_ref[0:1, tail_cols] = lse
    out = jnp.where(diagonal(tail, heads, tail_lanes), out, 0.0)
    ot_ref[:, full : full + tail_lanes] = out
    osum[full:L, :] = tail_rows(out, tail, heads)

    def finish(n, carry):
        at = pl.multiple_of(n * QB, QB)
        osum[pl.ds(at, QB), :] = ot_ref[:, pl.ds(at, QB)].T
        return carry

    lax.fori_loop(0, per_head, finish, 0)
    for at, size in key_tiles(L, QB):
        along, across = token_places(at, size, HALF)
        inside = jnp.logical_and(across < across_limit, along < along_limit)
        rows = slice(at + PAD, at + PAD + size)
        vpad[rows, :] = jnp.where(inside, vpad[rows, :], 0.0)

    def taps(a, l):
        t = wide_tap(a, l)
        return lw_ref[t : t + 1, :]

    for at, size in key_tiles(L, 224):
        along, across = token_places(at, size, HALF)
        lepe = conv_forward(vpad, at + PAD, size, taps, across)
        osum[at : at + size, :] = osum[at : at + size, :] + lepe + lb_ref[...]
    for c in range(z.C):
        out_ref[c] = osum[c * z.pix : c * z.pix + z.wide_rows1, : z.hc].astype(BF16)


def wide_backward_kernel(
    z,
    lim_ref,
    recv_ref,
    lw_ref,
    q_ref,
    v_ref,
    kcat,
    qtb,
    ot_ref,
    lse_ref,
    out_ref,
    dlw_ref,
    gpad,
    vpad,
    dotb,
    delta,
    kt,
    dq,
    dqt,
    dk,
    dkt,
    dv,
    dvt,
    stage,
    ss0,
    ss1,
    dp0,
    dp1,
    ps0,
    ps1,
    ds0,
    ds1,
):
    L = z.wide_len
    per_head, tail, blocks, tail_lanes = wide_plan(z)
    full = per_head * QB
    heads = z.wide_heads
    across_limit = lim_ref[0]
    along_limit = lim_ref[1]
    empty = across_limit * along_limit == 0
    scale = jnp.where(empty, 1e-20, LOG2E * HEAD_DIM**-0.5)
    gpad[...] = jnp.zeros_like(gpad)
    vpad[...] = jnp.zeros_like(vpad)
    dkt[...] = jnp.zeros_like(dkt)
    dvt[...] = jnp.zeros_like(dvt)
    stage[...] = jnp.zeros_like(stage)
    for c in range(z.C):
        stage[: z.wide_rows1, : z.hc] = recv_ref[c].astype(F32)
        gpad[PAD + c * z.pix : PAD + (c + 1) * z.pix, :] = stage[: z.pix, :]

    def prepare(at, size):
        rows = pl.ds(at, size)
        padded = pl.ds(pl.multiple_of(at + PAD, 8), size)
        kt[:, rows] = kcat[rows, :HALF].astype(F32).T.astype(BF16)
        along, across = token_places(at, size, HALF)
        inside = jnp.logical_and(across < across_limit, along < along_limit)
        vpad[padded, :] = jnp.where(inside, v_ref[rows, :].astype(F32), 0.0)
        return gpad[padded, :]

    def flip(n, carry):
        at = pl.multiple_of(n * QB, QB)
        gt = prepare(at, QB).T
        prod = gt * ot_ref[:, pl.ds(at, QB)]
        for h in range(heads):
            cols = pl.ds(pl.multiple_of((h * per_head + n) * QB, QB), QB)
            dotb[:, cols] = head_rows_mask(h, gt).astype(BF16)
            delta[0:1, cols] = jnp.sum(
                prod[h * HEAD_DIM : (h + 1) * HEAD_DIM], 0, keepdims=True
            )
        return carry

    lax.fori_loop(0, per_head, flip, 0)
    tail_cols = slice(blocks * QB, blocks * QB + tail_lanes)
    gt = tail_columns(prepare(full, tail), tail, heads, tail_lanes)
    dotb[:, tail_cols] = gt.astype(BF16)
    delta[0:1, tail_cols] = jnp.sum(
        gt * ot_ref[:, full : full + tail_lanes], 0, keepdims=True
    )

    def products(cols, s_slot, dp_slot):
        s_slot[...] = mm(kcat[...], qtb[:, cols])
        dp_slot[...] = mm(v_ref[...], dotb[:, cols])

    def weights(cols, s_slot, dp_slot, p_slot, ds_slot):
        lse = lse_ref[0:1, cols]
        dlt = delta[0:1, cols]
        for at, size in key_tiles(L, QB):
            rows = slice(at, at + size)
            p = jnp.exp2(s_slot[rows, :] * scale - lse)
            p_slot[rows, :] = p.astype(BF16)
            ds_slot[rows, :] = (p * (dp_slot[rows, :] - dlt)).astype(BF16)

    def sums(rows, cols, p_slot, ds_slot):
        dvt[rows, :] += mm_nt(dotb[rows, cols], p_slot[...])
        dkt[rows, :] += mm_nt(qtb[rows, cols], ds_slot[...])
        return mm(kt[rows, :], ds_slot[...])

    slots = ((ss0, dp0, ps0, ds0), (ss1, dp1, ps1, ds1))

    def block_cols(n):
        return pl.ds(pl.multiple_of(n * QB, QB), QB)

    def first(n, k):
        products(block_cols(n), *slots[k][:2])

    def second(n, k):
        weights(block_cols(n), *slots[k])

    def third(n, k):
        h = n // per_head
        rows = pl.ds(pl.multiple_of(h * HEAD_DIM, HEAD_DIM), HEAD_DIM)
        at = pl.ds(pl.multiple_of((n - h * per_head) * QB, QB), QB)
        dqt[rows, at] = sums(rows, block_cols(n), *slots[k][2:])

    first(0, 0)
    first(1, 1)
    second(0, 0)

    def pair(m, carry):
        n = 2 * m
        first(n, 0)
        second(n - 1, 1)
        third(n - 2, 0)
        first(n + 1, 1)
        second(n, 0)
        third(n - 1, 1)
        return carry

    lax.fori_loop(1, blocks // 2, pair, 0)
    tail_slots = [ref.at[:, :tail_lanes] for ref in slots[0]]
    products(tail_cols, *tail_slots[:2])
    second(blocks - 1, 1)
    third(blocks - 2, 0)
    weights(tail_cols, *tail_slots)
    third(blocks - 1, 1)
    last = sums(slice(0, z.hc), tail_cols, *tail_slots[2:])
    if z.hc < HALF:
        last = jnp.concatenate([last, jnp.zeros((HALF - z.hc, tail_lanes), F32)], 0)
    last = jnp.where(diagonal(tail, heads, tail_lanes), last, 0.0)
    norm = HEAD_DIM**-0.5
    dq[full:L, :] = tail_rows(last, tail, heads) * norm

    def finish(n, carry):
        rows = pl.ds(pl.multiple_of(n * QB, QB), QB)
        dq[rows, :] = dqt[:, rows].T * norm
        dk[rows, :] = dkt[:, rows].T * norm
        dv[rows, :] = dvt[:, rows].T
        return carry

    lax.fori_loop(0, per_head, finish, 0)
    dk[full:L, :] = dkt[:, full:L].T * norm
    dv[full:L, :] = dvt[:, full:L].T

    def taps(a, l):
        t = wide_tap(a, l)
        return lw_ref[t : t + 1, :]

    sums_of = {}
    for at, size in key_tiles(L, 224):
        along, across = token_places(at, size, HALF)
        inside = jnp.logical_and(across < across_limit, along < along_limit)
        lepe = conv_backward(gpad, at + PAD, size, taps, across)
        dv[at : at + size, :] += jnp.where(inside, lepe, 0.0)
        add_kernel_sums(sums_of, gpad, vpad, at + PAD, size, across, wide_tap)
    dlw_ref[...] = jnp.zeros_like(dlw_ref)
    for t, value in sums_of.items():
        dlw_ref[t : t + 1, :] = jnp.sum(value, 0, keepdims=True)
    stage[...] = jnp.zeros_like(stage)
    for c in range(z.C):
        own = slice(c * z.pix, (c + 1) * z.pix)
        stage[: z.pix, :] = dq[own, :]
        stage[z.pix : 2 * z.pix, :] = dk[own, :]
        stage[2 * z.pix : 3 * z.pix, :] = dv[own, :]
        out_ref[c] = stage[:, : z.hc].astype(BF16)


def add_kernel_sums(sums, gpad, vpad, base, size, across, tap):
    g = gpad[base : base + size, :]
    for a in (-1, 0, 1):
        ga = g
        if a == -1:
            ga = jnp.where(across >= 1, g, 0.0)
        if a == 1:
            ga = jnp.where(across <= SW - 2, g, 0.0)
        for l in (-1, 0, 1):
            at = base + SW * l + a
            term = (ga * vpad[at : at + size, :]).reshape(size // 8, 8, HALF).sum(0)
            t = tap(a, l)
            sums[t] = sums[t] + term if t in sums else term


def tall_prepare(z, p, lim_ref, L):
    across_limit = lim_ref[0, p]
    along_limit = lim_ref[1, p]
    empty = across_limit * along_limit == 0
    scale = jnp.where(empty, 1e-20, LOG2E * HEAD_DIM**-0.5)
    along, across = token_places(0, L, HALF)
    inside = jnp.logical_and(across < across_limit, along < along_limit)
    allowed = jnp.logical_or(inside, empty)
    token = lax.broadcasted_iota(jnp.int32, (L, HALF), 0)
    allowed = jnp.logical_and(allowed, token < z.tall_len)
    lane = lax.broadcasted_iota(jnp.int32, (L, HALF), 1) == 0
    bias = jnp.where(jnp.logical_and(lane, jnp.logical_not(allowed)), MASKED, 0.0).astype(BF16)
    return inside, across, scale, bias


def tall_pull(z, source, p, per, n, target, base):
    for r in range(z.R):
        at = pl.multiple_of((p * per + n) * z.tall_pad, 8)
        block = source[r, pl.ds(at, z.tall_pad), :]
        target[base + r * z.tall_own : base + (r + 1) * z.tall_own, :] = block[: z.tall_own]


def tall_push(z, source, p, per, n, target, base=0):
    for r in range(z.R):
        at = pl.multiple_of((p * per + n) * z.tall_pad, 8)
        target[r, pl.ds(at, z.tall_pad), :] = source[
            base + r * z.tall_own : base + r * z.tall_own + z.tall_pad, :
        ]


def tall_scores(z, k, q, bias, kstack, L):
    for h in range(BRANCH_HEADS):
        kstack[h * L : (h + 1) * L, :HALF] = jnp.where(head_lanes(h, L), k, 0.0).astype(BF16)
        kstack[h * L : (h + 1) * L, HALF:] = bias
    first = lax.broadcasted_iota(jnp.int32, (HALF, L), 0) == 0
    qt = jnp.concatenate([q.T, jnp.where(first, 1.0, 0.0)], 0).astype(BF16)
    return mm(kstack[...], qt)


TALL_GROUP = 4


def tall_forward_kernel(
    z, lim_ref, recv_ref, lw_ref, lb_ref, out_ref, ot_ref, lse_ref, src, dst, qs, ks, vs, vpad, osum, kstack
):
    L = qs.shape[1]
    src[...] = recv_ref[...].astype(F32)
    for ref in (qs, ks, vs, vpad, osum):
        ref[...] = jnp.zeros_like(ref)

    def taps(a, l):
        t = tall_tap(a, l)
        return lw_ref[t : t + 1, :]

    def group(m, carry):
        each = range(TALL_GROUP)
        ps = [m * TALL_GROUP + u for u in each]
        for u in each:
            for n, target in enumerate((qs, ks, vs)):
                tall_pull(z, src, ps[u], 3, n, target.at[u], 0)
        made = [tall_prepare(z, ps[u], lim_ref, L) for u in each]
        scores = [
            tall_scores(z, ks[u], qs[u], made[u][3], kstack.at[u], L) for u in each
        ]
        tail = lax.broadcasted_iota(jnp.int32, (16, L), 0) == 0
        tail = jnp.where(tail, 1.0, 0.0)
        vts = [vs[u].T for u in each]
        tops = [
            [jnp.max(scores[u][h * L : (h + 1) * L], 0, keepdims=True) for h in range(BRANCH_HEADS)]
            for u in each
        ]
        accs = []
        for u in each:
            row = []
            for h in range(BRANCH_HEADS):
                s = scores[u][h * L : (h + 1) * L]
                e = jnp.exp2((s - tops[u][h]) * made[u][2]).astype(BF16)
                vt = jnp.concatenate([vts[u][h * HEAD_DIM : (h + 1) * HEAD_DIM], tail], 0)
                row.append(mm(vt.astype(BF16), e))
            accs.append(row)
        for u in each:
            inside, across, scale, _ = made[u]
            outs = []
            for h in range(BRANCH_HEADS):
                total = accs[u][h][HEAD_DIM : HEAD_DIM + 1]
                outs.append(accs[u][h][:HEAD_DIM] * (1.0 / total))
                lse_ref[ps[u], h : h + 1, :] = tops[u][h] * scale + jnp.log2(total)
            ot = jnp.concatenate(outs, 0)
            ot_ref[ps[u]] = ot
            vpad[u, PAD : PAD + L, :] = jnp.where(inside, vs[u], 0.0)
            lepe = conv_forward(vpad.at[u], PAD, L, taps, across)
            osum[u, :L, :] = ot.T + lepe + lb_ref[...]
        for u in each:
            tall_push(z, osum.at[u], ps[u], 1, 0, dst)
        return carry

    lax.fori_loop(0, z.tall_slots // TALL_GROUP, group, 0)
    out_ref[...] = dst[...].astype(BF16)


def tall_backward_kernel(
    z,
    lim_ref,
    recv_ref,
    grad_ref,
    lw_ref,
    ot_ref,
    lse_ref,
    out_ref,
    dlw_ref,
    src,
    gsrc,
    dst,
    qs,
    ks,
    vs,
    gpad,
    vpad,
    stage,
    kstack,
):
    L = qs.shape[1]
    src[...] = recv_ref[...].astype(F32)
    gsrc[...] = grad_ref[...].astype(F32)
    for ref in (qs, ks, vs, gpad, vpad, stage):
        ref[...] = jnp.zeros_like(ref)
    dlw_ref[...] = jnp.zeros_like(dlw_ref)
    norm = HEAD_DIM**-0.5

    def taps(a, l):
        t = tall_tap(a, l)
        return lw_ref[t : t + 1, :]

    def group(m, carry):
        each = range(TALL_GROUP)
        heads = range(BRANCH_HEADS)
        ps = [m * TALL_GROUP + u for u in each]
        for u in each:
            for n, target in enumerate((qs, ks, vs)):
                tall_pull(z, src, ps[u], 3, n, target.at[u], 0)
            tall_pull(z, gsrc, ps[u], 1, 0, gpad.at[u], PAD)
        made = [tall_prepare(z, ps[u], lim_ref, L) for u in each]
        gts = [gpad[u, PAD : PAD + L, :].T for u in each]
        scores = []
        dps = []
        for u in each:
            scores.append(tall_scores(z, ks[u], qs[u], made[u][3], kstack.at[u], L))
            v = vs[u]
            vstack = jnp.concatenate([jnp.where(head_lanes(h, L), v, 0.0) for h in heads], 0)
            dps.append(mm(vstack.astype(BF16), gts[u].astype(BF16)))
        kts = [ks[u].T.astype(BF16) for u in each]
        weights = []
        for u in each:
            prod = gts[u] * ot_ref[ps[u]]
            lse = lse_ref[ps[u]]
            row = []
            for h in heads:
                rows = slice(h * L, (h + 1) * L)
                delta = jnp.sum(prod[h * HEAD_DIM : (h + 1) * HEAD_DIM], 0, keepdims=True)
                w = jnp.exp2(scores[u][rows] * made[u][2] - lse[h : h + 1])
                ds = (w * (dps[u][rows] - delta)).astype(BF16)
                row.append((w.astype(BF16), ds))
            weights.append(row)
        results = []
        for u in each:
            dv = None
            dk = None
            dqs = []
            for h in heads:
                keep = head_lanes(h, L)
                w, ds = weights[u][h]
                dv_h = mm(w, jnp.where(keep, gpad[u, PAD : PAD + L, :], 0.0).astype(BF16))
                dk_h = mm(ds, jnp.where(keep, qs[u], 0.0).astype(BF16))
                dv = dv_h if dv is None else dv + dv_h
                dk = dk_h if dk is None else dk + dk_h
                dqs.append(mm(kts[u][h * HEAD_DIM : (h + 1) * HEAD_DIM], ds))
            results.append((jnp.concatenate(dqs, 0), dk, dv))
        sums = {}
        for u in each:
            inside, across = made[u][:2]
            vpad[u, PAD : PAD + L, :] = jnp.where(inside, vs[u], 0.0)
            lepe = conv_backward(gpad.at[u], PAD, L, taps, across)
            add_kernel_sums(sums, gpad.at[u], vpad.at[u], PAD, L, across, tall_tap)
            dqt, dk, dv = results[u]
            stage[u, 0, :L, :] = dqt.T * norm
            stage[u, 1, :L, :] = dk * norm
            stage[u, 2, :L, :] = dv + jnp.where(inside, lepe, 0.0)
        for t, value in sums.items():
            dlw_ref[t : t + 1, :] += jnp.sum(value, 0, keepdims=True)
        for u in each:
            for n in range(3):
                tall_push(z, stage.at[u, n], ps[u], 3, n, dst)
        return carry

    lax.fori_loop(0, z.tall_slots // TALL_GROUP, group, 0)
    out_ref[...] = dst[...].astype(BF16)


def exchange_kernel(z, wide_ref, tall_ref, wide_out, tall_out, wsend, wrecv, tsend, trecv, local):
    C, R = z.C, z.R
    col = lax.axis_index("col")
    row = lax.axis_index("row")
    barrier = pltpu.get_barrier_semaphore()
    for k in range(1, C):
        pl.semaphore_signal(
            barrier, inc=1, device_id=(row, lax.rem(col + k, C)), device_id_type=MESH
        )
    for k in range(1, R):
        pl.semaphore_signal(
            barrier, inc=1, device_id=(lax.rem(row + k, R), col), device_id_type=MESH
        )
    pl.semaphore_wait(barrier, C - 1 + R - 1)
    copies = []
    for k in range(1, R):
        target = lax.rem(row + k, R)
        copies.append(
            pltpu.make_async_remote_copy(
                src_ref=tall_ref.at[target],
                dst_ref=tall_out.at[row],
                send_sem=tsend.at[k],
                recv_sem=trecv.at[k],
                device_id=(target, col),
                device_id_type=MESH,
            )
        )
    for k in range(1, C):
        target = lax.rem(col + k, C)
        copies.append(
            pltpu.make_async_remote_copy(
                src_ref=wide_ref.at[target],
                dst_ref=wide_out.at[col],
                send_sem=wsend.at[k],
                recv_sem=wrecv.at[k],
                device_id=(row, target),
                device_id_type=MESH,
            )
        )
    for copy in copies:
        copy.start()
    own = [
        pltpu.make_async_copy(wide_ref.at[col], wide_out.at[col], local.at[0]),
        pltpu.make_async_copy(tall_ref.at[row], tall_out.at[row], local.at[1]),
    ]
    for copy in own:
        copy.start()
    for copy in own:
        copy.wait()
    for copy in copies:
        copy.wait()


def exchange(z, wide, tall, collective_id):
    spec = pl.BlockSpec(memory_space=pl.ANY)
    dma = pltpu.SemaphoreType.DMA
    return pl.pallas_call(
        functools.partial(exchange_kernel, z),
        out_shape=(
            jax.ShapeDtypeStruct(wide.shape, wide.dtype),
            jax.ShapeDtypeStruct(tall.shape, tall.dtype),
        ),
        in_specs=[spec, spec],
        out_specs=(spec, spec),
        scratch_shapes=[dma((z.C,)), dma((z.C,)), dma((z.R,)), dma((z.R,)), dma((2,))],
        compiler_params=pltpu.CompilerParams(collective_id=collective_id, has_side_effects=True),
        name=f"exchange_{collective_id}",
    )(wide, tall)


def split_of(rows, lanes, parts):
    for by_rows in range(parts, 0, -1):
        if parts % by_rows == 0:
            by_lanes = parts // by_rows
            if rows % (16 * by_rows) == 0 and lanes % (128 * by_lanes) == 0:
                return by_rows, by_lanes
    raise ValueError("no split")


def reduce_stages(z):
    return [(2, 1), (2, 2), (z.R, None), (z.C // 4, 4)]


def reduce_plan(z, lanes):
    rows = z.dim
    plan = []
    for members, stride in reduce_stages(z):
        a, b = split_of(rows, lanes, members)
        rows, lanes = rows // a, lanes // b
        plan.append((members, stride, a, b, rows, lanes))
    return plan


def reduce_width(z, lanes):
    while True:
        try:
            reduce_plan(z, lanes)
            return lanes
        except ValueError:
            lanes += 128


def reduce_kernel(z, plan, dqkv_ref, dproj_ref, dfc1_ref, dfc2_ref, small_ref, *refs):
    D = z.dim
    n = len(plan)
    outs, refs = refs[:5], refs[5:]
    oqkv, oproj, ofc1, ofc2, osmall = outs
    full, refs = refs[0], refs[1:]
    recvs, refs = refs[:n], refs[n:]
    held, refs = refs[:n], refs[n:]
    gathers, refs = refs[:n], refs[n:]
    smalls, refs = refs[:n], refs[n:]
    ssem, rsem, gsem, hsem, vsem, wsem = refs
    col = lax.axis_index("col")
    row = lax.axis_index("row")

    def place(stage):
        members, stride = plan[stage][:2]
        if stride is None:
            return row
        return lax.rem(col // stride, members)

    def peer(stage, k):
        members, stride = plan[stage][:2]
        at = lax.rem(place(stage) + k, members)
        if stride is None:
            return at, (at, col)
        return at, (row, col + (at - place(stage)) * stride)

    barrier = pltpu.get_barrier_semaphore()
    count = 0
    for stage in range(n):
        for k in range(1, plan[stage][0]):
            pl.semaphore_signal(barrier, inc=1, device_id=peer(stage, k)[1], device_id_type=MESH)
            count += 1
    pl.semaphore_wait(barrier, count)
    lanes = full.shape[1]
    at = 0
    for ref in (dqkv_ref, dproj_ref, dfc1_ref):
        width = ref.shape[1]
        full[:, at : at + width] = ref[...].astype(BF16)
        at += width
    for k in range(dfc2_ref.shape[0] // D):
        full[:, at : at + D] = dfc2_ref[k * D : (k + 1) * D, :].astype(BF16)
        at += D
    if at < lanes:
        full[:, at:] = jnp.zeros((D, lanes - at), BF16)

    def window(ref, stage, index):
        members, stride, a, b, rows, width = plan[stage]
        r0 = pl.multiple_of((index // b) * rows, 16)
        l0 = pl.multiple_of(lax.rem(index, b) * width, 128)
        return ref.at[pl.ds(r0, rows), pl.ds(l0, width)]

    current = full
    small_now = small_ref
    for stage in range(n):
        members = plan[stage][0]
        me = place(stage)
        copies = []
        for k in range(1, members):
            index, device = peer(stage, k)
            copies.append(
                pltpu.make_async_remote_copy(
                    src_ref=window(current, stage, index),
                    dst_ref=recvs[stage].at[me],
                    send_sem=ssem.at[stage, k],
                    recv_sem=rsem.at[stage, k],
                    device_id=device,
                    device_id_type=MESH,
                )
            )
            copies.append(
                pltpu.make_async_remote_copy(
                    src_ref=small_now,
                    dst_ref=smalls[stage].at[me],
                    send_sem=vsem.at[stage, k],
                    recv_sem=wsem.at[stage, k],
                    device_id=device,
                    device_id_type=MESH,
                )
            )
        for copy in copies:
            copy.start()
        smalls[stage][me] = small_now[...]
        recvs[stage][me] = window(current, stage, me)[...]
        for copy in copies:
            copy.wait()
        total = recvs[stage][0].astype(F32)
        small = smalls[stage][0]
        for k in range(1, members):
            total = total + recvs[stage][k].astype(F32)
            small = small + smalls[stage][k]
        held[stage][...] = total.astype(BF16)
        osmall[...] = small
        current = held[stage]
        if stage + 1 < n:
            smalls[stage][0] = small
            small_now = smalls[stage].at[0]
    for stage in range(n - 1, -1, -1):
        members = plan[stage][0]
        me = place(stage)
        copies = []
        for k in range(1, members):
            index, device = peer(stage, k)
            copies.append(
                pltpu.make_async_remote_copy(
                    src_ref=current,
                    dst_ref=window(gathers[stage], stage, me),
                    send_sem=gsem.at[stage, k],
                    recv_sem=hsem.at[stage, k],
                    device_id=device,
                    device_id_type=MESH,
                )
            )
        for copy in copies:
            copy.start()
        window(gathers[stage], stage, me)[...] = current[...]
        for copy in copies:
            copy.wait()
        current = gathers[stage]
    at = 0
    for ref in (oqkv, oproj, ofc1):
        width = ref.shape[1]
        ref[...] = current[:, at : at + width].astype(F32)
        at += width
    for k in range(ofc2.shape[0] // D):
        ofc2[k * D : (k + 1) * D, :] = current[:, at : at + D].astype(F32)
        at += D


def reduce_all(z, dqkv, dproj, dfc1, dfc2, small, collective_id):
    arrays = (dqkv, dproj, dfc1, dfc2, small)
    lanes = reduce_width(z, sum(a.size for a in arrays[:4]) // z.dim)
    plan = reduce_plan(z, lanes)
    vmem = pl.BlockSpec(memory_space=pltpu.VMEM)
    dma = pltpu.SemaphoreType.DMA
    most = max(step[0] for step in plan)
    gathers = [pltpu.VMEM((z.dim, lanes), BF16)]
    gathers += [pltpu.VMEM((step[4], step[5]), BF16) for step in plan[:-1]]
    return pl.pallas_call(
        functools.partial(reduce_kernel, z, plan),
        out_shape=tuple(jax.ShapeDtypeStruct(a.shape, F32) for a in arrays),
        in_specs=[vmem] * 5,
        out_specs=(vmem,) * 5,
        scratch_shapes=[pltpu.VMEM((z.dim, lanes), BF16)]
        + [pltpu.VMEM((step[0], step[4], step[5]), BF16) for step in plan]
        + [pltpu.VMEM((step[4], step[5]), BF16) for step in plan]
        + gathers
        + [pltpu.VMEM((step[0],) + small.shape, F32) for step in plan]
        + [dma((len(plan), most)) for _ in range(6)],
        compiler_params=pltpu.CompilerParams(
            collective_id=collective_id, has_side_effects=True, vmem_limit_bytes=VMEM_LIMIT
        ),
        name="reduce_all",
    )(*arrays)


def local_call(kernel, z, name, outs, scratch, scalars, arrays):
    vmem = pl.BlockSpec(memory_space=pltpu.VMEM)
    smem = pl.BlockSpec(memory_space=pltpu.SMEM)
    return pl.pallas_call(
        functools.partial(kernel, z),
        out_shape=tuple(jax.ShapeDtypeStruct(shape, kind) for shape, kind in outs),
        in_specs=[smem] * len(scalars) + [vmem] * len(arrays),
        out_specs=(vmem,) * len(outs),
        scratch_shapes=[pltpu.VMEM(shape, kind) for shape, kind in scratch],
        compiler_params=pltpu.CompilerParams(vmem_limit_bytes=VMEM_LIMIT),
        name=name,
    )(*scalars, *arrays)


def per_device(
    mesh,
    features,
    heights,
    widths,
    norm1_gain,
    norm1_shift,
    qkv_weight,
    query_bias,
    value_bias,
    lepe_weight,
    lepe_bias,
    proj_weight,
    proj_bias,
    norm2_gain,
    norm2_shift,
    fc1_weight,
    fc1_bias,
    fc2_weight,
    fc2_bias,
    cotangent,
):
    z = Sizes(mesh, features.shape)
    B, D, TC, TR = z.images, z.dim, z.cols, z.rows
    col = lax.axis_index("col")
    row = lax.axis_index("row")
    row_start = row * TR
    col_start = col * TC
    x = features.transpose(1, 2, 0, 3)
    ct = cotangent.transpose(1, 2, 0, 3)
    qkv_bias = jnp.concatenate([query_bias, jnp.zeros_like(query_bias), value_bias])
    line = lambda v: v.reshape(1, -1)
    FF = fc1_weight.shape[1]

    image = col // z.G
    wide_lim = jnp.stack(
        [jnp.clip(heights[image] - row_start, 0, TR), jnp.clip(widths[image], 0, z.C * TC)]
    )
    own_images = row * z.tall_images + jnp.arange(z.tall_images)
    stripe_start = col_start + SW * jnp.arange(z.stripes)
    tall_across = jnp.clip(widths[own_images][:, None] - stripe_start[None], 0, SW)
    tall_along = jnp.broadcast_to(
        jnp.clip(heights[own_images], 0, z.R * TR)[:, None], tall_across.shape
    )
    tall_lim = jnp.stack([tall_across.reshape(-1), tall_along.reshape(-1)])
    part = lax.rem(col, z.G)
    pad_taps = lambda w: jnp.pad(w, ((0, 16 - w.shape[0]), (0, HALF - w.shape[1])))
    wide_taps = pad_taps(lax.dynamic_slice_in_dim(lepe_weight[:, :HALF], part * z.hc, z.hc, 1))
    wide_tap_bias = jnp.pad(
        lax.dynamic_slice_in_dim(lepe_bias[:HALF], part * z.hc, z.hc, 0), (0, HALF - z.hc)
    )
    tall_taps = pad_taps(lepe_weight[:, HALF:])
    tall_tap_bias = lepe_bias[HALF:]

    wide3 = (z.C, z.wide_rows3, z.hc)
    wide1 = (z.C, z.wide_rows1, z.hc)
    tall3 = (z.R, z.tall_rows3, HALF)
    tall1 = (z.R, z.tall_rows1, HALF)
    flat = up(z.tokens, 16 * B) + 16 * B

    send_wide, send_tall = local_call(
        dense_in_kernel,
        z,
        "dense_in",
        [(wide3, BF16), (tall3, BF16)],
        [((3, flat, HALF), F32), ((3, flat, HALF), F32), (wide3, F32), (tall3, F32)],
        [],
        [x, line(norm1_gain), line(norm1_shift), qkv_weight, line(qkv_bias)],
    )
    wide_qkv, tall_qkv = exchange(z, send_wide, send_tall, 0)

    LT = up(z.tall_len, 128)
    tall_out, tall_ot, tall_lse = local_call(
        tall_forward_kernel,
        z,
        "tall_forward",
        [(tall1, BF16), ((z.tall_slots, HALF, LT), F32), ((z.tall_slots, 8, LT), F32)],
        [
            (tall3, F32),
            (tall1, F32),
            ((TALL_GROUP, LT, HALF), F32),
            ((TALL_GROUP, LT, HALF), F32),
            ((TALL_GROUP, LT, HALF), F32),
            ((TALL_GROUP, LT + 16, HALF), F32),
            ((TALL_GROUP, LT + 16, HALF), F32),
            ((TALL_GROUP, BRANCH_HEADS * LT, 2 * HALF), BF16),
        ],
        [tall_lim],
        [tall_qkv, tall_taps, line(tall_tap_bias)],
    )
    L = z.wide_len
    per_head, tail, blocks, tail_lanes = wide_plan(z)
    LV = blocks * QB + tail_lanes
    LT_ALL = per_head * QB + tail_lanes
    LO = L + z.wide_rows1
    wide_out, q, v, kcat, qtb, ot, lse = local_call(
        wide_forward_kernel,
        z,
        "wide_forward",
        [
            (wide1, BF16),
            ((L, HALF), BF16),
            ((L, HALF), BF16),
            ((L, 2 * HALF), BF16),
            ((2 * HALF, LV), BF16),
            ((HALF, LT_ALL), F32),
            ((8, LV), F32),
        ],
        [
            ((L, HALF), F32),
            ((L, HALF), F32),
            ((L + 2 * PAD, HALF), F32),
            ((z.wide_rows3, HALF), F32),
            ((z.wide_heads, HEAD_DIM + 16, L), BF16),
            ((HALF + 16, L), BF16),
            ((L, QB), F32),
            ((L, QB), F32),
            ((LO, HALF), F32),
        ],
        [wide_lim],
        [wide_qkv, wide_taps, line(wide_tap_bias)],
    )
    back_wide, back_tall = exchange(z, wide_out, tall_out, 1)

    limits = jnp.broadcast_to(jnp.stack([heights, widths])[:, :, None], (2, B, D))
    y, gres, gmix_wide, gmix_tall, dproj, dfc1, dfc2, vec_mid, db1 = local_call(
        dense_mid_kernel,
        z,
        "dense_mid",
        [
            ((TR, TC, B, D), BF16),
            ((TR, TC, B, D), F32),
            (wide1, BF16),
            (tall1, BF16),
            ((D, D), F32),
            ((D, FF), F32),
            ((FF, D), F32),
            ((8, D), F32),
            ((8, D), F32),
        ],
        [((flat, HALF), F32)] * 4 + [(tall1, F32)],
        [jnp.stack([row_start, col_start])],
        [
            back_wide,
            back_tall,
            x,
            ct,
            limits,
            proj_weight,
            line(proj_bias),
            line(norm2_gain),
            line(norm2_shift),
            fc1_weight,
            line(fc1_bias),
            fc2_weight,
            line(fc2_bias),
        ],
    )
    grad_wide, grad_tall = exchange(z, gmix_wide, gmix_tall, 2)

    dtall, dtall_taps = local_call(
        tall_backward_kernel,
        z,
        "tall_backward",
        [(tall3, BF16), ((16, HALF), F32)],
        [
            (tall3, F32),
            (tall1, F32),
            (tall3, F32),
            ((TALL_GROUP, LT, HALF), F32),
            ((TALL_GROUP, LT, HALF), F32),
            ((TALL_GROUP, LT, HALF), F32),
            ((TALL_GROUP, LT + 16, HALF), F32),
            ((TALL_GROUP, LT + 16, HALF), F32),
            ((TALL_GROUP, 3, LT + 16, HALF), F32),
            ((TALL_GROUP, BRANCH_HEADS * LT, 2 * HALF), BF16),
        ],
        [tall_lim],
        [tall_qkv, grad_tall, tall_taps, tall_ot, tall_lse],
    )
    dwide, dwide_taps = local_call(
        wide_backward_kernel,
        z,
        "wide_backward",
        [(wide3, BF16), ((16, HALF), F32)],
        [
            ((L + 2 * PAD, HALF), F32),
            ((L + 2 * PAD, HALF), F32),
            ((HALF, LV), BF16),
            ((8, LV), F32),
            ((HALF, L), BF16),
            ((L, HALF), F32),
            ((HALF, per_head * QB), F32),
            ((L, HALF), F32),
            ((HALF, L), F32),
            ((L, HALF), F32),
            ((HALF, L), F32),
            ((z.wide_rows3, HALF), F32),
        ]
        + [((L, QB), F32)] * 4
        + [((L, QB), BF16)] * 4,
        [wide_lim],
        [grad_wide, wide_taps, q, v, kcat, qtb, ot, lse],
    )
    got_wide, got_tall = exchange(z, dwide, dtall, 3)

    grad_in, dqkv, vec_out = local_call(
        dense_out_kernel,
        z,
        "dense_out",
        [((TR, TC, B, D), F32), ((D, 3 * D), F32), ((8, D), F32)],
        [((3, flat, HALF), F32), ((3, flat, HALF), F32), (wide3, F32), (tall3, F32)],
        [],
        [got_wide, got_tall, x, gres, line(norm1_gain), line(norm1_shift), qkv_weight],
    )
    own_taps = dwide_taps[:, : z.hc]
    if z.G > 1:
        own_taps = lax.dynamic_update_slice(
            jnp.zeros((16, HALF), F32), own_taps, (0, part * z.hc)
        )
    small = jnp.concatenate(
        [vec_mid, vec_out, jnp.concatenate([own_taps, dtall_taps], -1), db1], 0
    )
    dqkv, dproj, dfc1, dfc2, small = reduce_all(z, dqkv, dproj, dfc1, dfc2, small, 4)
    return (
        y.transpose(2, 0, 1, 3),
        grad_in.transpose(2, 0, 1, 3),
        small[8],
        small[9],
        dqkv,
        small[10],
        small[11],
        small[16:25],
        small[4],
        dproj,
        small[2],
        small[0],
        small[1],
        dfc1,
        small[32 : 32 + FF // D].reshape(-1),
        dfc2,
        small[3],
    )


def solution(mesh):
    image = P(None, "row", "col", None)
    return jax.shard_map(
        functools.partial(per_device, mesh),
        mesh=mesh,
        in_specs=(image,) + (P(),) * 17 + (image,),
        out_specs=(image, image) + (P(),) * 15,
        check_vma=False,
    )
```

```python
import functools
import math

import jax
import jax.numpy as jnp
from jax import lax
from jax.experimental import pallas as pl
from jax.experimental.pallas import tpu as pltpu
from jax.sharding import PartitionSpec as P

HEADS = 8
SW = 7
BRANCH_HEADS = HEADS // 2
HALF = 128
HEAD_DIM = 32
NORM_EPSILON = 1e-05
MASKED = -1e30
LOG2E = math.log2(math.e)
PAD = 8
VMEM_LIMIT = 62 * 1024 * 1024
MESH = pl.DeviceIdType.MESH
F32 = jnp.float32
BF16 = jnp.bfloat16
NT = (((1,), (1,)), ((), ()))
TN = (((0,), (0,)), ((), ()))


def up(value, unit):
    return -(-value // unit) * unit


def mm(a, b):
    return jnp.dot(a, b, preferred_element_type=F32)


def mm_nt(a, b):
    return lax.dot_general(a, b, NT, preferred_element_type=F32)


def mm_tn(a, b):
    return lax.dot_general(a, b, TN, preferred_element_type=F32)


class Sizes:
    def __init__(self, mesh, shape):
        self.images, self.rows, self.cols, self.dim = shape
        self.R = mesh.shape["row"]
        self.C = mesh.shape["col"]
        self.pix = self.rows * self.cols
        self.tokens = self.pix * self.images
        self.stripes = self.cols // SW
        self.G = self.C // self.images
        self.wide_heads = BRANCH_HEADS // self.G
        self.hc = HALF // self.G
        self.tall_images = self.images // self.R
        self.wide_len = self.C * self.pix
        self.qb = 256 if self.wide_len <= 2048 else 128
        self.tall_own = self.rows * SW
        self.tall_len = self.R * self.tall_own
        self.tall_pad = up(self.tall_own, 8)
        self.pairs = self.wide_heads // 2
        self.fold = self.pix // 2
        self.pair_rows = up(self.pix + self.fold, 16)
        self.wide_rows1 = up(self.pix, 16)
        self.tall_slots = self.tall_images * self.stripes
        self.tall_group = 4 if self.tall_len <= 128 else 1
        heads = list(range(BRANCH_HEADS))
        self.tall_head_sets = [heads] if self.tall_group > 1 else [[h] for h in heads]
        self.tall_rows1 = self.tall_slots * self.tall_pad
        self.tall_rows3 = 3 * self.tall_rows1


def norm_parts(values):
    average = jnp.mean(values, -1, keepdims=True)
    centred = values - average
    spread = jnp.mean(centred * centred, -1, keepdims=True)
    inverse = lax.rsqrt(spread + NORM_EPSILON)
    return centred * inverse, inverse


def low_half(rows):
    return lax.broadcasted_iota(jnp.int32, (rows, HALF), 1) < HALF // 2


def turn(value):
    return jnp.concatenate([value[:, HALF // 2 :], value[:, : HALF // 2]], -1)


def dense_in(z, x_ref, gain_ref, shift_ref, w_ref, b_ref, sw_ref, st_ref, pw, pt, gw, gt):
    B, D, TC, TR = z.images, z.dim, z.cols, z.rows

    def one_row(i, carry):
        x = x_ref[i].astype(F32).reshape(TC * B, D)
        normed, _ = norm_parts(x)
        low = (normed * gain_ref[...] + shift_ref[...]).astype(BF16)
        proj = (mm(low, w_ref[...]) + b_ref[...]).reshape(TC, B, 3 * D)
        for j in range(TC):
            s, jj = divmod(j, SW)
            wide_at = pl.multiple_of((j * TR + i) * B, B)
            tall_at = pl.multiple_of(((s * TR + i) * SW + jj) * B, B)
            for n in range(3):
                pw[n, pl.ds(wide_at, B), :] = proj[j, :, n * D : n * D + HALF]
                pt[n, pl.ds(tall_at, B), :] = proj[j, :, n * D + HALF : (n + 1) * D]
        return carry

    lax.fori_loop(0, TR, one_row, 0)
    rows = up(z.pix, 8)
    half = up(z.fold, 8)
    lo = low_half(rows)
    lo_half = low_half(half)
    gw[:, :, z.pix + z.fold :, :] = jnp.zeros_like(gw[:, :, z.pix + z.fold :, :])
    for b in range(B):
        q = pw[0, pl.ds(b, rows, stride=B), :]
        k = pw[1, pl.ds(b, rows, stride=B), :]
        v1 = pw[2, pl.ds(b, half, stride=B), :]
        v2 = pw[2, pl.ds(z.fold * B + b, half, stride=B), :]
        qk = (jnp.where(lo, q, turn(k)), jnp.where(lo, turn(q), k))
        vv = (jnp.where(lo_half, v1, turn(v2)), jnp.where(lo_half, turn(v1), v2))
        for u in range(2):
            d = b * z.G + u // z.pairs
            gw[d, u % z.pairs, :rows, :] = qk[u]
            gw[d, u % z.pairs, z.pix : z.pix + z.fold, :] = vv[u][: z.fold]
    sw_ref[...] = gw[...].astype(BF16)
    gt[...] = jnp.zeros_like(gt)
    for b in range(B):
        for n in range(3):
            for s in range(z.stripes):
                part = pt[n, pl.ds(s * z.tall_own * B + b, z.tall_own, stride=B), :]
                at = (((b % z.tall_images) * z.stripes + s) * 3 + n) * z.tall_pad
                gt[b // z.tall_images, at : at + z.tall_own, :] = part
    st_ref[...] = gt[...].astype(BF16)


def erf_parts(values):
    cdf = 0.5 * (1.0 + lax.erf(values * (0.5**0.5)))
    density = jnp.exp(-0.5 * values * values) * (1.0 / math.sqrt(2.0 * math.pi))
    return cdf, density


def dense_mid_kernel(
    z,
    off_ref,
    rw_ref,
    rt_ref,
    x_ref,
    ct_ref,
    hw_ref,
    pw_ref,
    pb_ref,
    gain_ref,
    shift_ref,
    w1_ref,
    b1_ref,
    w2_ref,
    b2_ref,
    y_ref,
    gres_ref,
    gw_ref,
    gt_ref,
    dpw_ref,
    dw1_ref,
    dw2_ref,
    vec_ref,
    db1_ref,
    mw,
    mt,
    gmw,
    gmt,
    gts,
):
    B, D, TC, TR = z.images, z.dim, z.cols, z.rows
    T = TC * B
    for b in range(B):
        parts = [
            rw_ref[b * z.G + g].astype(F32)[: z.pix] for g in range(z.G)
        ]
        mw[pl.ds(b, z.pix, stride=B), :] = parts[0] if z.G == 1 else jnp.concatenate(parts, -1)
    gts[...] = rt_ref[...].astype(F32)
    for b in range(B):
        for s in range(z.stripes):
            at = ((b % z.tall_images) * z.stripes + s) * z.tall_pad
            mt[pl.ds(s * z.tall_own * B + b, z.tall_own, stride=B), :] = gts[
                b // z.tall_images, at : at + z.tall_own, :
            ]
    dpw_ref[...] = jnp.zeros_like(dpw_ref)
    dw1_ref[...] = jnp.zeros_like(dw1_ref)
    dw2_ref[...] = jnp.zeros_like(dw2_ref)
    vec_ref[...] = jnp.zeros_like(vec_ref)
    db1_ref[...] = jnp.zeros_like(db1_ref)
    gmw[...] = jnp.zeros_like(gmw)
    row_start = off_ref[0]
    col_start = off_ref[1]
    below_cols = (lax.broadcasted_iota(jnp.int32, (TC, B, D), 0) + col_start) < hw_ref[1][None]

    def one_row(i, carry):
        x = x_ref[i].astype(F32).reshape(T, D)
        wide = []
        tall = []
        for j in range(TC):
            s, jj = divmod(j, SW)
            wide_at = pl.multiple_of((j * TR + i) * B, B)
            tall_at = pl.multiple_of(((s * TR + i) * SW + jj) * B, B)
            wide.append(mw[pl.ds(wide_at, B), :])
            tall.append(mt[pl.ds(tall_at, B), :])
        mixture = jnp.concatenate(
            [jnp.concatenate(wide, 0), jnp.concatenate(tall, 0)], -1
        ).astype(BF16)
        residual = x + (mm(mixture, pw_ref[...]) + pb_ref[...])
        n2, r2 = norm_parts(residual)
        act = (n2 * gain_ref[...] + shift_ref[...]).astype(BF16)
        pre = mm(act, w1_ref[...]) + b1_ref[...]
        cdf, density = erf_parts(pre)
        hidden = (pre * cdf).astype(BF16)
        slope = cdf + pre * density
        out = residual + (mm(hidden, w2_ref[...]) + b2_ref[...])
        y_ref[i] = out.astype(BF16).reshape(TC, B, D)
        below_rows = (i + row_start) < hw_ref[0][None]
        inside = jnp.logical_and(below_cols, below_rows)
        gy = jnp.where(inside, ct_ref[i].astype(F32), 0.0).reshape(T, D)
        gy_low = gy.astype(BF16)
        dw2_ref[...] += mm_tn(hidden, gy_low)
        gpre = (mm_nt(gy_low, w2_ref[...]) * slope).astype(BF16)
        dw1_ref[...] += mm_tn(act, gpre)
        db1 = jnp.sum(gpre.astype(F32), 0, keepdims=True)
        for k in range(db1.shape[1] // D):
            db1_ref[k : k + 1, :] += db1[:, k * D : (k + 1) * D]
        gact = mm_nt(gpre, w1_ref[...])
        g = gact * gain_ref[...]
        gres = gy + r2 * (
            g - jnp.mean(g, -1, keepdims=True) - n2 * jnp.mean(g * n2, -1, keepdims=True)
        )
        gres_ref[i] = gres.reshape(TC, B, D)
        gattn = gres.astype(BF16)
        dpw_ref[...] += mm_tn(mixture, gattn)
        gmix = mm_nt(gattn, pw_ref[...]).astype(BF16).astype(F32)
        vec_ref[0:1, :] += jnp.sum(gact * n2, 0, keepdims=True)
        vec_ref[1:2, :] += jnp.sum(gact, 0, keepdims=True)
        vec_ref[2:3, :] += jnp.sum(gattn.astype(F32), 0, keepdims=True)
        vec_ref[3:4, :] += jnp.sum(gy, 0, keepdims=True)
        vec_ref[4:5, :] += jnp.sum(gmix, 0, keepdims=True)
        gm3 = gmix.reshape(TC, B, D)
        for j in range(TC):
            s, jj = divmod(j, SW)
            wide_at = pl.multiple_of((j * TR + i) * B, B)
            tall_at = pl.multiple_of(((s * TR + i) * SW + jj) * B, B)
            gmw[pl.ds(wide_at, B), :] = gm3[j, :, :HALF]
            gmt[pl.ds(tall_at, B), :] = gm3[j, :, HALF:]
        return carry

    lax.fori_loop(0, TR, one_row, 0)
    gts[...] = jnp.zeros_like(gts)
    for b in range(B):
        part = gmw[pl.ds(b, z.wide_rows1, stride=B), :].astype(BF16)
        for g in range(z.G):
            gw_ref[b * z.G + g] = part[:, g * z.hc : (g + 1) * z.hc]
        for s in range(z.stripes):
            at = ((b % z.tall_images) * z.stripes + s) * z.tall_pad
            gts[b // z.tall_images, at : at + z.tall_own, :] = gmt[
                pl.ds(s * z.tall_own * B + b, z.tall_own, stride=B), :
            ]
    gt_ref[...] = gts[...].astype(BF16)


def dense_out_kernel(
    z, rw_ref, rt_ref, x_ref, gres_ref, gain_ref, shift_ref, w_ref, gin_ref, dw_ref, vec_ref, pw, pt, gw, gt
):
    B, D, TC, TR = z.images, z.dim, z.cols, z.rows
    T = TC * B
    gw[...] = rw_ref[...].astype(F32)
    gt[...] = rt_ref[...].astype(F32)
    lo = low_half(z.pix)
    lo_half = low_half(z.fold)
    for b in range(B):
        qk = []
        vv = []
        for u in range(2):
            d = b * z.G + u // z.pairs
            qk.append(gw[d, u % z.pairs, : z.pix, :])
            vv.append(gw[d, u % z.pairs, z.pix : z.pix + z.fold, :])
        places = pl.ds(b, z.pix, stride=B)
        pw[0, places, :] = jnp.where(lo, qk[0], turn(qk[1]))
        pw[1, places, :] = jnp.where(lo, turn(qk[0]), qk[1])
        pw[2, pl.ds(b, z.fold, stride=B), :] = jnp.where(lo_half, vv[0], turn(vv[1]))
        pw[2, pl.ds(z.fold * B + b, z.fold, stride=B), :] = jnp.where(
            lo_half, turn(vv[0]), vv[1]
        )
        for n in range(3):
            for s in range(z.stripes):
                at = (((b % z.tall_images) * z.stripes + s) * 3 + n) * z.tall_pad
                pt[n, pl.ds(s * z.tall_own * B + b, z.tall_own, stride=B), :] = gt[
                    b // z.tall_images, at : at + z.tall_own, :
                ]
    dw_ref[...] = jnp.zeros_like(dw_ref)
    vec_ref[...] = jnp.zeros_like(vec_ref)

    def one_row(i, carry):
        x = x_ref[i].astype(F32).reshape(T, D)
        n1, r1 = norm_parts(x)
        low = (n1 * gain_ref[...] + shift_ref[...]).astype(BF16)
        lanes = []
        for n in range(3):
            wide = []
            tall = []
            for j in range(TC):
                s, jj = divmod(j, SW)
                wide_at = pl.multiple_of((j * TR + i) * B, B)
                tall_at = pl.multiple_of(((s * TR + i) * SW + jj) * B, B)
                wide.append(pw[n, pl.ds(wide_at, B), :])
                tall.append(pt[n, pl.ds(tall_at, B), :])
            lanes.append(jnp.concatenate(wide, 0))
            lanes.append(jnp.concatenate(tall, 0))
        gproj = jnp.concatenate(lanes, -1)
        vec_ref[2:3, :] += jnp.sum(gproj[:, :D], 0, keepdims=True)
        vec_ref[3:4, :] += jnp.sum(gproj[:, 2 * D :], 0, keepdims=True)
        gproj = gproj.astype(BF16)
        dw_ref[...] += mm_tn(low, gproj)
        gn = mm_nt(gproj, w_ref[...])
        vec_ref[0:1, :] += jnp.sum(gn * n1, 0, keepdims=True)
        vec_ref[1:2, :] += jnp.sum(gn, 0, keepdims=True)
        g = gn * gain_ref[...]
        gin = gres_ref[i].reshape(T, D) + r1 * (
            g - jnp.mean(g, -1, keepdims=True) - n1 * jnp.mean(g * n1, -1, keepdims=True)
        )
        gin_ref[i] = gin.reshape(TC, B, D)
        return carry

    lax.fori_loop(0, TR, one_row, 0)


def key_tiles(length, tile):
    return [(at, min(tile, length - at)) for at in range(0, length, tile)]


def token_places(start, count, lanes):
    token = (lax.broadcasted_iota(jnp.int32, (count, lanes), 0) + start).astype(F32)
    along = jnp.floor((token + 0.5) * (1.0 / SW))
    across = token - along * SW
    return along, across


def conv_forward(vpad, base, count, kernels, across):
    total = None
    for a in (-1, 0, 1):
        inner = None
        for l in (-1, 0, 1):
            term = kernels(a, l) * vpad[base + SW * l + a : base + SW * l + a + count, :]
            inner = term if inner is None else inner + term
        if a == -1:
            inner = jnp.where(across >= 1, inner, 0.0)
        if a == 1:
            inner = jnp.where(across <= SW - 2, inner, 0.0)
        total = inner if total is None else total + inner
    return total


def conv_backward(gpad, base, count, kernels, across):
    total = None
    for a in (-1, 0, 1):
        inner = None
        for l in (-1, 0, 1):
            at = base - SW * l - a
            term = kernels(a, l) * gpad[at : at + count, :]
            inner = term if inner is None else inner + term
        if a == -1:
            inner = jnp.where(across <= SW - 2, inner, 0.0)
        if a == 1:
            inner = jnp.where(across >= 1, inner, 0.0)
        total = inner if total is None else total + inner
    return total


def wide_tap(a, l):
    return 3 * (a + 1) + (l + 1)


def tall_tap(a, l):
    return 3 * (l + 1) + (a + 1)


def head_lanes(h, rows):
    lane = lax.broadcasted_iota(jnp.int32, (rows, HALF), 1)
    return jnp.logical_and(lane >= h * HEAD_DIM, lane < (h + 1) * HEAD_DIM)


def wide_plan(z):
    per_head = z.wide_len // z.qb
    tail = z.wide_len - per_head * z.qb
    blocks = 2 * per_head
    lanes = up(2 * tail, 128)
    return per_head, tail, blocks, lanes, blocks * z.qb + lanes


def diagonal(tail, first, lanes):
    channel = lax.broadcasted_iota(jnp.int32, (HALF, lanes), 0) - first * HEAD_DIM
    query = lax.broadcasted_iota(jnp.int32, (HALF, lanes), 1)
    keep = channel < -HALF
    for h in range(2):
        keep = jnp.logical_or(
            keep,
            jnp.logical_and(
                jnp.logical_and(channel >= h * HEAD_DIM, channel < (h + 1) * HEAD_DIM),
                jnp.logical_and(query >= h * tail, query < (h + 1) * tail),
            ),
        )
    return keep


def tail_columns(rows, tail, first, lanes):
    copies = [rows, rows]
    if lanes > 2 * tail:
        copies.append(jnp.zeros((lanes - 2 * tail, HALF), F32))
    return jnp.where(diagonal(tail, first, lanes), jnp.concatenate(copies, 0).T, 0.0)


def tail_rows(columns, tail):
    flat = columns.T
    return flat[:tail] + flat[tail : 2 * tail]


def head_rows_mask(h, value):
    row = lax.broadcasted_iota(jnp.int32, value.shape, 0)
    keep = jnp.logical_and(row >= h * HEAD_DIM, row < (h + 1) * HEAD_DIM)
    return jnp.where(keep, value, 0.0)


def wide_limits(lim_ref):
    across_limit = lim_ref[0]
    along_limit = lim_ref[1]
    empty = across_limit * along_limit == 0
    scale = jnp.where(empty, 1e-20, LOG2E * HEAD_DIM**-0.5)
    return across_limit, along_limit, empty, scale


def wide_inside(lim_ref, at, size):
    along, across = token_places(at, size, HALF)
    return jnp.logical_and(across < lim_ref[0], along < lim_ref[1]), across


def wide_pair_forward(z, pair, lim_ref, recv, kcat, qtb, kt, ot, lse, qk, vpad, stage, vt, vt_all, ss0, ss1, osum):
    L = z.wide_len
    per_head, tail, blocks, tail_lanes, span = wide_plan(z)
    full = per_head * z.qb
    base = pair * span
    _, _, empty, scale = wide_limits(lim_ref)
    lo = low_half(z.fold)
    for c in range(z.C):
        stage[...] = recv[c, pair].astype(F32)
        at = c * z.pix
        qk[at : at + z.pix, :] = stage[: z.pix, :]
        v = stage[z.pix : z.pix + z.fold, :]
        one = slice(PAD + at, PAD + at + z.fold)
        two = slice(PAD + at + z.fold, PAD + at + z.pix)
        if pair == 0:
            vpad[one, :] = jnp.where(lo, v, 0.0)
            vpad[two, :] = jnp.where(lo, turn(v), 0.0)
        else:
            vpad[one, :] = jnp.where(lo, vpad[one, :], turn(v))
            vpad[two, :] = jnp.where(lo, vpad[two, :], v)
    ones = jnp.where(lax.broadcasted_iota(jnp.int32, (HALF, z.qb), 0) == 0, 1.0, 0.0).astype(BF16)

    def prepare(at, size):
        rows = pl.ds(at, size)
        both = qk[rows, :]
        kcat[pair, rows, :HALF] = both.astype(BF16)
        inside, _ = wide_inside(lim_ref, at, size)
        allowed = jnp.logical_or(inside, empty)
        lane = lax.broadcasted_iota(jnp.int32, (size, HALF), 1) == 0
        bias = jnp.where(jnp.logical_and(lane, jnp.logical_not(allowed)), MASKED, 0.0)
        kcat[pair, rows, HALF:] = bias.astype(BF16)
        vt_full = vpad[pl.ds(pl.multiple_of(at + PAD, 8), size), :].T
        first = lax.broadcasted_iota(jnp.int32, (16, size), 0) == 0
        first = jnp.where(first, 1.0, 0.0)
        vt_all[:, pl.ds(at, size)] = jnp.concatenate([vt_full, first], 0).astype(BF16)
        for h in range(2):
            own = (2 * pair + h) * HEAD_DIM
            own = vt_full[own : own + HEAD_DIM]
            vt[h, :, pl.ds(at, size)] = jnp.concatenate([own, first], 0).astype(BF16)
        return both

    def flip(n, carry):
        at = pl.multiple_of(n * z.qb, z.qb)
        both = prepare(at, z.qb).T
        kt[pair, :, pl.ds(at, z.qb)] = both[HALF // 2 :].astype(BF16)
        for h in range(2):
            cols = pl.ds(pl.multiple_of((h * per_head + n) * z.qb, z.qb), z.qb)
            parts = [jnp.zeros((HALF // 2, z.qb), F32)] + [jnp.zeros((HEAD_DIM, z.qb), F32)] * 2
            parts[1 + h] = both[h * HEAD_DIM : (h + 1) * HEAD_DIM]
            qtb[pair, :HALF, cols] = jnp.concatenate(parts, 0).astype(BF16)
            qtb[pair, HALF:, cols] = ones
        return carry

    lax.fori_loop(0, per_head, flip, 0)
    tail_cols = slice(blocks * z.qb, span)
    tail_both = prepare(full, tail)
    kt[pair, :, full:L] = tail_both.T[HALF // 2 :].astype(BF16)
    qtb[pair, :HALF, tail_cols] = tail_columns(turn(tail_both), tail, 2, tail_lanes).astype(BF16)
    qtb[pair, HALF:, tail_cols] = ones[:, :tail_lanes]

    def scores(cols, slot):
        s = mm(kcat[pair], qtb[pair, :, cols])
        slot[...] = s
        return jnp.max(jnp.max(s.reshape(L // 8, 8, s.shape[1]), 0), 0, keepdims=True)

    def block_scores(n, slot):
        return scores(pl.ds(pl.multiple_of(n * z.qb, z.qb), z.qb), slot)

    def weigh(values, slot, top):
        p = jnp.exp2((slot[...] - top) * scale).astype(BF16)
        acc = mm(values, p)
        at = acc.shape[0] - 16
        total = acc[at : at + 1]
        return acc[:at] * (1.0 / total), top * scale + jnp.log2(total)

    def block_rest(n, slot, top):
        h = n // per_head
        out, low = weigh(vt[h], slot, top)
        rows = pl.ds(pl.multiple_of((2 * pair + h) * HEAD_DIM, HEAD_DIM), HEAD_DIM)
        ot[rows, pl.ds(pl.multiple_of((n - h * per_head) * z.qb, z.qb), z.qb)] = out
        lse[0:1, pl.ds(pl.multiple_of(base + n * z.qb, 128), z.qb)] = low

    def two(m, top):
        n = 2 * m
        top_next = block_scores(n + 1, ss1)
        block_rest(n, ss0, top)
        top = block_scores(n + 2, ss0)
        block_rest(n + 1, ss1, top_next)
        return top

    top = lax.fori_loop(0, blocks // 2 - 1, two, block_scores(0, ss0))
    top_next = block_scores(blocks - 1, ss1)
    block_rest(blocks - 2, ss0, top)
    tail_slot = ss0.at[:, :tail_lanes]
    top = scores(tail_cols, tail_slot)
    block_rest(blocks - 1, ss1, top_next)
    out, low = weigh(vt_all[...], tail_slot, top)
    lse[0:1, base + blocks * z.qb : base + span] = low
    out = jnp.where(diagonal(tail, 2 * pair, tail_lanes), out, 0.0)
    ot[:, full + pair * tail_lanes : full + (pair + 1) * tail_lanes] = out
    rows = tail_rows(out, tail)
    osum[full:L, :] = rows if pair == 0 else osum[full:L, :] + rows


def wide_mixture(z, lim_ref, lw_ref, lb_ref, ot, vpad, osum, out_ref):
    L = z.wide_len
    per_head = wide_plan(z)[0]

    def finish(n, carry):
        at = pl.multiple_of(n * z.qb, z.qb)
        osum[pl.ds(at, z.qb), :] = ot[:, pl.ds(at, z.qb)].T
        return carry

    lax.fori_loop(0, per_head, finish, 0)
    for at, size in key_tiles(L, z.qb):
        inside, _ = wide_inside(lim_ref, at, size)
        rows = slice(at + PAD, at + PAD + size)
        vpad[rows, :] = jnp.where(inside, vpad[rows, :], 0.0)

    def taps(a, l):
        t = wide_tap(a, l)
        return lw_ref[t : t + 1, :]

    for at, size in key_tiles(L, 224):
        along, across = token_places(at, size, HALF)
        lepe = conv_forward(vpad, at + PAD, size, taps, across)
        osum[at : at + size, :] = osum[at : at + size, :] + lepe + lb_ref[...]
    for c in range(z.C):
        out_ref[c] = osum[c * z.pix : c * z.pix + z.wide_rows1, : z.hc].astype(BF16)


def wide_backward_start(z, lim_ref, recv, lw_ref, v_ref, ot, dlw_ref, gpad, vpad, dotb, delta, dvl, stage):
    L = z.wide_len
    per_head, tail, blocks, tail_lanes, span = wide_plan(z)
    full = per_head * z.qb
    gpad[...] = jnp.zeros_like(gpad)
    vpad[...] = jnp.zeros_like(vpad)
    stage[...] = jnp.zeros_like(stage)
    for c in range(z.C):
        stage[: z.wide_rows1, : z.hc] = recv[c].astype(F32)
        gpad[PAD + c * z.pix : PAD + (c + 1) * z.pix, :] = stage[: z.pix, :]

    def prepare(at, size):
        rows = pl.ds(at, size)
        padded = pl.ds(pl.multiple_of(at + PAD, 8), size)
        inside, _ = wide_inside(lim_ref, at, size)
        vpad[padded, :] = jnp.where(inside, v_ref[rows, :].astype(F32), 0.0)
        return gpad[padded, :]

    def flip(n, carry):
        at = pl.multiple_of(n * z.qb, z.qb)
        gt = prepare(at, z.qb).T
        prod = gt * ot[:, pl.ds(at, z.qb)]
        for h in range(z.wide_heads):
            first = (h // 2) * span + (h % 2) * full
            cols = pl.ds(pl.multiple_of(first + n * z.qb, 128), z.qb)
            dotb[:, cols] = head_rows_mask(h, gt).astype(BF16)
            delta[0:1, cols] = jnp.sum(
                prod[h * HEAD_DIM : (h + 1) * HEAD_DIM], 0, keepdims=True
            )
        return carry

    lax.fori_loop(0, per_head, flip, 0)
    last = prepare(full, tail)
    for pair in range(z.pairs):
        cols = slice(pair * span + blocks * z.qb, (pair + 1) * span)
        gt = tail_columns(last, tail, 2 * pair, tail_lanes)
        dotb[:, cols] = gt.astype(BF16)
        out = ot[:, full + pair * tail_lanes : full + (pair + 1) * tail_lanes]
        delta[0:1, cols] = jnp.sum(gt * out, 0, keepdims=True)

    def taps(a, l):
        t = wide_tap(a, l)
        return lw_ref[t : t + 1, :]

    sums_of = {}
    for at, size in key_tiles(L, 224):
        inside, across = wide_inside(lim_ref, at, size)
        lepe = conv_backward(gpad, at + PAD, size, taps, across)
        dvl[at : at + size, :] = jnp.where(inside, lepe, 0.0)
        add_kernel_sums(sums_of, gpad, vpad, at + PAD, size, across, wide_tap)
    dlw_ref[...] = jnp.zeros_like(dlw_ref)
    for t, value in sums_of.items():
        dlw_ref[t : t + 1, :] = jnp.sum(value, 0, keepdims=True)


def wide_pair_backward(
    z,
    pair,
    lim_ref,
    v_ref,
    kcat,
    qtb,
    kt,
    lse,
    dotb,
    delta,
    dvl,
    dqt,
    dkt,
    dvt,
    dqk,
    dvv,
    stage,
    slots,
    out_ref,
    between,
):
    L = z.wide_len
    per_head, tail, blocks, tail_lanes, span = wide_plan(z)
    full = per_head * z.qb
    base = pair * span
    _, _, _, scale = wide_limits(lim_ref)
    dkt[...] = jnp.zeros_like(dkt)
    dvt[...] = jnp.zeros_like(dvt)
    tail_cols = slice(blocks * z.qb, span)

    def shifted(cols):
        if isinstance(cols, slice):
            return slice(base + cols.start, base + cols.stop)
        return pl.ds(pl.multiple_of(base + cols.start, 128), cols.size)

    def products(cols, s_slot, dp_slot):
        s_slot[...] = mm(kcat[pair], qtb[pair, :, cols])
        dp_slot[...] = mm(v_ref[...], dotb[:, shifted(cols)])

    def weights(cols, s_slot, dp_slot, p_slot, ds_slot):
        low = lse[0:1, shifted(cols)]
        dlt = delta[0:1, shifted(cols)]
        for at, size in key_tiles(L, z.qb):
            rows = slice(at, at + size)
            p = jnp.exp2(s_slot[rows, :] * scale - low)
            p_slot[rows, :] = p.astype(BF16)
            ds_slot[rows, :] = (p * (dp_slot[rows, :] - dlt)).astype(BF16)

    def block_cols(n):
        return pl.ds(pl.multiple_of(n * z.qb, z.qb), z.qb)

    def first(n, k):
        products(block_cols(n), *slots[k][:2])

    def second(n, k):
        weights(block_cols(n), *slots[k])

    def third(n, k):
        h = n // per_head
        p_slot, ds_slot = slots[k][2:]
        cols = block_cols(n)
        rows = pl.ds(pl.multiple_of(h * HEAD_DIM, HEAD_DIM), HEAD_DIM)
        g_rows = pl.ds(pl.multiple_of((2 * pair + h) * HEAD_DIM, HEAD_DIM), HEAD_DIM)
        q_rows = pl.ds(pl.multiple_of(HALF // 2 + h * HEAD_DIM, HEAD_DIM), HEAD_DIM)
        dvt[rows, :] += mm_nt(dotb[g_rows, shifted(cols)], p_slot[...])
        dkt[rows, :] += mm_nt(qtb[pair, q_rows, cols], ds_slot[...])
        at = pl.ds(pl.multiple_of((n - h * per_head) * z.qb, z.qb), z.qb)
        dqt[rows, at] = mm(kt[pair, rows, :], ds_slot[...])

    first(0, 0)
    first(1, 1)
    second(0, 0)

    def two(m, carry):
        n = 2 * m
        first(n, 0)
        second(n - 1, 1)
        third(n - 2, 0)
        first(n + 1, 1)
        second(n, 0)
        third(n - 1, 1)
        return carry

    middle = (1 + blocks // 2) // 2
    lax.fori_loop(1, middle, two, 0)
    between()
    lax.fori_loop(middle, blocks // 2, two, 0)
    tail_slots = [ref.at[:, :tail_lanes] for ref in slots[0]]
    products(tail_cols, *tail_slots[:2])
    second(blocks - 1, 1)
    third(blocks - 2, 0)
    weights(tail_cols, *tail_slots)
    third(blocks - 1, 1)
    half = HALF // 2
    dvt[...] += mm_nt(dotb[pair * half : (pair + 1) * half, shifted(tail_cols)], tail_slots[2][...])
    dkt[...] += mm_nt(qtb[pair, half:HALF, tail_cols], tail_slots[3][...])
    last = mm(kt[pair], tail_slots[3][...])
    empty_half = jnp.zeros((half, tail_lanes), F32)
    last = jnp.concatenate([last, empty_half], 0)
    last = jnp.where(diagonal(tail, 0, tail_lanes), last, 0.0)
    norm = HEAD_DIM**-0.5
    dk_last = jnp.concatenate([jnp.zeros((half, tail), F32), dkt[:, full:L]], 0).T
    dqk[full:L, :] = (tail_rows(last, tail) + dk_last) * norm

    def doubled(value):
        lo = low_half(value.shape[0])
        return jnp.where(lo, value, turn(value)) if pair == 0 else jnp.where(lo, turn(value), value)

    def finish(n, carry):
        rows = pl.ds(pl.multiple_of(n * z.qb, z.qb), z.qb)
        dqk[rows, :] = jnp.concatenate([dqt[:, rows], dkt[:, rows]], 0).T * norm
        dv = dvt[:, rows]
        dvv[rows, :] = jnp.concatenate([dv, dv], 0).T + doubled(dvl[rows, :])
        return carry

    lax.fori_loop(0, per_head, finish, 0)
    dv = dvt[:, full:L]
    dvv[full:L, :] = jnp.concatenate([dv, dv], 0).T + doubled(dvl[full:L, :])
    lo = low_half(z.fold)
    for c in range(z.C):
        at = c * z.pix
        stage[: z.pix, :] = dqk[at : at + z.pix, :]
        stage[z.pix : z.pix + z.fold, :] = jnp.where(
            lo, dvv[at : at + z.fold, :], dvv[at + z.fold : at + z.pix, :]
        )
        out_ref[c, pair] = stage[...].astype(BF16)


def add_kernel_sums(sums, gpad, vpad, base, size, across, tap):
    g = gpad[base : base + size, :]
    for a in (-1, 0, 1):
        ga = g
        if a == -1:
            ga = jnp.where(across >= 1, g, 0.0)
        if a == 1:
            ga = jnp.where(across <= SW - 2, g, 0.0)
        for l in (-1, 0, 1):
            at = base + SW * l + a
            term = (ga * vpad[at : at + size, :]).reshape(size // 8, 8, HALF).sum(0)
            t = tap(a, l)
            sums[t] = sums[t] + term if t in sums else term


def tall_prepare(z, p, lim_ref, L):
    across_limit = lim_ref[0, p]
    along_limit = lim_ref[1, p]
    empty = across_limit * along_limit == 0
    scale = jnp.where(empty, 1e-20, LOG2E * HEAD_DIM**-0.5)
    along, across = token_places(0, L, HALF)
    inside = jnp.logical_and(across < across_limit, along < along_limit)
    allowed = jnp.logical_or(inside, empty)
    token = lax.broadcasted_iota(jnp.int32, (L, HALF), 0)
    allowed = jnp.logical_and(allowed, token < z.tall_len)
    lane = lax.broadcasted_iota(jnp.int32, (L, HALF), 1) == 0
    bias = jnp.where(jnp.logical_and(lane, jnp.logical_not(allowed)), MASKED, 0.0).astype(BF16)
    return inside, across, scale, bias


def tall_pull(z, source, p, per, n, target, base):
    for r in range(z.R):
        at = pl.multiple_of((p * per + n) * z.tall_pad, 8)
        block = source[r, pl.ds(at, z.tall_pad), :]
        target[base + r * z.tall_own : base + (r + 1) * z.tall_own, :] = block[: z.tall_own]


def tall_push(z, source, p, per, n, target, base=0):
    for r in range(z.R):
        at = pl.multiple_of((p * per + n) * z.tall_pad, 8)
        target[r, pl.ds(at, z.tall_pad), :] = source[
            base + r * z.tall_own : base + r * z.tall_own + z.tall_pad, :
        ]


def tall_operands(z, k, q, bias, kstack, L):
    for h in range(BRANCH_HEADS):
        kstack[h * L : (h + 1) * L, :HALF] = jnp.where(head_lanes(h, L), k, 0.0).astype(BF16)
        kstack[h * L : (h + 1) * L, HALF:] = bias
    first = lax.broadcasted_iota(jnp.int32, (HALF, L), 0) == 0
    return jnp.concatenate([q.T, jnp.where(first, 1.0, 0.0)], 0).astype(BF16)


def tall_forward(
    z, start, stop, lim_ref, lw_ref, lb_ref, ot_ref, lse_ref, src, dst, qs, ks, vs, vpad, osum, kstack
):
    L = qs.shape[1]

    def taps(a, l):
        t = tall_tap(a, l)
        return lw_ref[t : t + 1, :]

    def group(m, carry):
        each = range(z.tall_group)
        ps = [m * z.tall_group + u for u in each]
        for u in each:
            for n, target in enumerate((qs, ks, vs)):
                tall_pull(z, src, ps[u], 3, n, target.at[u], 0)
        made = [tall_prepare(z, ps[u], lim_ref, L) for u in each]
        qts = [tall_operands(z, ks[u], qs[u], made[u][3], kstack.at[u], L) for u in each]
        scores = [mm(kstack[u], qts[u]) for u in each]
        tail = lax.broadcasted_iota(jnp.int32, (16, L), 0) == 0
        tail = jnp.where(tail, 1.0, 0.0)
        vts = [vs[u].T for u in each]
        tops = [
            [jnp.max(scores[u][h * L : (h + 1) * L], 0, keepdims=True) for h in range(BRANCH_HEADS)]
            for u in each
        ]
        accs = []
        for u in each:
            row = []
            for h in range(BRANCH_HEADS):
                s = scores[u][h * L : (h + 1) * L]
                e = jnp.exp2((s - tops[u][h]) * made[u][2]).astype(BF16)
                vt = jnp.concatenate([vts[u][h * HEAD_DIM : (h + 1) * HEAD_DIM], tail], 0)
                row.append(mm(vt.astype(BF16), e))
            accs.append(row)
        for u in each:
            inside, across, scale, _ = made[u]
            outs = []
            for h in range(BRANCH_HEADS):
                total = accs[u][h][HEAD_DIM : HEAD_DIM + 1]
                outs.append(accs[u][h][:HEAD_DIM] * (1.0 / total))
                lse_ref[ps[u], h : h + 1, :] = tops[u][h] * scale + jnp.log2(total)
            ot = jnp.concatenate(outs, 0)
            ot_ref[ps[u]] = ot
            vpad[u, PAD : PAD + L, :] = jnp.where(inside, vs[u], 0.0)
            lepe = conv_forward(vpad.at[u], PAD, L, taps, across)
            osum[u, :L, :] = ot.T + lepe + lb_ref[...]
        for u in each:
            tall_push(z, osum.at[u], ps[u], 1, 0, dst)
        return carry

    lax.fori_loop(start, stop, group, 0)


def tall_backward(
    z,
    start,
    stop,
    lim_ref,
    lw_ref,
    ot_ref,
    lse_ref,
    dlw_ref,
    src,
    gsrc,
    dst,
    qs,
    ks,
    vs,
    gpad,
    vpad,
    stage,
    kstack,
):
    L = qs.shape[1]
    norm = HEAD_DIM**-0.5

    def taps(a, l):
        t = tall_tap(a, l)
        return lw_ref[t : t + 1, :]

    def group(m, carry):
        each = range(z.tall_group)
        ps = [m * z.tall_group + u for u in each]
        for u in each:
            for n, target in enumerate((qs, ks, vs)):
                tall_pull(z, src, ps[u], 3, n, target.at[u], 0)
            tall_pull(z, gsrc, ps[u], 1, 0, gpad.at[u], PAD)
        made = [tall_prepare(z, ps[u], lim_ref, L) for u in each]
        gts = [gpad[u, PAD : PAD + L, :].T for u in each]
        qts = [tall_operands(z, ks[u], qs[u], made[u][3], kstack.at[u], L) for u in each]
        kts = [ks[u].T.astype(BF16) for u in each]
        dvs = [None] * len(ps)
        dks = [None] * len(ps)
        dqs = [[] for u in each]
        for some in z.tall_head_sets:
            scores = []
            dps = []
            for u in each:
                rows = slice(some[0] * L, (some[-1] + 1) * L)
                scores.append(mm(kstack[u, rows, :], qts[u]))
                v = vs[u]
                vstack = jnp.concatenate([jnp.where(head_lanes(h, L), v, 0.0) for h in some], 0)
                dps.append(mm(vstack.astype(BF16), gts[u].astype(BF16)))
            weights = []
            for u in each:
                prod = gts[u] * ot_ref[ps[u]]
                lse = lse_ref[ps[u]]
                row = []
                for i, h in enumerate(some):
                    rows = slice(i * L, (i + 1) * L)
                    delta = jnp.sum(prod[h * HEAD_DIM : (h + 1) * HEAD_DIM], 0, keepdims=True)
                    w = jnp.exp2(scores[u][rows] * made[u][2] - lse[h : h + 1])
                    ds = (w * (dps[u][rows] - delta)).astype(BF16)
                    row.append((w.astype(BF16), ds))
                weights.append(row)
            for u in each:
                for i, h in enumerate(some):
                    keep = head_lanes(h, L)
                    w, ds = weights[u][i]
                    dv_h = mm(w, jnp.where(keep, gpad[u, PAD : PAD + L, :], 0.0).astype(BF16))
                    dk_h = mm(ds, jnp.where(keep, qs[u], 0.0).astype(BF16))
                    dvs[u] = dv_h if dvs[u] is None else dvs[u] + dv_h
                    dks[u] = dk_h if dks[u] is None else dks[u] + dk_h
                    dqs[u].append(mm(kts[u][h * HEAD_DIM : (h + 1) * HEAD_DIM], ds))
        results = [(jnp.concatenate(dqs[u], 0), dks[u], dvs[u]) for u in each]
        sums = {}
        for u in each:
            inside, across = made[u][:2]
            vpad[u, PAD : PAD + L, :] = jnp.where(inside, vs[u], 0.0)
            lepe = conv_backward(gpad.at[u], PAD, L, taps, across)
            add_kernel_sums(sums, gpad.at[u], vpad.at[u], PAD, L, across, tall_tap)
            dqt, dk, dv = results[u]
            stage[u, 0, :L, :] = dqt.T * norm
            stage[u, 1, :L, :] = dk * norm
            stage[u, 2, :L, :] = dv + jnp.where(inside, lepe, 0.0)
        for t, value in sums.items():
            dlw_ref[t : t + 1, :] += jnp.sum(value, 0, keepdims=True)
        for u in each:
            for n in range(3):
                tall_push(z, stage.at[u, n], ps[u], 3, n, dst)
        return carry

    lax.fori_loop(start, stop, group, 0)


def greet(z):
    col = lax.axis_index("col")
    row = lax.axis_index("row")
    barrier = pltpu.get_barrier_semaphore()
    for k in range(1, z.C):
        pl.semaphore_signal(
            barrier, inc=1, device_id=(row, lax.rem(col + k, z.C)), device_id_type=MESH
        )
    for k in range(1, z.R):
        pl.semaphore_signal(
            barrier, inc=1, device_id=(lax.rem(row + k, z.R), col), device_id_type=MESH
        )


def all_greeted(z):
    pl.semaphore_wait(pltpu.get_barrier_semaphore(), z.C - 1 + z.R - 1)


class Exchange:
    def __init__(self, z, axis, source, target, sends, receives):
        self.axis = axis
        self.source, self.target = source, target
        self.me = lax.axis_index(axis)
        count = z.C if axis == "col" else z.R
        col = lax.axis_index("col")
        row = lax.axis_index("row")
        self.copies = []
        for k in range(1, count):
            other = lax.rem(self.me + k, count)
            self.copies.append(
                pltpu.make_async_remote_copy(
                    src_ref=source(other),
                    dst_ref=target(self.me),
                    send_sem=sends.at[k],
                    recv_sem=receives.at[k],
                    device_id=(row, other) if axis == "col" else (other, col),
                    device_id_type=MESH,
                )
            )

    def start(self):
        for copy in self.copies:
            copy.start()

    def keep_own(self):
        self.target(self.me)[...] = self.source(self.me)[...]

    def arrive(self):
        for copy in self.copies:
            copy.wait_recv()

    def sent(self):
        for copy in self.copies:
            copy.wait_send()


def split_of(rows, lanes, parts):
    for by_rows in range(parts, 0, -1):
        if parts % by_rows == 0:
            by_lanes = parts // by_rows
            if rows % (16 * by_rows) == 0 and lanes % (128 * by_lanes) == 0:
                return by_rows, by_lanes
    raise ValueError("no split")


def reduce_plan(z, lanes):
    rows = z.dim
    plan = []
    for members, stride in [(2, 1), (2, 2), (z.R, None), (z.C // 4, 4)]:
        a, b = split_of(rows, lanes, members)
        rows, lanes = rows // a, lanes // b
        plan.append((members, stride, a, b, rows, lanes))
    return plan


def reduce_width(z, lanes):
    while True:
        try:
            reduce_plan(z, lanes)
            return lanes
        except ValueError:
            lanes += 128


class Reduction:
    def __init__(self, z, plan, refs, small=None):
        n = len(plan)
        self.z, self.plan, self.n = z, plan, n
        self.full, refs = refs[0], refs[1:]
        self.recvs, refs = refs[:n], refs[n:]
        self.held, refs = refs[:n], refs[n:]
        self.gathers, refs = refs[:n], refs[n:]
        self.ssem, self.rsem, self.gsem, self.hsem = refs[:4]
        self.small = small
        if small is not None:
            self.smalls = refs[4 : 4 + n]
            self.vsem, self.wsem = refs[4 + n :]
        self.current = self.full
        self.copies = None

    @staticmethod
    def scratch(z, lanes, small_shape=None):
        plan = reduce_plan(z, lanes)
        dma = pltpu.SemaphoreType.DMA
        most = max(step[0] for step in plan)
        shapes = [pltpu.VMEM((z.dim, lanes), BF16)]
        shapes += [pltpu.VMEM((step[0], step[4], step[5]), BF16) for step in plan]
        shapes += [pltpu.VMEM((step[4], step[5]), BF16) for step in plan]
        shapes += [pltpu.VMEM((z.dim, lanes), BF16)]
        shapes += [pltpu.VMEM((step[4], step[5]), BF16) for step in plan[:-1]]
        shapes += [dma((len(plan), most)) for _ in range(4)]
        if small_shape is not None:
            shapes += [pltpu.VMEM((step[0],) + small_shape, F32) for step in plan]
            shapes += [dma((len(plan), most)) for _ in range(2)]
        return shapes

    def place(self, stage):
        members, stride = self.plan[stage][:2]
        if stride is None:
            return lax.axis_index("row")
        return lax.rem(lax.axis_index("col") // stride, members)

    def peer(self, stage, k):
        members, stride = self.plan[stage][:2]
        col = lax.axis_index("col")
        row = lax.axis_index("row")
        at = lax.rem(self.place(stage) + k, members)
        if stride is None:
            return at, (at, col)
        return at, (row, col + (at - self.place(stage)) * stride)

    def window(self, ref, stage, index):
        members, stride, a, b, rows, width = self.plan[stage]
        r0 = pl.multiple_of((index // b) * rows, 16)
        l0 = pl.multiple_of(lax.rem(index, b) * width, 128)
        return ref.at[pl.ds(r0, rows), pl.ds(l0, width)]

    def fill(self, pieces):
        D = self.z.dim
        at = 0
        for ref in pieces:
            for k in range(ref.shape[0] // D):
                width = ref.shape[1]
                self.full[:, at : at + width] = ref[k * D : (k + 1) * D, :].astype(BF16)
                at += width
        if at < self.full.shape[1]:
            self.full[:, at:] = jnp.zeros((D, self.full.shape[1] - at), BF16)

    def give(self, outs):
        D = self.z.dim
        at = 0
        for ref in outs:
            for k in range(ref.shape[0] // D):
                width = ref.shape[1]
                ref[k * D : (k + 1) * D, :] = self.current[:, at : at + width].astype(F32)
                at += width

    def scatter_start(self, stage):
        me = self.place(stage)
        self.copies = []
        for k in range(1, self.plan[stage][0]):
            index, device = self.peer(stage, k)
            self.copies.append(
                pltpu.make_async_remote_copy(
                    src_ref=self.window(self.current, stage, index),
                    dst_ref=self.recvs[stage].at[me],
                    send_sem=self.ssem.at[stage, k],
                    recv_sem=self.rsem.at[stage, k],
                    device_id=device,
                    device_id_type=MESH,
                )
            )
            if self.small is not None:
                self.copies.append(
                    pltpu.make_async_remote_copy(
                        src_ref=self.small,
                        dst_ref=self.smalls[stage].at[me],
                        send_sem=self.vsem.at[stage, k],
                        recv_sem=self.wsem.at[stage, k],
                        device_id=device,
                        device_id_type=MESH,
                    )
                )
        for copy in self.copies:
            copy.start()
        self.recvs[stage][me] = self.window(self.current, stage, me)[...]
        if self.small is not None:
            self.smalls[stage][me] = self.small[...]

    def scatter_end(self, stage, small_out=None):
        for copy in self.copies:
            copy.wait()
        members = self.plan[stage][0]
        rows, width = self.plan[stage][4:]
        for at, size in key_tiles(width, 512):
            lanes = slice(at, at + size)
            total = self.recvs[stage][0, :, lanes].astype(F32)
            for k in range(1, members):
                total = total + self.recvs[stage][k, :, lanes].astype(F32)
            self.held[stage][:, lanes] = total.astype(BF16)
        self.current = self.held[stage]
        if self.small is not None:
            small = self.smalls[stage][0]
            for k in range(1, members):
                small = small + self.smalls[stage][k]
            if stage + 1 < self.n:
                self.smalls[stage][0] = small
                self.small = self.smalls[stage].at[0]
            else:
                small_out[...] = small

    def gather_start(self, stage):
        me = self.place(stage)
        self.copies = []
        for k in range(1, self.plan[stage][0]):
            index, device = self.peer(stage, k)
            self.copies.append(
                pltpu.make_async_remote_copy(
                    src_ref=self.current,
                    dst_ref=self.window(self.gathers[stage], stage, me),
                    send_sem=self.gsem.at[stage, k],
                    recv_sem=self.hsem.at[stage, k],
                    device_id=device,
                    device_id_type=MESH,
                )
            )
        for copy in self.copies:
            copy.start()
        self.window(self.gathers[stage], stage, me)[...] = self.current[...]

    def gather_end(self, stage):
        for copy in self.copies:
            copy.wait()
        self.current = self.gathers[stage]

    def steps(self):
        n = self.n
        ends = [functools.partial(self.scatter_end, s) for s in range(n)]
        ends += [functools.partial(self.gather_end, s) for s in range(n - 1, -1, -1)]
        starts = [functools.partial(self.scatter_start, s) for s in range(n)]
        starts += [functools.partial(self.gather_start, s) for s in range(n - 1, -1, -1)]
        return starts, ends


def reduce_kernel(z, plan, dqkv_ref, small_ref, oqkv, osmall, *refs):
    greet(z)
    work = Reduction(z, plan, refs, small_ref)
    work.fill((dqkv_ref,))
    all_greeted(z)
    for stage in range(work.n):
        work.scatter_start(stage)
        work.scatter_end(stage, osmall)
    for stage in range(work.n - 1, -1, -1):
        work.gather_start(stage)
        work.gather_end(stage)
    work.give((oqkv,))


def reduce_last(z, dqkv, small, collective_id):
    arrays = (dqkv, small)
    lanes = reduce_width(z, dqkv.size // z.dim)
    vmem = pl.BlockSpec(memory_space=pltpu.VMEM)
    return pl.pallas_call(
        functools.partial(reduce_kernel, z, reduce_plan(z, lanes)),
        out_shape=tuple(jax.ShapeDtypeStruct(a.shape, F32) for a in arrays),
        in_specs=[vmem] * 2,
        out_specs=(vmem,) * 2,
        scratch_shapes=Reduction.scratch(z, lanes, small.shape),
        compiler_params=pltpu.CompilerParams(
            collective_id=collective_id, has_side_effects=True, vmem_limit_bytes=VMEM_LIMIT
        ),
        name="reduce_last",
    )(*arrays)


def front_kernel(
    z,
    wlim_ref,
    tlim_ref,
    x_ref,
    gain_ref,
    shift_ref,
    w_ref,
    b_ref,
    wtap_ref,
    wbias_ref,
    ttap_ref,
    tbias_ref,
    back_wide,
    back_tall,
    tq_ref,
    tot_ref,
    tlse_ref,
    v_ref,
    kcat,
    qtb,
    kt,
    ot,
    lse,
    pw,
    pt,
    gw,
    gt,
    send_wide,
    send_tall,
    recv_wide,
    recv_tall,
    out_wide,
    out_tall,
    t_src,
    t_dst,
    t_q,
    t_k,
    t_v,
    t_vpad,
    t_osum,
    t_kstack,
    qk,
    vpad,
    stage,
    vt,
    vt_all,
    ss0,
    ss1,
    osum,
    wsend,
    wrecv,
    tsend,
    trecv,
    wsend1,
    wrecv1,
    tsend1,
    trecv1,
    local,
):
    greet(z)
    dense_in(z, x_ref, gain_ref, shift_ref, w_ref, b_ref, send_wide, send_tall, pw, pt, gw, gt)
    all_greeted(z)
    wides = [
        Exchange(
            z,
            "col",
            lambda d, pair=pair: send_wide.at[d, pair],
            lambda d, pair=pair: recv_wide.at[d, pair],
            wsend.at[pair],
            wrecv.at[pair],
        )
        for pair in range(z.pairs)
    ]
    tall = Exchange(
        z, "row", lambda d: send_tall.at[d], lambda d: recv_tall.at[d], tsend, trecv
    )
    wides[0].start()
    tall.start()
    for wide in wides:
        wide.keep_own()
    tall.keep_own()
    for ref in (t_q, t_k, t_v, t_vpad, t_osum, vpad, qk):
        ref[...] = jnp.zeros_like(ref)
    groups = z.tall_slots // z.tall_group

    def tall_part(start, stop):
        tall_forward(
            z, start, stop, tlim_ref, ttap_ref, tbias_ref, tot_ref, tlse_ref,
            t_src, t_dst, t_q, t_k, t_v, t_vpad, t_osum, t_kstack,
        )

    early = groups // 2
    for pair in range(z.pairs):
        wides[pair].arrive()
        if pair + 1 < z.pairs:
            wides[pair + 1].start()
        wide_pair_forward(
            z, pair, wlim_ref, recv_wide, kcat, qtb, kt, ot, lse, qk, vpad, stage, vt, vt_all,
            ss0, ss1, osum,
        )
        if pair == 0:
            tall.arrive()
            tq_ref[...] = recv_tall[...]
            t_src[...] = recv_tall[...].astype(F32)
            tall_part(0, early)
    v_ref[...] = vpad[PAD : PAD + z.wide_len, :].astype(BF16)
    wide_mixture(z, wlim_ref, wtap_ref, wbias_ref, ot, vpad, osum, out_wide)
    back = Exchange(
        z, "col", lambda d: out_wide.at[d], lambda d: back_wide.at[d], wsend1, wrecv1
    )
    back.start()
    col = lax.axis_index("col")
    row = lax.axis_index("row")
    own_wide = pltpu.make_async_copy(out_wide.at[col], back_wide.at[col], local.at[0])
    own_wide.start()
    tall_part(early, groups)
    out_tall[...] = t_dst[...].astype(BF16)
    back_t = Exchange(
        z, "row", lambda d: out_tall.at[d], lambda d: back_tall.at[d], tsend1, trecv1
    )
    back_t.start()
    own_tall = pltpu.make_async_copy(out_tall.at[row], back_tall.at[row], local.at[1])
    own_tall.start()
    own_wide.wait()
    own_tall.wait()
    for job in wides + [tall, back, back_t]:
        job.sent()
    back.arrive()
    back_t.arrive()


def back_kernel(
    z,
    plan,
    wlim_ref,
    tlim_ref,
    gw_ref,
    gt_ref,
    tq_ref,
    tot_ref,
    tlse_ref,
    wtap_ref,
    ttap_ref,
    dpw_ref,
    dw1_ref,
    dw2_ref,
    v_any,
    kcat_any,
    qtb_any,
    kt_any,
    ot_any,
    lse_any,
    got_wide,
    got_tall,
    dwt_ref,
    dtt_ref,
    opw_ref,
    ow1_ref,
    ow2_ref,
    v_ref,
    kcat,
    qtb,
    kt,
    ot,
    lse,
    recv_wide,
    recv_tall,
    send_wide,
    send_tall,
    t_src,
    t_gsrc,
    t_q,
    t_k,
    t_v,
    t_gpad,
    t_vpad,
    t_stage,
    t_kstack,
    gpad,
    vpad,
    dotb,
    delta,
    dvl,
    dqt,
    dkt,
    dvt,
    stage,
    ss0,
    ss1,
    dp0,
    dp1,
    ps0,
    ps1,
    ds0,
    ds1,
    wsend,
    wrecv,
    tsend,
    trecv,
    wsend1,
    wrecv1,
    tsend1,
    trecv1,
    local,
    *refs,
):
    greet(z)
    loads = [
        pltpu.make_async_copy(a, b, local.at[i])
        for i, (a, b) in enumerate(
            zip((v_any, kcat_any, qtb_any, kt_any, ot_any, lse_any), (v_ref, kcat, qtb, kt, ot, lse))
        )
    ]
    for load in loads:
        load.start()
    work = Reduction(z, plan, refs)
    starts, ends = work.steps()
    work.fill((dpw_ref, dw1_ref, dw2_ref))
    all_greeted(z)
    tall = Exchange(z, "row", lambda d: gt_ref.at[d], lambda d: recv_tall.at[d], tsend, trecv)
    wide = Exchange(z, "col", lambda d: gw_ref.at[d], lambda d: recv_wide.at[d], wsend, wrecv)
    tall.start()
    wide.start()
    starts[0]()
    tall.keep_own()
    wide.keep_own()
    for ref in (t_q, t_k, t_v, t_gpad, t_vpad, t_stage):
        ref[...] = jnp.zeros_like(ref)
    dtt_ref[...] = jnp.zeros_like(dtt_ref)
    t_src[...] = tq_ref[...].astype(F32)
    groups = z.tall_slots // z.tall_group
    early = groups // 2

    def tall_part(start, stop):
        tall_backward(
            z, start, stop, tlim_ref, ttap_ref, tot_ref, tlse_ref, dtt_ref, t_src, t_gsrc, t_src,
            t_q, t_k, t_v, t_gpad, t_vpad, t_stage, t_kstack,
        )

    def point(i):
        ends[i]()
        starts[i + 1]()

    tall.arrive()
    t_gsrc[...] = recv_tall[...].astype(F32)
    tall_part(0, early)
    point(0)
    for load in loads:
        load.wait()
    wide.arrive()
    wide_backward_start(
        z, wlim_ref, recv_wide, wtap_ref, v_ref, ot, dwt_ref, gpad, vpad, dotb, delta, dvl, stage
    )
    point(1)
    slots = ((ss0, dp0, ps0, ds0), (ss1, dp1, ps1, ds1))
    outs = []
    at = 2
    col = lax.axis_index("col")
    row = lax.axis_index("row")
    own = []
    for pair in range(z.pairs):
        wide_pair_backward(
            z, pair, wlim_ref, v_ref, kcat, qtb, kt, lse, dotb, delta, dvl, dqt, dkt, dvt, gpad, vpad,
            stage, slots, send_wide, lambda: point(at),
        )
        point(at + 1)
        at += 2
        job = Exchange(
            z,
            "col",
            lambda d, pair=pair: send_wide.at[d, pair],
            lambda d, pair=pair: got_wide.at[d, pair],
            wsend1.at[pair],
            wrecv1.at[pair],
        )
        job.start()
        outs.append(job)
        copy = pltpu.make_async_copy(
            send_wide.at[col, pair], got_wide.at[col, pair], local.at[6 + pair]
        )
        copy.start()
        own.append(copy)
    tall_part(early, groups)
    send_tall[...] = t_src[...].astype(BF16)
    job = Exchange(
        z, "row", lambda d: send_tall.at[d], lambda d: got_tall.at[d], tsend1, trecv1
    )
    job.start()
    outs.append(job)
    copy = pltpu.make_async_copy(send_tall.at[row], got_tall.at[row], local.at[8])
    copy.start()
    own.append(copy)
    while at < len(ends) - 1:
        point(at)
        at += 1
    ends[at]()
    work.give((opw_ref, ow1_ref, ow2_ref))
    for copy in own:
        copy.wait()
    tall.sent()
    wide.sent()
    for job in outs:
        job.sent()
        job.arrive()


def local_call(kernel, z, name, outs, scratch, scalars, arrays):
    vmem = pl.BlockSpec(memory_space=pltpu.VMEM)
    smem = pl.BlockSpec(memory_space=pltpu.SMEM)
    return pl.pallas_call(
        functools.partial(kernel, z),
        out_shape=tuple(jax.ShapeDtypeStruct(shape, kind) for shape, kind in outs),
        in_specs=[smem] * len(scalars) + [vmem] * len(arrays),
        out_specs=(vmem,) * len(outs),
        scratch_shapes=[pltpu.VMEM(shape, kind) for shape, kind in scratch],
        compiler_params=pltpu.CompilerParams(vmem_limit_bytes=VMEM_LIMIT),
        name=name,
    )(*scalars, *arrays)


def per_device(
    mesh,
    features,
    heights,
    widths,
    norm1_gain,
    norm1_shift,
    qkv_weight,
    query_bias,
    value_bias,
    lepe_weight,
    lepe_bias,
    proj_weight,
    proj_bias,
    norm2_gain,
    norm2_shift,
    fc1_weight,
    fc1_bias,
    fc2_weight,
    fc2_bias,
    cotangent,
):
    z = Sizes(mesh, features.shape)
    B, D, TC, TR = z.images, z.dim, z.cols, z.rows
    col = lax.axis_index("col")
    row = lax.axis_index("row")
    row_start = row * TR
    col_start = col * TC
    x = features.transpose(1, 2, 0, 3)
    ct = cotangent.transpose(1, 2, 0, 3)
    qkv_bias = jnp.concatenate([query_bias, jnp.zeros_like(query_bias), value_bias])
    line = lambda v: v.reshape(1, -1)
    FF = fc1_weight.shape[1]

    image = col // z.G
    wide_lim = jnp.stack(
        [jnp.clip(heights[image] - row_start, 0, TR), jnp.clip(widths[image], 0, z.C * TC)]
    )
    own_images = row * z.tall_images + jnp.arange(z.tall_images)
    stripe_start = col_start + SW * jnp.arange(z.stripes)
    tall_across = jnp.clip(widths[own_images][:, None] - stripe_start[None], 0, SW)
    tall_along = jnp.broadcast_to(
        jnp.clip(heights[own_images], 0, z.R * TR)[:, None], tall_across.shape
    )
    tall_lim = jnp.stack([tall_across.reshape(-1), tall_along.reshape(-1)])
    part = lax.rem(col, z.G)
    pad_taps = lambda w: jnp.pad(w, ((0, 16 - w.shape[0]), (0, HALF - w.shape[1])))
    wide_taps = pad_taps(lax.dynamic_slice_in_dim(lepe_weight[:, :HALF], part * z.hc, z.hc, 1))
    wide_tap_bias = jnp.pad(
        lax.dynamic_slice_in_dim(lepe_bias[:HALF], part * z.hc, z.hc, 0), (0, HALF - z.hc)
    )
    tall_taps = pad_taps(lepe_weight[:, HALF:])
    tall_tap_bias = lepe_bias[HALF:]

    wide3 = (z.C, z.pairs, z.pair_rows, HALF)
    wide1 = (z.C, z.wide_rows1, z.hc)
    tall3 = (z.R, z.tall_rows3, HALF)
    tall1 = (z.R, z.tall_rows1, HALF)
    flat = up(z.tokens, 16 * B) + 16 * B
    L = z.wide_len
    LT = up(z.tall_len, 128)
    per_head, tail, blocks, tail_lanes, span = wide_plan(z)
    vmem = pl.BlockSpec(memory_space=pltpu.VMEM)
    smem = pl.BlockSpec(memory_space=pltpu.SMEM)
    anywhere = pl.BlockSpec(memory_space=pl.ANY)
    dma = pltpu.SemaphoreType.DMA
    saved = [
        ((L, HALF), BF16),
        ((z.pairs, L, 2 * HALF), BF16),
        ((z.pairs, 2 * HALF, span), BF16),
        ((z.pairs, HALF // 2, L), BF16),
        ((HALF, per_head * z.qb + z.pairs * tail_lanes), F32),
        ((8, z.pairs * span), F32),
    ]
    tall_scratch = [
        ((z.tall_group, LT, HALF), F32),
        ((z.tall_group, LT, HALF), F32),
        ((z.tall_group, LT, HALF), F32),
        ((z.tall_group, LT + 16, HALF), F32),
        ((z.tall_group, LT + 16, HALF), F32),
        ((z.tall_group, BRANCH_HEADS * LT, 2 * HALF), BF16),
    ]
    sems = [
        dma((z.pairs, z.C)),
        dma((z.pairs, z.C)),
        dma((z.R,)),
        dma((z.R,)),
        dma((z.C,)),
        dma((z.C,)),
        dma((z.R,)),
        dma((z.R,)),
    ]
    shapes = lambda items: tuple(jax.ShapeDtypeStruct(s, k) for s, k in items)
    scratches = lambda items: [pltpu.VMEM(s, k) for s, k in items]

    back_wide, back_tall, tall_qkv, tall_ot, tall_lse, *wide_saved = pl.pallas_call(
        functools.partial(front_kernel, z),
        out_shape=shapes(
            [
                (wide1, BF16),
                (tall1, BF16),
                (tall3, BF16),
                ((z.tall_slots, HALF, LT), F32),
                ((z.tall_slots, 8, LT), F32),
            ]
            + saved
        ),
        in_specs=[smem] * 2 + [vmem] * 9,
        out_specs=(anywhere, anywhere) + (vmem,) * (3 + len(saved)),
        scratch_shapes=scratches(
            [
                ((3, flat, HALF), F32),
                ((3, flat, HALF), F32),
                (wide3, F32),
                (tall3, F32),
                (wide3, BF16),
                (tall3, BF16),
                (wide3, BF16),
                (tall3, BF16),
                (wide1, BF16),
                (tall1, BF16),
                (tall3, F32),
                (tall1, F32),
            ]
            + tall_scratch
            + [
                ((L, HALF), F32),
                ((L + 2 * PAD, HALF), F32),
                ((z.pair_rows, HALF), F32),
                ((2, HEAD_DIM + 16, L), BF16),
                ((HALF + 16, L), BF16),
                ((L, z.qb), F32),
                ((L, z.qb), F32),
                ((L + z.wide_rows1, HALF), F32),
            ]
        )
        + sems
        + [dma((2,))],
        compiler_params=pltpu.CompilerParams(
            collective_id=0, has_side_effects=True, vmem_limit_bytes=VMEM_LIMIT
        ),
        name="front",
    )(
        wide_lim,
        tall_lim,
        x,
        line(norm1_gain),
        line(norm1_shift),
        qkv_weight,
        line(qkv_bias),
        wide_taps,
        line(wide_tap_bias),
        tall_taps,
        line(tall_tap_bias),
    )

    limits = jnp.broadcast_to(jnp.stack([heights, widths])[:, :, None], (2, B, D))
    y, gres, gmix_wide, gmix_tall, dproj, dfc1, dfc2, vec_mid, db1 = local_call(
        dense_mid_kernel,
        z,
        "dense_mid",
        [
            ((TR, TC, B, D), BF16),
            ((TR, TC, B, D), F32),
            (wide1, BF16),
            (tall1, BF16),
            ((D, D), F32),
            ((D, FF), F32),
            ((FF, D), F32),
            ((8, D), F32),
            ((8, D), F32),
        ],
        [((flat, HALF), F32)] * 4 + [(tall1, F32)],
        [jnp.stack([row_start, col_start])],
        [
            back_wide,
            back_tall,
            x,
            ct,
            limits,
            proj_weight,
            line(proj_bias),
            line(norm2_gain),
            line(norm2_shift),
            fc1_weight,
            line(fc1_bias),
            fc2_weight,
            line(fc2_bias),
        ],
    )
    lanes = reduce_width(z, (dproj.size + dfc1.size + dfc2.size) // D)
    plan = reduce_plan(z, lanes)
    got_wide, got_tall, dwide_taps, dtall_taps, dproj, dfc1, dfc2 = pl.pallas_call(
        functools.partial(back_kernel, z, plan),
        out_shape=shapes(
            [
                (wide3, BF16),
                (tall3, BF16),
                ((16, HALF), F32),
                ((16, HALF), F32),
                (dproj.shape, F32),
                (dfc1.shape, F32),
                (dfc2.shape, F32),
            ]
        ),
        in_specs=[smem] * 2 + [vmem] * 10 + [anywhere] * len(saved),
        out_specs=(anywhere, anywhere) + (vmem,) * 5,
        scratch_shapes=scratches(
            saved
            + [
                (wide1, BF16),
                (tall1, BF16),
                (wide3, BF16),
                (tall3, BF16),
                (tall3, F32),
                (tall1, F32),
            ]
            + tall_scratch[:5]
            + [((z.tall_group, 3, LT + 16, HALF), F32), tall_scratch[5]]
            + [
                ((L + 2 * PAD, HALF), F32),
                ((L + 2 * PAD, HALF), F32),
                ((HALF, z.pairs * span), BF16),
                ((8, z.pairs * span), F32),
                ((L, HALF), F32),
                ((HALF // 2, per_head * z.qb), F32),
                ((HALF // 2, L), F32),
                ((HALF // 2, L), F32),
                ((z.pair_rows, HALF), F32),
            ]
            + [((L, z.qb), F32)] * 4
            + [((L, z.qb), BF16)] * 4
        )
        + [sems[4], sems[5], sems[2], sems[3], sems[0], sems[1], sems[6], sems[7]]
        + [dma((9,))]
        + Reduction.scratch(z, lanes),
        compiler_params=pltpu.CompilerParams(
            collective_id=1, has_side_effects=True, vmem_limit_bytes=VMEM_LIMIT
        ),
        name="back",
    )(
        wide_lim,
        tall_lim,
        gmix_wide,
        gmix_tall,
        tall_qkv,
        tall_ot,
        tall_lse,
        wide_taps,
        tall_taps,
        dproj,
        dfc1,
        dfc2,
        *wide_saved,
    )

    grad_in, dqkv, vec_out = local_call(
        dense_out_kernel,
        z,
        "dense_out",
        [((TR, TC, B, D), F32), ((D, 3 * D), F32), ((8, D), F32)],
        [((3, flat, HALF), F32), ((3, flat, HALF), F32), (wide3, F32), (tall3, F32)],
        [],
        [got_wide, got_tall, x, gres, line(norm1_gain), line(norm1_shift), qkv_weight],
    )
    own_taps = dwide_taps[:, : z.hc]
    if z.G > 1:
        own_taps = lax.dynamic_update_slice(
            jnp.zeros((16, HALF), F32), own_taps, (0, part * z.hc)
        )
    small = jnp.concatenate(
        [vec_mid, vec_out, jnp.concatenate([own_taps, dtall_taps], -1), db1], 0
    )
    dqkv, small = reduce_last(z, dqkv, small, 2)
    return (
        y.transpose(2, 0, 1, 3),
        grad_in.transpose(2, 0, 1, 3),
        small[8],
        small[9],
        dqkv,
        small[10],
        small[11],
        small[16:25],
        small[4],
        dproj,
        small[2],
        small[0],
        small[1],
        dfc1,
        small[32 : 32 + FF // D].reshape(-1),
        dfc2,
        small[3],
    )


def solution(mesh):
    image = P(None, "row", "col", None)
    return jax.shard_map(
        functools.partial(per_device, mesh),
        mesh=mesh,
        in_specs=(image,) + (P(),) * 17 + (image,),
        out_specs=(image, image) + (P(),) * 15,
        check_vma=False,
    )
```

```python
import functools
import math

import jax
import jax.numpy as jnp
from jax import lax
from jax.experimental import pallas as pl
from jax.experimental.pallas import tpu as pltpu
from jax.sharding import PartitionSpec as P

HEADS = 8
SW = 7
BRANCH_HEADS = HEADS // 2
HALF = 128
HEAD_DIM = 32
NORM_EPSILON = 1e-05
MASKED = -1e30
LOG2E = math.log2(math.e)
PAD = 8
VMEM_LIMIT = 62 * 1024 * 1024
MESH = pl.DeviceIdType.MESH
F32 = jnp.float32
BF16 = jnp.bfloat16
NT = (((1,), (1,)), ((), ()))
TN = (((0,), (0,)), ((), ()))


def up(value, unit):
    return -(-value // unit) * unit


def mm(a, b):
    return jnp.dot(a, b, preferred_element_type=F32)


def mm_nt(a, b):
    return lax.dot_general(a, b, NT, preferred_element_type=F32)


def mm_tn(a, b):
    return lax.dot_general(a, b, TN, preferred_element_type=F32)


class Sizes:
    def __init__(self, mesh, shape):
        self.images, self.rows, self.cols, self.dim = shape
        self.R = mesh.shape["row"]
        self.C = mesh.shape["col"]
        self.pix = self.rows * self.cols
        self.tokens = self.pix * self.images
        self.stripes = self.cols // SW
        self.G = self.C // self.images
        self.wide_heads = BRANCH_HEADS // self.G
        self.hc = HALF // self.G
        self.tall_images = self.images // self.R
        self.wide_len = self.C * self.pix
        self.qb = 256 if self.wide_len <= 2048 else 128
        self.tall_own = self.rows * SW
        self.tall_len = self.R * self.tall_own
        self.tall_pad = up(self.tall_own, 8)
        self.pairs = self.wide_heads // 2
        self.fold = self.pix // 2
        self.pair_rows = up(self.pix + self.fold, 16)
        self.wide_rows1 = up(self.pix, 16)
        self.tall_slots = self.tall_images * self.stripes
        self.tall_group = 4 if self.tall_len <= 128 else 1
        heads = list(range(BRANCH_HEADS))
        self.tall_head_sets = [heads] if self.tall_group > 1 else [[h] for h in heads]
        self.tall_rows1 = self.tall_slots * self.tall_pad
        self.tall_rows3 = 3 * self.tall_rows1


def norm_parts(values):
    average = jnp.mean(values, -1, keepdims=True)
    centred = values - average
    spread = jnp.mean(centred * centred, -1, keepdims=True)
    inverse = lax.rsqrt(spread + NORM_EPSILON)
    return centred * inverse, inverse


def low_half(rows):
    return lax.broadcasted_iota(jnp.int32, (rows, HALF), 1) < HALF // 2


def turn(value):
    return jnp.concatenate([value[:, HALF // 2 :], value[:, : HALF // 2]], -1)


def dense_in(z, x_ref, gain_ref, shift_ref, w_ref, bias, sw_ref, st_ref, pw, pt, gw, gt):
    B, D, TC, TR = z.images, z.dim, z.cols, z.rows

    def one_row(i, carry):
        x = x_ref[i].astype(F32).reshape(TC * B, D)
        normed, _ = norm_parts(x)
        low = (normed * gain_ref[...] + shift_ref[...]).astype(BF16)
        proj = (mm(low, w_ref[...]) + bias).reshape(TC, B, 3 * D)
        for j in range(TC):
            s, jj = divmod(j, SW)
            wide_at = pl.multiple_of((j * TR + i) * B, B)
            tall_at = pl.multiple_of(((s * TR + i) * SW + jj) * B, B)
            for n in range(3):
                pw[n, pl.ds(wide_at, B), :] = proj[j, :, n * D : n * D + HALF]
                pt[n, pl.ds(tall_at, B), :] = proj[j, :, n * D + HALF : (n + 1) * D]
        return carry

    lax.fori_loop(0, TR, one_row, 0)
    rows = up(z.pix, 8)
    half = up(z.fold, 8)
    lo = low_half(rows)
    lo_half = low_half(half)
    gw[:, :, z.pix + z.fold :, :] = jnp.zeros_like(gw[:, :, z.pix + z.fold :, :])
    for b in range(B):
        q = pw[0, pl.ds(b, rows, stride=B), :]
        k = pw[1, pl.ds(b, rows, stride=B), :]
        v1 = pw[2, pl.ds(b, half, stride=B), :]
        v2 = pw[2, pl.ds(z.fold * B + b, half, stride=B), :]
        qk = (jnp.where(lo, q, turn(k)), jnp.where(lo, turn(q), k))
        vv = (jnp.where(lo_half, v1, turn(v2)), jnp.where(lo_half, turn(v1), v2))
        for u in range(2):
            d = b * z.G + u // z.pairs
            gw[d, u % z.pairs, :rows, :] = qk[u]
            gw[d, u % z.pairs, z.pix : z.pix + z.fold, :] = vv[u][: z.fold]
    sw_ref[...] = gw[...].astype(BF16)
    gt[...] = jnp.zeros_like(gt)
    for b in range(B):
        for n in range(3):
            for s in range(z.stripes):
                part = pt[n, pl.ds(s * z.tall_own * B + b, z.tall_own, stride=B), :]
                at = (((b % z.tall_images) * z.stripes + s) * 3 + n) * z.tall_pad
                gt[b // z.tall_images, at : at + z.tall_own, :] = part
    st_ref[...] = gt[...].astype(BF16)


def erf_parts(values):
    cdf = 0.5 * (1.0 + lax.erf(values * (0.5**0.5)))
    density = jnp.exp(-0.5 * values * values) * (1.0 / math.sqrt(2.0 * math.pi))
    return cdf, density


def dense_mid_kernel(
    z,
    heights_ref,
    widths_ref,
    rw_ref,
    rt_ref,
    x_ref,
    ct_ref,
    pw_ref,
    pb_ref,
    gain_ref,
    shift_ref,
    w1_ref,
    b1_ref,
    w2_ref,
    b2_ref,
    y_ref,
    gres_ref,
    gw_ref,
    gt_ref,
    dpw_ref,
    dw1_ref,
    dw2_ref,
    vec_ref,
    mw,
    mt,
    gmw,
    gmt,
    gts,
):
    B, D, TC, TR = z.images, z.dim, z.cols, z.rows
    T = TC * B
    for b in range(B):
        parts = [
            rw_ref[b * z.G + g].astype(F32)[: z.pix] for g in range(z.G)
        ]
        mw[pl.ds(b, z.pix, stride=B), :] = parts[0] if z.G == 1 else jnp.concatenate(parts, -1)
    gts[...] = rt_ref[...].astype(F32)
    for b in range(B):
        for s in range(z.stripes):
            at = ((b % z.tall_images) * z.stripes + s) * z.tall_pad
            mt[pl.ds(s * z.tall_own * B + b, z.tall_own, stride=B), :] = gts[
                b // z.tall_images, at : at + z.tall_own, :
            ]
    dpw_ref[...] = jnp.zeros_like(dpw_ref)
    dw1_ref[...] = jnp.zeros_like(dw1_ref)
    dw2_ref[...] = jnp.zeros_like(dw2_ref)
    vec_ref[...] = jnp.zeros_like(vec_ref)
    gmw[...] = jnp.zeros_like(gmw)
    row_start = lax.axis_index("row") * TR
    col_start = lax.axis_index("col") * TC
    image = lax.broadcasted_iota(jnp.int32, (B, D), 0)
    height = jnp.zeros((B, D), jnp.int32)
    width = jnp.zeros((B, D), jnp.int32)
    for b in range(B):
        height = jnp.where(image == b, heights_ref[b], height)
        width = jnp.where(image == b, widths_ref[b], width)
    below_cols = (lax.broadcasted_iota(jnp.int32, (TC, B, D), 0) + col_start) < width[None]

    def one_row(i, carry):
        x = x_ref[i].astype(F32).reshape(T, D)
        wide = []
        tall = []
        for j in range(TC):
            s, jj = divmod(j, SW)
            wide_at = pl.multiple_of((j * TR + i) * B, B)
            tall_at = pl.multiple_of(((s * TR + i) * SW + jj) * B, B)
            wide.append(mw[pl.ds(wide_at, B), :])
            tall.append(mt[pl.ds(tall_at, B), :])
        mixture = jnp.concatenate(
            [jnp.concatenate(wide, 0), jnp.concatenate(tall, 0)], -1
        ).astype(BF16)
        residual = x + (mm(mixture, pw_ref[...]) + pb_ref[...])
        n2, r2 = norm_parts(residual)
        act = (n2 * gain_ref[...] + shift_ref[...]).astype(BF16)
        pre = mm(act, w1_ref[...]) + b1_ref[...]
        cdf, density = erf_parts(pre)
        hidden = (pre * cdf).astype(BF16)
        slope = cdf + pre * density
        out = residual + (mm(hidden, w2_ref[...]) + b2_ref[...])
        y_ref[i] = out.astype(BF16).reshape(TC, B, D)
        below_rows = (i + row_start) < height[None]
        inside = jnp.logical_and(below_cols, below_rows)
        gy = jnp.where(inside, ct_ref[i].astype(F32), 0.0).reshape(T, D)
        gy_low = gy.astype(BF16)
        dw2_ref[...] += mm_tn(hidden, gy_low)
        gpre = (mm_nt(gy_low, w2_ref[...]) * slope).astype(BF16)
        dw1_ref[...] += mm_tn(act, gpre)
        db1 = jnp.sum(gpre.astype(F32), 0, keepdims=True)
        for k in range(db1.shape[1] // D):
            vec_ref[8 + k : 9 + k, :] += db1[:, k * D : (k + 1) * D]
        gact = mm_nt(gpre, w1_ref[...])
        g = gact * gain_ref[...]
        gres = gy + r2 * (
            g - jnp.mean(g, -1, keepdims=True) - n2 * jnp.mean(g * n2, -1, keepdims=True)
        )
        gres_ref[i] = gres.reshape(TC, B, D)
        gattn = gres.astype(BF16)
        dpw_ref[...] += mm_tn(mixture, gattn)
        gmix = mm_nt(gattn, pw_ref[...]).astype(BF16).astype(F32)
        vec_ref[0:1, :] += jnp.sum(gact * n2, 0, keepdims=True)
        vec_ref[1:2, :] += jnp.sum(gact, 0, keepdims=True)
        vec_ref[2:3, :] += jnp.sum(gattn.astype(F32), 0, keepdims=True)
        vec_ref[3:4, :] += jnp.sum(gy, 0, keepdims=True)
        vec_ref[4:5, :] += jnp.sum(gmix, 0, keepdims=True)
        gm3 = gmix.reshape(TC, B, D)
        for j in range(TC):
            s, jj = divmod(j, SW)
            wide_at = pl.multiple_of((j * TR + i) * B, B)
            tall_at = pl.multiple_of(((s * TR + i) * SW + jj) * B, B)
            gmw[pl.ds(wide_at, B), :] = gm3[j, :, :HALF]
            gmt[pl.ds(tall_at, B), :] = gm3[j, :, HALF:]
        return carry

    lax.fori_loop(0, TR, one_row, 0)
    gts[...] = jnp.zeros_like(gts)
    for b in range(B):
        part = gmw[pl.ds(b, z.wide_rows1, stride=B), :].astype(BF16)
        for g in range(z.G):
            gw_ref[b * z.G + g] = part[:, g * z.hc : (g + 1) * z.hc]
        for s in range(z.stripes):
            at = ((b % z.tall_images) * z.stripes + s) * z.tall_pad
            gts[b // z.tall_images, at : at + z.tall_own, :] = gmt[
                pl.ds(s * z.tall_own * B + b, z.tall_own, stride=B), :
            ]
    gt_ref[...] = gts[...].astype(BF16)


def dense_out_kernel(
    z,
    rw_ref,
    rt_ref,
    x_ref,
    gres_ref,
    gain_ref,
    shift_ref,
    w_ref,
    sum_ref,
    gin_ref,
    dw_ref,
    vec_ref,
    dpw_ref,
    dw1_ref,
    dw2_ref,
    pw,
    pt,
    gw,
    gt,
):
    B, D, TC, TR = z.images, z.dim, z.cols, z.rows
    T = TC * B
    gw[...] = rw_ref[...].astype(F32)
    gt[...] = rt_ref[...].astype(F32)
    spread(sum_ref, (dpw_ref, dw1_ref, dw2_ref))
    lo = low_half(z.pix)
    lo_half = low_half(z.fold)
    for b in range(B):
        qk = []
        vv = []
        for u in range(2):
            d = b * z.G + u // z.pairs
            qk.append(gw[d, u % z.pairs, : z.pix, :])
            vv.append(gw[d, u % z.pairs, z.pix : z.pix + z.fold, :])
        places = pl.ds(b, z.pix, stride=B)
        pw[0, places, :] = jnp.where(lo, qk[0], turn(qk[1]))
        pw[1, places, :] = jnp.where(lo, turn(qk[0]), qk[1])
        pw[2, pl.ds(b, z.fold, stride=B), :] = jnp.where(lo_half, vv[0], turn(vv[1]))
        pw[2, pl.ds(z.fold * B + b, z.fold, stride=B), :] = jnp.where(
            lo_half, turn(vv[0]), vv[1]
        )
        for n in range(3):
            for s in range(z.stripes):
                at = (((b % z.tall_images) * z.stripes + s) * 3 + n) * z.tall_pad
                pt[n, pl.ds(s * z.tall_own * B + b, z.tall_own, stride=B), :] = gt[
                    b // z.tall_images, at : at + z.tall_own, :
                ]
    dw_ref[...] = jnp.zeros_like(dw_ref)
    vec_ref[...] = jnp.zeros_like(vec_ref)

    def one_row(i, carry):
        x = x_ref[i].astype(F32).reshape(T, D)
        n1, r1 = norm_parts(x)
        low = (n1 * gain_ref[...] + shift_ref[...]).astype(BF16)
        lanes = []
        for n in range(3):
            wide = []
            tall = []
            for j in range(TC):
                s, jj = divmod(j, SW)
                wide_at = pl.multiple_of((j * TR + i) * B, B)
                tall_at = pl.multiple_of(((s * TR + i) * SW + jj) * B, B)
                wide.append(pw[n, pl.ds(wide_at, B), :])
                tall.append(pt[n, pl.ds(tall_at, B), :])
            lanes.append(jnp.concatenate(wide, 0))
            lanes.append(jnp.concatenate(tall, 0))
        gproj = jnp.concatenate(lanes, -1)
        vec_ref[2:3, :] += jnp.sum(gproj[:, :D], 0, keepdims=True)
        vec_ref[3:4, :] += jnp.sum(gproj[:, 2 * D :], 0, keepdims=True)
        gproj = gproj.astype(BF16)
        dw_ref[...] += mm_tn(low, gproj)
        gn = mm_nt(gproj, w_ref[...])
        vec_ref[0:1, :] += jnp.sum(gn * n1, 0, keepdims=True)
        vec_ref[1:2, :] += jnp.sum(gn, 0, keepdims=True)
        g = gn * gain_ref[...]
        gin = gres_ref[i].reshape(T, D) + r1 * (
            g - jnp.mean(g, -1, keepdims=True) - n1 * jnp.mean(g * n1, -1, keepdims=True)
        )
        gin_ref[i] = gin.reshape(TC, B, D)
        return carry

    lax.fori_loop(0, TR, one_row, 0)


def key_tiles(length, tile):
    return [(at, min(tile, length - at)) for at in range(0, length, tile)]


def token_places(start, count, lanes):
    token = (lax.broadcasted_iota(jnp.int32, (count, lanes), 0) + start).astype(F32)
    along = jnp.floor((token + 0.5) * (1.0 / SW))
    across = token - along * SW
    return along, across


def conv_forward(vpad, base, count, kernels, across):
    total = None
    for a in (-1, 0, 1):
        inner = None
        for l in (-1, 0, 1):
            term = kernels(a, l) * vpad[base + SW * l + a : base + SW * l + a + count, :]
            inner = term if inner is None else inner + term
        if a == -1:
            inner = jnp.where(across >= 1, inner, 0.0)
        if a == 1:
            inner = jnp.where(across <= SW - 2, inner, 0.0)
        total = inner if total is None else total + inner
    return total


def conv_backward(gpad, base, count, kernels, across):
    total = None
    for a in (-1, 0, 1):
        inner = None
        for l in (-1, 0, 1):
            at = base - SW * l - a
            term = kernels(a, l) * gpad[at : at + count, :]
            inner = term if inner is None else inner + term
        if a == -1:
            inner = jnp.where(across <= SW - 2, inner, 0.0)
        if a == 1:
            inner = jnp.where(across >= 1, inner, 0.0)
        total = inner if total is None else total + inner
    return total


def wide_tap(a, l):
    return 3 * (a + 1) + (l + 1)


def tall_tap(a, l):
    return 3 * (l + 1) + (a + 1)


def head_lanes(h, rows):
    lane = lax.broadcasted_iota(jnp.int32, (rows, HALF), 1)
    return jnp.logical_and(lane >= h * HEAD_DIM, lane < (h + 1) * HEAD_DIM)


def wide_plan(z):
    per_head = z.wide_len // z.qb
    tail = z.wide_len - per_head * z.qb
    blocks = 2 * per_head
    lanes = up(2 * tail, 128)
    return per_head, tail, blocks, lanes, blocks * z.qb + lanes


def diagonal(tail, first, lanes):
    channel = lax.broadcasted_iota(jnp.int32, (HALF, lanes), 0) - first * HEAD_DIM
    query = lax.broadcasted_iota(jnp.int32, (HALF, lanes), 1)
    keep = channel < -HALF
    for h in range(2):
        keep = jnp.logical_or(
            keep,
            jnp.logical_and(
                jnp.logical_and(channel >= h * HEAD_DIM, channel < (h + 1) * HEAD_DIM),
                jnp.logical_and(query >= h * tail, query < (h + 1) * tail),
            ),
        )
    return keep


def tail_columns(rows, tail, first, lanes):
    copies = [rows, rows]
    if lanes > 2 * tail:
        copies.append(jnp.zeros((lanes - 2 * tail, HALF), F32))
    return jnp.where(diagonal(tail, first, lanes), jnp.concatenate(copies, 0).T, 0.0)


def tail_rows(columns, tail):
    flat = columns.T
    return flat[:tail] + flat[tail : 2 * tail]


def head_rows_mask(h, value):
    row = lax.broadcasted_iota(jnp.int32, value.shape, 0)
    keep = jnp.logical_and(row >= h * HEAD_DIM, row < (h + 1) * HEAD_DIM)
    return jnp.where(keep, value, 0.0)


def between(value, high):
    return jnp.maximum(jnp.minimum(value, high), 0)


def wide_ends(z, heights_ref, widths_ref):
    image = lax.axis_index("col") // z.G
    start = lax.axis_index("row") * z.rows
    return (
        between(heights_ref[image] - start, z.rows),
        between(widths_ref[image], z.C * z.cols),
    )


def tall_ends(z, heights_ref, widths_ref):
    def ends(p):
        image = lax.axis_index("row") * z.tall_images + p // z.stripes
        start = lax.axis_index("col") * z.cols + lax.rem(p, z.stripes) * SW
        return (
            between(widths_ref[image] - start, SW),
            between(heights_ref[image], z.R * z.rows),
        )

    return ends


def own_lanes(z, value):
    if z.G == 1:
        return value
    turned = jnp.where(lax.rem(lax.axis_index("col"), z.G) == 0, value, turn(value))
    return jnp.where(low_half(value.shape[0]), turned, 0.0)


def wide_limits(lim_ref):
    across_limit, along_limit = lim_ref
    empty = across_limit * along_limit == 0
    scale = jnp.where(empty, 1e-20, LOG2E * HEAD_DIM**-0.5)
    return across_limit, along_limit, empty, scale


def wide_inside(lim_ref, at, size):
    along, across = token_places(at, size, HALF)
    return jnp.logical_and(across < lim_ref[0], along < lim_ref[1]), across


def wide_pair_forward(z, pair, lim_ref, recv, kcat, qtb, kt, ot, lse, qk, vpad, stage, vt, vt_all, ss0, ss1, osum):
    L = z.wide_len
    per_head, tail, blocks, tail_lanes, span = wide_plan(z)
    full = per_head * z.qb
    base = pair * span
    _, _, empty, scale = wide_limits(lim_ref)
    lo = low_half(z.fold)
    for c in range(z.C):
        stage[...] = recv[c, pair].astype(F32)
        at = c * z.pix
        qk[at : at + z.pix, :] = stage[: z.pix, :]
        v = stage[z.pix : z.pix + z.fold, :]
        one = slice(PAD + at, PAD + at + z.fold)
        two = slice(PAD + at + z.fold, PAD + at + z.pix)
        if pair == 0:
            vpad[one, :] = jnp.where(lo, v, 0.0)
            vpad[two, :] = jnp.where(lo, turn(v), 0.0)
        else:
            vpad[one, :] = jnp.where(lo, vpad[one, :], turn(v))
            vpad[two, :] = jnp.where(lo, vpad[two, :], v)
    ones = jnp.where(lax.broadcasted_iota(jnp.int32, (HALF, z.qb), 0) == 0, 1.0, 0.0).astype(BF16)

    def prepare(at, size):
        rows = pl.ds(at, size)
        both = qk[rows, :]
        kcat[pair, rows, :HALF] = both.astype(BF16)
        inside, _ = wide_inside(lim_ref, at, size)
        allowed = jnp.logical_or(inside, empty)
        lane = lax.broadcasted_iota(jnp.int32, (size, HALF), 1) == 0
        bias = jnp.where(jnp.logical_and(lane, jnp.logical_not(allowed)), MASKED, 0.0)
        kcat[pair, rows, HALF:] = bias.astype(BF16)
        vt_full = vpad[pl.ds(pl.multiple_of(at + PAD, 8), size), :].T
        first = lax.broadcasted_iota(jnp.int32, (16, size), 0) == 0
        first = jnp.where(first, 1.0, 0.0)
        vt_all[:, pl.ds(at, size)] = jnp.concatenate([vt_full, first], 0).astype(BF16)
        for h in range(2):
            own = (2 * pair + h) * HEAD_DIM
            own = vt_full[own : own + HEAD_DIM]
            vt[h, :, pl.ds(at, size)] = jnp.concatenate([own, first], 0).astype(BF16)
        return both

    def flip(n, carry):
        at = pl.multiple_of(n * z.qb, z.qb)
        both = prepare(at, z.qb).T
        kt[pair, :, pl.ds(at, z.qb)] = both[HALF // 2 :].astype(BF16)
        for h in range(2):
            cols = pl.ds(pl.multiple_of((h * per_head + n) * z.qb, z.qb), z.qb)
            parts = [jnp.zeros((HALF // 2, z.qb), F32)] + [jnp.zeros((HEAD_DIM, z.qb), F32)] * 2
            parts[1 + h] = both[h * HEAD_DIM : (h + 1) * HEAD_DIM]
            qtb[pair, :HALF, cols] = jnp.concatenate(parts, 0).astype(BF16)
            qtb[pair, HALF:, cols] = ones
        return carry

    lax.fori_loop(0, per_head, flip, 0)
    tail_cols = slice(blocks * z.qb, span)
    tail_both = prepare(full, tail)
    kt[pair, :, full:L] = tail_both.T[HALF // 2 :].astype(BF16)
    qtb[pair, :HALF, tail_cols] = tail_columns(turn(tail_both), tail, 2, tail_lanes).astype(BF16)
    qtb[pair, HALF:, tail_cols] = ones[:, :tail_lanes]

    def scores(cols, slot):
        s = mm(kcat[pair], qtb[pair, :, cols])
        slot[...] = s
        return jnp.max(jnp.max(s.reshape(L // 8, 8, s.shape[1]), 0), 0, keepdims=True)

    def block_scores(n, slot):
        return scores(pl.ds(pl.multiple_of(n * z.qb, z.qb), z.qb), slot)

    def weigh(values, slot, top):
        p = jnp.exp2((slot[...] - top) * scale).astype(BF16)
        acc = mm(values, p)
        at = acc.shape[0] - 16
        total = acc[at : at + 1]
        return acc[:at] * (1.0 / total), top * scale + jnp.log2(total)

    def block_rest(n, slot, top):
        h = n // per_head
        out, low = weigh(vt[h], slot, top)
        rows = pl.ds(pl.multiple_of((2 * pair + h) * HEAD_DIM, HEAD_DIM), HEAD_DIM)
        ot[rows, pl.ds(pl.multiple_of((n - h * per_head) * z.qb, z.qb), z.qb)] = out
        lse[0:1, pl.ds(pl.multiple_of(base + n * z.qb, 128), z.qb)] = low

    def two(m, top):
        n = 2 * m
        top_next = block_scores(n + 1, ss1)
        block_rest(n, ss0, top)
        top = block_scores(n + 2, ss0)
        block_rest(n + 1, ss1, top_next)
        return top

    top = lax.fori_loop(0, blocks // 2 - 1, two, block_scores(0, ss0))
    top_next = block_scores(blocks - 1, ss1)
    block_rest(blocks - 2, ss0, top)
    tail_slot = ss0.at[:, :tail_lanes]
    top = scores(tail_cols, tail_slot)
    block_rest(blocks - 1, ss1, top_next)
    out, low = weigh(vt_all[...], tail_slot, top)
    lse[0:1, base + blocks * z.qb : base + span] = low
    out = jnp.where(diagonal(tail, 2 * pair, tail_lanes), out, 0.0)
    ot[:, full + pair * tail_lanes : full + (pair + 1) * tail_lanes] = out
    rows = tail_rows(out, tail)
    osum[full:L, :] = rows if pair == 0 else osum[full:L, :] + rows


def wide_mixture(z, lim_ref, lw_ref, lb_ref, ot, vpad, osum, out_ref):
    L = z.wide_len
    per_head = wide_plan(z)[0]

    def finish(n, carry):
        at = pl.multiple_of(n * z.qb, z.qb)
        osum[pl.ds(at, z.qb), :] = ot[:, pl.ds(at, z.qb)].T
        return carry

    lax.fori_loop(0, per_head, finish, 0)
    for at, size in key_tiles(L, z.qb):
        inside, _ = wide_inside(lim_ref, at, size)
        rows = slice(at + PAD, at + PAD + size)
        vpad[rows, :] = jnp.where(inside, vpad[rows, :], 0.0)

    def taps(a, l):
        t = wide_tap(a, l)
        return lw_ref[t : t + 1, :]

    for at, size in key_tiles(L, 224):
        along, across = token_places(at, size, HALF)
        lepe = conv_forward(vpad, at + PAD, size, taps, across)
        osum[at : at + size, :] = osum[at : at + size, :] + lepe + lb_ref
    for c in range(z.C):
        out_ref[c] = osum[c * z.pix : c * z.pix + z.wide_rows1, : z.hc].astype(BF16)


def wide_backward_start(z, lim_ref, recv, lw_ref, v_ref, ot, dlw_ref, gpad, vpad, dotb, delta, dvl, stage):
    L = z.wide_len
    per_head, tail, blocks, tail_lanes, span = wide_plan(z)
    full = per_head * z.qb
    gpad[...] = jnp.zeros_like(gpad)
    vpad[...] = jnp.zeros_like(vpad)
    stage[...] = jnp.zeros_like(stage)
    for c in range(z.C):
        stage[: z.wide_rows1, : z.hc] = recv[c].astype(F32)
        gpad[PAD + c * z.pix : PAD + (c + 1) * z.pix, :] = stage[: z.pix, :]

    def prepare(at, size):
        rows = pl.ds(at, size)
        padded = pl.ds(pl.multiple_of(at + PAD, 8), size)
        inside, _ = wide_inside(lim_ref, at, size)
        vpad[padded, :] = jnp.where(inside, v_ref[rows, :].astype(F32), 0.0)
        return gpad[padded, :]

    def flip(n, carry):
        at = pl.multiple_of(n * z.qb, z.qb)
        gt = prepare(at, z.qb).T
        prod = gt * ot[:, pl.ds(at, z.qb)]
        for h in range(z.wide_heads):
            first = (h // 2) * span + (h % 2) * full
            cols = pl.ds(pl.multiple_of(first + n * z.qb, 128), z.qb)
            dotb[:, cols] = head_rows_mask(h, gt).astype(BF16)
            delta[0:1, cols] = jnp.sum(
                prod[h * HEAD_DIM : (h + 1) * HEAD_DIM], 0, keepdims=True
            )
        return carry

    lax.fori_loop(0, per_head, flip, 0)
    last = prepare(full, tail)
    for pair in range(z.pairs):
        cols = slice(pair * span + blocks * z.qb, (pair + 1) * span)
        gt = tail_columns(last, tail, 2 * pair, tail_lanes)
        dotb[:, cols] = gt.astype(BF16)
        out = ot[:, full + pair * tail_lanes : full + (pair + 1) * tail_lanes]
        delta[0:1, cols] = jnp.sum(gt * out, 0, keepdims=True)

    def taps(a, l):
        t = wide_tap(a, l)
        return lw_ref[t : t + 1, :]

    sums_of = {}
    for at, size in key_tiles(L, 224):
        inside, across = wide_inside(lim_ref, at, size)
        lepe = conv_backward(gpad, at + PAD, size, taps, across)
        dvl[at : at + size, :] = jnp.where(inside, lepe, 0.0)
        add_kernel_sums(sums_of, gpad, vpad, at + PAD, size, across, wide_tap)
    dlw_ref[...] = jnp.zeros_like(dlw_ref)
    for t, value in sums_of.items():
        dlw_ref[t : t + 1, :] = jnp.sum(value, 0, keepdims=True)


def wide_pair_backward(
    z,
    pair,
    lim_ref,
    v_ref,
    kcat,
    qtb,
    kt,
    lse,
    dotb,
    delta,
    dvl,
    dqt,
    dkt,
    dvt,
    dqk,
    dvv,
    stage,
    slots,
    out_ref,
    midway,
):
    L = z.wide_len
    per_head, tail, blocks, tail_lanes, span = wide_plan(z)
    full = per_head * z.qb
    base = pair * span
    _, _, _, scale = wide_limits(lim_ref)
    dkt[...] = jnp.zeros_like(dkt)
    dvt[...] = jnp.zeros_like(dvt)
    tail_cols = slice(blocks * z.qb, span)

    def shifted(cols):
        if isinstance(cols, slice):
            return slice(base + cols.start, base + cols.stop)
        return pl.ds(pl.multiple_of(base + cols.start, 128), cols.size)

    def products(cols, s_slot, dp_slot):
        s_slot[...] = mm(kcat[pair], qtb[pair, :, cols])
        dp_slot[...] = mm(v_ref[...], dotb[:, shifted(cols)])

    def weights(cols, s_slot, dp_slot, p_slot, ds_slot):
        low = lse[0:1, shifted(cols)]
        dlt = delta[0:1, shifted(cols)]
        for at, size in key_tiles(L, z.qb):
            rows = slice(at, at + size)
            p = jnp.exp2(s_slot[rows, :] * scale - low)
            p_slot[rows, :] = p.astype(BF16)
            ds_slot[rows, :] = (p * (dp_slot[rows, :] - dlt)).astype(BF16)

    def block_cols(n):
        return pl.ds(pl.multiple_of(n * z.qb, z.qb), z.qb)

    def first(n, k):
        products(block_cols(n), *slots[k][:2])

    def second(n, k):
        weights(block_cols(n), *slots[k])

    def third(n, k):
        h = n // per_head
        p_slot, ds_slot = slots[k][2:]
        cols = block_cols(n)
        rows = pl.ds(pl.multiple_of(h * HEAD_DIM, HEAD_DIM), HEAD_DIM)
        g_rows = pl.ds(pl.multiple_of((2 * pair + h) * HEAD_DIM, HEAD_DIM), HEAD_DIM)
        q_rows = pl.ds(pl.multiple_of(HALF // 2 + h * HEAD_DIM, HEAD_DIM), HEAD_DIM)
        dvt[rows, :] += mm_nt(dotb[g_rows, shifted(cols)], p_slot[...])
        dkt[rows, :] += mm_nt(qtb[pair, q_rows, cols], ds_slot[...])
        at = pl.ds(pl.multiple_of((n - h * per_head) * z.qb, z.qb), z.qb)
        dqt[rows, at] = mm(kt[pair, rows, :], ds_slot[...])

    first(0, 0)
    first(1, 1)
    second(0, 0)

    def two(m, carry):
        n = 2 * m
        first(n, 0)
        second(n - 1, 1)
        third(n - 2, 0)
        first(n + 1, 1)
        second(n, 0)
        third(n - 1, 1)
        return carry

    middle = (1 + blocks // 2) // 2
    lax.fori_loop(1, middle, two, 0)
    midway()
    lax.fori_loop(middle, blocks // 2, two, 0)
    tail_slots = [ref.at[:, :tail_lanes] for ref in slots[0]]
    products(tail_cols, *tail_slots[:2])
    second(blocks - 1, 1)
    third(blocks - 2, 0)
    weights(tail_cols, *tail_slots)
    third(blocks - 1, 1)
    half = HALF // 2
    dvt[...] += mm_nt(dotb[pair * half : (pair + 1) * half, shifted(tail_cols)], tail_slots[2][...])
    dkt[...] += mm_nt(qtb[pair, half:HALF, tail_cols], tail_slots[3][...])
    last = mm(kt[pair], tail_slots[3][...])
    empty_half = jnp.zeros((half, tail_lanes), F32)
    last = jnp.concatenate([last, empty_half], 0)
    last = jnp.where(diagonal(tail, 0, tail_lanes), last, 0.0)
    norm = HEAD_DIM**-0.5
    dk_last = jnp.concatenate([jnp.zeros((half, tail), F32), dkt[:, full:L]], 0).T
    dqk[full:L, :] = (tail_rows(last, tail) + dk_last) * norm

    def doubled(value):
        lo = low_half(value.shape[0])
        return jnp.where(lo, value, turn(value)) if pair == 0 else jnp.where(lo, turn(value), value)

    def finish(n, carry):
        rows = pl.ds(pl.multiple_of(n * z.qb, z.qb), z.qb)
        dqk[rows, :] = jnp.concatenate([dqt[:, rows], dkt[:, rows]], 0).T * norm
        dv = dvt[:, rows]
        dvv[rows, :] = jnp.concatenate([dv, dv], 0).T + doubled(dvl[rows, :])
        return carry

    lax.fori_loop(0, per_head, finish, 0)
    dv = dvt[:, full:L]
    dvv[full:L, :] = jnp.concatenate([dv, dv], 0).T + doubled(dvl[full:L, :])
    lo = low_half(z.fold)
    for c in range(z.C):
        at = c * z.pix
        stage[: z.pix, :] = dqk[at : at + z.pix, :]
        stage[z.pix : z.pix + z.fold, :] = jnp.where(
            lo, dvv[at : at + z.fold, :], dvv[at + z.fold : at + z.pix, :]
        )
        out_ref[c, pair] = stage[...].astype(BF16)


def add_kernel_sums(sums, gpad, vpad, base, size, across, tap):
    g = gpad[base : base + size, :]
    for a in (-1, 0, 1):
        ga = g
        if a == -1:
            ga = jnp.where(across >= 1, g, 0.0)
        if a == 1:
            ga = jnp.where(across <= SW - 2, g, 0.0)
        for l in (-1, 0, 1):
            at = base + SW * l + a
            term = (ga * vpad[at : at + size, :]).reshape(size // 8, 8, HALF).sum(0)
            t = tap(a, l)
            sums[t] = sums[t] + term if t in sums else term


def tall_prepare(z, p, lim_ref, L):
    across_limit, along_limit = lim_ref(p)
    empty = across_limit * along_limit == 0
    scale = jnp.where(empty, 1e-20, LOG2E * HEAD_DIM**-0.5)
    along, across = token_places(0, L, HALF)
    inside = jnp.logical_and(across < across_limit, along < along_limit)
    allowed = jnp.logical_or(inside, empty)
    token = lax.broadcasted_iota(jnp.int32, (L, HALF), 0)
    allowed = jnp.logical_and(allowed, token < z.tall_len)
    lane = lax.broadcasted_iota(jnp.int32, (L, HALF), 1) == 0
    bias = jnp.where(jnp.logical_and(lane, jnp.logical_not(allowed)), MASKED, 0.0).astype(BF16)
    return inside, across, scale, bias


def tall_pull(z, source, p, per, n, target, base):
    for r in range(z.R):
        at = pl.multiple_of((p * per + n) * z.tall_pad, 8)
        block = source[r, pl.ds(at, z.tall_pad), :]
        target[base + r * z.tall_own : base + (r + 1) * z.tall_own, :] = block[: z.tall_own]


def tall_push(z, source, p, per, n, target, base=0):
    for r in range(z.R):
        at = pl.multiple_of((p * per + n) * z.tall_pad, 8)
        target[r, pl.ds(at, z.tall_pad), :] = source[
            base + r * z.tall_own : base + r * z.tall_own + z.tall_pad, :
        ]


def tall_operands(z, k, q, bias, kstack, L):
    for h in range(BRANCH_HEADS):
        kstack[h * L : (h + 1) * L, :HALF] = jnp.where(head_lanes(h, L), k, 0.0).astype(BF16)
        kstack[h * L : (h + 1) * L, HALF:] = bias
    first = lax.broadcasted_iota(jnp.int32, (HALF, L), 0) == 0
    return jnp.concatenate([q.T, jnp.where(first, 1.0, 0.0)], 0).astype(BF16)


def tall_forward(
    z, start, stop, lim_ref, lw_ref, lb_ref, ot_ref, lse_ref, src, dst, qs, ks, vs, vpad, osum, kstack
):
    L = qs.shape[1]

    def taps(a, l):
        t = tall_tap(a, l)
        return lw_ref[t : t + 1, :]

    def group(m, carry):
        each = range(z.tall_group)
        ps = [m * z.tall_group + u for u in each]
        for u in each:
            for n, target in enumerate((qs, ks, vs)):
                tall_pull(z, src, ps[u], 3, n, target.at[u], 0)
        made = [tall_prepare(z, ps[u], lim_ref, L) for u in each]
        qts = [tall_operands(z, ks[u], qs[u], made[u][3], kstack.at[u], L) for u in each]
        scores = [mm(kstack[u], qts[u]) for u in each]
        tail = lax.broadcasted_iota(jnp.int32, (16, L), 0) == 0
        tail = jnp.where(tail, 1.0, 0.0)
        vts = [vs[u].T for u in each]
        tops = [
            [jnp.max(scores[u][h * L : (h + 1) * L], 0, keepdims=True) for h in range(BRANCH_HEADS)]
            for u in each
        ]
        accs = []
        for u in each:
            row = []
            for h in range(BRANCH_HEADS):
                s = scores[u][h * L : (h + 1) * L]
                e = jnp.exp2((s - tops[u][h]) * made[u][2]).astype(BF16)
                vt = jnp.concatenate([vts[u][h * HEAD_DIM : (h + 1) * HEAD_DIM], tail], 0)
                row.append(mm(vt.astype(BF16), e))
            accs.append(row)
        for u in each:
            inside, across, scale, _ = made[u]
            outs = []
            for h in range(BRANCH_HEADS):
                total = accs[u][h][HEAD_DIM : HEAD_DIM + 1]
                outs.append(accs[u][h][:HEAD_DIM] * (1.0 / total))
                lse_ref[ps[u], h : h + 1, :] = tops[u][h] * scale + jnp.log2(total)
            ot = jnp.concatenate(outs, 0)
            ot_ref[ps[u]] = ot
            vpad[u, PAD : PAD + L, :] = jnp.where(inside, vs[u], 0.0)
            lepe = conv_forward(vpad.at[u], PAD, L, taps, across)
            osum[u, :L, :] = ot.T + lepe + lb_ref
        for u in each:
            tall_push(z, osum.at[u], ps[u], 1, 0, dst)
        return carry

    lax.fori_loop(start, stop, group, 0)


def tall_backward(
    z,
    start,
    stop,
    lim_ref,
    lw_ref,
    ot_ref,
    lse_ref,
    dlw_ref,
    src,
    gsrc,
    dst,
    qs,
    ks,
    vs,
    gpad,
    vpad,
    stage,
    kstack,
):
    L = qs.shape[1]
    norm = HEAD_DIM**-0.5

    def taps(a, l):
        t = tall_tap(a, l)
        return lw_ref[t : t + 1, :]

    def group(m, carry):
        each = range(z.tall_group)
        ps = [m * z.tall_group + u for u in each]
        for u in each:
            for n, target in enumerate((qs, ks, vs)):
                tall_pull(z, src, ps[u], 3, n, target.at[u], 0)
            tall_pull(z, gsrc, ps[u], 1, 0, gpad.at[u], PAD)
        made = [tall_prepare(z, ps[u], lim_ref, L) for u in each]
        gts = [gpad[u, PAD : PAD + L, :].T for u in each]
        qts = [tall_operands(z, ks[u], qs[u], made[u][3], kstack.at[u], L) for u in each]
        kts = [ks[u].T.astype(BF16) for u in each]
        dvs = [None] * len(ps)
        dks = [None] * len(ps)
        dqs = [[] for u in each]
        for some in z.tall_head_sets:
            scores = []
            dps = []
            for u in each:
                rows = slice(some[0] * L, (some[-1] + 1) * L)
                scores.append(mm(kstack[u, rows, :], qts[u]))
                v = vs[u]
                vstack = jnp.concatenate([jnp.where(head_lanes(h, L), v, 0.0) for h in some], 0)
                dps.append(mm(vstack.astype(BF16), gts[u].astype(BF16)))
            weights = []
            for u in each:
                prod = gts[u] * ot_ref[ps[u]]
                lse = lse_ref[ps[u]]
                row = []
                for i, h in enumerate(some):
                    rows = slice(i * L, (i + 1) * L)
                    delta = jnp.sum(prod[h * HEAD_DIM : (h + 1) * HEAD_DIM], 0, keepdims=True)
                    w = jnp.exp2(scores[u][rows] * made[u][2] - lse[h : h + 1])
                    ds = (w * (dps[u][rows] - delta)).astype(BF16)
                    row.append((w.astype(BF16), ds))
                weights.append(row)
            for u in each:
                for i, h in enumerate(some):
                    keep = head_lanes(h, L)
                    w, ds = weights[u][i]
                    dv_h = mm(w, jnp.where(keep, gpad[u, PAD : PAD + L, :], 0.0).astype(BF16))
                    dk_h = mm(ds, jnp.where(keep, qs[u], 0.0).astype(BF16))
                    dvs[u] = dv_h if dvs[u] is None else dvs[u] + dv_h
                    dks[u] = dk_h if dks[u] is None else dks[u] + dk_h
                    dqs[u].append(mm(kts[u][h * HEAD_DIM : (h + 1) * HEAD_DIM], ds))
        results = [(jnp.concatenate(dqs[u], 0), dks[u], dvs[u]) for u in each]
        sums = {}
        for u in each:
            inside, across = made[u][:2]
            vpad[u, PAD : PAD + L, :] = jnp.where(inside, vs[u], 0.0)
            lepe = conv_backward(gpad.at[u], PAD, L, taps, across)
            add_kernel_sums(sums, gpad.at[u], vpad.at[u], PAD, L, across, tall_tap)
            dqt, dk, dv = results[u]
            stage[u, 0, :L, :] = dqt.T * norm
            stage[u, 1, :L, :] = dk * norm
            stage[u, 2, :L, :] = dv + jnp.where(inside, lepe, 0.0)
        for t, value in sums.items():
            dlw_ref[t : t + 1, :] += jnp.sum(value, 0, keepdims=True)
        for u in each:
            for n in range(3):
                tall_push(z, stage.at[u, n], ps[u], 3, n, dst)
        return carry

    lax.fori_loop(start, stop, group, 0)


def greet(z):
    col = lax.axis_index("col")
    row = lax.axis_index("row")
    barrier = pltpu.get_barrier_semaphore()
    for k in range(1, z.C):
        pl.semaphore_signal(
            barrier, inc=1, device_id=(row, lax.rem(col + k, z.C)), device_id_type=MESH
        )
    for k in range(1, z.R):
        pl.semaphore_signal(
            barrier, inc=1, device_id=(lax.rem(row + k, z.R), col), device_id_type=MESH
        )


def all_greeted(z):
    pl.semaphore_wait(pltpu.get_barrier_semaphore(), z.C - 1 + z.R - 1)


class Exchange:
    def __init__(self, z, axis, source, target, sends, receives):
        self.axis = axis
        self.source, self.target = source, target
        self.me = lax.axis_index(axis)
        count = z.C if axis == "col" else z.R
        col = lax.axis_index("col")
        row = lax.axis_index("row")
        self.copies = []
        for k in range(1, count):
            other = lax.rem(self.me + k, count)
            self.copies.append(
                pltpu.make_async_remote_copy(
                    src_ref=source(other),
                    dst_ref=target(self.me),
                    send_sem=sends.at[k],
                    recv_sem=receives.at[k],
                    device_id=(row, other) if axis == "col" else (other, col),
                    device_id_type=MESH,
                )
            )

    def start(self):
        for copy in self.copies:
            copy.start()

    def keep_own(self):
        self.target(self.me)[...] = self.source(self.me)[...]

    def arrive(self):
        for copy in self.copies:
            copy.wait_recv()

    def sent(self):
        for copy in self.copies:
            copy.wait_send()


def split_of(rows, lanes, parts):
    for by_rows in range(parts, 0, -1):
        if parts % by_rows == 0:
            by_lanes = parts // by_rows
            if rows % (16 * by_rows) == 0 and lanes % (128 * by_lanes) == 0:
                return by_rows, by_lanes
    raise ValueError("no split")


def reduce_plan(z, lanes, steps):
    rows = z.dim
    plan = []
    for step in steps:
        members = {"core": 2, "x": 2, "row": z.R, "slab": 4 * z.R, "far": z.C // 4}[step]
        a, b = split_of(rows, lanes, members)
        rows, lanes = rows // a, lanes // b
        plan.append((members, step, a, b, rows, lanes))
    return plan


def reduce_width(z, lanes, steps):
    while True:
        try:
            reduce_plan(z, lanes, steps)
            return lanes
        except ValueError:
            lanes += 128


class Reduction:
    def __init__(self, z, plan, refs, small=None):
        n = len(plan)
        self.z, self.plan, self.n = z, plan, n
        self.full, refs = refs[0], refs[1:]
        self.recvs, refs = refs[:n], refs[n:]
        self.held, refs = refs[:n], refs[n:]
        self.gathers, refs = refs[:n], refs[n:]
        self.ssem, self.rsem, self.gsem, self.hsem = refs[:4]
        self.small = small
        if small is not None:
            self.smalls = refs[4 : 4 + n]
            self.vsem, self.wsem = refs[4 + n :]
        self.current = self.full
        self.copies = None

    @staticmethod
    def scratch(z, plan, lanes, small_shape=None):
        dma = pltpu.SemaphoreType.DMA
        most = max(step[0] for step in plan)
        shapes = [pltpu.VMEM((z.dim, lanes), BF16)]
        shapes += [pltpu.VMEM((step[0], step[4], step[5]), BF16) for step in plan]
        shapes += [pltpu.VMEM((step[4], step[5]), BF16) for step in plan]
        shapes += [pltpu.VMEM((z.dim, lanes), BF16)]
        shapes += [pltpu.VMEM((step[4], step[5]), BF16) for step in plan[:-1]]
        shapes += [dma((len(plan), most)) for _ in range(4)]
        if small_shape is not None:
            shapes += [pltpu.VMEM((step[0],) + small_shape, F32) for step in plan]
            shapes += [dma((len(plan), most)) for _ in range(2)]
        return shapes

    def place(self, stage):
        step = self.plan[stage][1]
        col = lax.axis_index("col")
        row = lax.axis_index("row")
        if step == "row":
            return row
        if step == "slab":
            return row * 4 + lax.rem(col, 4)
        if step == "far":
            return col // 4
        return lax.rem(col // {"core": 1, "x": 2}[step], 2)

    def peer(self, stage, k):
        members, step = self.plan[stage][:2]
        col = lax.axis_index("col")
        row = lax.axis_index("row")
        me = self.place(stage)
        at = lax.rem(me + k, members)
        if step == "row":
            return at, (at, col)
        if step == "slab":
            return at, (at // 4, col - lax.rem(col, 4) + lax.rem(at, 4))
        return at, (row, col + (at - me) * {"core": 1, "x": 2, "far": 4}[step])

    def window(self, ref, stage, index):
        members, stride, a, b, rows, width = self.plan[stage]
        r0 = pl.multiple_of((index // b) * rows, 16)
        l0 = pl.multiple_of(lax.rem(index, b) * width, 128)
        return ref.at[pl.ds(r0, rows), pl.ds(l0, width)]

    def fill(self, pieces):
        D = self.z.dim
        at = 0
        for ref in pieces:
            for k in range(ref.shape[0] // D):
                width = ref.shape[1]
                self.full[:, at : at + width] = ref[k * D : (k + 1) * D, :].astype(BF16)
                at += width
        if at < self.full.shape[1]:
            self.full[:, at:] = jnp.zeros((D, self.full.shape[1] - at), BF16)

    def scatter_start(self, stage):
        me = self.place(stage)
        self.copies = []
        for k in range(1, self.plan[stage][0]):
            index, device = self.peer(stage, k)
            self.copies.append(
                pltpu.make_async_remote_copy(
                    src_ref=self.window(self.current, stage, index),
                    dst_ref=self.recvs[stage].at[me],
                    send_sem=self.ssem.at[stage, k],
                    recv_sem=self.rsem.at[stage, k],
                    device_id=device,
                    device_id_type=MESH,
                )
            )
            if self.small is not None:
                self.copies.append(
                    pltpu.make_async_remote_copy(
                        src_ref=self.small,
                        dst_ref=self.smalls[stage].at[me],
                        send_sem=self.vsem.at[stage, k],
                        recv_sem=self.wsem.at[stage, k],
                        device_id=device,
                        device_id_type=MESH,
                    )
                )
        for copy in self.copies:
            copy.start()
        self.recvs[stage][me] = self.window(self.current, stage, me)[...]
        if self.small is not None:
            self.smalls[stage][me] = self.small[...]

    def scatter_end(self, stage, small_out=None):
        for copy in self.copies:
            copy.wait()
        members = self.plan[stage][0]
        rows, width = self.plan[stage][4:]
        for at, size in key_tiles(width, 512):
            lanes = slice(at, at + size)
            total = self.recvs[stage][0, :, lanes].astype(F32)
            for k in range(1, members):
                total = total + self.recvs[stage][k, :, lanes].astype(F32)
            self.held[stage][:, lanes] = total.astype(BF16)
        self.current = self.held[stage]
        if self.small is not None:
            small = self.smalls[stage][0]
            for k in range(1, members):
                small = small + self.smalls[stage][k]
            if stage + 1 < self.n:
                self.smalls[stage][0] = small
                self.small = self.smalls[stage].at[0]
            else:
                small_out[...] = small

    def gather_start(self, stage):
        me = self.place(stage)
        self.copies = []
        for k in range(1, self.plan[stage][0]):
            index, device = self.peer(stage, k)
            self.copies.append(
                pltpu.make_async_remote_copy(
                    src_ref=self.current,
                    dst_ref=self.window(self.gathers[stage], stage, me),
                    send_sem=self.gsem.at[stage, k],
                    recv_sem=self.hsem.at[stage, k],
                    device_id=device,
                    device_id_type=MESH,
                )
            )
        for copy in self.copies:
            copy.start()
        self.window(self.gathers[stage], stage, me)[...] = self.current[...]

    def gather_end(self, stage):
        for copy in self.copies:
            copy.wait()
        self.current = self.gathers[stage]

    def steps(self, small_out=None):
        n = self.n
        ends = [functools.partial(self.scatter_end, s, small_out) for s in range(n)]
        ends += [functools.partial(self.gather_end, s) for s in range(n - 1, -1, -1)]
        starts = [functools.partial(self.scatter_start, s) for s in range(n)]
        starts += [functools.partial(self.gather_start, s) for s in range(n - 1, -1, -1)]
        return starts, ends


def spread(block, outs):
    D = block.shape[0]
    at = 0
    for ref in outs:
        for k in range(ref.shape[0] // D):
            width = ref.shape[1]
            ref[k * D : (k + 1) * D, :] = block[:, at : at + width].astype(F32)
            at += width


def reduce_kernel(z, plan, dqkv_ref, vec_ref, dwt_ref, dtt_ref, sum_ref, osmall, small, *refs):
    greet_sum(z)
    small[:16, :HALF] = own_lanes_back(z, dwt_ref[...])
    small[:16, HALF:] = dtt_ref[...]
    small[16:, :] = vec_ref[...]
    work = Reduction(z, plan, refs, small)
    work.fill((dqkv_ref,))
    all_greeted_sum(z)
    starts, ends = work.steps(osmall)
    for start, end in zip(starts, ends):
        start()
        end()
    sum_ref[...] = work.current[...]


def own_lanes_back(z, value):
    if z.G == 1:
        return value
    return jnp.where(lax.rem(lax.axis_index("col"), z.G) == 0, value, turn(value))


def greet_sum(z):
    col = lax.axis_index("col")
    row = lax.axis_index("row")
    barrier = pltpu.get_barrier_semaphore()
    me = row * 4 + lax.rem(col, 4)
    for k in range(1, 4 * z.R):
        at = lax.rem(me + k, 4 * z.R)
        pl.semaphore_signal(
            barrier,
            inc=1,
            device_id=(at // 4, col - lax.rem(col, 4) + lax.rem(at, 4)),
            device_id_type=MESH,
        )
    for k in range(1, z.C // 4):
        pl.semaphore_signal(
            barrier, inc=1, device_id=(row, lax.rem(col + 4 * k, z.C)), device_id_type=MESH
        )


def all_greeted_sum(z):
    pl.semaphore_wait(pltpu.get_barrier_semaphore(), 4 * z.R - 1 + z.C // 4 - 1)


def reduce_last(z, dqkv, vec, dwt, dtt, collective_id):
    steps = ("slab", "far")
    lanes = reduce_width(z, dqkv.size // z.dim, steps)
    plan = reduce_plan(z, lanes, steps)
    vmem = pl.BlockSpec(memory_space=pltpu.VMEM)
    small = (24, z.dim)
    return pl.pallas_call(
        functools.partial(reduce_kernel, z, plan),
        out_shape=(
            jax.ShapeDtypeStruct((z.dim, lanes), BF16),
            jax.ShapeDtypeStruct(small, F32),
        ),
        in_specs=[vmem] * 4,
        out_specs=(vmem,) * 2,
        scratch_shapes=[pltpu.VMEM(small, F32)] + Reduction.scratch(z, plan, lanes, small),
        compiler_params=pltpu.CompilerParams(
            collective_id=collective_id, has_side_effects=True, vmem_limit_bytes=VMEM_LIMIT
        ),
        name="reduce_last",
    )(dqkv, vec, dwt, dtt)


def split_kernel(z, sum_ref, late_ref, early_ref, dw_ref, *outs):
    spread(sum_ref, (dw_ref,))
    n1g, n1s, qb, vb, taps, lb, pb, n2g, n2s, b1, b2 = outs
    taps[...] = late_ref[:9, :]
    for ref, row in ((n1g, 16), (n1s, 17), (qb, 18), (vb, 19)):
        ref[...] = late_ref[row : row + 1, :]
    for ref, row in ((n2g, 0), (n2s, 1), (pb, 2), (b2, 3), (lb, 4)):
        ref[...] = early_ref[row : row + 1, :]
    D = z.dim
    for k in range(b1.shape[1] // D):
        b1[:, k * D : (k + 1) * D] = early_ref[8 + k : 9 + k, :]


def front_kernel(
    z,
    heights_ref,
    widths_ref,
    x_ref,
    gain_ref,
    shift_ref,
    w_ref,
    qb_ref,
    vb_ref,
    tap_ref,
    tap_bias_ref,
    back_wide,
    back_tall,
    tq_ref,
    tot_ref,
    tlse_ref,
    v_ref,
    kcat,
    qtb,
    kt,
    ot,
    lse,
    pw,
    pt,
    gw,
    gt,
    send_wide,
    send_tall,
    recv_wide,
    recv_tall,
    out_wide,
    out_tall,
    t_src,
    t_dst,
    t_q,
    t_k,
    t_v,
    t_vpad,
    t_osum,
    t_kstack,
    qk,
    vpad,
    stage,
    vt,
    vt_all,
    ss0,
    ss1,
    osum,
    wsend,
    wrecv,
    tsend,
    trecv,
    wsend1,
    wrecv1,
    tsend1,
    trecv1,
    local,
):
    greet(z)
    wlim_ref = wide_ends(z, heights_ref, widths_ref)
    tlim_ref = tall_ends(z, heights_ref, widths_ref)
    ttap_ref = tap_ref[:, HALF:]
    tbias_ref = tap_bias_ref[:, HALF:]
    wtap_ref = own_lanes(z, tap_ref[:, :HALF])
    wbias_ref = own_lanes(z, tap_bias_ref[:, :HALF])
    bias = jnp.concatenate([qb_ref[...], jnp.zeros_like(qb_ref), vb_ref[...]], -1)
    dense_in(z, x_ref, gain_ref, shift_ref, w_ref, bias, send_wide, send_tall, pw, pt, gw, gt)
    all_greeted(z)
    wides = [
        Exchange(
            z,
            "col",
            lambda d, pair=pair: send_wide.at[d, pair],
            lambda d, pair=pair: recv_wide.at[d, pair],
            wsend.at[pair],
            wrecv.at[pair],
        )
        for pair in range(z.pairs)
    ]
    tall = Exchange(
        z, "row", lambda d: send_tall.at[d], lambda d: recv_tall.at[d], tsend, trecv
    )
    wides[0].start()
    tall.start()
    for wide in wides:
        wide.keep_own()
    tall.keep_own()
    for ref in (t_q, t_k, t_v, t_vpad, t_osum, vpad, qk):
        ref[...] = jnp.zeros_like(ref)
    groups = z.tall_slots // z.tall_group

    def tall_part(start, stop):
        tall_forward(
            z, start, stop, tlim_ref, ttap_ref, tbias_ref, tot_ref, tlse_ref,
            t_src, t_dst, t_q, t_k, t_v, t_vpad, t_osum, t_kstack,
        )

    early = groups // 2
    for pair in range(z.pairs):
        wides[pair].arrive()
        if pair + 1 < z.pairs:
            wides[pair + 1].start()
        wide_pair_forward(
            z, pair, wlim_ref, recv_wide, kcat, qtb, kt, ot, lse, qk, vpad, stage, vt, vt_all,
            ss0, ss1, osum,
        )
        if pair == 0:
            tall.arrive()
            tq_ref[...] = recv_tall[...]
            t_src[...] = recv_tall[...].astype(F32)
            tall_part(0, early)
    v_ref[...] = vpad[PAD : PAD + z.wide_len, :].astype(BF16)
    wide_mixture(z, wlim_ref, wtap_ref, wbias_ref, ot, vpad, osum, out_wide)
    back = Exchange(
        z, "col", lambda d: out_wide.at[d], lambda d: back_wide.at[d], wsend1, wrecv1
    )
    back.start()
    col = lax.axis_index("col")
    row = lax.axis_index("row")
    own_wide = pltpu.make_async_copy(out_wide.at[col], back_wide.at[col], local.at[0])
    own_wide.start()
    tall_part(early, groups)
    out_tall[...] = t_dst[...].astype(BF16)
    back_t = Exchange(
        z, "row", lambda d: out_tall.at[d], lambda d: back_tall.at[d], tsend1, trecv1
    )
    back_t.start()
    own_tall = pltpu.make_async_copy(out_tall.at[row], back_tall.at[row], local.at[1])
    own_tall.start()
    own_wide.wait()
    own_tall.wait()
    for job in wides + [tall, back, back_t]:
        job.sent()
    back.arrive()
    back_t.arrive()


def back_kernel(
    z,
    plan,
    heights_ref,
    widths_ref,
    gw_ref,
    gt_ref,
    tq_ref,
    tot_ref,
    tlse_ref,
    tap_ref,
    dpw_ref,
    dw1_ref,
    dw2_ref,
    vec_ref,
    v_any,
    kcat_any,
    qtb_any,
    kt_any,
    ot_any,
    lse_any,
    got_wide,
    got_tall,
    dwt_ref,
    dtt_ref,
    sum_ref,
    osmall_ref,
    v_ref,
    kcat,
    qtb,
    kt,
    ot,
    lse,
    recv_wide,
    recv_tall,
    send_wide,
    send_tall,
    t_src,
    t_gsrc,
    t_q,
    t_k,
    t_v,
    t_gpad,
    t_vpad,
    t_stage,
    t_kstack,
    gpad,
    vpad,
    dotb,
    delta,
    dvl,
    dqt,
    dkt,
    dvt,
    stage,
    ss0,
    ss1,
    dp0,
    dp1,
    ps0,
    ps1,
    ds0,
    ds1,
    wsend,
    wrecv,
    tsend,
    trecv,
    wsend1,
    wrecv1,
    tsend1,
    trecv1,
    local,
    *refs,
):
    greet(z)
    loads = [
        pltpu.make_async_copy(a, b, local.at[i])
        for i, (a, b) in enumerate(
            zip((v_any, kcat_any, qtb_any, kt_any, ot_any, lse_any), (v_ref, kcat, qtb, kt, ot, lse))
        )
    ]
    for load in loads:
        load.start()
    wlim_ref = wide_ends(z, heights_ref, widths_ref)
    tlim_ref = tall_ends(z, heights_ref, widths_ref)
    ttap_ref = tap_ref[:, HALF:]
    wtap_ref = own_lanes(z, tap_ref[:, :HALF])
    work = Reduction(z, plan, refs, vec_ref)
    starts, ends = work.steps(osmall_ref)
    work.fill((dpw_ref, dw1_ref, dw2_ref))
    all_greeted(z)
    tall = Exchange(z, "row", lambda d: gt_ref.at[d], lambda d: recv_tall.at[d], tsend, trecv)
    wide = Exchange(z, "col", lambda d: gw_ref.at[d], lambda d: recv_wide.at[d], wsend, wrecv)
    tall.start()
    wide.start()
    starts[0]()
    tall.keep_own()
    wide.keep_own()
    for ref in (t_q, t_k, t_v, t_gpad, t_vpad, t_stage):
        ref[...] = jnp.zeros_like(ref)
    dtt_ref[...] = jnp.zeros_like(dtt_ref)
    t_src[...] = tq_ref[...].astype(F32)
    groups = z.tall_slots // z.tall_group
    early = groups // 2

    def tall_part(start, stop):
        tall_backward(
            z, start, stop, tlim_ref, ttap_ref, tot_ref, tlse_ref, dtt_ref, t_src, t_gsrc, t_src,
            t_q, t_k, t_v, t_gpad, t_vpad, t_stage, t_kstack,
        )

    def point(i):
        ends[i]()
        starts[i + 1]()

    tall.arrive()
    t_gsrc[...] = recv_tall[...].astype(F32)
    tall_part(0, early)
    point(0)
    for load in loads:
        load.wait()
    wide.arrive()
    wide_backward_start(
        z, wlim_ref, recv_wide, wtap_ref, v_ref, ot, dwt_ref, gpad, vpad, dotb, delta, dvl, stage
    )
    point(1)
    slots = ((ss0, dp0, ps0, ds0), (ss1, dp1, ps1, ds1))
    outs = []
    at = 2
    col = lax.axis_index("col")
    row = lax.axis_index("row")
    own = []
    for pair in range(z.pairs):
        wide_pair_backward(
            z, pair, wlim_ref, v_ref, kcat, qtb, kt, lse, dotb, delta, dvl, dqt, dkt, dvt, gpad, vpad,
            stage, slots, send_wide, lambda: point(at),
        )
        point(at + 1)
        at += 2
        job = Exchange(
            z,
            "col",
            lambda d, pair=pair: send_wide.at[d, pair],
            lambda d, pair=pair: got_wide.at[d, pair],
            wsend1.at[pair],
            wrecv1.at[pair],
        )
        job.start()
        outs.append(job)
        copy = pltpu.make_async_copy(
            send_wide.at[col, pair], got_wide.at[col, pair], local.at[6 + pair]
        )
        copy.start()
        own.append(copy)
    tall_part(early, groups)
    send_tall[...] = t_src[...].astype(BF16)
    job = Exchange(
        z, "row", lambda d: send_tall.at[d], lambda d: got_tall.at[d], tsend1, trecv1
    )
    job.start()
    outs.append(job)
    copy = pltpu.make_async_copy(send_tall.at[row], got_tall.at[row], local.at[8])
    copy.start()
    own.append(copy)
    while at < len(ends) - 1:
        point(at)
        at += 1
    ends[at]()
    sum_ref[...] = work.current[...]
    for copy in own:
        copy.wait()
    tall.sent()
    wide.sent()
    for job in outs:
        job.sent()
        job.arrive()


def local_call(kernel, z, name, outs, scratch, scalars, arrays):
    vmem = pl.BlockSpec(memory_space=pltpu.VMEM)
    smem = pl.BlockSpec(memory_space=pltpu.SMEM)
    return pl.pallas_call(
        functools.partial(kernel, z),
        out_shape=tuple(jax.ShapeDtypeStruct(shape, kind) for shape, kind in outs),
        in_specs=[smem] * len(scalars) + [vmem] * len(arrays),
        out_specs=(vmem,) * len(outs),
        scratch_shapes=[pltpu.VMEM(shape, kind) for shape, kind in scratch],
        compiler_params=pltpu.CompilerParams(vmem_limit_bytes=VMEM_LIMIT),
        name=name,
    )(*scalars, *arrays)


def per_device(
    mesh,
    features,
    heights,
    widths,
    norm1_gain,
    norm1_shift,
    qkv_weight,
    query_bias,
    value_bias,
    lepe_weight,
    lepe_bias,
    proj_weight,
    proj_bias,
    norm2_gain,
    norm2_shift,
    fc1_weight,
    fc1_bias,
    fc2_weight,
    fc2_bias,
    cotangent,
):
    z = Sizes(mesh, features.shape)
    B, D, TC, TR = z.images, z.dim, z.cols, z.rows
    x = features.transpose(1, 2, 0, 3)
    ct = cotangent.transpose(1, 2, 0, 3)
    line = lambda v: v.reshape(1, -1)
    FF = fc1_weight.shape[1]
    wide3 = (z.C, z.pairs, z.pair_rows, HALF)
    wide1 = (z.C, z.wide_rows1, z.hc)
    tall3 = (z.R, z.tall_rows3, HALF)
    tall1 = (z.R, z.tall_rows1, HALF)
    flat = up(z.tokens, 16 * B) + 16 * B
    L = z.wide_len
    LT = up(z.tall_len, 128)
    per_head, tail, blocks, tail_lanes, span = wide_plan(z)
    vmem = pl.BlockSpec(memory_space=pltpu.VMEM)
    smem = pl.BlockSpec(memory_space=pltpu.SMEM)
    anywhere = pl.BlockSpec(memory_space=pl.ANY)
    dma = pltpu.SemaphoreType.DMA
    saved = [
        ((L, HALF), BF16),
        ((z.pairs, L, 2 * HALF), BF16),
        ((z.pairs, 2 * HALF, span), BF16),
        ((z.pairs, HALF // 2, L), BF16),
        ((HALF, per_head * z.qb + z.pairs * tail_lanes), F32),
        ((8, z.pairs * span), F32),
    ]
    tall_scratch = [
        ((z.tall_group, LT, HALF), F32),
        ((z.tall_group, LT, HALF), F32),
        ((z.tall_group, LT, HALF), F32),
        ((z.tall_group, LT + 16, HALF), F32),
        ((z.tall_group, LT + 16, HALF), F32),
        ((z.tall_group, BRANCH_HEADS * LT, 2 * HALF), BF16),
    ]
    sems = [
        dma((z.pairs, z.C)),
        dma((z.pairs, z.C)),
        dma((z.R,)),
        dma((z.R,)),
        dma((z.C,)),
        dma((z.C,)),
        dma((z.R,)),
        dma((z.R,)),
    ]
    shapes = lambda items: tuple(jax.ShapeDtypeStruct(s, k) for s, k in items)
    scratches = lambda items: [pltpu.VMEM(s, k) for s, k in items]

    back_wide, back_tall, tall_qkv, tall_ot, tall_lse, *wide_saved = pl.pallas_call(
        functools.partial(front_kernel, z),
        out_shape=shapes(
            [
                (wide1, BF16),
                (tall1, BF16),
                (tall3, BF16),
                ((z.tall_slots, HALF, LT), F32),
                ((z.tall_slots, 8, LT), F32),
            ]
            + saved
        ),
        in_specs=[smem] * 2 + [vmem] * 8,
        out_specs=(anywhere, anywhere) + (vmem,) * (3 + len(saved)),
        scratch_shapes=scratches(
            [
                ((3, flat, HALF), F32),
                ((3, flat, HALF), F32),
                (wide3, F32),
                (tall3, F32),
                (wide3, BF16),
                (tall3, BF16),
                (wide3, BF16),
                (tall3, BF16),
                (wide1, BF16),
                (tall1, BF16),
                (tall3, F32),
                (tall1, F32),
            ]
            + tall_scratch
            + [
                ((L, HALF), F32),
                ((L + 2 * PAD, HALF), F32),
                ((z.pair_rows, HALF), F32),
                ((2, HEAD_DIM + 16, L), BF16),
                ((HALF + 16, L), BF16),
                ((L, z.qb), F32),
                ((L, z.qb), F32),
                ((L + z.wide_rows1, HALF), F32),
            ]
        )
        + sems
        + [dma((2,))],
        compiler_params=pltpu.CompilerParams(
            collective_id=0, has_side_effects=True, vmem_limit_bytes=VMEM_LIMIT
        ),
        name="front",
    )(
        heights,
        widths,
        x,
        line(norm1_gain),
        line(norm1_shift),
        qkv_weight,
        line(query_bias),
        line(value_bias),
        lepe_weight,
        line(lepe_bias),
    )

    vec_rows = 8 + up(FF // D, 8)
    y, gres, gmix_wide, gmix_tall, dproj, dfc1, dfc2, vec_mid = local_call(
        dense_mid_kernel,
        z,
        "dense_mid",
        [
            ((TR, TC, B, D), BF16),
            ((TR, TC, B, D), F32),
            (wide1, BF16),
            (tall1, BF16),
            ((D, D), F32),
            ((D, FF), F32),
            ((FF, D), F32),
            ((vec_rows, D), F32),
        ],
        [((flat, HALF), F32)] * 4 + [(tall1, F32)],
        [heights, widths],
        [
            back_wide,
            back_tall,
            x,
            ct,
            proj_weight,
            line(proj_bias),
            line(norm2_gain),
            line(norm2_shift),
            fc1_weight,
            line(fc1_bias),
            fc2_weight,
            line(fc2_bias),
        ],
    )
    steps = ("core", "x", "row", "far")
    lanes = reduce_width(z, (dproj.size + dfc1.size + dfc2.size) // D, steps)
    plan = reduce_plan(z, lanes, steps)
    got_wide, got_tall, dwide_taps, dtall_taps, early, vec_mid = pl.pallas_call(
        functools.partial(back_kernel, z, plan),
        out_shape=shapes(
            [
                (wide3, BF16),
                (tall3, BF16),
                ((16, HALF), F32),
                ((16, HALF), F32),
                ((D, lanes), BF16),
                ((vec_rows, D), F32),
            ]
        ),
        in_specs=[smem] * 2 + [vmem] * 10 + [anywhere] * len(saved),
        out_specs=(anywhere, anywhere) + (vmem,) * 4,
        scratch_shapes=scratches(
            saved
            + [
                (wide1, BF16),
                (tall1, BF16),
                (wide3, BF16),
                (tall3, BF16),
                (tall3, F32),
                (tall1, F32),
            ]
            + tall_scratch[:5]
            + [((z.tall_group, 3, LT + 16, HALF), F32), tall_scratch[5]]
            + [
                ((L + 2 * PAD, HALF), F32),
                ((L + 2 * PAD, HALF), F32),
                ((HALF, z.pairs * span), BF16),
                ((8, z.pairs * span), F32),
                ((L, HALF), F32),
                ((HALF // 2, per_head * z.qb), F32),
                ((HALF // 2, L), F32),
                ((HALF // 2, L), F32),
                ((z.pair_rows, HALF), F32),
            ]
            + [((L, z.qb), F32)] * 4
            + [((L, z.qb), BF16)] * 4
        )
        + [sems[4], sems[5], sems[2], sems[3], sems[0], sems[1], sems[6], sems[7]]
        + [dma((9,))]
        + Reduction.scratch(z, plan, lanes, (vec_rows, D)),
        compiler_params=pltpu.CompilerParams(
            collective_id=1, has_side_effects=True, vmem_limit_bytes=VMEM_LIMIT
        ),
        name="back",
    )(
        heights,
        widths,
        gmix_wide,
        gmix_tall,
        tall_qkv,
        tall_ot,
        tall_lse,
        lepe_weight,
        dproj,
        dfc1,
        dfc2,
        vec_mid,
        *wide_saved,
    )

    grad_in, dqkv, vec_out, dproj, dfc1, dfc2 = local_call(
        dense_out_kernel,
        z,
        "dense_out",
        [
            ((TR, TC, B, D), F32),
            ((D, 3 * D), F32),
            ((8, D), F32),
            (dproj.shape, F32),
            (dfc1.shape, F32),
            (dfc2.shape, F32),
        ],
        [((3, flat, HALF), F32), ((3, flat, HALF), F32), (wide3, F32), (tall3, F32)],
        [],
        [got_wide, got_tall, x, gres, line(norm1_gain), line(norm1_shift), qkv_weight, early],
    )
    late, vec_late = reduce_last(z, dqkv, vec_out, dwide_taps, dtall_taps, 2)
    dqkv, n1g, n1s, qb, vb, taps, lb, pb, n2g, n2s, b1, b2 = local_call(
        split_kernel,
        z,
        "split",
        [(dqkv.shape, F32)]
        + [((1, D), F32)] * 4
        + [((9, D), F32)]
        + [((1, D), F32)] * 4
        + [((1, FF), F32), ((1, D), F32)],
        [],
        [],
        [late, vec_late, vec_mid],
    )
    flat_of = lambda v: v.reshape(-1)
    return (
        y.transpose(2, 0, 1, 3),
        grad_in.transpose(2, 0, 1, 3),
        flat_of(n1g),
        flat_of(n1s),
        dqkv,
        flat_of(qb),
        flat_of(vb),
        taps,
        flat_of(lb),
        dproj,
        flat_of(pb),
        flat_of(n2g),
        flat_of(n2s),
        dfc1,
        flat_of(b1),
        dfc2,
        flat_of(b2),
    )


def solution(mesh):
    image = P(None, "row", "col", None)
    return jax.shard_map(
        functools.partial(per_device, mesh),
        mesh=mesh,
        in_specs=(image,) + (P(),) * 17 + (image,),
        out_specs=(image, image) + (P(),) * 15,
        check_vma=False,
    )
```

```python
import functools
import math
import types

import jax
import jax.numpy as jnp
from jax import lax
from jax.experimental import pallas as pl
from jax.experimental.pallas import tpu as pltpu
from jax.sharding import PartitionSpec as P

HEADS = 8
SW = 7
BRANCH_HEADS = HEADS // 2
HALF = 128
HEAD_DIM = 32
NORM_EPSILON = 1e-05
MASKED = -1e30
LOG2E = math.log2(math.e)
PAD = 8
VMEM_LIMIT = 62 * 1024 * 1024
MESH = pl.DeviceIdType.MESH
F32 = jnp.float32
BF16 = jnp.bfloat16
NT = (((1,), (1,)), ((), ()))
TN = (((0,), (0,)), ((), ()))


def up(value, unit):
    return -(-value // unit) * unit


def mm(a, b):
    return jnp.dot(a, b, preferred_element_type=F32)


def mm_nt(a, b):
    return lax.dot_general(a, b, NT, preferred_element_type=F32)


def mm_tn(a, b):
    return lax.dot_general(a, b, TN, preferred_element_type=F32)


class Sizes:
    def __init__(self, mesh, shape):
        self.images, self.rows, self.cols, self.dim = shape
        self.R = mesh.shape["row"]
        self.C = mesh.shape["col"]
        self.pix = self.rows * self.cols
        self.tokens = self.pix * self.images
        self.stripes = self.cols // SW
        self.G = self.C // self.images
        self.wide_heads = BRANCH_HEADS // self.G
        self.hc = HALF // self.G
        self.tall_images = self.images // self.R
        self.wide_len = self.C * self.pix
        self.qb = 256 if self.wide_len <= 2048 else 128
        self.merged = self.G == 1 and self.wide_len <= 2048
        self.tall_own = self.rows * SW
        self.tall_len = self.R * self.tall_own
        self.tall_pad = up(self.tall_own, 8)
        self.pairs = self.wide_heads // 2
        self.fold = self.pix // 2
        self.pair_rows = up(self.pix + self.fold, 16)
        self.fold_rows = up(self.fold, 16)
        self.wide_rows1 = up(self.pix, 16)
        self.tall_slots = self.tall_images * self.stripes
        self.tall_group = 4 if self.tall_len <= 128 else 1
        heads = list(range(BRANCH_HEADS))
        self.tall_head_sets = [heads] if self.tall_group > 1 else [[h] for h in heads]
        self.tall_rows1 = self.tall_slots * self.tall_pad
        self.tall_rows3 = 3 * self.tall_rows1


def norm_parts(values):
    average = jnp.mean(values, -1, keepdims=True)
    centred = values - average
    spread = jnp.mean(centred * centred, -1, keepdims=True)
    inverse = lax.rsqrt(spread + NORM_EPSILON)
    return centred * inverse, inverse


def low_lanes(shape):
    return lax.broadcasted_iota(jnp.int32, shape, len(shape) - 1) < HALF // 2


def low_half(rows):
    return lax.broadcasted_iota(jnp.int32, (rows, HALF), 1) < HALF // 2


def turn(value):
    return jnp.concatenate([value[..., HALF // 2 :], value[..., : HALF // 2]], -1)


def dense_in_wide(z, x_ref, gain_ref, shift_ref, w_ref, bias, sw_ref, low_ref, pw, gw):
    B, D, TC, TR = z.images, z.dim, z.cols, z.rows

    def one_row(i, carry):
        x = x_ref[i].astype(F32).reshape(TC * B, D)
        normed, _ = norm_parts(x)
        low = (normed * gain_ref[...] + shift_ref[...]).astype(BF16)
        low_ref[i] = low
        proj = branch_projection(z, low, w_ref, bias, 0)
        for j in range(TC):
            at = pl.multiple_of((j * TR + i) * B, B)
            for n in range(3):
                pw[n, pl.ds(at, B), :] = proj[j, :, n * HALF : (n + 1) * HALF]
        return carry

    lax.fori_loop(0, TR, one_row, 0)
    rows = up(z.pix, 8)
    half = up(z.fold, 8)
    lo = low_half(rows)
    lo_half = low_half(half)
    gw[:, :, z.pix + z.fold :, :] = jnp.zeros_like(gw[:, :, z.pix + z.fold :, :])
    for b in range(B):
        q = pw[0, pl.ds(b, rows, stride=B), :]
        k = pw[1, pl.ds(b, rows, stride=B), :]
        v1 = pw[2, pl.ds(b, half, stride=B), :]
        v2 = pw[2, pl.ds(z.fold * B + b, half, stride=B), :]
        qk = (jnp.where(lo, q, turn(k)), jnp.where(lo, turn(q), k))
        vv = (jnp.where(lo_half, v1, turn(v2)), jnp.where(lo_half, turn(v1), v2))
        for u in range(2):
            d = b * z.G + u // z.pairs
            gw[d, u % z.pairs, :rows, :] = qk[u]
            gw[d, u % z.pairs, z.pix : z.pix + z.fold, :] = vv[u][: z.fold]
    for pair in range(z.pairs):
        sw_ref[:, pair] = gw[:, pair].astype(BF16)


def branch_projection(z, low, w_ref, bias, first):
    D = z.dim
    lanes = [slice(n * D + first, n * D + first + HALF) for n in range(3)]
    weight = jnp.concatenate([w_ref[:, own] for own in lanes], -1)
    own_bias = jnp.concatenate([bias[:, own] for own in lanes], -1)
    return (mm(low, weight) + own_bias).reshape(z.cols, z.images, 3 * HALF)


def dense_in_tall(z, w_ref, bias, st_ref, low_ref, pt, gt):
    B, TC, TR = z.images, z.cols, z.rows

    def one_row(i, carry):
        proj = branch_projection(z, low_ref[i], w_ref, bias, HALF)
        for j in range(TC):
            s, jj = divmod(j, SW)
            at = pl.multiple_of(((s * TR + i) * SW + jj) * B, B)
            for n in range(3):
                pt[n, pl.ds(at, B), :] = proj[j, :, n * HALF : (n + 1) * HALF]
        return carry

    lax.fori_loop(0, TR, one_row, 0)
    size = up(z.tall_own, 8)
    for b in range(B):
        for n in range(3):
            for s in range(z.stripes):
                part = pt[n, pl.ds(s * z.tall_own * B + b, size, stride=B), :]
                at = (((b % z.tall_images) * z.stripes + s) * 3 + n) * z.tall_pad
                gt[b // z.tall_images, at : at + size, :] = part
    st_ref[...] = gt[...].astype(BF16)


def erf_parts(values):
    cdf = 0.5 * (1.0 + lax.erf(values * (0.5**0.5)))
    density = jnp.exp(-0.5 * values * values) * (1.0 / math.sqrt(2.0 * math.pi))
    return cdf, density


def dense_mid_kernel(
    z,
    heights_ref,
    widths_ref,
    rw_ref,
    rt_ref,
    x_ref,
    ct_ref,
    pw_ref,
    pb_ref,
    gain_ref,
    shift_ref,
    w1_ref,
    b1_ref,
    w2_ref,
    b2_ref,
    y_ref,
    gres_ref,
    gw_ref,
    gt_ref,
    dpw_ref,
    dw1_ref,
    dw2_ref,
    vec_ref,
    mw,
    mt,
    gmw,
    gmt,
    gws,
    gts,
    res,
    n2s,
    r2s,
    gys,
    acts,
    mixes,
    pre0,
    pre1,
    gh0,
    gh1,
    hid0,
    hid1,
    gpre0,
    gpre1,
):
    B, D, TC, TR = z.images, z.dim, z.cols, z.rows
    T = TC * B
    count = z.tall_own * B
    blocks = [rw_ref[:, u].astype(F32)[:, : z.fold, :] for u in range(z.pairs)]
    if z.G > 1:
        pairs = rw_ref[:, 0].astype(F32).reshape(B, z.G, z.fold_rows, HALF)
        blocks = [pairs[:, g, : z.fold, :] for g in range(2)]
    lo = low_lanes((B, z.fold, HALF))
    for half, value in enumerate(
        (jnp.where(lo, blocks[0], turn(blocks[1])), jnp.where(lo, turn(blocks[0]), blocks[1]))
    ):
        size = z.fold * B
        value = jnp.swapaxes(value, 0, 1).reshape(size, HALF)
        mw[half * size : (half + 1) * size, :] = value.astype(BF16)
    gts[...] = rt_ref[...].astype(F32)
    for s in range(z.stripes):
        rows = []
        for b in range(B):
            at = ((b % z.tall_images) * z.stripes + s) * z.tall_pad
            rows.append(gts[b // z.tall_images, at : at + z.tall_own, :])
        value = jnp.swapaxes(jnp.stack(rows), 0, 1).reshape(count, HALF)
        mt[s * count : (s + 1) * count, :] = value.astype(BF16)
    for ref in (dpw_ref, dw1_ref, dw2_ref, vec_ref):
        ref[...] = jnp.zeros_like(ref)
    row_start = lax.axis_index("row") * TR
    col_start = lax.axis_index("col") * TC
    image = lax.broadcasted_iota(jnp.int32, (B, D), 0)
    height = jnp.zeros((B, D), jnp.int32)
    width = jnp.zeros((B, D), jnp.int32)
    for b in range(B):
        height = jnp.where(image == b, heights_ref[b], height)
        width = jnp.where(image == b, widths_ref[b], width)
    below_cols = (lax.broadcasted_iota(jnp.int32, (TC, B, D), 0) + col_start) < width[None]
    slots = ((pre0, gh0, hid0, gpre0), (pre1, gh1, hid1, gpre1))

    def places(i, j):
        s, jj = divmod(j, SW)
        return (j * TR + i) * B, ((s * TR + i) * SW + jj) * B

    def first(i):
        pre, gh = slots[i % 2][:2]
        own = slice(i * T, (i + 1) * T)
        at = [places(i, j) for j in range(TC)]
        wide = jnp.concatenate([mw[w : w + B, :] for w, _ in at], 0)
        tall = jnp.concatenate([mt[t : t + B, :] for _, t in at], 0)
        mixture = jnp.concatenate([wide, tall], -1)
        mixes[own, :] = mixture
        x = x_ref[i].astype(F32).reshape(T, D)
        residual = x + (mm(mixture, pw_ref[...]) + pb_ref[...])
        res[own, :] = residual
        n2, r2 = norm_parts(residual)
        n2s[own, :] = n2
        r2s[own, :] = jnp.broadcast_to(r2, (T, HALF))
        act = (n2 * gain_ref[...] + shift_ref[...]).astype(BF16)
        acts[own, :] = act
        pre[...] = mm(act, w1_ref[...]) + b1_ref[...]
        below_rows = (i + row_start) < height[None]
        inside = jnp.logical_and(below_cols, below_rows)
        gy = jnp.where(inside, ct_ref[i].astype(F32), 0.0).reshape(T, D).astype(BF16)
        gys[own, :] = gy
        gh[...] = mm_nt(gy, w2_ref[...])

    def second(i):
        pre, gh, hid, gpre = slots[i % 2]
        FF = pre.shape[1]
        for at, size in key_tiles(FF, 256):
            lanes = slice(at, at + size)
            value = pre[:, lanes]
            cdf, density = erf_parts(value)
            hid[:, lanes] = (value * cdf).astype(BF16)
            low = (gh[:, lanes] * (cdf + value * density)).astype(BF16)
            gpre[:, lanes] = low
            total = jnp.sum(low.astype(F32), 0, keepdims=True)
            for k in range(size // D):
                row = 8 + at // D + k
                vec_ref[row : row + 1, :] += total[:, k * D : (k + 1) * D]

    def third(i):
        hid, gpre = slots[i % 2][2:]
        own = slice(i * T, (i + 1) * T)
        out = res[own, :] + (mm(hid[...], w2_ref[...]) + b2_ref[...])
        y_ref[i] = out.astype(BF16).reshape(TC, B, D)
        gy = gys[own, :]
        dw2_ref[...] += mm_tn(hid[...], gy)
        dw1_ref[...] += mm_tn(acts[own, :], gpre[...])
        gact = mm_nt(gpre[...], w1_ref[...])
        n2 = n2s[own, :]
        r2 = r2s[own, :1]
        gy = gy.astype(F32)
        g = gact * gain_ref[...]
        gres = gy + r2 * (
            g - jnp.mean(g, -1, keepdims=True) - n2 * jnp.mean(g * n2, -1, keepdims=True)
        )
        gres_ref[i] = gres.reshape(TC, B, D)
        gattn = gres.astype(BF16)
        dpw_ref[...] += mm_tn(mixes[own, :], gattn)
        gmix = mm_nt(gattn, pw_ref[...]).astype(BF16).astype(F32)
        vec_ref[0:1, :] += jnp.sum(gact * n2, 0, keepdims=True)
        vec_ref[1:2, :] += jnp.sum(gact, 0, keepdims=True)
        vec_ref[2:3, :] += jnp.sum(gattn.astype(F32), 0, keepdims=True)
        vec_ref[3:4, :] += jnp.sum(gy, 0, keepdims=True)
        vec_ref[4:5, :] += jnp.sum(gmix, 0, keepdims=True)
        gm3 = gmix.reshape(TC, B, D)
        for j in range(TC):
            wide_at, tall_at = places(i, j)
            gmw[wide_at : wide_at + B, :] = gm3[j, :, :HALF]
            gmt[tall_at : tall_at + B, :] = gm3[j, :, HALF:]

    for t in range(TR + 2):
        if t < TR:
            first(t)
        if 0 <= t - 1 < TR:
            second(t - 1)
        if t - 2 >= 0:
            third(t - 2)
    gws[:, : z.pix, :] = jnp.swapaxes(gmw[...].reshape(z.pix, B, HALF), 0, 1)
    if z.G == 1:
        gw_ref[...] = gws[...].astype(BF16)
    else:
        for b in range(B):
            for g in range(z.G):
                gw_ref[b * z.G + g] = gws[b, :, g * z.hc : (g + 1) * z.hc].astype(BF16)
    for s in range(z.stripes):
        value = gmt[s * count : (s + 1) * count, :].reshape(z.tall_own, B, HALF)
        value = jnp.swapaxes(value, 0, 1)
        for b in range(B):
            at = ((b % z.tall_images) * z.stripes + s) * z.tall_pad
            gts[b // z.tall_images, at : at + z.tall_own, :] = value[b]
    gt_ref[...] = gts[...].astype(BF16)


def dense_out_kernel(
    z,
    rw_ref,
    rt_ref,
    x_ref,
    gres_ref,
    gain_ref,
    shift_ref,
    w_ref,
    gin_ref,
    dw_ref,
    vec_ref,
    pw,
    pt,
    gw,
    gt,
):
    B, D, TC, TR = z.images, z.dim, z.cols, z.rows
    T = TC * B
    gw[...] = rw_ref[...].astype(F32)
    gt[...] = rt_ref[...].astype(F32)
    lo = low_half(z.pix)
    lo_half = low_half(z.fold)
    for b in range(B):
        qk = []
        vv = []
        for u in range(2):
            d = b * z.G + u // z.pairs
            qk.append(gw[d, u % z.pairs, : z.pix, :])
            vv.append(gw[d, u % z.pairs, z.pix : z.pix + z.fold, :])
        places = pl.ds(b, z.pix, stride=B)
        pw[0, places, :] = jnp.where(lo, qk[0], turn(qk[1]))
        pw[1, places, :] = jnp.where(lo, turn(qk[0]), qk[1])
        pw[2, pl.ds(b, z.fold, stride=B), :] = jnp.where(lo_half, vv[0], turn(vv[1]))
        pw[2, pl.ds(z.fold * B + b, z.fold, stride=B), :] = jnp.where(
            lo_half, turn(vv[0]), vv[1]
        )
        for n in range(3):
            for s in range(z.stripes):
                at = (((b % z.tall_images) * z.stripes + s) * 3 + n) * z.tall_pad
                pt[n, pl.ds(s * z.tall_own * B + b, z.tall_own, stride=B), :] = gt[
                    b // z.tall_images, at : at + z.tall_own, :
                ]
    dw_ref[...] = jnp.zeros_like(dw_ref)
    vec_ref[...] = jnp.zeros_like(vec_ref)

    def one_row(i, carry):
        x = x_ref[i].astype(F32).reshape(T, D)
        n1, r1 = norm_parts(x)
        low = (n1 * gain_ref[...] + shift_ref[...]).astype(BF16)
        lanes = []
        for n in range(3):
            wide = []
            tall = []
            for j in range(TC):
                s, jj = divmod(j, SW)
                wide_at = pl.multiple_of((j * TR + i) * B, B)
                tall_at = pl.multiple_of(((s * TR + i) * SW + jj) * B, B)
                wide.append(pw[n, pl.ds(wide_at, B), :])
                tall.append(pt[n, pl.ds(tall_at, B), :])
            lanes.append(jnp.concatenate(wide, 0))
            lanes.append(jnp.concatenate(tall, 0))
        gproj = jnp.concatenate(lanes, -1)
        vec_ref[2:3, :] += jnp.sum(gproj[:, :D], 0, keepdims=True)
        vec_ref[3:4, :] += jnp.sum(gproj[:, 2 * D :], 0, keepdims=True)
        gproj = gproj.astype(BF16)
        dw_ref[...] += mm_tn(low, gproj)
        gn = mm_nt(gproj, w_ref[...])
        vec_ref[0:1, :] += jnp.sum(gn * n1, 0, keepdims=True)
        vec_ref[1:2, :] += jnp.sum(gn, 0, keepdims=True)
        g = gn * gain_ref[...]
        gin = gres_ref[i].reshape(T, D) + r1 * (
            g - jnp.mean(g, -1, keepdims=True) - n1 * jnp.mean(g * n1, -1, keepdims=True)
        )
        gin_ref[i] = gin.reshape(TC, B, D)
        return carry

    lax.fori_loop(0, TR, one_row, 0)


def key_tiles(length, tile):
    return [(at, min(tile, length - at)) for at in range(0, length, tile)]


def token_places(start, count, lanes):
    token = (lax.broadcasted_iota(jnp.int32, (count, lanes), 0) + start).astype(F32)
    along = jnp.floor((token + 0.5) * (1.0 / SW))
    across = token - along * SW
    return along, across


def conv_forward(vpad, base, count, kernels, across):
    total = None
    for a in (-1, 0, 1):
        inner = None
        for l in (-1, 0, 1):
            term = kernels(a, l) * vpad[base + SW * l + a : base + SW * l + a + count, :]
            inner = term if inner is None else inner + term
        if a == -1:
            inner = jnp.where(across >= 1, inner, 0.0)
        if a == 1:
            inner = jnp.where(across <= SW - 2, inner, 0.0)
        total = inner if total is None else total + inner
    return total


def conv_backward(gpad, base, count, kernels, across):
    total = None
    for a in (-1, 0, 1):
        inner = None
        for l in (-1, 0, 1):
            at = base - SW * l - a
            term = kernels(a, l) * gpad[at : at + count, :]
            inner = term if inner is None else inner + term
        if a == -1:
            inner = jnp.where(across <= SW - 2, inner, 0.0)
        if a == 1:
            inner = jnp.where(across >= 1, inner, 0.0)
        total = inner if total is None else total + inner
    return total


def wide_tap(a, l):
    return 3 * (a + 1) + (l + 1)


def tall_tap(a, l):
    return 3 * (l + 1) + (a + 1)


def head_lanes(h, rows):
    lane = lax.broadcasted_iota(jnp.int32, (rows, HALF), 1)
    return jnp.logical_and(lane >= h * HEAD_DIM, lane < (h + 1) * HEAD_DIM)


def wide_plan(z):
    per_head = z.wide_len // z.qb
    tail = z.wide_len - per_head * z.qb
    blocks = 2 * per_head
    lanes = up(2 * tail, 128)
    return per_head, tail, blocks, lanes, blocks * z.qb + lanes


def diagonal(tail, first, lanes):
    channel = lax.broadcasted_iota(jnp.int32, (HALF, lanes), 0) - first * HEAD_DIM
    query = lax.broadcasted_iota(jnp.int32, (HALF, lanes), 1)
    keep = channel < -HALF
    for h in range(2):
        keep = jnp.logical_or(
            keep,
            jnp.logical_and(
                jnp.logical_and(channel >= h * HEAD_DIM, channel < (h + 1) * HEAD_DIM),
                jnp.logical_and(query >= h * tail, query < (h + 1) * tail),
            ),
        )
    return keep


def tail_columns(rows, tail, first, lanes):
    copies = [rows, rows]
    if lanes > 2 * tail:
        copies.append(jnp.zeros((lanes - 2 * tail, HALF), F32))
    return jnp.where(diagonal(tail, first, lanes), jnp.concatenate(copies, 0).T, 0.0)


def tail_rows(columns, tail):
    flat = columns.T
    return flat[:tail] + flat[tail : 2 * tail]


def head_rows_mask(h, value):
    row = lax.broadcasted_iota(jnp.int32, value.shape, 0)
    keep = jnp.logical_and(row >= h * HEAD_DIM, row < (h + 1) * HEAD_DIM)
    return jnp.where(keep, value, 0.0)


def between(value, high):
    return jnp.maximum(jnp.minimum(value, high), 0)


def wide_ends(z, heights_ref, widths_ref):
    image = lax.axis_index("col") // z.G
    start = lax.axis_index("row") * z.rows
    return (
        between(heights_ref[image] - start, z.rows),
        between(widths_ref[image], z.C * z.cols),
    )


def tall_ends(z, heights_ref, widths_ref):
    def ends(p):
        image = lax.axis_index("row") * z.tall_images + p // z.stripes
        start = lax.axis_index("col") * z.cols + lax.rem(p, z.stripes) * SW
        return (
            between(widths_ref[image] - start, SW),
            between(heights_ref[image], z.R * z.rows),
        )

    return ends


def own_lanes(z, value):
    if z.G == 1:
        return value
    turned = jnp.where(lax.rem(lax.axis_index("col"), z.G) == 0, value, turn(value))
    return jnp.where(low_half(value.shape[0]), turned, 0.0)


def wide_limits(lim_ref):
    across_limit, along_limit = lim_ref
    empty = across_limit * along_limit == 0
    scale = jnp.where(empty, 1e-20, LOG2E * HEAD_DIM**-0.5)
    return across_limit, along_limit, empty, scale


def wide_inside(lim_ref, at, size):
    along, across = token_places(at, size, HALF)
    return jnp.logical_and(across < lim_ref[0], along < lim_ref[1]), across


def wide_pair_prepare(
    z, pair, lim_ref, recv, kcat, qtb, kt, qk, vpad, stage, vt, vt_all, waits=()
):
    L = z.wide_len
    per_head, tail, blocks, tail_lanes, span = wide_plan(z)
    full = per_head * z.qb
    _, _, empty, _ = wide_limits(lim_ref)
    cut = up(z.pix, 16)
    if waits:
        waits[0].arrive()
        for later in waits[2:]:
            later.start()
    for c in range(z.C):
        stage[:cut, :] = recv[c, pair, :cut].astype(F32)
        qk[c * z.pix : (c + 1) * z.pix, :] = stage[: z.pix, :]
    ones = jnp.where(lax.broadcasted_iota(jnp.int32, (HALF, z.qb), 0) == 0, 1.0, 0.0).astype(BF16)

    def keys(at, size):
        rows = pl.ds(at, size)
        both = qk[rows, :]
        kcat[pair, rows, :HALF] = both.astype(BF16)
        inside, _ = wide_inside(lim_ref, at, size)
        allowed = jnp.logical_or(inside, empty)
        lane = lax.broadcasted_iota(jnp.int32, (size, HALF), 1) == 0
        bias = jnp.where(jnp.logical_and(lane, jnp.logical_not(allowed)), MASKED, 0.0)
        kcat[pair, rows, HALF:] = bias.astype(BF16)
        return both

    def flip(n, carry):
        at = pl.multiple_of(n * z.qb, z.qb)
        both = keys(at, z.qb).T
        kt[pair, :, pl.ds(at, z.qb)] = both[HALF // 2 :].astype(BF16)
        for h in range(2):
            cols = pl.ds(pl.multiple_of((h * per_head + n) * z.qb, z.qb), z.qb)
            parts = [jnp.zeros((HALF // 2, z.qb), F32)] + [jnp.zeros((HEAD_DIM, z.qb), F32)] * 2
            parts[1 + h] = both[h * HEAD_DIM : (h + 1) * HEAD_DIM]
            qtb[pair, :HALF, cols] = jnp.concatenate(parts, 0).astype(BF16)
            qtb[pair, HALF:, cols] = ones
        return carry

    lax.fori_loop(0, per_head, flip, 0)
    tail_cols = slice(blocks * z.qb, span)
    tail_both = keys(full, tail)
    kt[pair, :, full:L] = tail_both.T[HALF // 2 :].astype(BF16)
    qtb[pair, :HALF, tail_cols] = tail_columns(turn(tail_both), tail, 2, tail_lanes).astype(BF16)
    qtb[pair, HALF:, tail_cols] = ones[:, :tail_lanes]
    if waits:
        waits[1].arrive()
    lo = low_half(z.fold)
    start = z.pix // 16 * 16
    for c in range(z.C):
        stage[start:, :] = recv[c, pair, start:].astype(F32)
        v = stage[z.pix : z.pix + z.fold, :]
        at = c * z.pix
        one = slice(PAD + at, PAD + at + z.fold)
        two = slice(PAD + at + z.fold, PAD + at + z.pix)
        if pair == 0:
            vpad[one, :] = jnp.where(lo, v, 0.0)
            vpad[two, :] = jnp.where(lo, turn(v), 0.0)
        else:
            vpad[one, :] = jnp.where(lo, vpad[one, :], turn(v))
            vpad[two, :] = jnp.where(lo, vpad[two, :], v)

    def values(at, size):
        vt_full = vpad[pl.ds(pl.multiple_of(at + PAD, 8), size), :].T
        first = lax.broadcasted_iota(jnp.int32, (16, size), 0) == 0
        first = jnp.where(first, 1.0, 0.0)
        vt_all[:, pl.ds(at, size)] = jnp.concatenate([vt_full, first], 0).astype(BF16)
        for h in range(2):
            own = (2 * pair + h) * HEAD_DIM
            own = vt_full[own : own + HEAD_DIM]
            vt[h, :, pl.ds(at, size)] = jnp.concatenate([own, first], 0).astype(BF16)

    def flip_values(n, carry):
        values(pl.multiple_of(n * z.qb, z.qb), z.qb)
        return carry

    lax.fori_loop(0, per_head, flip_values, 0)
    values(full, tail)


def wide_pair_attend(z, pair, lim_ref, kcat, qtb, ot, lse, vt, vt_all, ss0, ss1):
    L = z.wide_len
    per_head, tail, blocks, tail_lanes, span = wide_plan(z)
    full = per_head * z.qb
    base = pair * span
    _, _, _, scale = wide_limits(lim_ref)
    tail_cols = slice(blocks * z.qb, span)

    def scores(cols, slot):
        s = mm(kcat[pair], qtb[pair, :, cols])
        slot[...] = s
        return jnp.max(jnp.max(s.reshape(L // 8, 8, s.shape[1]), 0), 0, keepdims=True)

    def block_scores(n, slot):
        return scores(pl.ds(pl.multiple_of(n * z.qb, z.qb), z.qb), slot)

    def weigh(values, slot, top):
        p = jnp.exp2((slot[...] - top) * scale).astype(BF16)
        acc = mm(values, p)
        at = acc.shape[0] - 16
        total = acc[at : at + 1]
        return acc[:at] * (1.0 / total), top * scale + jnp.log2(total)

    def block_rest(n, slot, top):
        h = n // per_head
        out, low = weigh(vt[h], slot, top)
        rows = pl.ds(pl.multiple_of((2 * pair + h) * HEAD_DIM, HEAD_DIM), HEAD_DIM)
        ot[rows, pl.ds(pl.multiple_of((n - h * per_head) * z.qb, z.qb), z.qb)] = out
        lse[0:1, pl.ds(pl.multiple_of(base + n * z.qb, 128), z.qb)] = low

    def two(m, top):
        n = 2 * m
        top_next = block_scores(n + 1, ss1)
        block_rest(n, ss0, top)
        top = block_scores(n + 2, ss0)
        block_rest(n + 1, ss1, top_next)
        return top

    top = lax.fori_loop(0, blocks // 2 - 1, two, block_scores(0, ss0))
    top_next = block_scores(blocks - 1, ss1)
    block_rest(blocks - 2, ss0, top)
    tail_slot = ss0.at[:, :tail_lanes]
    top = scores(tail_cols, tail_slot)
    block_rest(blocks - 1, ss1, top_next)
    out, low = weigh(vt_all[...], tail_slot, top)
    lse[0:1, base + blocks * z.qb : base + span] = low
    out = jnp.where(diagonal(tail, 2 * pair, tail_lanes), out, 0.0)
    ot[:, full + pair * tail_lanes : full + (pair + 1) * tail_lanes] = out


def wide_lepe(z, lim_ref, lw_ref, lb_ref, vpad, lepe):
    L = z.wide_len
    for at, size in key_tiles(L, z.qb):
        inside, _ = wide_inside(lim_ref, at, size)
        rows = slice(at + PAD, at + PAD + size)
        vpad[rows, :] = jnp.where(inside, vpad[rows, :], 0.0)

    def taps(a, l):
        t = wide_tap(a, l)
        return lw_ref[t : t + 1, :]

    for at, size in key_tiles(L, 224):
        along, across = token_places(at, size, HALF)
        lepe[at : at + size, :] = conv_forward(vpad, at + PAD, size, taps, across) + lb_ref


def wide_pair_mixture(z, pair, ot, lepe, osum, out_ref):
    L = z.wide_len
    per_head, tail, _, tail_lanes, _ = wide_plan(z)
    full = per_head * z.qb

    def doubled(value):
        lo = low_half(value.shape[0])
        return jnp.where(lo, value, turn(value)) if pair == 0 else jnp.where(lo, turn(value), value)

    def finish(n, carry):
        rows = pl.ds(pl.multiple_of(n * z.qb, z.qb), z.qb)
        osum[rows, :] = doubled(ot[:, rows].T + lepe[rows, :])
        return carry

    lax.fori_loop(0, per_head, finish, 0)
    last = tail_rows(ot[:, full + pair * tail_lanes : full + (pair + 1) * tail_lanes], tail)
    osum[full:L, :] = doubled(last + lepe[full:L, :])
    lo = low_half(z.fold_rows)
    for c in range(z.C):
        at = c * z.pix
        one = osum[at : at + z.fold_rows, :]
        two = osum[at + z.fold : at + z.fold + z.fold_rows, :]
        out_ref[c, pair] = jnp.where(lo, one, two).astype(BF16)


def wide_backward_start(z, lim_ref, recv, lw_ref, v_ref, ot, dlw_ref, gpad, vpad, dotb, delta, dvl, stage):
    L = z.wide_len
    per_head, tail, blocks, tail_lanes, span = wide_plan(z)
    full = per_head * z.qb
    gpad[...] = jnp.zeros_like(gpad)
    vpad[...] = jnp.zeros_like(vpad)
    stage[...] = jnp.zeros_like(stage)
    for c in range(z.C):
        stage[: z.wide_rows1, : z.hc] = recv[c].astype(F32)
        gpad[PAD + c * z.pix : PAD + (c + 1) * z.pix, :] = stage[: z.pix, :]

    def prepare(at, size):
        rows = pl.ds(at, size)
        padded = pl.ds(pl.multiple_of(at + PAD, 8), size)
        inside, _ = wide_inside(lim_ref, at, size)
        vpad[padded, :] = jnp.where(inside, v_ref[rows, :].astype(F32), 0.0)
        return gpad[padded, :]

    def flip(n, carry):
        at = pl.multiple_of(n * z.qb, z.qb)
        gt = prepare(at, z.qb).T
        prod = gt * ot[:, pl.ds(at, z.qb)]
        for h in range(z.wide_heads):
            first = (h // 2) * span + (h % 2) * full
            cols = pl.ds(pl.multiple_of(first + n * z.qb, 128), z.qb)
            dotb[:, cols] = head_rows_mask(h, gt).astype(BF16)
            delta[0:1, cols] = jnp.sum(
                prod[h * HEAD_DIM : (h + 1) * HEAD_DIM], 0, keepdims=True
            )
        return carry

    lax.fori_loop(0, per_head, flip, 0)
    last = prepare(full, tail)
    for pair in range(z.pairs):
        cols = slice(pair * span + blocks * z.qb, (pair + 1) * span)
        gt = tail_columns(last, tail, 2 * pair, tail_lanes)
        dotb[:, cols] = gt.astype(BF16)
        out = ot[:, full + pair * tail_lanes : full + (pair + 1) * tail_lanes]
        delta[0:1, cols] = jnp.sum(gt * out, 0, keepdims=True)

    def taps(a, l):
        t = wide_tap(a, l)
        return lw_ref[t : t + 1, :]

    sums_of = {}
    for at, size in key_tiles(L, 224):
        inside, across = wide_inside(lim_ref, at, size)
        lepe = conv_backward(gpad, at + PAD, size, taps, across)
        dvl[at : at + size, :] = jnp.where(inside, lepe, 0.0)
        add_kernel_sums(sums_of, gpad, vpad, at + PAD, size, across, wide_tap)
    dlw_ref[...] = jnp.zeros_like(dlw_ref)
    for t, value in sums_of.items():
        dlw_ref[t : t + 1, :] = jnp.sum(value, 0, keepdims=True)


def wide_pair_backward(
    z,
    pair,
    lim_ref,
    v_ref,
    kcat,
    qtb,
    kt,
    lse,
    dotb,
    delta,
    dvl,
    dqt,
    dkt,
    dvt,
    dqk,
    dvv,
    stage,
    slots,
    out_ref,
    midway,
    segments,
):
    L = z.wide_len
    per_head, tail, blocks, tail_lanes, span = wide_plan(z)
    full = per_head * z.qb
    base = pair * span
    _, _, _, scale = wide_limits(lim_ref)
    dkt[...] = jnp.zeros_like(dkt)
    dvt[...] = jnp.zeros_like(dvt)
    tail_cols = slice(blocks * z.qb, span)

    def shifted(cols):
        if isinstance(cols, slice):
            return slice(base + cols.start, base + cols.stop)
        return pl.ds(pl.multiple_of(base + cols.start, 128), cols.size)

    def products(cols, s_slot, dp_slot):
        s_slot[...] = mm(kcat[pair], qtb[pair, :, cols])
        dp_slot[...] = mm(v_ref[...], dotb[:, shifted(cols)])

    def weights(cols, s_slot, dp_slot, p_slot, ds_slot):
        low = lse[0:1, shifted(cols)]
        dlt = delta[0:1, shifted(cols)]
        for at, size in key_tiles(L, z.qb):
            rows = slice(at, at + size)
            p = jnp.exp2(s_slot[rows, :] * scale - low)
            p_slot[rows, :] = p.astype(BF16)
            ds_slot[rows, :] = (p * (dp_slot[rows, :] - dlt)).astype(BF16)

    def block_cols(n):
        return pl.ds(pl.multiple_of(n * z.qb, z.qb), z.qb)

    def first(n, k):
        products(block_cols(n), *slots[k][:2])

    def second(n, k):
        weights(block_cols(n), *slots[k])

    def third(n, k):
        h = n // per_head
        p_slot, ds_slot = slots[k][2:]
        cols = block_cols(n)
        rows = pl.ds(pl.multiple_of(h * HEAD_DIM, HEAD_DIM), HEAD_DIM)
        g_rows = pl.ds(pl.multiple_of((2 * pair + h) * HEAD_DIM, HEAD_DIM), HEAD_DIM)
        q_rows = pl.ds(pl.multiple_of(HALF // 2 + h * HEAD_DIM, HEAD_DIM), HEAD_DIM)
        dvt[rows, :] += mm_nt(dotb[g_rows, shifted(cols)], p_slot[...])
        dkt[rows, :] += mm_nt(qtb[pair, q_rows, cols], ds_slot[...])
        at = pl.ds(pl.multiple_of((n - h * per_head) * z.qb, z.qb), z.qb)
        dqt[rows, at] = mm(kt[pair, rows, :], ds_slot[...])

    first(0, 0)
    first(1, 1)
    second(0, 0)

    def two(m, carry):
        n = 2 * m
        first(n, 0)
        second(n - 1, 1)
        third(n - 2, 0)
        first(n + 1, 1)
        second(n, 0)
        third(n - 1, 1)
        return carry

    marks = [1 + (blocks // 2 - 1) * k // segments for k in range(segments + 1)]
    for k in range(segments):
        lax.fori_loop(marks[k], marks[k + 1], two, 0)
        if k + 1 < segments:
            midway()
    tail_slots = [ref.at[:, :tail_lanes] for ref in slots[0]]
    products(tail_cols, *tail_slots[:2])
    second(blocks - 1, 1)
    third(blocks - 2, 0)
    weights(tail_cols, *tail_slots)
    third(blocks - 1, 1)
    half = HALF // 2
    dvt[...] += mm_nt(dotb[pair * half : (pair + 1) * half, shifted(tail_cols)], tail_slots[2][...])
    dkt[...] += mm_nt(qtb[pair, half:HALF, tail_cols], tail_slots[3][...])
    last = mm(kt[pair], tail_slots[3][...])
    empty_half = jnp.zeros((half, tail_lanes), F32)
    last = jnp.concatenate([last, empty_half], 0)
    last = jnp.where(diagonal(tail, 0, tail_lanes), last, 0.0)
    norm = HEAD_DIM**-0.5
    dk_last = jnp.concatenate([jnp.zeros((half, tail), F32), dkt[:, full:L]], 0).T
    dqk[full:L, :] = (tail_rows(last, tail) + dk_last) * norm

    def doubled(value):
        lo = low_half(value.shape[0])
        return jnp.where(lo, value, turn(value)) if pair == 0 else jnp.where(lo, turn(value), value)

    def finish(n, carry):
        rows = pl.ds(pl.multiple_of(n * z.qb, z.qb), z.qb)
        dqk[rows, :] = jnp.concatenate([dqt[:, rows], dkt[:, rows]], 0).T * norm
        dv = dvt[:, rows]
        dvv[rows, :] = jnp.concatenate([dv, dv], 0).T + doubled(dvl[rows, :])
        return carry

    lax.fori_loop(0, per_head, finish, 0)
    dv = dvt[:, full:L]
    dvv[full:L, :] = jnp.concatenate([dv, dv], 0).T + doubled(dvl[full:L, :])
    lo = low_half(z.fold)
    for c in range(z.C):
        at = c * z.pix
        stage[: z.pix, :] = dqk[at : at + z.pix, :]
        stage[z.pix : z.pix + z.fold, :] = jnp.where(
            lo, dvv[at : at + z.fold, :], dvv[at + z.fold : at + z.pix, :]
        )
        out_ref[c, pair] = stage[...].astype(BF16)


def add_kernel_sums(sums, gpad, vpad, base, size, across, tap):
    g = gpad[base : base + size, :]
    for a in (-1, 0, 1):
        ga = g
        if a == -1:
            ga = jnp.where(across >= 1, g, 0.0)
        if a == 1:
            ga = jnp.where(across <= SW - 2, g, 0.0)
        for l in (-1, 0, 1):
            at = base + SW * l + a
            term = (ga * vpad[at : at + size, :]).reshape(size // 8, 8, HALF).sum(0)
            t = tap(a, l)
            sums[t] = sums[t] + term if t in sums else term


def tall_prepare(z, p, lim_ref, L):
    across_limit, along_limit = lim_ref(p)
    empty = across_limit * along_limit == 0
    scale = jnp.where(empty, 1e-20, LOG2E * HEAD_DIM**-0.5)
    along, across = token_places(0, L, HALF)
    inside = jnp.logical_and(across < across_limit, along < along_limit)
    allowed = jnp.logical_or(inside, empty)
    token = lax.broadcasted_iota(jnp.int32, (L, HALF), 0)
    allowed = jnp.logical_and(allowed, token < z.tall_len)
    lane = lax.broadcasted_iota(jnp.int32, (L, HALF), 1) == 0
    bias = jnp.where(jnp.logical_and(lane, jnp.logical_not(allowed)), MASKED, 0.0).astype(BF16)
    return inside, across, scale, bias


def tall_pull(z, source, p, per, n, target, base):
    for r in range(z.R):
        at = pl.multiple_of((p * per + n) * z.tall_pad, 8)
        block = source[r, pl.ds(at, z.tall_pad), :]
        target[base + r * z.tall_own : base + (r + 1) * z.tall_own, :] = block[: z.tall_own]


def tall_push(z, source, p, per, n, target, base=0):
    for r in range(z.R):
        at = pl.multiple_of((p * per + n) * z.tall_pad, 8)
        target[r, pl.ds(at, z.tall_pad), :] = source[
            base + r * z.tall_own : base + r * z.tall_own + z.tall_pad, :
        ]


def tall_operands(z, k, q, bias, kstack, L):
    for h in range(BRANCH_HEADS):
        kstack[h * L : (h + 1) * L, :HALF] = jnp.where(head_lanes(h, L), k, 0.0).astype(BF16)
        kstack[h * L : (h + 1) * L, HALF:] = bias
    first = lax.broadcasted_iota(jnp.int32, (HALF, L), 0) == 0
    return jnp.concatenate([q.T, jnp.where(first, 1.0, 0.0)], 0).astype(BF16)


def tall_forward(
    z, start, stop, lim_ref, lw_ref, lb_ref, ot_ref, lse_ref, src, dst, qs, ks, vs, vpad, osum, kstack
):
    L = qs.shape[1]

    def taps(a, l):
        t = tall_tap(a, l)
        return lw_ref[t : t + 1, :]

    def group(m, carry):
        each = range(z.tall_group)
        ps = [m * z.tall_group + u for u in each]
        for u in each:
            for n, target in enumerate((qs, ks, vs)):
                tall_pull(z, src, ps[u], 3, n, target.at[u], 0)
        made = [tall_prepare(z, ps[u], lim_ref, L) for u in each]
        qts = [tall_operands(z, ks[u], qs[u], made[u][3], kstack.at[u], L) for u in each]
        scores = [mm(kstack[u], qts[u]) for u in each]
        tail = lax.broadcasted_iota(jnp.int32, (16, L), 0) == 0
        tail = jnp.where(tail, 1.0, 0.0)
        vts = [vs[u].T for u in each]
        tops = [
            [jnp.max(scores[u][h * L : (h + 1) * L], 0, keepdims=True) for h in range(BRANCH_HEADS)]
            for u in each
        ]
        accs = []
        for u in each:
            row = []
            for h in range(BRANCH_HEADS):
                s = scores[u][h * L : (h + 1) * L]
                e = jnp.exp2((s - tops[u][h]) * made[u][2]).astype(BF16)
                vt = jnp.concatenate([vts[u][h * HEAD_DIM : (h + 1) * HEAD_DIM], tail], 0)
                row.append(mm(vt.astype(BF16), e))
            accs.append(row)
        for u in each:
            inside, across, scale, _ = made[u]
            outs = []
            for h in range(BRANCH_HEADS):
                total = accs[u][h][HEAD_DIM : HEAD_DIM + 1]
                outs.append(accs[u][h][:HEAD_DIM] * (1.0 / total))
                lse_ref[ps[u], h : h + 1, :] = tops[u][h] * scale + jnp.log2(total)
            ot = jnp.concatenate(outs, 0)
            ot_ref[ps[u]] = ot
            vpad[u, PAD : PAD + L, :] = jnp.where(inside, vs[u], 0.0)
            lepe = conv_forward(vpad.at[u], PAD, L, taps, across)
            osum[u, :L, :] = ot.T + lepe + lb_ref
        for u in each:
            tall_push(z, osum.at[u], ps[u], 1, 0, dst)
        return carry

    lax.fori_loop(start, stop, group, 0)


def tall_backward(
    z,
    start,
    stop,
    lim_ref,
    lw_ref,
    ot_ref,
    lse_ref,
    dlw_ref,
    src,
    gsrc,
    dst,
    qs,
    ks,
    vs,
    gpad,
    vpad,
    stage,
    kstack,
):
    L = qs.shape[1]
    norm = HEAD_DIM**-0.5

    def taps(a, l):
        t = tall_tap(a, l)
        return lw_ref[t : t + 1, :]

    def group(m, carry):
        each = range(z.tall_group)
        ps = [m * z.tall_group + u for u in each]
        for u in each:
            for n, target in enumerate((qs, ks, vs)):
                tall_pull(z, src, ps[u], 3, n, target.at[u], 0)
            tall_pull(z, gsrc, ps[u], 1, 0, gpad.at[u], PAD)
        made = [tall_prepare(z, ps[u], lim_ref, L) for u in each]
        gts = [gpad[u, PAD : PAD + L, :].T for u in each]
        qts = [tall_operands(z, ks[u], qs[u], made[u][3], kstack.at[u], L) for u in each]
        kts = [ks[u].T.astype(BF16) for u in each]
        dvs = [None] * len(ps)
        dks = [None] * len(ps)
        dqs = [[] for u in each]
        for some in z.tall_head_sets:
            scores = []
            dps = []
            for u in each:
                rows = slice(some[0] * L, (some[-1] + 1) * L)
                scores.append(mm(kstack[u, rows, :], qts[u]))
                v = vs[u]
                vstack = jnp.concatenate([jnp.where(head_lanes(h, L), v, 0.0) for h in some], 0)
                dps.append(mm(vstack.astype(BF16), gts[u].astype(BF16)))
            weights = []
            for u in each:
                prod = gts[u] * ot_ref[ps[u]]
                lse = lse_ref[ps[u]]
                row = []
                for i, h in enumerate(some):
                    rows = slice(i * L, (i + 1) * L)
                    delta = jnp.sum(prod[h * HEAD_DIM : (h + 1) * HEAD_DIM], 0, keepdims=True)
                    w = jnp.exp2(scores[u][rows] * made[u][2] - lse[h : h + 1])
                    ds = (w * (dps[u][rows] - delta)).astype(BF16)
                    row.append((w.astype(BF16), ds))
                weights.append(row)
            for u in each:
                for i, h in enumerate(some):
                    keep = head_lanes(h, L)
                    w, ds = weights[u][i]
                    dv_h = mm(w, jnp.where(keep, gpad[u, PAD : PAD + L, :], 0.0).astype(BF16))
                    dk_h = mm(ds, jnp.where(keep, qs[u], 0.0).astype(BF16))
                    dvs[u] = dv_h if dvs[u] is None else dvs[u] + dv_h
                    dks[u] = dk_h if dks[u] is None else dks[u] + dk_h
                    dqs[u].append(mm(kts[u][h * HEAD_DIM : (h + 1) * HEAD_DIM], ds))
        results = [(jnp.concatenate(dqs[u], 0), dks[u], dvs[u]) for u in each]
        sums = {}
        for u in each:
            inside, across = made[u][:2]
            vpad[u, PAD : PAD + L, :] = jnp.where(inside, vs[u], 0.0)
            lepe = conv_backward(gpad.at[u], PAD, L, taps, across)
            add_kernel_sums(sums, gpad.at[u], vpad.at[u], PAD, L, across, tall_tap)
            dqt, dk, dv = results[u]
            stage[u, 0, :L, :] = dqt.T * norm
            stage[u, 1, :L, :] = dk * norm
            stage[u, 2, :L, :] = dv + jnp.where(inside, lepe, 0.0)
        for t, value in sums.items():
            dlw_ref[t : t + 1, :] += jnp.sum(value, 0, keepdims=True)
        for u in each:
            for n in range(3):
                tall_push(z, stage.at[u, n], ps[u], 3, n, dst)
        return carry

    lax.fori_loop(start, stop, group, 0)


def partners(z):
    col = lax.axis_index("col")
    row = lax.axis_index("row")
    found = [(row, lax.rem(col + k, z.C)) for k in range(1, z.C)]
    found += [(lax.rem(row + k, z.R), col) for k in range(1, z.R)]
    first = col - lax.rem(col, 4)
    for r in range(1, z.R):
        for k in range(1, 4):
            found.append((lax.rem(row + r, z.R), first + lax.rem(col + k, 4)))
    return found


def greet(z):
    barrier = pltpu.get_barrier_semaphore()
    for device in partners(z):
        pl.semaphore_signal(barrier, inc=1, device_id=device, device_id_type=MESH)


def all_greeted(z):
    pl.semaphore_wait(pltpu.get_barrier_semaphore(), len(partners(z)))


class Exchange:
    def __init__(self, z, axis, source, target, sends, receives):
        self.axis = axis
        self.source, self.target = source, target
        self.me = lax.axis_index(axis)
        count = z.C if axis == "col" else z.R
        col = lax.axis_index("col")
        row = lax.axis_index("row")
        self.copies = []
        for k in range(1, count):
            other = lax.rem(self.me + k, count)
            self.copies.append(
                pltpu.make_async_remote_copy(
                    src_ref=source(other),
                    dst_ref=target(self.me),
                    send_sem=sends.at[k],
                    recv_sem=receives.at[k],
                    device_id=(row, other) if axis == "col" else (other, col),
                    device_id_type=MESH,
                )
            )

    def start(self):
        for copy in self.copies:
            copy.start()

    def keep_own(self):
        self.target(self.me)[...] = self.source(self.me)[...]

    def arrive(self):
        for copy in self.copies:
            copy.wait_recv()

    def sent(self):
        for copy in self.copies:
            copy.wait_send()


def split_of(rows, lanes, parts):
    for by_rows in range(parts, 0, -1):
        if parts % by_rows == 0:
            by_lanes = parts // by_rows
            if rows % (16 * by_rows) == 0 and lanes % (128 * by_lanes) == 0:
                return by_rows, by_lanes
    raise ValueError("no split")


def reduce_plan(z, lanes, steps):
    rows = z.dim
    plan = []
    for step in steps:
        members = {"core": 2, "x": 2, "row": z.R, "slab": 4 * z.R}.get(step, z.C // 4)
        a, b = (1, 1) if step == "far_all" else split_of(rows, lanes, members)
        rows, lanes = rows // a, lanes // b
        plan.append((members, step, a, b, rows, lanes))
    return plan


def reduce_width(z, lanes, steps):
    while True:
        try:
            reduce_plan(z, lanes, steps)
            return lanes
        except ValueError:
            lanes += 128


def place_of(step):
    col = lax.axis_index("col")
    row = lax.axis_index("row")
    if step == "row":
        return row
    if step == "slab":
        return row * 4 + lax.rem(col, 4)
    if step in ("far", "far_all"):
        return col // 4
    return lax.rem(col // {"core": 1, "x": 2}[step], 2)


def peer_of(step, members, k):
    col = lax.axis_index("col")
    row = lax.axis_index("row")
    me = place_of(step)
    at = lax.rem(me + k, members)
    if step == "row":
        return at, (at, col)
    if step == "slab":
        return at, (at // 4, col - lax.rem(col, 4) + lax.rem(at, 4))
    return at, (row, col + (at - me) * {"core": 1, "x": 2, "far": 4, "far_all": 4}[step])


class SmallSum:
    def __init__(self, plan, value, slots, sends, receives):
        self.plan, self.value, self.slots = plan, value, slots
        self.sends, self.receives = sends, receives

    def start(self, stage):
        members, step = self.plan[stage][:2]
        me = place_of(step)
        self.copies = []
        for k in range(1, members):
            self.copies.append(
                pltpu.make_async_remote_copy(
                    src_ref=self.value,
                    dst_ref=self.slots[stage].at[me],
                    send_sem=self.sends.at[stage, k],
                    recv_sem=self.receives.at[stage, k],
                    device_id=peer_of(step, members, k)[1],
                    device_id_type=MESH,
                )
            )
        for copy in self.copies:
            copy.start()
        self.slots[stage][me] = self.value[...]

    def end(self, stage, out):
        for copy in self.copies:
            copy.wait()
        total = self.slots[stage][0]
        for k in range(1, self.plan[stage][0]):
            total = total + self.slots[stage][k]
        out[...] = total
        self.value = out


class Reduction:
    def __init__(self, z, plan, refs, small=None):
        n = len(plan)
        self.z, self.plan, self.n = z, plan, n
        self.full, refs = refs[0], refs[1:]
        self.recvs, refs = refs[:n], refs[n:]
        self.held, refs = refs[:n], refs[n:]
        self.gathers, refs = refs[:n], refs[n:]
        self.ssem, self.rsem, self.gsem, self.hsem = refs[:4]
        self.small = small
        if small is not None:
            self.smalls = refs[4 : 4 + n]
            self.vsem, self.wsem = refs[4 + n :]
        self.current = self.full
        self.copies = None

    @staticmethod
    def scratch(z, plan, lanes, small_shape=None):
        dma = pltpu.SemaphoreType.DMA
        most = max(step[0] for step in plan)
        shapes = [pltpu.VMEM((z.dim, lanes), BF16)]
        shapes += [pltpu.VMEM((step[0], step[4], step[5]), BF16) for step in plan]
        shapes += [pltpu.VMEM((step[4], step[5]), BF16) for step in plan]
        shapes += [pltpu.VMEM((z.dim, lanes), BF16)]
        shapes += [pltpu.VMEM((step[4], step[5]), BF16) for step in plan[:-1]]
        shapes += [dma((len(plan), most)) for _ in range(4)]
        if small_shape is not None:
            shapes += [pltpu.VMEM((step[0],) + small_shape, F32) for step in plan]
            shapes += [dma((len(plan), most)) for _ in range(2)]
        return shapes

    def place(self, stage):
        return place_of(self.plan[stage][1])

    def peer(self, stage, k):
        members, step = self.plan[stage][:2]
        return peer_of(step, members, k)

    def window(self, ref, stage, index):
        members, step, a, b, rows, width = self.plan[stage]
        if a * b == 1:
            return ref
        r0 = pl.multiple_of((index // b) * rows, 16)
        l0 = pl.multiple_of(lax.rem(index, b) * width, 128)
        return ref.at[pl.ds(r0, rows), pl.ds(l0, width)]

    def fill(self, pieces):
        D = self.z.dim
        at = 0
        for ref in pieces:
            for k in range(ref.shape[0] // D):
                width = ref.shape[1]
                self.full[:, at : at + width] = ref[k * D : (k + 1) * D, :].astype(BF16)
                at += width
        if at < self.full.shape[1]:
            self.full[:, at:] = jnp.zeros((D, self.full.shape[1] - at), BF16)

    def scatter_start(self, stage):
        me = self.place(stage)
        self.copies = []
        for k in range(1, self.plan[stage][0]):
            index, device = self.peer(stage, k)
            self.copies.append(
                pltpu.make_async_remote_copy(
                    src_ref=self.window(self.current, stage, index),
                    dst_ref=self.recvs[stage].at[me],
                    send_sem=self.ssem.at[stage, k],
                    recv_sem=self.rsem.at[stage, k],
                    device_id=device,
                    device_id_type=MESH,
                )
            )
            if self.small is not None:
                self.copies.append(
                    pltpu.make_async_remote_copy(
                        src_ref=self.small,
                        dst_ref=self.smalls[stage].at[me],
                        send_sem=self.vsem.at[stage, k],
                        recv_sem=self.wsem.at[stage, k],
                        device_id=device,
                        device_id_type=MESH,
                    )
                )
        for copy in self.copies:
            copy.start()
        self.recvs[stage][me] = self.window(self.current, stage, me)[...]
        if self.small is not None:
            self.smalls[stage][me] = self.small[...]

    def scatter_end(self, stage, small_out=None):
        for copy in self.copies:
            copy.wait()
        members = self.plan[stage][0]
        rows, width = self.plan[stage][4:]
        for at, size in key_tiles(width, 512):
            lanes = slice(at, at + size)
            total = self.recvs[stage][0, :, lanes].astype(F32)
            for k in range(1, members):
                total = total + self.recvs[stage][k, :, lanes].astype(F32)
            self.held[stage][:, lanes] = total.astype(BF16)
        self.current = self.held[stage]
        if self.small is not None:
            small = self.smalls[stage][0]
            for k in range(1, members):
                small = small + self.smalls[stage][k]
            if stage + 1 < self.n:
                self.smalls[stage][0] = small
                self.small = self.smalls[stage].at[0]
            else:
                small_out[...] = small

    def gather_start(self, stage):
        me = self.place(stage)
        self.copies = []
        for k in range(1, self.plan[stage][0]):
            index, device = self.peer(stage, k)
            self.copies.append(
                pltpu.make_async_remote_copy(
                    src_ref=self.current,
                    dst_ref=self.window(self.gathers[stage], stage, me),
                    send_sem=self.gsem.at[stage, k],
                    recv_sem=self.hsem.at[stage, k],
                    device_id=device,
                    device_id_type=MESH,
                )
            )
        for copy in self.copies:
            copy.start()
        self.window(self.gathers[stage], stage, me)[...] = self.current[...]

    def gather_end(self, stage):
        for copy in self.copies:
            copy.wait()
        self.current = self.gathers[stage]

    def steps(self, small_out=None):
        n = self.n
        ends = [functools.partial(self.scatter_end, s, small_out) for s in range(n)]
        back = [s for s in range(n - 1, -1, -1) if self.plan[s][1] != "far_all"]
        ends += [functools.partial(self.gather_end, s) for s in back]
        starts = [functools.partial(self.scatter_start, s) for s in range(n)]
        starts += [functools.partial(self.gather_start, s) for s in back]
        return starts, ends


def spread(block, outs):
    D = block.shape[0]
    at = 0
    for ref in outs:
        for k in range(ref.shape[0] // D):
            width = ref.shape[1]
            ref[k * D : (k + 1) * D, :] = block[:, at : at + width].astype(F32)
            at += width


def reduce_kernel(z, plan, dqkv_ref, vec_ref, dwt_ref, dtt_ref, sum_ref, osmall, small, *refs):
    greet(z)
    small[:16, :HALF] = own_lanes_back(z, dwt_ref[...])
    small[:16, HALF:] = dtt_ref[...]
    small[16:, :] = vec_ref[...]
    work = Reduction(z, plan, refs, small)
    work.fill((dqkv_ref,))
    all_greeted(z)
    starts, ends = work.steps(osmall)
    for start, end in zip(starts, ends):
        start()
        end()
    sum_ref[...] = work.current[...]


def own_lanes_back(z, value):
    if z.G == 1:
        return value
    return jnp.where(lax.rem(lax.axis_index("col"), z.G) == 0, value, turn(value))


def reduce_last(z, dqkv, vec, dwt, dtt, collective_id):
    steps = ("slab", "far")
    lanes = reduce_width(z, dqkv.size // z.dim, steps)
    plan = reduce_plan(z, lanes, steps)
    vmem = pl.BlockSpec(memory_space=pltpu.VMEM)
    small = (24, z.dim)
    return pl.pallas_call(
        functools.partial(reduce_kernel, z, plan),
        out_shape=(
            jax.ShapeDtypeStruct((z.dim, lanes), BF16),
            jax.ShapeDtypeStruct(small, F32),
        ),
        in_specs=[vmem] * 4,
        out_specs=(vmem,) * 2,
        scratch_shapes=[pltpu.VMEM(small, F32)] + Reduction.scratch(z, plan, lanes, small),
        compiler_params=pltpu.CompilerParams(
            collective_id=collective_id, has_side_effects=True, vmem_limit_bytes=VMEM_LIMIT
        ),
        name="reduce_last",
    )(dqkv, vec, dwt, dtt)


def split_kernel(z, sum_ref, late_ref, early_ref, first_ref, dw_ref, dpw_ref, dw1_ref, dw2_ref, *outs):
    spread(sum_ref, (dw_ref,))
    spread(first_ref, (dpw_ref, dw1_ref, dw2_ref))
    n1g, n1s, qb, vb, taps, lb, pb, n2g, n2s, b1, b2 = outs
    taps[...] = late_ref[:9, :]
    for ref, row in ((n1g, 16), (n1s, 17), (qb, 18), (vb, 19)):
        ref[...] = late_ref[row : row + 1, :]
    for ref, row in ((n2g, 0), (n2s, 1), (pb, 2), (b2, 3), (lb, 4)):
        ref[...] = early_ref[row : row + 1, :]
    D = z.dim
    for k in range(b1.shape[1] // D):
        b1[:, k * D : (k + 1) * D] = early_ref[8 + k : 9 + k, :]


def front_kernel(
    z,
    heights_ref,
    widths_ref,
    x_ref,
    gain_ref,
    shift_ref,
    w_ref,
    qb_ref,
    vb_ref,
    tap_ref,
    tap_bias_ref,
    back_wide,
    back_tall,
    tq_out,
    tot_out,
    tlse_out,
    v_out,
    kcat_out,
    qtb_out,
    kt_out,
    ot_out,
    lse_out,
    tot_ref,
    tlse_ref,
    v_ref,
    kcat,
    qtb,
    kt,
    ot,
    lse,
    pw,
    pt,
    gw,
    gt,
    low,
    send_wide,
    send_tall,
    recv_wide,
    recv_tall,
    out_wide,
    out_tall,
    t_src,
    t_dst,
    t_q,
    t_k,
    t_v,
    t_vpad,
    t_osum,
    t_kstack,
    qk,
    vpad,
    stage,
    vt,
    vt_all,
    ss0,
    ss1,
    osum,
    lepe,
    wsend,
    wrecv,
    tsend,
    trecv,
    wsend1,
    wrecv1,
    tsend1,
    trecv1,
    local,
):
    greet(z)
    wlim_ref = wide_ends(z, heights_ref, widths_ref)
    tlim_ref = tall_ends(z, heights_ref, widths_ref)
    ttap_ref = tap_ref[:, HALF:]
    tbias_ref = tap_bias_ref[:, HALF:]
    wtap_ref = own_lanes(z, tap_ref[:, :HALF])
    wbias_ref = own_lanes(z, tap_bias_ref[:, :HALF])
    bias = jnp.concatenate([qb_ref[...], jnp.zeros_like(qb_ref), vb_ref[...]], -1)
    dense_in_wide(z, x_ref, gain_ref, shift_ref, w_ref, bias, send_wide, low, pw, gw)
    all_greeted(z)
    cut = up(z.pix, 16)
    parts = [(0, 0, cut), (0, cut, z.pair_rows)]
    parts += [(pair, 0, z.pair_rows) for pair in range(1, z.pairs)]
    wides = [
        Exchange(
            z,
            "col",
            lambda d, pair=pair, at=at, end=end: send_wide.at[d, pair, at:end],
            lambda d, pair=pair, at=at, end=end: recv_wide.at[d, pair, at:end],
            wsend.at[k],
            wrecv.at[k],
        )
        for k, (pair, at, end) in enumerate(parts)
    ]
    tall = Exchange(
        z, "row", lambda d: send_tall.at[d], lambda d: recv_tall.at[d], tsend, trecv
    )
    for wide in wides[:2]:
        wide.start()
    dense_in_tall(z, w_ref, bias, send_tall, low, pt, gt)
    tall.start()
    for wide in wides:
        wide.keep_own()
    tall.keep_own()
    for ref in (t_q, t_k, t_v, t_vpad, t_osum, vpad, qk):
        ref[...] = jnp.zeros_like(ref)
    groups = z.tall_slots // z.tall_group
    early = groups // 2
    half = z.tall_rows1 // 2
    col = lax.axis_index("col")
    row = lax.axis_index("row")
    jobs = []
    own = []

    def wide_back(pair):
        wide_pair_mixture(z, pair, ot, lepe, osum, out_wide)
        job = Exchange(
            z,
            "col",
            lambda d: out_wide.at[d, pair],
            lambda d: back_wide.at[d, pair],
            wsend1.at[pair],
            wrecv1.at[pair],
        )
        job.start()
        jobs.append(job)
        copy = pltpu.make_async_copy(
            out_wide.at[col, pair], back_wide.at[col, pair], local.at[pair]
        )
        copy.start()
        own.append(copy)

    def tall_part(k, start, stop):
        tall_forward(
            z, start, stop, tlim_ref, ttap_ref, tbias_ref, tot_ref, tlse_ref,
            t_src, t_dst, t_q, t_k, t_v, t_vpad, t_osum, t_kstack,
        )
        rows = pl.ds(k * half, half)
        out_tall[:, rows, :] = t_dst[:, rows, :].astype(BF16)
        job = Exchange(
            z,
            "row",
            lambda d: out_tall.at[d, rows],
            lambda d: back_tall.at[d, rows],
            tsend1.at[k],
            trecv1.at[k],
        )
        job.start()
        jobs.append(job)
        copy = pltpu.make_async_copy(
            out_tall.at[row, rows], back_tall.at[row, rows], local.at[2 + k]
        )
        copy.start()
        own.append(copy)

    def save(source, target):
        copy = pltpu.make_async_copy(source, target, local.at[4 + len(saves)])
        copy.start()
        saves.append(copy)

    saves = []
    for pair in range(z.pairs):
        if pair > 0:
            wides[pair + 1].arrive()
        wide_pair_prepare(
            z, pair, wlim_ref, recv_wide, kcat, qtb, kt, qk, vpad, stage, vt, vt_all,
            wides if pair == 0 else (),
        )
        save(kcat.at[pair], kcat_out.at[pair])
        save(qtb.at[pair], qtb_out.at[pair])
        save(kt.at[pair], kt_out.at[pair])
        if pair + 1 == z.pairs:
            v_ref[...] = vpad[PAD : PAD + z.wide_len, :].astype(BF16)
            save(v_ref, v_out)
            wide_lepe(z, wlim_ref, wtap_ref, wbias_ref, vpad, lepe)
            for done in range(pair):
                wide_back(done)
        wide_pair_attend(z, pair, wlim_ref, kcat, qtb, ot, lse, vt, vt_all, ss0, ss1)
        if pair == 0:
            tall.arrive()
            save(recv_tall, tq_out)
            t_src[...] = recv_tall[...].astype(F32)
            tall_part(0, 0, early)
    save(ot, ot_out)
    save(lse, lse_out)
    wide_back(z.pairs - 1)
    tall_part(1, early, groups)
    save(tot_ref, tot_out)
    save(tlse_ref, tlse_out)
    for copy in own + saves:
        copy.wait()
    for job in wides + [tall] + jobs:
        job.sent()
    for job in jobs:
        job.arrive()


def out_wide_planes(z, pair, got, wide, thirds):
    wide[...] = got[:, pair].astype(F32)

    def place(n, start, value):
        lo = low_lanes(value.shape)
        value = jnp.where(lo, value, 0.0) if pair == 0 else jnp.where(lo, 0.0, value)
        count = value.shape[1] * z.images
        value = jnp.swapaxes(value, 0, 1).reshape(count, HALF)
        thirds[n][start * z.images : start * z.images + count, :HALF] = value.astype(BF16)

    both = wide[:, : z.pix, :]
    folded = wide[:, z.pix : z.pix + z.fold, :]
    place(0, 0, both if pair == 0 else turn(both))
    place(1, 0, turn(both) if pair == 0 else both)
    place(2, 0, folded if pair == 0 else turn(folded))
    place(2, z.fold, turn(folded) if pair == 0 else folded)


def out_tall_planes(z, got, tall, thirds):
    tall[...] = got[...].astype(F32)
    count = z.tall_own * z.images
    for n in range(3):
        for s in range(z.stripes):
            blocks = []
            for b in range(z.images):
                at = (((b % z.tall_images) * z.stripes + s) * 3 + n) * z.tall_pad
                blocks.append(tall[b // z.tall_images, at : at + z.tall_own, :])
            value = jnp.swapaxes(jnp.stack(blocks), 0, 1).reshape(count, HALF)
            thirds[n][s * count : (s + 1) * count, HALF:] = value.astype(BF16)


def wide_rows_of(z, third, i):
    rows = []
    for j in range(z.cols):
        at = pl.multiple_of((j * z.rows + i) * z.images, z.images)
        rows.append(third[pl.ds(at, z.images), :HALF])
    return jnp.concatenate(rows, 0)


def tall_rows_of(z, third, i):
    rows = []
    for j in range(z.cols):
        s, jj = divmod(j, SW)
        at = pl.multiple_of(((s * z.rows + i) * SW + jj) * z.images, z.images)
        rows.append(third[pl.ds(at, z.images), HALF:])
    return jnp.concatenate(rows, 0)


def own_rows(z, i):
    T = z.cols * z.images
    return pl.ds(pl.multiple_of(i * T, 16), T)


def out_first(z, x_ref, gain_ref, shift_ref, w_ref, thirds, low, dw, gn, vec):
    T = z.cols * z.images
    D = z.dim
    dw[...] = jnp.zeros_like(dw)
    vec[...] = jnp.zeros_like(vec)

    def one_row(i, carry):
        normed, _ = norm_parts(x_ref[i].astype(F32).reshape(T, D))
        low_i = (normed * gain_ref[...] + shift_ref[...]).astype(BF16)
        low[own_rows(z, i), :] = low_i
        parts = []
        for third in thirds:
            parts += [wide_rows_of(z, third, i), tall_rows_of(z, third, i)]
        gproj = jnp.concatenate(parts, -1)
        vec[2:3, :] += jnp.sum(gproj[:, :D].astype(F32), 0, keepdims=True)
        vec[3:4, :] += jnp.sum(gproj[:, 2 * D :].astype(F32), 0, keepdims=True)
        dw[...] += mm_tn(low_i, gproj)
        gn[own_rows(z, i), :] = mm_nt(gproj, w_ref[...])
        return carry

    lax.fori_loop(0, z.rows, one_row, 0)


def out_second(z, thirds, low, dw, vec):
    D = z.dim

    def one_row(i, carry):
        gproj = jnp.concatenate([wide_rows_of(z, third, i) for third in thirds], -1)
        vec[2:3, :HALF] += jnp.sum(gproj[:, :HALF].astype(F32), 0, keepdims=True)
        vec[3:4, :HALF] += jnp.sum(gproj[:, 2 * HALF :].astype(F32), 0, keepdims=True)
        part = mm_tn(low[own_rows(z, i), :], gproj)
        for n in range(3):
            dw[:, n * D : n * D + HALF] += part[:, n * HALF : (n + 1) * HALF]
        return carry

    lax.fori_loop(0, z.rows, one_row, 0)


def out_third(z, x_ref, gain_ref, w_ref, thirds, gn, gres, gin_ref, vec):
    T = z.cols * z.images
    D = z.dim

    def one_row(i, carry):
        rows = own_rows(z, i)
        gproj = jnp.concatenate([wide_rows_of(z, third, i) for third in thirds], -1)
        weight = jnp.concatenate([w_ref[:, n * D : n * D + HALF] for n in range(3)], -1)
        gnorm = gn[rows, :] + mm_nt(gproj, weight)
        n1, r1 = norm_parts(x_ref[i].astype(F32).reshape(T, D))
        vec[0:1, :] += jnp.sum(gnorm * n1, 0, keepdims=True)
        vec[1:2, :] += jnp.sum(gnorm, 0, keepdims=True)
        g = gnorm * gain_ref[...]
        gin = gres[rows, :] + r1 * (
            g - jnp.mean(g, -1, keepdims=True) - n1 * jnp.mean(g * n1, -1, keepdims=True)
        )
        gin_ref[i] = gin.reshape(z.cols, z.images, D)
        return carry

    lax.fori_loop(0, z.rows, one_row, 0)


BACK_LOADS = ("dpw", "dw1", "dw2", "tq", "tot", "tlse", "v", "kcat", "qtb", "kt", "ot", "lse")


def back_names(z):
    names = ["heights", "widths", "gw", "gt", "tap", "vec"]
    names += [name + "_any" for name in BACK_LOADS]
    if z.merged:
        names += ["gain", "shift", "x_any", "w_any", "gres_any", "gin", "late", "late_small"]
    else:
        names += ["got_wide", "got_tall", "dwt", "dtt"]
    names += ["sums", "smalls", *BACK_LOADS]
    names += ["recv_wide", "recv_tall", "send_wide", "send_tall", "t_src", "t_gsrc"]
    names += ["t_q", "t_k", "t_v", "t_gpad", "t_vpad", "t_stage", "t_kstack"]
    names += ["gpad", "vpad", "dotb", "delta", "dvl", "dqt", "dkt", "dvt", "stage"]
    names += ["ss0", "ss1", "dp0", "dp1", "ps0", "ps1", "ds0", "ds1"]
    names += ["wsend", "wrecv", "tsend", "trecv", "wsend1", "wrecv1", "tsend1", "trecv1", "local"]
    if z.merged:
        names += ["got_wide", "got_tall", "dwt", "dtt", "wide_block", "dw", "last_vec", "small", "x", "w"]
    return names


def back_kernel(z, plan, late_plan, *refs):
    names = back_names(z)
    r = types.SimpleNamespace(**dict(zip(names, refs)))
    refs = refs[len(names) :]
    size = len(Reduction.scratch(z, plan, z.dim, (8, z.dim)))
    early_refs, late_refs = refs[:size], refs[size:]
    greet(z)
    loads = {}
    for i, name in enumerate(BACK_LOADS + (("x", "w") if z.merged else ())):
        loads[name] = pltpu.make_async_copy(
            getattr(r, name + "_any"), getattr(r, name), r.local.at[5 + i]
        )
        loads[name].start()
    wlim = wide_ends(z, r.heights, r.widths)
    tlim = tall_ends(z, r.heights, r.widths)
    tall_taps = r.tap[:, HALF:]
    wide_taps = own_lanes(z, r.tap[:, :HALF])
    work = Reduction(z, plan, early_refs, r.vec)
    starts, ends = work.steps(r.smalls)
    all_greeted(z)
    tall = Exchange(z, "row", lambda d: r.gt.at[d], lambda d: r.recv_tall.at[d], r.tsend, r.trecv)
    wide = Exchange(z, "col", lambda d: r.gw.at[d], lambda d: r.recv_wide.at[d], r.wsend, r.wrecv)
    tall.start()
    wide.start()
    for name in ("dpw", "dw1", "dw2"):
        loads[name].wait()
    work.fill((r.dpw, r.dw1, r.dw2))
    starts[0]()
    tall.keep_own()
    wide.keep_own()
    for ref in (r.t_q, r.t_k, r.t_v, r.t_gpad, r.t_vpad, r.t_stage):
        ref[...] = jnp.zeros_like(ref)
    r.dtt[...] = jnp.zeros_like(r.dtt)
    loads["tq"].wait()
    r.t_src[...] = r.tq[...].astype(F32)
    loads["tot"].wait()
    loads["tlse"].wait()
    groups = z.tall_slots // z.tall_group
    early = groups // 2
    half = z.tall_rows3 // 2
    col = lax.axis_index("col")
    row = lax.axis_index("row")
    outs = []
    own = []

    def keep(source, target, k):
        copy = pltpu.make_async_copy(source, target, r.local.at[k])
        copy.start()
        own.append(copy)

    def tall_part(k, start, stop):
        tall_backward(
            z, start, stop, tlim, tall_taps, r.tot, r.tlse, r.dtt, r.t_src, r.t_gsrc, r.t_src,
            r.t_q, r.t_k, r.t_v, r.t_gpad, r.t_vpad, r.t_stage, r.t_kstack,
        )
        rows = pl.ds(k * half, half)
        r.send_tall[:, rows, :] = r.t_src[:, rows, :].astype(BF16)
        job = Exchange(
            z,
            "row",
            lambda d: r.send_tall.at[d, rows],
            lambda d: r.got_tall.at[d, rows],
            r.tsend1.at[k],
            r.trecv1.at[k],
        )
        job.start()
        keep(r.send_tall.at[row, rows], r.got_tall.at[row, rows], 2 + k)
        return job

    done = [0]

    def point():
        if done[0] < len(ends) - 1:
            ends[done[0]]()
            starts[done[0] + 1]()
            done[0] += 1

    tall.arrive()
    r.t_gsrc[...] = r.recv_tall[...].astype(F32)
    outs.append(tall_part(0, 0, early))
    point()
    for name in BACK_LOADS[6:]:
        loads[name].wait()
    wide.arrive()
    wide_backward_start(
        z, wlim, r.recv_wide, wide_taps, r.v, r.ot, r.dwt, r.gpad, r.vpad, r.dotb, r.delta, r.dvl,
        r.stage,
    )
    point()
    slots = ((r.ss0, r.dp0, r.ps0, r.ds0), (r.ss1, r.dp1, r.ps1, r.ds1))
    for pair in range(z.pairs):
        wide_pair_backward(
            z, pair, wlim, r.v, r.kcat, r.qtb, r.kt, r.lse, r.dotb, r.delta, r.dvl, r.dqt, r.dkt,
            r.dvt, r.gpad, r.vpad, r.stage, slots, r.send_wide, point, 3 if pair == 0 else 2,
        )
        job = Exchange(
            z,
            "col",
            lambda d, pair=pair: r.send_wide.at[d, pair],
            lambda d, pair=pair: r.got_wide.at[d, pair],
            r.wsend1.at[pair],
            r.wrecv1.at[pair],
        )
        point()
        job.start()
        keep(r.send_wide.at[col, pair], r.got_wide.at[col, pair], pair)
        outs.append(job)
        if pair == 0:
            outs.append(tall_part(1, early, groups))
    while done[0] < len(ends) - 1:
        point()
    if not z.merged:
        ends[-1]()
        r.sums[...] = work.current[...]
        for copy in own:
            copy.wait()
        tall.sent()
        wide.sent()
        for job in outs:
            job.sent()
            job.arrive()
        return
    loads["x"].wait()
    loads["w"].wait()
    back_finish(z, r, late_plan, late_refs, work, ends, outs, own)
    tall.sent()
    wide.sent()
    for job in outs:
        job.sent()


def back_finish(z, r, late_plan, refs, work, ends, outs, own):
    size = len(Reduction.scratch(z, late_plan, z.dim))
    late = Reduction(z, late_plan, refs[:size])
    slots, (sends, receives) = refs[size : size + len(late_plan)], refs[size + len(late_plan) :]
    starts, late_ends = late.steps()
    low, gn, gres, thirds = r.ps0, r.ss0, r.ss1, (r.ps1, r.ds0, r.ds1)
    load = pltpu.make_async_copy(r.gres_any, gres, r.local.at[4])
    load.start()
    for copy in own:
        copy.wait()
    for job in outs[:-1]:
        job.arrive()
    out_wide_planes(z, 0, r.got_wide, r.wide_block, thirds)
    out_tall_planes(z, r.got_tall, r.t_src, thirds)
    out_first(z, r.x, r.gain, r.shift, r.w, thirds, low, r.dw, gn, r.last_vec)
    ends[-1]()
    r.sums[...] = work.current[...]
    outs[-1].arrive()
    out_wide_planes(z, 1, r.got_wide, r.wide_block, thirds)
    out_second(z, thirds, low, r.dw, r.last_vec)
    late.fill((r.dw,))
    starts[0]()
    load.wait()
    out_third(z, r.x, r.gain, r.w, thirds, gn, gres, r.gin, r.last_vec)
    r.small[:16, :HALF] = r.dwt[...]
    r.small[:16, HALF:] = r.dtt[...]
    r.small[16:, :] = r.last_vec[...]
    small = SmallSum(late_plan, r.small, slots, sends, receives)
    small.start(0)
    late_ends[0]()
    starts[1]()
    small.end(0, r.small)
    small.start(1)
    late_ends[1]()
    starts[2]()
    small.end(1, r.late_small)
    late_ends[2]()
    r.late[...] = late.current[...]


def local_call(kernel, z, name, outs, scratch, scalars, arrays):
    vmem = pl.BlockSpec(memory_space=pltpu.VMEM)
    smem = pl.BlockSpec(memory_space=pltpu.SMEM)
    return pl.pallas_call(
        functools.partial(kernel, z),
        out_shape=tuple(jax.ShapeDtypeStruct(shape, kind) for shape, kind in outs),
        in_specs=[smem] * len(scalars) + [vmem] * len(arrays),
        out_specs=(vmem,) * len(outs),
        scratch_shapes=[pltpu.VMEM(shape, kind) for shape, kind in scratch],
        compiler_params=pltpu.CompilerParams(vmem_limit_bytes=VMEM_LIMIT),
        name=name,
    )(*scalars, *arrays)


def per_device(
    mesh,
    features,
    heights,
    widths,
    norm1_gain,
    norm1_shift,
    qkv_weight,
    query_bias,
    value_bias,
    lepe_weight,
    lepe_bias,
    proj_weight,
    proj_bias,
    norm2_gain,
    norm2_shift,
    fc1_weight,
    fc1_bias,
    fc2_weight,
    fc2_bias,
    cotangent,
):
    z = Sizes(mesh, features.shape)
    B, D, TC, TR = z.images, z.dim, z.cols, z.rows
    x = features.transpose(1, 2, 0, 3)
    ct = cotangent.transpose(1, 2, 0, 3)
    line = lambda v: v.reshape(1, -1)
    FF = fc1_weight.shape[1]
    wide3 = (z.C, z.pairs, z.pair_rows, HALF)
    wide1 = (z.C, z.wide_rows1, z.hc)
    fold1 = (z.C, z.pairs, z.fold_rows, HALF)
    tall3 = (z.R, z.tall_rows3, HALF)
    tall1 = (z.R, z.tall_rows1, HALF)
    flat = up(z.tokens, 16 * B) + 16 * B
    L = z.wide_len
    LT = up(z.tall_len, 128)
    per_head, tail, blocks, tail_lanes, span = wide_plan(z)
    vmem = pl.BlockSpec(memory_space=pltpu.VMEM)
    smem = pl.BlockSpec(memory_space=pltpu.SMEM)
    anywhere = pl.BlockSpec(memory_space=pl.ANY)
    dma = pltpu.SemaphoreType.DMA
    saved = [
        ((L, HALF), BF16),
        ((z.pairs, L, 2 * HALF), BF16),
        ((z.pairs, 2 * HALF, span), BF16),
        ((z.pairs, HALF // 2, L), BF16),
        ((HALF, per_head * z.qb + z.pairs * tail_lanes), F32),
        ((8, z.pairs * span), F32),
    ]
    tall_scratch = [
        ((z.tall_group, LT, HALF), F32),
        ((z.tall_group, LT, HALF), F32),
        ((z.tall_group, LT, HALF), F32),
        ((z.tall_group, LT + 16, HALF), F32),
        ((z.tall_group, LT + 16, HALF), F32),
        ((z.tall_group, BRANCH_HEADS * LT, 2 * HALF), BF16),
    ]
    sems = [
        dma((z.pairs + 1, z.C)),
        dma((z.pairs + 1, z.C)),
        dma((z.R,)),
        dma((z.R,)),
        dma((z.pairs, z.C)),
        dma((z.pairs, z.C)),
        dma((2, z.R)),
        dma((2, z.R)),
        dma((z.C,)),
        dma((z.C,)),
    ]
    shapes = lambda items: tuple(jax.ShapeDtypeStruct(s, k) for s, k in items)
    scratches = lambda items: [pltpu.VMEM(s, k) for s, k in items]

    back_wide, back_tall, tall_qkv, tall_ot, tall_lse, *wide_saved = pl.pallas_call(
        functools.partial(front_kernel, z),
        out_shape=shapes(
            [
                (fold1, BF16),
                (tall1, BF16),
                (tall3, BF16),
                ((z.tall_slots, HALF, LT), F32),
                ((z.tall_slots, 8, LT), F32),
            ]
            + saved
        ),
        in_specs=[smem] * 2 + [vmem] * 8,
        out_specs=(anywhere,) * (5 + len(saved)),
        scratch_shapes=scratches(
            [((z.tall_slots, HALF, LT), F32), ((z.tall_slots, 8, LT), F32)]
            + saved
            + [
                ((3, flat, HALF), F32),
                ((3, flat, HALF), F32),
                (wide3, F32),
                (tall3, F32),
                ((TR, TC * B, D), BF16),
                (wide3, BF16),
                (tall3, BF16),
                (wide3, BF16),
                (tall3, BF16),
                (fold1, BF16),
                (tall1, BF16),
                (tall3, F32),
                (tall1, F32),
            ]
            + tall_scratch
            + [
                ((L, HALF), F32),
                ((L + 2 * PAD, HALF), F32),
                ((z.pair_rows, HALF), F32),
                ((2, HEAD_DIM + 16, L), BF16),
                ((HALF + 16, L), BF16),
                ((L, z.qb), F32),
                ((L, z.qb), F32),
                ((L + z.fold_rows, HALF), F32),
                ((L, HALF), F32),
            ]
        )
        + sems[:8]
        + [dma((18,))],
        compiler_params=pltpu.CompilerParams(
            collective_id=0, has_side_effects=True, vmem_limit_bytes=VMEM_LIMIT
        ),
        name="front",
    )(
        heights,
        widths,
        x,
        line(norm1_gain),
        line(norm1_shift),
        qkv_weight,
        line(query_bias),
        line(value_bias),
        lepe_weight,
        line(lepe_bias),
    )

    vec_rows = 8 + up(FF // D, 8)
    y, gres, gmix_wide, gmix_tall, dproj, dfc1, dfc2, vec_mid = local_call(
        dense_mid_kernel,
        z,
        "dense_mid",
        [
            ((TR, TC, B, D), BF16),
            ((TR, TC, B, D), F32),
            (wide1, BF16),
            (tall1, BF16),
            ((D, D), F32),
            ((D, FF), F32),
            ((FF, D), F32),
            ((vec_rows, D), F32),
        ],
        [((z.tokens, HALF), BF16)] * 2
        + [((z.tokens, HALF), F32)] * 2
        + [((B, z.wide_rows1, HALF), F32), (tall1, F32)]
        + [((z.tokens, D), F32)] * 2
        + [((z.tokens, HALF), F32)]
        + [((z.tokens, D), BF16)] * 3
        + [((TC * B, FF), F32)] * 4
        + [((TC * B, FF), BF16)] * 4,
        [heights, widths],
        [
            back_wide,
            back_tall,
            x,
            ct,
            proj_weight,
            line(proj_bias),
            line(norm2_gain),
            line(norm2_shift),
            fc1_weight,
            line(fc1_bias),
            fc2_weight,
            line(fc2_bias),
        ],
    )
    steps = ("core", "x", "row", "far")
    lanes = reduce_width(z, (dproj.size + dfc1.size + dfc2.size) // D, steps)
    plan = reduce_plan(z, lanes, steps)
    small = (24, D)
    late_steps = ("slab", "far_all")
    late_lanes = reduce_width(z, 3 * D, late_steps)
    late_plan = reduce_plan(z, late_lanes, late_steps)
    most = max(step[0] for step in late_plan)
    taps16 = ((16, HALF), F32)
    sums = [((D, lanes), BF16), ((vec_rows, D), F32)]
    arguments = [heights, widths, gmix_wide, gmix_tall, lepe_weight, vec_mid]
    arguments += [dproj, dfc1, dfc2, tall_qkv, tall_ot, tall_lse, *wide_saved]
    in_specs = [smem] * 2 + [vmem] * 4 + [anywhere] * (6 + len(saved))
    more = []
    late_scratch = []
    if z.merged:
        arguments += [line(norm1_gain), line(norm1_shift), x, qkv_weight, gres.reshape(-1, D)]
        in_specs += [vmem] * 2 + [anywhere] * 3
        outs = [((TR, TC, B, D), F32), ((D, late_lanes), BF16), (small, F32)] + sums
        out_specs = (vmem,) * 5
        more = [(wide3, BF16), (tall3, BF16), taps16, taps16, ((z.C, z.pair_rows, HALF), F32)]
        more += [((D, 3 * D), F32), ((8, D), F32), (small, F32)]
        more += [((TR, TC, B, D), BF16), ((D, 3 * D), BF16)]
        late_scratch = Reduction.scratch(z, late_plan, late_lanes)
        late_scratch += scratches([((step[0],) + small, F32) for step in late_plan])
        late_scratch += [dma((len(late_plan), most))] * 2
    else:
        outs = [(wide3, BF16), (tall3, BF16), taps16, taps16] + sums
        out_specs = (anywhere, anywhere) + (vmem,) * 4
    results = pl.pallas_call(
        functools.partial(back_kernel, z, plan, late_plan),
        out_shape=shapes(outs),
        in_specs=in_specs,
        out_specs=out_specs,
        scratch_shapes=scratches(
            [(dproj.shape, F32), (dfc1.shape, F32), (dfc2.shape, F32), (tall3, BF16)]
            + [((z.tall_slots, HALF, LT), F32), ((z.tall_slots, 8, LT), F32)]
            + saved
            + [
                (wide1, BF16),
                (tall1, BF16),
                (wide3, BF16),
                (tall3, BF16),
                (tall3, F32),
                (tall1, F32),
            ]
            + tall_scratch[:5]
            + [((z.tall_group, 3, LT + 16, HALF), F32), tall_scratch[5]]
            + [
                ((L + 2 * PAD, HALF), F32),
                ((L + 2 * PAD, HALF), F32),
                ((HALF, z.pairs * span), BF16),
                ((8, z.pairs * span), F32),
                ((L, HALF), F32),
                ((HALF // 2, per_head * z.qb), F32),
                ((HALF // 2, L), F32),
                ((HALF // 2, L), F32),
                ((z.pair_rows, HALF), F32),
            ]
            + [((L, z.qb), F32)] * 4
            + [((L, z.qb), BF16)] * 4
        )
        + [sems[8], sems[9], sems[2], sems[3], sems[0], sems[1], sems[6], sems[7]]
        + [dma((19,))]
        + scratches(more)
        + Reduction.scratch(z, plan, lanes, (vec_rows, D))
        + late_scratch,
        compiler_params=pltpu.CompilerParams(
            collective_id=1, has_side_effects=True, vmem_limit_bytes=VMEM_LIMIT
        ),
        name="back",
    )(*arguments)
    if z.merged:
        grad_in, late, vec_late, early, vec_mid = results
    else:
        got_wide, got_tall, dwide_taps, dtall_taps, early, vec_mid = results
        grad_in, dqkv, vec_out = local_call(
            dense_out_kernel,
            z,
            "dense_out",
            [((TR, TC, B, D), F32), ((D, 3 * D), F32), ((8, D), F32)],
            [((3, flat, HALF), F32), ((3, flat, HALF), F32), (wide3, F32), (tall3, F32)],
            [],
            [got_wide, got_tall, x, gres, line(norm1_gain), line(norm1_shift), qkv_weight],
        )
        late, vec_late = reduce_last(z, dqkv, vec_out, dwide_taps, dtall_taps, 2)
    dqkv, dproj, dfc1, dfc2, n1g, n1s, qb, vb, taps, lb, pb, n2g, n2s, b1, b2 = local_call(
        split_kernel,
        z,
        "split",
        [((D, 3 * D), F32), (dproj.shape, F32), (dfc1.shape, F32), (dfc2.shape, F32)]
        + [((1, D), F32)] * 4
        + [((9, D), F32)]
        + [((1, D), F32)] * 4
        + [((1, FF), F32), ((1, D), F32)],
        [],
        [],
        [late, vec_late, vec_mid, early],
    )
    flat_of = lambda v: v.reshape(-1)
    return (
        y.transpose(2, 0, 1, 3),
        grad_in.transpose(2, 0, 1, 3),
        flat_of(n1g),
        flat_of(n1s),
        dqkv,
        flat_of(qb),
        flat_of(vb),
        taps,
        flat_of(lb),
        dproj,
        flat_of(pb),
        flat_of(n2g),
        flat_of(n2s),
        dfc1,
        flat_of(b1),
        dfc2,
        flat_of(b2),
    )


def solution(mesh):
    image = P(None, "row", "col", None)
    return jax.shard_map(
        functools.partial(per_device, mesh),
        mesh=mesh,
        in_specs=(image,) + (P(),) * 17 + (image,),
        out_specs=(image, image) + (P(),) * 15,
        check_vma=False,
    )
```

```python
import functools
import math
import types

import jax
import jax.numpy as jnp
from jax import lax
from jax.experimental import pallas as pl
from jax.experimental.pallas import tpu as pltpu
from jax.sharding import PartitionSpec as P

HEADS = 8
SW = 7
BRANCH_HEADS = HEADS // 2
HALF = 128
HEAD_DIM = 32
NORM_EPSILON = 1e-05
MASKED = -1e30
LOG2E = math.log2(math.e)
PAD = 8
VMEM_LIMIT = 62 * 1024 * 1024
MESH = pl.DeviceIdType.MESH
F32 = jnp.float32
BF16 = jnp.bfloat16
NT = (((1,), (1,)), ((), ()))
TN = (((0,), (0,)), ((), ()))


def up(value, unit):
    return -(-value // unit) * unit


def mm(a, b):
    return jnp.dot(a, b, preferred_element_type=F32)


def mm_nt(a, b):
    return lax.dot_general(a, b, NT, preferred_element_type=F32)


def mm_tn(a, b):
    return lax.dot_general(a, b, TN, preferred_element_type=F32)


class Sizes:
    def __init__(self, mesh, shape):
        self.images, self.rows, self.cols, self.dim = shape
        self.R = mesh.shape["row"]
        self.C = mesh.shape["col"]
        self.pix = self.rows * self.cols
        self.tokens = self.pix * self.images
        self.stripes = self.cols // SW
        self.G = self.C // self.images
        self.wide_heads = BRANCH_HEADS // self.G
        self.hc = HALF // self.G
        self.tall_images = self.images // self.R
        self.wide_len = self.C * self.pix
        self.qb = 256 if self.wide_len <= 2048 else 128
        self.merged = self.G == 1 and self.wide_len <= 2048
        self.tall_own = self.rows * SW
        self.tall_len = self.R * self.tall_own
        self.tall_pad = up(self.tall_own, 8)
        self.pairs = self.wide_heads // 2
        self.fold = self.pix // 2
        self.pair_rows = up(self.pix + self.fold, 16)
        self.fold_rows = up(self.fold, 16)
        self.wide_rows1 = up(self.pix, 16)
        self.tall_slots = self.tall_images * self.stripes
        self.tall_group = 4 if self.tall_len <= 128 else 1
        heads = list(range(BRANCH_HEADS))
        self.tall_head_sets = [heads] if self.tall_group > 1 else [[h] for h in heads]
        self.tall_rows1 = self.tall_slots * self.tall_pad
        self.tall_rows3 = 3 * self.tall_rows1


def norm_parts(values):
    average = jnp.mean(values, -1, keepdims=True)
    centred = values - average
    spread = jnp.mean(centred * centred, -1, keepdims=True)
    inverse = lax.rsqrt(spread + NORM_EPSILON)
    return centred * inverse, inverse


def low_lanes(shape):
    return lax.broadcasted_iota(jnp.int32, shape, len(shape) - 1) < HALF // 2


def low_half(rows):
    return lax.broadcasted_iota(jnp.int32, (rows, HALF), 1) < HALF // 2


def turn(value):
    return jnp.concatenate([value[..., HALF // 2 :], value[..., : HALF // 2]], -1)


def dense_in_wide(z, x_ref, gain_ref, shift_ref, w_ref, bias, sw_ref, low_ref, pw, gw):
    B, D, TC, TR = z.images, z.dim, z.cols, z.rows

    def one_row(i, carry):
        x = x_ref[i].astype(F32).reshape(TC * B, D)
        normed, _ = norm_parts(x)
        low = (normed * gain_ref[...] + shift_ref[...]).astype(BF16)
        low_ref[i] = low
        proj = branch_projection(z, low, w_ref, bias, 0)
        for j in range(TC):
            at = pl.multiple_of((j * TR + i) * B, B)
            for n in range(3):
                pw[n, pl.ds(at, B), :] = proj[j, :, n * HALF : (n + 1) * HALF]
        return carry

    lax.fori_loop(0, TR, one_row, 0)
    rows = up(z.pix, 8)
    half = up(z.fold, 8)
    lo = low_half(rows)
    lo_half = low_half(half)
    gw[:, :, z.pix + z.fold :, :] = jnp.zeros_like(gw[:, :, z.pix + z.fold :, :])
    for b in range(B):
        q = pw[0, pl.ds(b, rows, stride=B), :]
        k = pw[1, pl.ds(b, rows, stride=B), :]
        v1 = pw[2, pl.ds(b, half, stride=B), :]
        v2 = pw[2, pl.ds(z.fold * B + b, half, stride=B), :]
        qk = (jnp.where(lo, q, turn(k)), jnp.where(lo, turn(q), k))
        vv = (jnp.where(lo_half, v1, turn(v2)), jnp.where(lo_half, turn(v1), v2))
        for u in range(2):
            d = b * z.G + u // z.pairs
            gw[d, u % z.pairs, :rows, :] = qk[u]
            gw[d, u % z.pairs, z.pix : z.pix + z.fold, :] = vv[u][: z.fold]
    for pair in range(z.pairs):
        sw_ref[:, pair] = gw[:, pair].astype(BF16)


def branch_projection(z, low, w_ref, bias, first):
    D = z.dim
    lanes = [slice(n * D + first, n * D + first + HALF) for n in range(3)]
    weight = jnp.concatenate([w_ref[:, own] for own in lanes], -1)
    own_bias = jnp.concatenate([bias[:, own] for own in lanes], -1)
    return (mm(low, weight) + own_bias).reshape(z.cols, z.images, 3 * HALF)


def dense_in_tall(z, w_ref, bias, st_ref, low_ref, pt, gt):
    B, TC, TR = z.images, z.cols, z.rows

    def one_row(i, carry):
        proj = branch_projection(z, low_ref[i], w_ref, bias, HALF)
        for j in range(TC):
            s, jj = divmod(j, SW)
            at = pl.multiple_of(((s * TR + i) * SW + jj) * B, B)
            for n in range(3):
                pt[n, pl.ds(at, B), :] = proj[j, :, n * HALF : (n + 1) * HALF]
        return carry

    lax.fori_loop(0, TR, one_row, 0)
    size = up(z.tall_own, 8)
    for b in range(B):
        for n in range(3):
            for s in range(z.stripes):
                part = pt[n, pl.ds(s * z.tall_own * B + b, size, stride=B), :]
                at = (((b % z.tall_images) * z.stripes + s) * 3 + n) * z.tall_pad
                gt[b // z.tall_images, at : at + size, :] = part
    st_ref[...] = gt[...].astype(BF16)


def erf_parts(values):
    cdf = 0.5 * (1.0 + lax.erf(values * (0.5**0.5)))
    density = jnp.exp(-0.5 * values * values) * (1.0 / math.sqrt(2.0 * math.pi))
    return cdf, density


def dense_mid_kernel(
    z,
    heights_ref,
    widths_ref,
    rw_ref,
    rt_ref,
    x_ref,
    ct_ref,
    pw_ref,
    pb_ref,
    gain_ref,
    shift_ref,
    w1_ref,
    b1_ref,
    w2_ref,
    b2_ref,
    y_ref,
    gres_ref,
    gw_ref,
    gt_ref,
    dpw_ref,
    dw1_ref,
    dw2_ref,
    vec_ref,
    mw,
    mt,
    gmw,
    gmt,
    gws,
    gts,
    res,
    n2s,
    r2s,
    gys,
    acts,
    mixes,
    pre0,
    pre1,
    gh0,
    gh1,
    hid0,
    hid1,
    gpre0,
    gpre1,
):
    B, D, TC, TR = z.images, z.dim, z.cols, z.rows
    T = TC * B
    count = z.tall_own * B
    blocks = [rw_ref[:, u].astype(F32)[:, : z.fold, :] for u in range(z.pairs)]
    if z.G > 1:
        pairs = rw_ref[:, 0].astype(F32).reshape(B, z.G, z.fold_rows, HALF)
        blocks = [pairs[:, g, : z.fold, :] for g in range(2)]
    lo = low_lanes((B, z.fold, HALF))
    for half, value in enumerate(
        (jnp.where(lo, blocks[0], turn(blocks[1])), jnp.where(lo, turn(blocks[0]), blocks[1]))
    ):
        size = z.fold * B
        value = jnp.swapaxes(value, 0, 1).reshape(size, HALF)
        mw[half * size : (half + 1) * size, :] = value.astype(BF16)
    gts[...] = rt_ref[...].astype(F32)
    for s in range(z.stripes):
        rows = []
        for b in range(B):
            at = ((b % z.tall_images) * z.stripes + s) * z.tall_pad
            rows.append(gts[b // z.tall_images, at : at + z.tall_own, :])
        value = jnp.swapaxes(jnp.stack(rows), 0, 1).reshape(count, HALF)
        mt[s * count : (s + 1) * count, :] = value.astype(BF16)
    for ref in (dpw_ref, dw1_ref, dw2_ref, vec_ref):
        ref[...] = jnp.zeros_like(ref)
    row_start = lax.axis_index("row") * TR
    col_start = lax.axis_index("col") * TC
    image = lax.broadcasted_iota(jnp.int32, (B, D), 0)
    height = jnp.zeros((B, D), jnp.int32)
    width = jnp.zeros((B, D), jnp.int32)
    for b in range(B):
        height = jnp.where(image == b, heights_ref[b], height)
        width = jnp.where(image == b, widths_ref[b], width)
    below_cols = (lax.broadcasted_iota(jnp.int32, (TC, B, D), 0) + col_start) < width[None]
    slots = ((pre0, gh0, hid0, gpre0), (pre1, gh1, hid1, gpre1))

    def places(i, j):
        s, jj = divmod(j, SW)
        return (j * TR + i) * B, ((s * TR + i) * SW + jj) * B

    def first(i):
        pre, gh = slots[i % 2][:2]
        own = slice(i * T, (i + 1) * T)
        at = [places(i, j) for j in range(TC)]
        wide = jnp.concatenate([mw[w : w + B, :] for w, _ in at], 0)
        tall = jnp.concatenate([mt[t : t + B, :] for _, t in at], 0)
        mixture = jnp.concatenate([wide, tall], -1)
        mixes[own, :] = mixture
        x = x_ref[i].astype(F32).reshape(T, D)
        residual = x + (mm(mixture, pw_ref[...]) + pb_ref[...])
        res[own, :] = residual
        n2, r2 = norm_parts(residual)
        n2s[own, :] = n2
        r2s[own, :] = jnp.broadcast_to(r2, (T, HALF))
        act = (n2 * gain_ref[...] + shift_ref[...]).astype(BF16)
        acts[own, :] = act
        pre[...] = mm(act, w1_ref[...]) + b1_ref[...]
        below_rows = (i + row_start) < height[None]
        inside = jnp.logical_and(below_cols, below_rows)
        gy = jnp.where(inside, ct_ref[i].astype(F32), 0.0).reshape(T, D).astype(BF16)
        gys[own, :] = gy
        gh[...] = mm_nt(gy, w2_ref[...])

    def second(i):
        pre, gh, hid, gpre = slots[i % 2]
        FF = pre.shape[1]
        for at, size in key_tiles(FF, 256):
            lanes = slice(at, at + size)
            value = pre[:, lanes]
            cdf, density = erf_parts(value)
            hid[:, lanes] = (value * cdf).astype(BF16)
            low = (gh[:, lanes] * (cdf + value * density)).astype(BF16)
            gpre[:, lanes] = low
            total = jnp.sum(low.astype(F32), 0, keepdims=True)
            for k in range(size // D):
                row = 8 + at // D + k
                vec_ref[row : row + 1, :] += total[:, k * D : (k + 1) * D]

    def third(i):
        hid, gpre = slots[i % 2][2:]
        own = slice(i * T, (i + 1) * T)
        out = res[own, :] + (mm(hid[...], w2_ref[...]) + b2_ref[...])
        y_ref[i] = out.astype(BF16).reshape(TC, B, D)
        gy = gys[own, :]
        dw2_ref[...] += mm_tn(hid[...], gy)
        dw1_ref[...] += mm_tn(acts[own, :], gpre[...])
        gact = mm_nt(gpre[...], w1_ref[...])
        n2 = n2s[own, :]
        r2 = r2s[own, :1]
        gy = gy.astype(F32)
        g = gact * gain_ref[...]
        gres = gy + r2 * (
            g - jnp.mean(g, -1, keepdims=True) - n2 * jnp.mean(g * n2, -1, keepdims=True)
        )
        gres_ref[i] = gres.reshape(TC, B, D)
        gattn = gres.astype(BF16)
        dpw_ref[...] += mm_tn(mixes[own, :], gattn)
        gmix = mm_nt(gattn, pw_ref[...]).astype(BF16).astype(F32)
        vec_ref[0:1, :] += jnp.sum(gact * n2, 0, keepdims=True)
        vec_ref[1:2, :] += jnp.sum(gact, 0, keepdims=True)
        vec_ref[2:3, :] += jnp.sum(gattn.astype(F32), 0, keepdims=True)
        vec_ref[3:4, :] += jnp.sum(gy, 0, keepdims=True)
        vec_ref[4:5, :] += jnp.sum(gmix, 0, keepdims=True)
        gm3 = gmix.reshape(TC, B, D)
        for j in range(TC):
            wide_at, tall_at = places(i, j)
            gmw[wide_at : wide_at + B, :] = gm3[j, :, :HALF]
            gmt[tall_at : tall_at + B, :] = gm3[j, :, HALF:]

    for t in range(TR + 2):
        if t < TR:
            first(t)
        if 0 <= t - 1 < TR:
            second(t - 1)
        if t - 2 >= 0:
            third(t - 2)
    gws[:, : z.pix, :] = jnp.swapaxes(gmw[...].reshape(z.pix, B, HALF), 0, 1)
    if z.G == 1:
        gw_ref[...] = gws[...].astype(BF16)
    else:
        for b in range(B):
            for g in range(z.G):
                gw_ref[b * z.G + g] = gws[b, :, g * z.hc : (g + 1) * z.hc].astype(BF16)
    for s in range(z.stripes):
        value = gmt[s * count : (s + 1) * count, :].reshape(z.tall_own, B, HALF)
        value = jnp.swapaxes(value, 0, 1)
        for b in range(B):
            at = ((b % z.tall_images) * z.stripes + s) * z.tall_pad
            gts[b // z.tall_images, at : at + z.tall_own, :] = value[b]
    gt_ref[...] = gts[...].astype(BF16)


def dense_out_kernel(
    z,
    rw_ref,
    rt_ref,
    x_ref,
    gres_ref,
    gain_ref,
    shift_ref,
    w_ref,
    gin_ref,
    dw_ref,
    vec_ref,
    pw,
    pt,
    gw,
    gt,
):
    B, D, TC, TR = z.images, z.dim, z.cols, z.rows
    T = TC * B
    gw[...] = rw_ref[...].astype(F32)
    gt[...] = rt_ref[...].astype(F32)
    lo = low_half(z.pix)
    lo_half = low_half(z.fold)
    for b in range(B):
        qk = []
        vv = []
        for u in range(2):
            d = b * z.G + u // z.pairs
            qk.append(gw[d, u % z.pairs, : z.pix, :])
            vv.append(gw[d, u % z.pairs, z.pix : z.pix + z.fold, :])
        places = pl.ds(b, z.pix, stride=B)
        pw[0, places, :] = jnp.where(lo, qk[0], turn(qk[1]))
        pw[1, places, :] = jnp.where(lo, turn(qk[0]), qk[1])
        pw[2, pl.ds(b, z.fold, stride=B), :] = jnp.where(lo_half, vv[0], turn(vv[1]))
        pw[2, pl.ds(z.fold * B + b, z.fold, stride=B), :] = jnp.where(
            lo_half, turn(vv[0]), vv[1]
        )
        for n in range(3):
            for s in range(z.stripes):
                at = (((b % z.tall_images) * z.stripes + s) * 3 + n) * z.tall_pad
                pt[n, pl.ds(s * z.tall_own * B + b, z.tall_own, stride=B), :] = gt[
                    b // z.tall_images, at : at + z.tall_own, :
                ]
    dw_ref[...] = jnp.zeros_like(dw_ref)
    vec_ref[...] = jnp.zeros_like(vec_ref)

    def one_row(i, carry):
        x = x_ref[i].astype(F32).reshape(T, D)
        n1, r1 = norm_parts(x)
        low = (n1 * gain_ref[...] + shift_ref[...]).astype(BF16)
        lanes = []
        for n in range(3):
            wide = []
            tall = []
            for j in range(TC):
                s, jj = divmod(j, SW)
                wide_at = pl.multiple_of((j * TR + i) * B, B)
                tall_at = pl.multiple_of(((s * TR + i) * SW + jj) * B, B)
                wide.append(pw[n, pl.ds(wide_at, B), :])
                tall.append(pt[n, pl.ds(tall_at, B), :])
            lanes.append(jnp.concatenate(wide, 0))
            lanes.append(jnp.concatenate(tall, 0))
        gproj = jnp.concatenate(lanes, -1)
        vec_ref[2:3, :] += jnp.sum(gproj[:, :D], 0, keepdims=True)
        vec_ref[3:4, :] += jnp.sum(gproj[:, 2 * D :], 0, keepdims=True)
        gproj = gproj.astype(BF16)
        dw_ref[...] += mm_tn(low, gproj)
        gn = mm_nt(gproj, w_ref[...])
        vec_ref[0:1, :] += jnp.sum(gn * n1, 0, keepdims=True)
        vec_ref[1:2, :] += jnp.sum(gn, 0, keepdims=True)
        g = gn * gain_ref[...]
        gin = gres_ref[i].reshape(T, D) + r1 * (
            g - jnp.mean(g, -1, keepdims=True) - n1 * jnp.mean(g * n1, -1, keepdims=True)
        )
        gin_ref[i] = gin.reshape(TC, B, D)
        return carry

    lax.fori_loop(0, TR, one_row, 0)


def key_tiles(length, tile):
    return [(at, min(tile, length - at)) for at in range(0, length, tile)]


def token_places(start, count, lanes):
    token = (lax.broadcasted_iota(jnp.int32, (count, lanes), 0) + start).astype(F32)
    along = jnp.floor((token + 0.5) * (1.0 / SW))
    across = token - along * SW
    return along, across


def conv_forward(vpad, base, count, kernels, across):
    total = None
    for a in (-1, 0, 1):
        inner = None
        for l in (-1, 0, 1):
            term = kernels(a, l) * vpad[base + SW * l + a : base + SW * l + a + count, :]
            inner = term if inner is None else inner + term
        if a == -1:
            inner = jnp.where(across >= 1, inner, 0.0)
        if a == 1:
            inner = jnp.where(across <= SW - 2, inner, 0.0)
        total = inner if total is None else total + inner
    return total


def conv_backward(gpad, base, count, kernels, across):
    total = None
    for a in (-1, 0, 1):
        inner = None
        for l in (-1, 0, 1):
            at = base - SW * l - a
            term = kernels(a, l) * gpad[at : at + count, :]
            inner = term if inner is None else inner + term
        if a == -1:
            inner = jnp.where(across <= SW - 2, inner, 0.0)
        if a == 1:
            inner = jnp.where(across >= 1, inner, 0.0)
        total = inner if total is None else total + inner
    return total


def wide_tap(a, l):
    return 3 * (a + 1) + (l + 1)


def tall_tap(a, l):
    return 3 * (l + 1) + (a + 1)


def head_lanes(h, rows):
    lane = lax.broadcasted_iota(jnp.int32, (rows, HALF), 1)
    return jnp.logical_and(lane >= h * HEAD_DIM, lane < (h + 1) * HEAD_DIM)


def wide_plan(z):
    per_head = z.wide_len // z.qb
    tail = z.wide_len - per_head * z.qb
    blocks = 2 * per_head
    lanes = up(2 * tail, 128)
    return per_head, tail, blocks, lanes, blocks * z.qb + lanes


def diagonal(tail, first, lanes):
    channel = lax.broadcasted_iota(jnp.int32, (HALF, lanes), 0) - first * HEAD_DIM
    query = lax.broadcasted_iota(jnp.int32, (HALF, lanes), 1)
    keep = channel < -HALF
    for h in range(2):
        keep = jnp.logical_or(
            keep,
            jnp.logical_and(
                jnp.logical_and(channel >= h * HEAD_DIM, channel < (h + 1) * HEAD_DIM),
                jnp.logical_and(query >= h * tail, query < (h + 1) * tail),
            ),
        )
    return keep


def tail_columns(rows, tail, first, lanes):
    copies = [rows, rows]
    if lanes > 2 * tail:
        copies.append(jnp.zeros((lanes - 2 * tail, HALF), F32))
    return jnp.where(diagonal(tail, first, lanes), jnp.concatenate(copies, 0).T, 0.0)


def tail_rows(columns, tail):
    flat = columns.T
    return flat[:tail] + flat[tail : 2 * tail]


def head_rows_mask(h, value):
    row = lax.broadcasted_iota(jnp.int32, value.shape, 0)
    keep = jnp.logical_and(row >= h * HEAD_DIM, row < (h + 1) * HEAD_DIM)
    return jnp.where(keep, value, 0.0)


def between(value, high):
    return jnp.maximum(jnp.minimum(value, high), 0)


def wide_ends(z, heights_ref, widths_ref):
    image = lax.axis_index("col") // z.G
    start = lax.axis_index("row") * z.rows
    return (
        between(heights_ref[image] - start, z.rows),
        between(widths_ref[image], z.C * z.cols),
    )


def tall_ends(z, heights_ref, widths_ref):
    def ends(p):
        image = lax.axis_index("row") * z.tall_images + p // z.stripes
        start = lax.axis_index("col") * z.cols + lax.rem(p, z.stripes) * SW
        return (
            between(widths_ref[image] - start, SW),
            between(heights_ref[image], z.R * z.rows),
        )

    return ends


def own_lanes(z, value):
    if z.G == 1:
        return value
    turned = jnp.where(lax.rem(lax.axis_index("col"), z.G) == 0, value, turn(value))
    return jnp.where(low_half(value.shape[0]), turned, 0.0)


def wide_limits(lim_ref):
    across_limit, along_limit = lim_ref
    empty = across_limit * along_limit == 0
    scale = jnp.where(empty, 1e-20, LOG2E * HEAD_DIM**-0.5)
    return across_limit, along_limit, empty, scale


def wide_inside(lim_ref, at, size):
    along, across = token_places(at, size, HALF)
    return jnp.logical_and(across < lim_ref[0], along < lim_ref[1]), across


def wide_pair_prepare(
    z, pair, lim_ref, recv, kcat, qtb, kt, qk, vpad, stage, vt, vt_all, waits=()
):
    L = z.wide_len
    per_head, tail, blocks, tail_lanes, span = wide_plan(z)
    full = per_head * z.qb
    _, _, empty, _ = wide_limits(lim_ref)
    cut = up(z.pix, 16)
    if waits:
        waits[0].arrive()
        for later in waits[2:]:
            later.start()
    for c in range(z.C):
        stage[:cut, :] = recv[c, pair, :cut].astype(F32)
        qk[c * z.pix : (c + 1) * z.pix, :] = stage[: z.pix, :]
    ones = jnp.where(lax.broadcasted_iota(jnp.int32, (HALF, z.qb), 0) == 0, 1.0, 0.0).astype(BF16)

    def keys(at, size):
        rows = pl.ds(at, size)
        both = qk[rows, :]
        kcat[pair, rows, :HALF] = both.astype(BF16)
        inside, _ = wide_inside(lim_ref, at, size)
        allowed = jnp.logical_or(inside, empty)
        lane = lax.broadcasted_iota(jnp.int32, (size, HALF), 1) == 0
        bias = jnp.where(jnp.logical_and(lane, jnp.logical_not(allowed)), MASKED, 0.0)
        kcat[pair, rows, HALF:] = bias.astype(BF16)
        return both

    def flip(n, carry):
        at = pl.multiple_of(n * z.qb, z.qb)
        both = keys(at, z.qb).T
        kt[pair, :, pl.ds(at, z.qb)] = both[HALF // 2 :].astype(BF16)
        for h in range(2):
            cols = pl.ds(pl.multiple_of((h * per_head + n) * z.qb, z.qb), z.qb)
            parts = [jnp.zeros((HALF // 2, z.qb), F32)] + [jnp.zeros((HEAD_DIM, z.qb), F32)] * 2
            parts[1 + h] = both[h * HEAD_DIM : (h + 1) * HEAD_DIM]
            qtb[pair, :HALF, cols] = jnp.concatenate(parts, 0).astype(BF16)
            qtb[pair, HALF:, cols] = ones
        return carry

    lax.fori_loop(0, per_head, flip, 0)
    tail_cols = slice(blocks * z.qb, span)
    tail_both = keys(full, tail)
    kt[pair, :, full:L] = tail_both.T[HALF // 2 :].astype(BF16)
    qtb[pair, :HALF, tail_cols] = tail_columns(turn(tail_both), tail, 2, tail_lanes).astype(BF16)
    qtb[pair, HALF:, tail_cols] = ones[:, :tail_lanes]
    if waits:
        waits[1].arrive()
    lo = low_half(z.fold)
    start = z.pix // 16 * 16
    for c in range(z.C):
        stage[start:, :] = recv[c, pair, start:].astype(F32)
        v = stage[z.pix : z.pix + z.fold, :]
        at = c * z.pix
        one = slice(PAD + at, PAD + at + z.fold)
        two = slice(PAD + at + z.fold, PAD + at + z.pix)
        if pair == 0:
            vpad[one, :] = jnp.where(lo, v, 0.0)
            vpad[two, :] = jnp.where(lo, turn(v), 0.0)
        else:
            vpad[one, :] = jnp.where(lo, vpad[one, :], turn(v))
            vpad[two, :] = jnp.where(lo, vpad[two, :], v)

    def values(at, size):
        vt_full = vpad[pl.ds(pl.multiple_of(at + PAD, 8), size), :].T
        first = lax.broadcasted_iota(jnp.int32, (16, size), 0) == 0
        first = jnp.where(first, 1.0, 0.0)
        vt_all[:, pl.ds(at, size)] = jnp.concatenate([vt_full, first], 0).astype(BF16)
        for h in range(2):
            own = (2 * pair + h) * HEAD_DIM
            own = vt_full[own : own + HEAD_DIM]
            vt[h, :, pl.ds(at, size)] = jnp.concatenate([own, first], 0).astype(BF16)

    def flip_values(n, carry):
        values(pl.multiple_of(n * z.qb, z.qb), z.qb)
        return carry

    lax.fori_loop(0, per_head, flip_values, 0)
    values(full, tail)


def wide_pair_attend(z, pair, lim_ref, kcat, qtb, ot, lse, vt, vt_all, ss0, ss1):
    L = z.wide_len
    per_head, tail, blocks, tail_lanes, span = wide_plan(z)
    full = per_head * z.qb
    base = pair * span
    _, _, _, scale = wide_limits(lim_ref)
    tail_cols = slice(blocks * z.qb, span)

    def scores(cols, slot):
        s = mm(kcat[pair], qtb[pair, :, cols])
        slot[...] = s
        return jnp.max(jnp.max(s.reshape(L // 8, 8, s.shape[1]), 0), 0, keepdims=True)

    def block_scores(n, slot):
        return scores(pl.ds(pl.multiple_of(n * z.qb, z.qb), z.qb), slot)

    def weigh(values, slot, top):
        p = jnp.exp2((slot[...] - top) * scale).astype(BF16)
        acc = mm(values, p)
        at = acc.shape[0] - 16
        total = acc[at : at + 1]
        return acc[:at] * (1.0 / total), top * scale + jnp.log2(total)

    def block_rest(n, slot, top):
        h = n // per_head
        out, low = weigh(vt[h], slot, top)
        rows = pl.ds(pl.multiple_of((2 * pair + h) * HEAD_DIM, HEAD_DIM), HEAD_DIM)
        ot[rows, pl.ds(pl.multiple_of((n - h * per_head) * z.qb, z.qb), z.qb)] = out
        lse[0:1, pl.ds(pl.multiple_of(base + n * z.qb, 128), z.qb)] = low

    def two(m, top):
        n = 2 * m
        top_next = block_scores(n + 1, ss1)
        block_rest(n, ss0, top)
        top = block_scores(n + 2, ss0)
        block_rest(n + 1, ss1, top_next)
        return top

    top = lax.fori_loop(0, blocks // 2 - 1, two, block_scores(0, ss0))
    top_next = block_scores(blocks - 1, ss1)
    block_rest(blocks - 2, ss0, top)
    tail_slot = ss0.at[:, :tail_lanes]
    top = scores(tail_cols, tail_slot)
    block_rest(blocks - 1, ss1, top_next)
    out, low = weigh(vt_all[...], tail_slot, top)
    lse[0:1, base + blocks * z.qb : base + span] = low
    out = jnp.where(diagonal(tail, 2 * pair, tail_lanes), out, 0.0)
    ot[:, full + pair * tail_lanes : full + (pair + 1) * tail_lanes] = out


def wide_lepe(z, lim_ref, lw_ref, lb_ref, vpad, lepe):
    L = z.wide_len
    for at, size in key_tiles(L, z.qb):
        inside, _ = wide_inside(lim_ref, at, size)
        rows = slice(at + PAD, at + PAD + size)
        vpad[rows, :] = jnp.where(inside, vpad[rows, :], 0.0)

    def taps(a, l):
        t = wide_tap(a, l)
        return lw_ref[t : t + 1, :]

    for at, size in key_tiles(L, 224):
        along, across = token_places(at, size, HALF)
        lepe[at : at + size, :] = conv_forward(vpad, at + PAD, size, taps, across) + lb_ref


def wide_pair_mixture(z, pair, ot, lepe, osum, out_ref):
    L = z.wide_len
    per_head, tail, _, tail_lanes, _ = wide_plan(z)
    full = per_head * z.qb

    def doubled(value):
        lo = low_half(value.shape[0])
        return jnp.where(lo, value, turn(value)) if pair == 0 else jnp.where(lo, turn(value), value)

    def finish(n, carry):
        rows = pl.ds(pl.multiple_of(n * z.qb, z.qb), z.qb)
        osum[rows, :] = doubled(ot[:, rows].T + lepe[rows, :])
        return carry

    lax.fori_loop(0, per_head, finish, 0)
    last = tail_rows(ot[:, full + pair * tail_lanes : full + (pair + 1) * tail_lanes], tail)
    osum[full:L, :] = doubled(last + lepe[full:L, :])
    lo = low_half(z.fold_rows)
    for c in range(z.C):
        at = c * z.pix
        one = osum[at : at + z.fold_rows, :]
        two = osum[at + z.fold : at + z.fold + z.fold_rows, :]
        out_ref[c, pair] = jnp.where(lo, one, two).astype(BF16)


def wide_backward_start(z, lim_ref, recv, lw_ref, v_ref, ot, dlw_ref, gpad, vpad, dotb, delta, dvl, stage):
    L = z.wide_len
    per_head, tail, blocks, tail_lanes, span = wide_plan(z)
    full = per_head * z.qb
    gpad[...] = jnp.zeros_like(gpad)
    vpad[...] = jnp.zeros_like(vpad)
    stage[...] = jnp.zeros_like(stage)
    for c in range(z.C):
        stage[: z.wide_rows1, : z.hc] = recv[c].astype(F32)
        gpad[PAD + c * z.pix : PAD + (c + 1) * z.pix, :] = stage[: z.pix, :]

    def prepare(at, size):
        rows = pl.ds(at, size)
        padded = pl.ds(pl.multiple_of(at + PAD, 8), size)
        inside, _ = wide_inside(lim_ref, at, size)
        vpad[padded, :] = jnp.where(inside, v_ref[rows, :].astype(F32), 0.0)
        return gpad[padded, :]

    def flip(n, carry):
        at = pl.multiple_of(n * z.qb, z.qb)
        gt = prepare(at, z.qb).T
        prod = gt * ot[:, pl.ds(at, z.qb)]
        for h in range(z.wide_heads):
            first = (h // 2) * span + (h % 2) * full
            cols = pl.ds(pl.multiple_of(first + n * z.qb, 128), z.qb)
            dotb[:, cols] = head_rows_mask(h, gt).astype(BF16)
            delta[0:1, cols] = jnp.sum(
                prod[h * HEAD_DIM : (h + 1) * HEAD_DIM], 0, keepdims=True
            )
        return carry

    lax.fori_loop(0, per_head, flip, 0)
    last = prepare(full, tail)
    for pair in range(z.pairs):
        cols = slice(pair * span + blocks * z.qb, (pair + 1) * span)
        gt = tail_columns(last, tail, 2 * pair, tail_lanes)
        dotb[:, cols] = gt.astype(BF16)
        out = ot[:, full + pair * tail_lanes : full + (pair + 1) * tail_lanes]
        delta[0:1, cols] = jnp.sum(gt * out, 0, keepdims=True)

    def taps(a, l):
        t = wide_tap(a, l)
        return lw_ref[t : t + 1, :]

    sums_of = {}
    for at, size in key_tiles(L, 224):
        inside, across = wide_inside(lim_ref, at, size)
        lepe = conv_backward(gpad, at + PAD, size, taps, across)
        dvl[at : at + size, :] = jnp.where(inside, lepe, 0.0)
        add_kernel_sums(sums_of, gpad, vpad, at + PAD, size, across, wide_tap)
    dlw_ref[...] = jnp.zeros_like(dlw_ref)
    for t, value in sums_of.items():
        dlw_ref[t : t + 1, :] = jnp.sum(value, 0, keepdims=True)


def wide_pair_backward(
    z,
    pair,
    lim_ref,
    v_ref,
    kcat,
    qtb,
    kt,
    lse,
    dotb,
    delta,
    dvl,
    dqt,
    dkt,
    dvt,
    dqk,
    dvv,
    stage,
    slots,
    out_ref,
    midway,
    segments,
):
    L = z.wide_len
    per_head, tail, blocks, tail_lanes, span = wide_plan(z)
    full = per_head * z.qb
    base = pair * span
    _, _, _, scale = wide_limits(lim_ref)
    dkt[...] = jnp.zeros_like(dkt)
    dvt[...] = jnp.zeros_like(dvt)
    tail_cols = slice(blocks * z.qb, span)

    def shifted(cols):
        if isinstance(cols, slice):
            return slice(base + cols.start, base + cols.stop)
        return pl.ds(pl.multiple_of(base + cols.start, 128), cols.size)

    def products(cols, s_slot, dp_slot):
        s_slot[...] = mm(kcat[pair], qtb[pair, :, cols])
        dp_slot[...] = mm(v_ref[...], dotb[:, shifted(cols)])

    def weights(cols, s_slot, dp_slot, p_slot, ds_slot):
        low = lse[0:1, shifted(cols)]
        dlt = delta[0:1, shifted(cols)]
        for at, size in key_tiles(L, z.qb):
            rows = slice(at, at + size)
            p = jnp.exp2(s_slot[rows, :] * scale - low)
            p_slot[rows, :] = p.astype(BF16)
            ds_slot[rows, :] = (p * (dp_slot[rows, :] - dlt)).astype(BF16)

    def block_cols(n):
        return pl.ds(pl.multiple_of(n * z.qb, z.qb), z.qb)

    def first(n, k):
        products(block_cols(n), *slots[k][:2])

    def second(n, k):
        weights(block_cols(n), *slots[k])

    def third(n, k):
        h = n // per_head
        p_slot, ds_slot = slots[k][2:]
        cols = block_cols(n)
        rows = pl.ds(pl.multiple_of(h * HEAD_DIM, HEAD_DIM), HEAD_DIM)
        g_rows = pl.ds(pl.multiple_of((2 * pair + h) * HEAD_DIM, HEAD_DIM), HEAD_DIM)
        q_rows = pl.ds(pl.multiple_of(HALF // 2 + h * HEAD_DIM, HEAD_DIM), HEAD_DIM)
        dvt[rows, :] += mm_nt(dotb[g_rows, shifted(cols)], p_slot[...])
        dkt[rows, :] += mm_nt(qtb[pair, q_rows, cols], ds_slot[...])
        at = pl.ds(pl.multiple_of((n - h * per_head) * z.qb, z.qb), z.qb)
        dqt[rows, at] = mm(kt[pair, rows, :], ds_slot[...])

    first(0, 0)
    first(1, 1)
    second(0, 0)

    def two(m, carry):
        n = 2 * m
        first(n, 0)
        second(n - 1, 1)
        third(n - 2, 0)
        first(n + 1, 1)
        second(n, 0)
        third(n - 1, 1)
        return carry

    marks = [1 + (blocks // 2 - 1) * k // segments for k in range(segments + 1)]
    for k in range(segments):
        lax.fori_loop(marks[k], marks[k + 1], two, 0)
        if k + 1 < segments:
            midway()
    tail_slots = [ref.at[:, :tail_lanes] for ref in slots[0]]
    products(tail_cols, *tail_slots[:2])
    second(blocks - 1, 1)
    third(blocks - 2, 0)
    weights(tail_cols, *tail_slots)
    third(blocks - 1, 1)
    half = HALF // 2
    dvt[...] += mm_nt(dotb[pair * half : (pair + 1) * half, shifted(tail_cols)], tail_slots[2][...])
    dkt[...] += mm_nt(qtb[pair, half:HALF, tail_cols], tail_slots[3][...])
    last = mm(kt[pair], tail_slots[3][...])
    empty_half = jnp.zeros((half, tail_lanes), F32)
    last = jnp.concatenate([last, empty_half], 0)
    last = jnp.where(diagonal(tail, 0, tail_lanes), last, 0.0)
    norm = HEAD_DIM**-0.5
    dk_last = jnp.concatenate([jnp.zeros((half, tail), F32), dkt[:, full:L]], 0).T
    dqk[full:L, :] = (tail_rows(last, tail) + dk_last) * norm

    def doubled(value):
        lo = low_half(value.shape[0])
        return jnp.where(lo, value, turn(value)) if pair == 0 else jnp.where(lo, turn(value), value)

    def finish(n, carry):
        rows = pl.ds(pl.multiple_of(n * z.qb, z.qb), z.qb)
        dqk[rows, :] = jnp.concatenate([dqt[:, rows], dkt[:, rows]], 0).T * norm
        dv = dvt[:, rows]
        dvv[rows, :] = jnp.concatenate([dv, dv], 0).T + doubled(dvl[rows, :])
        return carry

    lax.fori_loop(0, per_head, finish, 0)
    dv = dvt[:, full:L]
    dvv[full:L, :] = jnp.concatenate([dv, dv], 0).T + doubled(dvl[full:L, :])
    lo = low_half(z.fold)
    for c in range(z.C):
        at = c * z.pix
        stage[: z.pix, :] = dqk[at : at + z.pix, :]
        stage[z.pix : z.pix + z.fold, :] = jnp.where(
            lo, dvv[at : at + z.fold, :], dvv[at + z.fold : at + z.pix, :]
        )
        out_ref[c, pair] = stage[...].astype(BF16)


def add_kernel_sums(sums, gpad, vpad, base, size, across, tap):
    g = gpad[base : base + size, :]
    for a in (-1, 0, 1):
        ga = g
        if a == -1:
            ga = jnp.where(across >= 1, g, 0.0)
        if a == 1:
            ga = jnp.where(across <= SW - 2, g, 0.0)
        for l in (-1, 0, 1):
            at = base + SW * l + a
            term = (ga * vpad[at : at + size, :]).reshape(size // 8, 8, HALF).sum(0)
            t = tap(a, l)
            sums[t] = sums[t] + term if t in sums else term


def tall_prepare(z, p, lim_ref, L):
    across_limit, along_limit = lim_ref(p)
    empty = across_limit * along_limit == 0
    scale = jnp.where(empty, 1e-20, LOG2E * HEAD_DIM**-0.5)
    along, across = token_places(0, L, HALF)
    inside = jnp.logical_and(across < across_limit, along < along_limit)
    allowed = jnp.logical_or(inside, empty)
    token = lax.broadcasted_iota(jnp.int32, (L, HALF), 0)
    allowed = jnp.logical_and(allowed, token < z.tall_len)
    lane = lax.broadcasted_iota(jnp.int32, (L, HALF), 1) == 0
    bias = jnp.where(jnp.logical_and(lane, jnp.logical_not(allowed)), MASKED, 0.0).astype(BF16)
    return inside, across, scale, bias


def tall_pull(z, source, p, per, n, target, base):
    for r in range(z.R):
        at = pl.multiple_of((p * per + n) * z.tall_pad, 8)
        block = source[r, pl.ds(at, z.tall_pad), :]
        target[base + r * z.tall_own : base + (r + 1) * z.tall_own, :] = block[: z.tall_own]


def tall_push(z, source, p, per, n, target, base=0):
    for r in range(z.R):
        at = pl.multiple_of((p * per + n) * z.tall_pad, 8)
        target[r, pl.ds(at, z.tall_pad), :] = source[
            base + r * z.tall_own : base + r * z.tall_own + z.tall_pad, :
        ]


def tall_operands(z, k, q, bias, kstack, L):
    for h in range(BRANCH_HEADS):
        kstack[h * L : (h + 1) * L, :HALF] = jnp.where(head_lanes(h, L), k, 0.0).astype(BF16)
        kstack[h * L : (h + 1) * L, HALF:] = bias
    first = lax.broadcasted_iota(jnp.int32, (HALF, L), 0) == 0
    return jnp.concatenate([q.T, jnp.where(first, 1.0, 0.0)], 0).astype(BF16)


def tall_forward(
    z, start, stop, lim_ref, lw_ref, lb_ref, ot_ref, lse_ref, src, dst, qs, ks, vs, vpad, osum, kstack
):
    L = qs.shape[1]

    def taps(a, l):
        t = tall_tap(a, l)
        return lw_ref[t : t + 1, :]

    def group(m, carry):
        each = range(z.tall_group)
        ps = [m * z.tall_group + u for u in each]
        for u in each:
            for n, target in enumerate((qs, ks, vs)):
                tall_pull(z, src, ps[u], 3, n, target.at[u], 0)
        made = [tall_prepare(z, ps[u], lim_ref, L) for u in each]
        qts = [tall_operands(z, ks[u], qs[u], made[u][3], kstack.at[u], L) for u in each]
        scores = [mm(kstack[u], qts[u]) for u in each]
        tail = lax.broadcasted_iota(jnp.int32, (16, L), 0) == 0
        tail = jnp.where(tail, 1.0, 0.0)
        vts = [vs[u].T for u in each]
        tops = [
            [jnp.max(scores[u][h * L : (h + 1) * L], 0, keepdims=True) for h in range(BRANCH_HEADS)]
            for u in each
        ]
        accs = []
        for u in each:
            row = []
            for h in range(BRANCH_HEADS):
                s = scores[u][h * L : (h + 1) * L]
                e = jnp.exp2((s - tops[u][h]) * made[u][2]).astype(BF16)
                vt = jnp.concatenate([vts[u][h * HEAD_DIM : (h + 1) * HEAD_DIM], tail], 0)
                row.append(mm(vt.astype(BF16), e))
            accs.append(row)
        for u in each:
            inside, across, scale, _ = made[u]
            outs = []
            for h in range(BRANCH_HEADS):
                total = accs[u][h][HEAD_DIM : HEAD_DIM + 1]
                outs.append(accs[u][h][:HEAD_DIM] * (1.0 / total))
                lse_ref[ps[u], h : h + 1, :] = tops[u][h] * scale + jnp.log2(total)
            ot = jnp.concatenate(outs, 0)
            ot_ref[ps[u]] = ot
            vpad[u, PAD : PAD + L, :] = jnp.where(inside, vs[u], 0.0)
            lepe = conv_forward(vpad.at[u], PAD, L, taps, across)
            osum[u, :L, :] = ot.T + lepe + lb_ref
        for u in each:
            tall_push(z, osum.at[u], ps[u], 1, 0, dst)
        return carry

    lax.fori_loop(start, stop, group, 0)


def tall_backward(
    z,
    start,
    stop,
    lim_ref,
    lw_ref,
    ot_ref,
    lse_ref,
    dlw_ref,
    src,
    gsrc,
    dst,
    qs,
    ks,
    vs,
    gpad,
    vpad,
    stage,
    kstack,
):
    L = qs.shape[1]
    norm = HEAD_DIM**-0.5

    def taps(a, l):
        t = tall_tap(a, l)
        return lw_ref[t : t + 1, :]

    def group(m, carry):
        each = range(z.tall_group)
        ps = [m * z.tall_group + u for u in each]
        for u in each:
            for n, target in enumerate((qs, ks, vs)):
                tall_pull(z, src, ps[u], 3, n, target.at[u], 0)
            tall_pull(z, gsrc, ps[u], 1, 0, gpad.at[u], PAD)
        made = [tall_prepare(z, ps[u], lim_ref, L) for u in each]
        gts = [gpad[u, PAD : PAD + L, :].T for u in each]
        qts = [tall_operands(z, ks[u], qs[u], made[u][3], kstack.at[u], L) for u in each]
        kts = [ks[u].T.astype(BF16) for u in each]
        dvs = [None] * len(ps)
        dks = [None] * len(ps)
        dqs = [[] for u in each]
        for some in z.tall_head_sets:
            scores = []
            dps = []
            for u in each:
                rows = slice(some[0] * L, (some[-1] + 1) * L)
                scores.append(mm(kstack[u, rows, :], qts[u]))
                v = vs[u]
                vstack = jnp.concatenate([jnp.where(head_lanes(h, L), v, 0.0) for h in some], 0)
                dps.append(mm(vstack.astype(BF16), gts[u].astype(BF16)))
            weights = []
            for u in each:
                prod = gts[u] * ot_ref[ps[u]]
                lse = lse_ref[ps[u]]
                row = []
                for i, h in enumerate(some):
                    rows = slice(i * L, (i + 1) * L)
                    delta = jnp.sum(prod[h * HEAD_DIM : (h + 1) * HEAD_DIM], 0, keepdims=True)
                    w = jnp.exp2(scores[u][rows] * made[u][2] - lse[h : h + 1])
                    ds = (w * (dps[u][rows] - delta)).astype(BF16)
                    row.append((w.astype(BF16), ds))
                weights.append(row)
            for u in each:
                for i, h in enumerate(some):
                    keep = head_lanes(h, L)
                    w, ds = weights[u][i]
                    dv_h = mm(w, jnp.where(keep, gpad[u, PAD : PAD + L, :], 0.0).astype(BF16))
                    dk_h = mm(ds, jnp.where(keep, qs[u], 0.0).astype(BF16))
                    dvs[u] = dv_h if dvs[u] is None else dvs[u] + dv_h
                    dks[u] = dk_h if dks[u] is None else dks[u] + dk_h
                    dqs[u].append(mm(kts[u][h * HEAD_DIM : (h + 1) * HEAD_DIM], ds))
        results = [(jnp.concatenate(dqs[u], 0), dks[u], dvs[u]) for u in each]
        sums = {}
        for u in each:
            inside, across = made[u][:2]
            vpad[u, PAD : PAD + L, :] = jnp.where(inside, vs[u], 0.0)
            lepe = conv_backward(gpad.at[u], PAD, L, taps, across)
            add_kernel_sums(sums, gpad.at[u], vpad.at[u], PAD, L, across, tall_tap)
            dqt, dk, dv = results[u]
            stage[u, 0, :L, :] = dqt.T * norm
            stage[u, 1, :L, :] = dk * norm
            stage[u, 2, :L, :] = dv + jnp.where(inside, lepe, 0.0)
        for t, value in sums.items():
            dlw_ref[t : t + 1, :] += jnp.sum(value, 0, keepdims=True)
        for u in each:
            for n in range(3):
                tall_push(z, stage.at[u, n], ps[u], 3, n, dst)
        return carry

    lax.fori_loop(start, stop, group, 0)


def partners(z):
    col = lax.axis_index("col")
    row = lax.axis_index("row")
    found = [(row, lax.rem(col + k, z.C)) for k in range(1, z.C)]
    found += [(lax.rem(row + k, z.R), col) for k in range(1, z.R)]
    first = col - lax.rem(col, 4)
    for r in range(1, z.R):
        for k in range(1, 4):
            found.append((lax.rem(row + r, z.R), first + lax.rem(col + k, 4)))
    return found


def greet(z):
    barrier = pltpu.get_barrier_semaphore()
    for device in partners(z):
        pl.semaphore_signal(barrier, inc=1, device_id=device, device_id_type=MESH)


def all_greeted(z):
    pl.semaphore_wait(pltpu.get_barrier_semaphore(), len(partners(z)))


class Exchange:
    def __init__(self, z, axis, source, target, sends, receives):
        self.axis = axis
        self.source, self.target = source, target
        self.me = lax.axis_index(axis)
        count = z.C if axis == "col" else z.R
        col = lax.axis_index("col")
        row = lax.axis_index("row")
        self.copies = []
        for k in range(1, count):
            other = lax.rem(self.me + k, count)
            self.copies.append(
                pltpu.make_async_remote_copy(
                    src_ref=source(other),
                    dst_ref=target(self.me),
                    send_sem=sends.at[k],
                    recv_sem=receives.at[k],
                    device_id=(row, other) if axis == "col" else (other, col),
                    device_id_type=MESH,
                )
            )

    def start(self):
        for copy in self.copies:
            copy.start()

    def keep_own(self):
        self.target(self.me)[...] = self.source(self.me)[...]

    def arrive(self):
        for copy in self.copies:
            copy.wait_recv()

    def sent(self):
        for copy in self.copies:
            copy.wait_send()


def split_of(rows, lanes, parts):
    for by_rows in range(parts, 0, -1):
        if parts % by_rows == 0:
            by_lanes = parts // by_rows
            if rows % (16 * by_rows) == 0 and lanes % (128 * by_lanes) == 0:
                return by_rows, by_lanes
    raise ValueError("no split")


def reduce_plan(z, lanes, steps):
    rows = z.dim
    plan = []
    for step in steps:
        members = {"core": 2, "x": 2, "row": z.R, "slab": 4 * z.R}.get(step, z.C // 4)
        a, b = (1, 1) if step == "far_all" else split_of(rows, lanes, members)
        rows, lanes = rows // a, lanes // b
        plan.append((members, step, a, b, rows, lanes))
    return plan


def reduce_width(z, lanes, steps):
    while True:
        try:
            reduce_plan(z, lanes, steps)
            return lanes
        except ValueError:
            lanes += 128


def place_of(step):
    col = lax.axis_index("col")
    row = lax.axis_index("row")
    if step == "row":
        return row
    if step == "slab":
        return row * 4 + lax.rem(col, 4)
    if step in ("far", "far_all"):
        return col // 4
    return lax.rem(col // {"core": 1, "x": 2}[step], 2)


def peer_of(step, members, k):
    col = lax.axis_index("col")
    row = lax.axis_index("row")
    me = place_of(step)
    at = lax.rem(me + k, members)
    if step == "row":
        return at, (at, col)
    if step == "slab":
        return at, (at // 4, col - lax.rem(col, 4) + lax.rem(at, 4))
    return at, (row, col + (at - me) * {"core": 1, "x": 2, "far": 4, "far_all": 4}[step])


class SmallSum:
    def __init__(self, plan, value, slots, sends, receives):
        self.plan, self.value, self.slots = plan, value, slots
        self.sends, self.receives = sends, receives

    def start(self, stage):
        members, step = self.plan[stage][:2]
        me = place_of(step)
        self.copies = []
        for k in range(1, members):
            self.copies.append(
                pltpu.make_async_remote_copy(
                    src_ref=self.value,
                    dst_ref=self.slots[stage].at[me],
                    send_sem=self.sends.at[stage, k],
                    recv_sem=self.receives.at[stage, k],
                    device_id=peer_of(step, members, k)[1],
                    device_id_type=MESH,
                )
            )
        for copy in self.copies:
            copy.start()
        self.slots[stage][me] = self.value[...]

    def end(self, stage, out):
        for copy in self.copies:
            copy.wait()
        total = self.slots[stage][0]
        for k in range(1, self.plan[stage][0]):
            total = total + self.slots[stage][k]
        out[...] = total
        self.value = out


class Reduction:
    def __init__(self, z, plan, refs, small=None):
        n = len(plan)
        self.z, self.plan, self.n = z, plan, n
        self.full, refs = refs[0], refs[1:]
        self.recvs, refs = refs[:n], refs[n:]
        self.held, refs = refs[:n], refs[n:]
        self.gathers, refs = refs[:n], refs[n:]
        self.ssem, self.rsem, self.gsem, self.hsem = refs[:4]
        self.small = small
        if small is not None:
            self.smalls = refs[4 : 4 + n]
            self.vsem, self.wsem = refs[4 + n :]
        self.current = self.full
        self.copies = None

    @staticmethod
    def scratch(z, plan, lanes, small_shape=None):
        dma = pltpu.SemaphoreType.DMA
        most = max(step[0] for step in plan)
        shapes = [pltpu.VMEM((z.dim, lanes), BF16)]
        shapes += [pltpu.VMEM((step[0], step[4], step[5]), BF16) for step in plan]
        shapes += [pltpu.VMEM((step[4], step[5]), BF16) for step in plan]
        shapes += [pltpu.VMEM((z.dim, lanes), BF16)]
        shapes += [pltpu.VMEM((step[4], step[5]), BF16) for step in plan[:-1]]
        shapes += [dma((len(plan), most)) for _ in range(4)]
        if small_shape is not None:
            shapes += [pltpu.VMEM((step[0],) + small_shape, F32) for step in plan]
            shapes += [dma((len(plan), most)) for _ in range(2)]
        return shapes

    def place(self, stage):
        return place_of(self.plan[stage][1])

    def peer(self, stage, k):
        members, step = self.plan[stage][:2]
        return peer_of(step, members, k)

    def window(self, ref, stage, index):
        members, step, a, b, rows, width = self.plan[stage]
        if a * b == 1:
            return ref
        r0 = pl.multiple_of((index // b) * rows, 16)
        l0 = pl.multiple_of(lax.rem(index, b) * width, 128)
        return ref.at[pl.ds(r0, rows), pl.ds(l0, width)]

    def fill(self, pieces):
        D = self.z.dim
        at = 0
        for ref in pieces:
            for k in range(ref.shape[0] // D):
                width = ref.shape[1]
                self.full[:, at : at + width] = ref[k * D : (k + 1) * D, :].astype(BF16)
                at += width
        if at < self.full.shape[1]:
            self.full[:, at:] = jnp.zeros((D, self.full.shape[1] - at), BF16)

    def scatter_start(self, stage):
        me = self.place(stage)
        self.copies = []
        for k in range(1, self.plan[stage][0]):
            index, device = self.peer(stage, k)
            self.copies.append(
                pltpu.make_async_remote_copy(
                    src_ref=self.window(self.current, stage, index),
                    dst_ref=self.recvs[stage].at[me],
                    send_sem=self.ssem.at[stage, k],
                    recv_sem=self.rsem.at[stage, k],
                    device_id=device,
                    device_id_type=MESH,
                )
            )
            if self.small is not None:
                self.copies.append(
                    pltpu.make_async_remote_copy(
                        src_ref=self.small,
                        dst_ref=self.smalls[stage].at[me],
                        send_sem=self.vsem.at[stage, k],
                        recv_sem=self.wsem.at[stage, k],
                        device_id=device,
                        device_id_type=MESH,
                    )
                )
        for copy in self.copies:
            copy.start()
        self.recvs[stage][me] = self.window(self.current, stage, me)[...]
        if self.small is not None:
            self.smalls[stage][me] = self.small[...]

    def scatter_end(self, stage, small_out=None):
        for copy in self.copies:
            copy.wait()
        members = self.plan[stage][0]
        rows, width = self.plan[stage][4:]
        for at, size in key_tiles(width, 512):
            lanes = slice(at, at + size)
            total = self.recvs[stage][0, :, lanes].astype(F32)
            for k in range(1, members):
                total = total + self.recvs[stage][k, :, lanes].astype(F32)
            self.held[stage][:, lanes] = total.astype(BF16)
        self.current = self.held[stage]
        if self.small is not None:
            small = self.smalls[stage][0]
            for k in range(1, members):
                small = small + self.smalls[stage][k]
            if stage + 1 < self.n:
                self.smalls[stage][0] = small
                self.small = self.smalls[stage].at[0]
            else:
                small_out[...] = small

    def gather_start(self, stage):
        me = self.place(stage)
        self.copies = []
        for k in range(1, self.plan[stage][0]):
            index, device = self.peer(stage, k)
            self.copies.append(
                pltpu.make_async_remote_copy(
                    src_ref=self.current,
                    dst_ref=self.window(self.gathers[stage], stage, me),
                    send_sem=self.gsem.at[stage, k],
                    recv_sem=self.hsem.at[stage, k],
                    device_id=device,
                    device_id_type=MESH,
                )
            )
        for copy in self.copies:
            copy.start()
        self.window(self.gathers[stage], stage, me)[...] = self.current[...]

    def gather_end(self, stage):
        for copy in self.copies:
            copy.wait()
        self.current = self.gathers[stage]

    def steps(self, small_out=None):
        n = self.n
        ends = [functools.partial(self.scatter_end, s, small_out) for s in range(n)]
        back = [s for s in range(n - 1, -1, -1) if self.plan[s][1] != "far_all"]
        ends += [functools.partial(self.gather_end, s) for s in back]
        starts = [functools.partial(self.scatter_start, s) for s in range(n)]
        starts += [functools.partial(self.gather_start, s) for s in back]
        return starts, ends


def spread(block, outs):
    D = block.shape[0]
    at = 0
    for ref in outs:
        for k in range(ref.shape[0] // D):
            width = ref.shape[1]
            ref[k * D : (k + 1) * D, :] = block[:, at : at + width].astype(F32)
            at += width


def reduce_kernel(z, plan, dqkv_ref, vec_ref, dwt_ref, dtt_ref, sum_ref, osmall, small, *refs):
    greet(z)
    small[:16, :HALF] = own_lanes_back(z, dwt_ref[...])
    small[:16, HALF:] = dtt_ref[...]
    small[9:13, :] = vec_ref[:4, :]
    work = Reduction(z, plan, refs, small)
    work.fill((dqkv_ref,))
    all_greeted(z)
    starts, ends = work.steps(osmall)
    for start, end in zip(starts, ends):
        start()
        end()
    sum_ref[...] = work.current[...]


def own_lanes_back(z, value):
    if z.G == 1:
        return value
    return jnp.where(lax.rem(lax.axis_index("col"), z.G) == 0, value, turn(value))


def reduce_last(z, dqkv, vec, dwt, dtt, collective_id):
    steps = ("slab", "far")
    lanes = reduce_width(z, dqkv.size // z.dim, steps)
    plan = reduce_plan(z, lanes, steps)
    vmem = pl.BlockSpec(memory_space=pltpu.VMEM)
    small = (16, z.dim)
    return pl.pallas_call(
        functools.partial(reduce_kernel, z, plan),
        out_shape=(
            jax.ShapeDtypeStruct((z.dim, lanes), BF16),
            jax.ShapeDtypeStruct(small, F32),
        ),
        in_specs=[vmem] * 4,
        out_specs=(vmem,) * 2,
        scratch_shapes=[pltpu.VMEM(small, F32)] + Reduction.scratch(z, plan, lanes, small),
        compiler_params=pltpu.CompilerParams(
            collective_id=collective_id, has_side_effects=True, vmem_limit_bytes=VMEM_LIMIT
        ),
        name="reduce_last",
    )(dqkv, vec, dwt, dtt)


def split_kernel(z, sum_ref, late_ref, early_ref, first_ref, dw_ref, dpw_ref, dw1_ref, dw2_ref, *outs):
    if z.merged:
        width = sum_ref.shape[1] // 2
        for n in range(3):
            own = slice(n * HALF, (n + 1) * HALF)
            dw_ref[:, n * z.dim + HALF : (n + 1) * z.dim] = sum_ref[:, own].astype(F32)
            own = slice(width + n * HALF, width + (n + 1) * HALF)
            dw_ref[:, n * z.dim : n * z.dim + HALF] = sum_ref[:, own].astype(F32)
    else:
        spread(sum_ref, (dw_ref,))
    spread(first_ref, (dpw_ref, dw1_ref, dw2_ref))
    n1g, n1s, qb, vb, taps, lb, pb, n2g, n2s, b1, b2 = outs
    taps[...] = late_ref[:9, :]
    for ref, row in ((n1g, 9), (n1s, 10), (qb, 11), (vb, 12)):
        ref[...] = late_ref[row : row + 1, :]
    for ref, row in ((n2g, 0), (n2s, 1), (pb, 2), (b2, 3), (lb, 4)):
        ref[...] = early_ref[row : row + 1, :]
    D = z.dim
    for k in range(b1.shape[1] // D):
        b1[:, k * D : (k + 1) * D] = early_ref[8 + k : 9 + k, :]


def front_kernel(
    z,
    heights_ref,
    widths_ref,
    x_ref,
    gain_ref,
    shift_ref,
    w_ref,
    qb_ref,
    vb_ref,
    tap_ref,
    tap_bias_ref,
    back_wide,
    back_tall,
    tq_out,
    tot_out,
    tlse_out,
    v_out,
    kcat_out,
    qtb_out,
    kt_out,
    ot_out,
    lse_out,
    tot_ref,
    tlse_ref,
    v_ref,
    kcat,
    qtb,
    kt,
    ot,
    lse,
    pw,
    pt,
    gw,
    gt,
    low,
    send_wide,
    send_tall,
    recv_wide,
    recv_tall,
    out_wide,
    out_tall,
    t_src,
    t_dst,
    t_q,
    t_k,
    t_v,
    t_vpad,
    t_osum,
    t_kstack,
    qk,
    vpad,
    stage,
    vt,
    vt_all,
    ss0,
    ss1,
    osum,
    lepe,
    wsend,
    wrecv,
    tsend,
    trecv,
    wsend1,
    wrecv1,
    tsend1,
    trecv1,
    local,
):
    greet(z)
    wlim_ref = wide_ends(z, heights_ref, widths_ref)
    tlim_ref = tall_ends(z, heights_ref, widths_ref)
    ttap_ref = tap_ref[:, HALF:]
    tbias_ref = tap_bias_ref[:, HALF:]
    wtap_ref = own_lanes(z, tap_ref[:, :HALF])
    wbias_ref = own_lanes(z, tap_bias_ref[:, :HALF])
    bias = jnp.concatenate([qb_ref[...], jnp.zeros_like(qb_ref), vb_ref[...]], -1)
    dense_in_wide(z, x_ref, gain_ref, shift_ref, w_ref, bias, send_wide, low, pw, gw)
    all_greeted(z)
    cut = up(z.pix, 16)
    parts = [(0, 0, cut), (0, cut, z.pair_rows)]
    parts += [(pair, 0, z.pair_rows) for pair in range(1, z.pairs)]
    wides = [
        Exchange(
            z,
            "col",
            lambda d, pair=pair, at=at, end=end: send_wide.at[d, pair, at:end],
            lambda d, pair=pair, at=at, end=end: recv_wide.at[d, pair, at:end],
            wsend.at[k],
            wrecv.at[k],
        )
        for k, (pair, at, end) in enumerate(parts)
    ]
    tall = Exchange(
        z, "row", lambda d: send_tall.at[d], lambda d: recv_tall.at[d], tsend, trecv
    )
    for wide in wides[:2]:
        wide.start()
    dense_in_tall(z, w_ref, bias, send_tall, low, pt, gt)
    tall.start()
    for wide in wides:
        wide.keep_own()
    tall.keep_own()
    for ref in (t_q, t_k, t_v, t_vpad, t_osum, vpad, qk):
        ref[...] = jnp.zeros_like(ref)
    groups = z.tall_slots // z.tall_group
    early = groups // 2
    half = z.tall_rows1 // 2
    col = lax.axis_index("col")
    row = lax.axis_index("row")
    jobs = []
    own = []

    def wide_back(pair):
        wide_pair_mixture(z, pair, ot, lepe, osum, out_wide)
        job = Exchange(
            z,
            "col",
            lambda d: out_wide.at[d, pair],
            lambda d: back_wide.at[d, pair],
            wsend1.at[pair],
            wrecv1.at[pair],
        )
        job.start()
        jobs.append(job)
        copy = pltpu.make_async_copy(
            out_wide.at[col, pair], back_wide.at[col, pair], local.at[pair]
        )
        copy.start()
        own.append(copy)

    def tall_part(k, start, stop):
        tall_forward(
            z, start, stop, tlim_ref, ttap_ref, tbias_ref, tot_ref, tlse_ref,
            t_src, t_dst, t_q, t_k, t_v, t_vpad, t_osum, t_kstack,
        )
        rows = pl.ds(k * half, half)
        out_tall[:, rows, :] = t_dst[:, rows, :].astype(BF16)
        job = Exchange(
            z,
            "row",
            lambda d: out_tall.at[d, rows],
            lambda d: back_tall.at[d, rows],
            tsend1.at[k],
            trecv1.at[k],
        )
        job.start()
        jobs.append(job)
        copy = pltpu.make_async_copy(
            out_tall.at[row, rows], back_tall.at[row, rows], local.at[2 + k]
        )
        copy.start()
        own.append(copy)

    def save(source, target):
        copy = pltpu.make_async_copy(source, target, local.at[4 + len(saves)])
        copy.start()
        saves.append(copy)

    saves = []
    for pair in range(z.pairs):
        if pair > 0:
            wides[pair + 1].arrive()
        wide_pair_prepare(
            z, pair, wlim_ref, recv_wide, kcat, qtb, kt, qk, vpad, stage, vt, vt_all,
            wides if pair == 0 else (),
        )
        save(kcat.at[pair], kcat_out.at[pair])
        save(qtb.at[pair], qtb_out.at[pair])
        save(kt.at[pair], kt_out.at[pair])
        if pair + 1 == z.pairs:
            v_ref[...] = vpad[PAD : PAD + z.wide_len, :].astype(BF16)
            save(v_ref, v_out)
            wide_lepe(z, wlim_ref, wtap_ref, wbias_ref, vpad, lepe)
            for done in range(pair):
                wide_back(done)
        wide_pair_attend(z, pair, wlim_ref, kcat, qtb, ot, lse, vt, vt_all, ss0, ss1)
        if pair == 0:
            tall.arrive()
            save(recv_tall, tq_out)
            t_src[...] = recv_tall[...].astype(F32)
            tall_part(0, 0, early)
    save(ot, ot_out)
    save(lse, lse_out)
    wide_back(z.pairs - 1)
    tall_part(1, early, groups)
    save(tot_ref, tot_out)
    save(tlse_ref, tlse_out)
    for copy in own + saves:
        copy.wait()
    for job in wides + [tall] + jobs:
        job.sent()
    for job in jobs:
        job.arrive()


def out_wide_planes(z, pair, got, wide, thirds):
    wide[...] = got[:, pair].astype(F32)

    def place(n, start, value):
        lo = low_lanes(value.shape)
        value = jnp.where(lo, value, 0.0) if pair == 0 else jnp.where(lo, 0.0, value)
        count = value.shape[1] * z.images
        value = jnp.swapaxes(value, 0, 1).reshape(count, HALF)
        thirds[n][start * z.images : start * z.images + count, :HALF] = value.astype(BF16)

    both = wide[:, : z.pix, :]
    folded = wide[:, z.pix : z.pix + z.fold, :]
    place(0, 0, both if pair == 0 else turn(both))
    place(1, 0, turn(both) if pair == 0 else both)
    place(2, 0, folded if pair == 0 else turn(folded))
    place(2, z.fold, turn(folded) if pair == 0 else folded)


def out_tall_planes(z, got, tall, thirds):
    tall[...] = got[...].astype(F32)
    count = z.tall_own * z.images
    for n in range(3):
        for s in range(z.stripes):
            blocks = []
            for b in range(z.images):
                at = (((b % z.tall_images) * z.stripes + s) * 3 + n) * z.tall_pad
                blocks.append(tall[b // z.tall_images, at : at + z.tall_own, :])
            value = jnp.swapaxes(jnp.stack(blocks), 0, 1).reshape(count, HALF)
            thirds[n][s * count : (s + 1) * count, HALF:] = value.astype(BF16)


def wide_rows_of(z, third, i):
    rows = []
    for j in range(z.cols):
        at = pl.multiple_of((j * z.rows + i) * z.images, z.images)
        rows.append(third[pl.ds(at, z.images), :HALF])
    return jnp.concatenate(rows, 0)


def tall_rows_of(z, third, i):
    rows = []
    for j in range(z.cols):
        s, jj = divmod(j, SW)
        at = pl.multiple_of(((s * z.rows + i) * SW + jj) * z.images, z.images)
        rows.append(third[pl.ds(at, z.images), HALF:])
    return jnp.concatenate(rows, 0)


def own_rows(z, i):
    T = z.cols * z.images
    return pl.ds(pl.multiple_of(i * T, 16), T)


def out_first(z, x_ref, gain_ref, shift_ref, w_ref, thirds, low, dw, gn, vec):
    T = z.cols * z.images
    D = z.dim
    dw[...] = jnp.zeros_like(dw)
    vec[...] = jnp.zeros_like(vec)

    def one_row(i, carry):
        normed, _ = norm_parts(x_ref[i].astype(F32).reshape(T, D))
        low_i = (normed * gain_ref[...] + shift_ref[...]).astype(BF16)
        for j in range(z.cols):
            at = pl.multiple_of((j * z.rows + i) * z.images, z.images)
            low[pl.ds(at, z.images), :] = low_i[j * z.images : (j + 1) * z.images]
        parts = []
        for third in thirds:
            parts += [wide_rows_of(z, third, i), tall_rows_of(z, third, i)]
        gproj = jnp.concatenate(parts, -1)
        vec[2:3, :] += jnp.sum(gproj[:, :D].astype(F32), 0, keepdims=True)
        vec[3:4, :] += jnp.sum(gproj[:, 2 * D :].astype(F32), 0, keepdims=True)
        dw[...] += mm_tn(low_i, gproj)
        gn[own_rows(z, i), :] = mm_nt(gproj, w_ref[...])
        return carry

    lax.fori_loop(0, z.rows, one_row, 0)


def out_second(z, thirds, low, dw, vec):
    D = z.dim
    for n, third in enumerate(thirds):
        own = third[:, :HALF]
        dw[:, n * D : n * D + HALF] += mm_tn(low[...], own)
        if n != 1:
            row = 2 if n == 0 else 3
            vec[row : row + 1, :HALF] += jnp.sum(own.astype(F32), 0, keepdims=True)


def out_third(z, x_ref, gain_ref, w_ref, thirds, gn, gres, gin_ref, vec):
    T = z.cols * z.images
    D = z.dim

    def one_row(i, carry):
        rows = own_rows(z, i)
        gproj = jnp.concatenate([wide_rows_of(z, third, i) for third in thirds], -1)
        weight = jnp.concatenate([w_ref[:, n * D : n * D + HALF] for n in range(3)], -1)
        gnorm = gn[rows, :] + mm_nt(gproj, weight)
        n1, r1 = norm_parts(x_ref[i].astype(F32).reshape(T, D))
        vec[0:1, :] += jnp.sum(gnorm * n1, 0, keepdims=True)
        vec[1:2, :] += jnp.sum(gnorm, 0, keepdims=True)
        g = gnorm * gain_ref[...]
        gin = gres[rows, :] + r1 * (
            g - jnp.mean(g, -1, keepdims=True) - n1 * jnp.mean(g * n1, -1, keepdims=True)
        )
        gin_ref[i] = gin.reshape(z.cols, z.images, D)
        return carry

    lax.fori_loop(0, z.rows, one_row, 0)


BACK_LOADS = ("dpw", "dw1", "dw2", "tq", "tot", "tlse", "v", "kcat", "qtb", "kt", "ot", "lse")


def back_names(z):
    names = ["heights", "widths", "gw", "gt", "tap", "vec"]
    names += [name + "_any" for name in BACK_LOADS]
    if z.merged:
        names += ["gain", "shift", "x_any", "w_any", "gres_any", "gin", "late", "late_small"]
    else:
        names += ["got_wide", "got_tall", "dwt", "dtt"]
    names += ["sums", "smalls", *BACK_LOADS]
    names += ["recv_wide", "recv_tall", "send_wide", "send_tall", "t_src", "t_gsrc"]
    names += ["t_q", "t_k", "t_v", "t_gpad", "t_vpad", "t_stage", "t_kstack"]
    names += ["gpad", "vpad", "dotb", "delta", "dvl", "dqt", "dkt", "dvt", "stage"]
    names += ["ss0", "ss1", "dp0", "dp1", "ps0", "ps1", "ds0", "ds1"]
    names += ["wsend", "wrecv", "tsend", "trecv", "wsend1", "wrecv1", "tsend1", "trecv1", "local"]
    if z.merged:
        names += ["got_wide", "got_tall", "dwt", "dtt", "wide_block", "dw", "last_vec", "small", "x", "w"]
    return names


def back_kernel(z, plan, late_plan, *refs):
    names = back_names(z)
    r = types.SimpleNamespace(**dict(zip(names, refs)))
    refs = refs[len(names) :]
    size = len(Reduction.scratch(z, plan, z.dim, (8, z.dim)))
    early_refs, late_refs = refs[:size], refs[size:]
    greet(z)
    loads = {}
    for i, name in enumerate(BACK_LOADS + (("x", "w") if z.merged else ())):
        loads[name] = pltpu.make_async_copy(
            getattr(r, name + "_any"), getattr(r, name), r.local.at[5 + i]
        )
        loads[name].start()
    wlim = wide_ends(z, r.heights, r.widths)
    tlim = tall_ends(z, r.heights, r.widths)
    tall_taps = r.tap[:, HALF:]
    wide_taps = own_lanes(z, r.tap[:, :HALF])
    work = Reduction(z, plan, early_refs, r.vec)
    starts, ends = work.steps(r.smalls)
    all_greeted(z)
    tall = Exchange(z, "row", lambda d: r.gt.at[d], lambda d: r.recv_tall.at[d], r.tsend, r.trecv)
    wide = Exchange(z, "col", lambda d: r.gw.at[d], lambda d: r.recv_wide.at[d], r.wsend, r.wrecv)
    tall.start()
    wide.start()
    for name in ("dpw", "dw1", "dw2"):
        loads[name].wait()
    work.fill((r.dpw, r.dw1, r.dw2))
    starts[0]()
    tall.keep_own()
    wide.keep_own()
    for ref in (r.t_q, r.t_k, r.t_v, r.t_gpad, r.t_vpad, r.t_stage):
        ref[...] = jnp.zeros_like(ref)
    r.dtt[...] = jnp.zeros_like(r.dtt)
    loads["tq"].wait()
    r.t_src[...] = r.tq[...].astype(F32)
    loads["tot"].wait()
    loads["tlse"].wait()
    groups = z.tall_slots // z.tall_group
    early = groups // 2
    half = z.tall_rows3 // 2
    col = lax.axis_index("col")
    row = lax.axis_index("row")
    outs = []
    own = []

    def keep(source, target, k):
        copy = pltpu.make_async_copy(source, target, r.local.at[k])
        copy.start()
        own.append(copy)

    def tall_part(k, start, stop):
        tall_backward(
            z, start, stop, tlim, tall_taps, r.tot, r.tlse, r.dtt, r.t_src, r.t_gsrc, r.t_src,
            r.t_q, r.t_k, r.t_v, r.t_gpad, r.t_vpad, r.t_stage, r.t_kstack,
        )
        rows = pl.ds(k * half, half)
        r.send_tall[:, rows, :] = r.t_src[:, rows, :].astype(BF16)
        job = Exchange(
            z,
            "row",
            lambda d: r.send_tall.at[d, rows],
            lambda d: r.got_tall.at[d, rows],
            r.tsend1.at[k],
            r.trecv1.at[k],
        )
        job.start()
        keep(r.send_tall.at[row, rows], r.got_tall.at[row, rows], 2 + k)
        return job

    done = [0]

    def point():
        if done[0] < len(ends) - 1:
            ends[done[0]]()
            starts[done[0] + 1]()
            done[0] += 1

    tall.arrive()
    r.t_gsrc[...] = r.recv_tall[...].astype(F32)
    outs.append(tall_part(0, 0, early))
    point()
    for name in BACK_LOADS[6:]:
        loads[name].wait()
    wide.arrive()
    wide_backward_start(
        z, wlim, r.recv_wide, wide_taps, r.v, r.ot, r.dwt, r.gpad, r.vpad, r.dotb, r.delta, r.dvl,
        r.stage,
    )
    point()
    slots = ((r.ss0, r.dp0, r.ps0, r.ds0), (r.ss1, r.dp1, r.ps1, r.ds1))
    for pair in range(z.pairs):
        wide_pair_backward(
            z, pair, wlim, r.v, r.kcat, r.qtb, r.kt, r.lse, r.dotb, r.delta, r.dvl, r.dqt, r.dkt,
            r.dvt, r.gpad, r.vpad, r.stage, slots, r.send_wide, point, 3 if pair == 0 else 2,
        )
        job = Exchange(
            z,
            "col",
            lambda d, pair=pair: r.send_wide.at[d, pair],
            lambda d, pair=pair: r.got_wide.at[d, pair],
            r.wsend1.at[pair],
            r.wrecv1.at[pair],
        )
        point()
        job.start()
        keep(r.send_wide.at[col, pair], r.got_wide.at[col, pair], pair)
        outs.append(job)
        if pair == 0:
            outs.append(tall_part(1, early, groups))
    while done[0] < len(ends) - 1:
        point()
    if not z.merged:
        ends[-1]()
        r.sums[...] = work.current[...]
        for copy in own:
            copy.wait()
        tall.sent()
        wide.sent()
        for job in outs:
            job.sent()
            job.arrive()
        return
    loads["x"].wait()
    loads["w"].wait()
    back_finish(z, r, late_plan, late_refs, work, ends, outs, own)
    tall.sent()
    wide.sent()
    for job in outs:
        job.sent()


def late_scratch(z, late_plan, late_lanes, small):
    most = max(step[0] for step in late_plan)
    shapes = Reduction.scratch(z, late_plan, late_lanes) * 2
    shapes += [pltpu.VMEM((step[0],) + small, F32) for step in late_plan]
    shapes += [pltpu.SemaphoreType.DMA((len(late_plan), most))] * 2
    return shapes


def back_finish(z, r, late_plan, refs, work, ends, outs, own):
    size = len(Reduction.scratch(z, late_plan, z.dim))
    lates = [Reduction(z, late_plan, refs[:size]), Reduction(z, late_plan, refs[size : 2 * size])]
    (start_a, end_a), (start_b, end_b) = [late.steps() for late in lates]
    refs = refs[2 * size :]
    n = len(late_plan)
    small = SmallSum(late_plan, r.small, refs[:n], refs[n], refs[n + 1])
    low, gn, gres, thirds = r.ps0, r.ss0, r.ss1, (r.ps1, r.ds0, r.ds1)
    load = pltpu.make_async_copy(r.gres_any, gres, r.local.at[4])
    load.start()
    for copy in own:
        copy.wait()
    for job in outs[:-1]:
        job.arrive()
    out_wide_planes(z, 0, r.got_wide, r.wide_block, thirds)
    out_tall_planes(z, r.got_tall, r.t_src, thirds)
    out_first(z, r.x, r.gain, r.shift, r.w, thirds, low, r.dw, gn, r.last_vec)
    lates[0].fill([r.dw.at[:, n * z.dim + HALF : (n + 1) * z.dim] for n in range(3)])
    start_a[0]()
    ends[-1]()
    r.sums[...] = work.current[...]
    outs[-1].arrive()
    out_wide_planes(z, 1, r.got_wide, r.wide_block, thirds)
    out_second(z, thirds, low, r.dw, r.last_vec)
    lates[1].fill([r.dw.at[:, n * z.dim : n * z.dim + HALF] for n in range(3)])
    start_b[0]()
    end_a[0]()
    start_a[1]()
    load.wait()
    out_third(z, r.x, r.gain, r.w, thirds, gn, gres, r.gin, r.last_vec)
    r.small[:, :HALF] = r.dwt[...]
    r.small[:, HALF:] = r.dtt[...]
    r.small[9:13, :] = r.last_vec[:4, :]
    small.start(0)
    end_b[0]()
    start_b[1]()
    end_a[1]()
    start_a[2]()
    small.end(0, r.small)
    small.start(1)
    end_b[1]()
    start_b[2]()
    end_a[2]()
    width = lates[0].full.shape[1]
    r.late[:, :width] = lates[0].current[...]
    small.end(1, r.late_small)
    end_b[2]()
    r.late[:, width:] = lates[1].current[...]


def local_call(kernel, z, name, outs, scratch, scalars, arrays):
    vmem = pl.BlockSpec(memory_space=pltpu.VMEM)
    smem = pl.BlockSpec(memory_space=pltpu.SMEM)
    return pl.pallas_call(
        functools.partial(kernel, z),
        out_shape=tuple(jax.ShapeDtypeStruct(shape, kind) for shape, kind in outs),
        in_specs=[smem] * len(scalars) + [vmem] * len(arrays),
        out_specs=(vmem,) * len(outs),
        scratch_shapes=[pltpu.VMEM(shape, kind) for shape, kind in scratch],
        compiler_params=pltpu.CompilerParams(vmem_limit_bytes=VMEM_LIMIT),
        name=name,
    )(*scalars, *arrays)


def per_device(
    mesh,
    features,
    heights,
    widths,
    norm1_gain,
    norm1_shift,
    qkv_weight,
    query_bias,
    value_bias,
    lepe_weight,
    lepe_bias,
    proj_weight,
    proj_bias,
    norm2_gain,
    norm2_shift,
    fc1_weight,
    fc1_bias,
    fc2_weight,
    fc2_bias,
    cotangent,
):
    z = Sizes(mesh, features.shape)
    B, D, TC, TR = z.images, z.dim, z.cols, z.rows
    x = features.transpose(1, 2, 0, 3)
    ct = cotangent.transpose(1, 2, 0, 3)
    line = lambda v: v.reshape(1, -1)
    FF = fc1_weight.shape[1]
    wide3 = (z.C, z.pairs, z.pair_rows, HALF)
    wide1 = (z.C, z.wide_rows1, z.hc)
    fold1 = (z.C, z.pairs, z.fold_rows, HALF)
    tall3 = (z.R, z.tall_rows3, HALF)
    tall1 = (z.R, z.tall_rows1, HALF)
    flat = up(z.tokens, 16 * B) + 16 * B
    L = z.wide_len
    LT = up(z.tall_len, 128)
    per_head, tail, blocks, tail_lanes, span = wide_plan(z)
    vmem = pl.BlockSpec(memory_space=pltpu.VMEM)
    smem = pl.BlockSpec(memory_space=pltpu.SMEM)
    anywhere = pl.BlockSpec(memory_space=pl.ANY)
    dma = pltpu.SemaphoreType.DMA
    saved = [
        ((L, HALF), BF16),
        ((z.pairs, L, 2 * HALF), BF16),
        ((z.pairs, 2 * HALF, span), BF16),
        ((z.pairs, HALF // 2, L), BF16),
        ((HALF, per_head * z.qb + z.pairs * tail_lanes), F32),
        ((8, z.pairs * span), F32),
    ]
    tall_scratch = [
        ((z.tall_group, LT, HALF), F32),
        ((z.tall_group, LT, HALF), F32),
        ((z.tall_group, LT, HALF), F32),
        ((z.tall_group, LT + 16, HALF), F32),
        ((z.tall_group, LT + 16, HALF), F32),
        ((z.tall_group, BRANCH_HEADS * LT, 2 * HALF), BF16),
    ]
    sems = [
        dma((z.pairs + 1, z.C)),
        dma((z.pairs + 1, z.C)),
        dma((z.R,)),
        dma((z.R,)),
        dma((z.pairs, z.C)),
        dma((z.pairs, z.C)),
        dma((2, z.R)),
        dma((2, z.R)),
        dma((z.C,)),
        dma((z.C,)),
    ]
    shapes = lambda items: tuple(jax.ShapeDtypeStruct(s, k) for s, k in items)
    scratches = lambda items: [pltpu.VMEM(s, k) for s, k in items]

    back_wide, back_tall, tall_qkv, tall_ot, tall_lse, *wide_saved = pl.pallas_call(
        functools.partial(front_kernel, z),
        out_shape=shapes(
            [
                (fold1, BF16),
                (tall1, BF16),
                (tall3, BF16),
                ((z.tall_slots, HALF, LT), F32),
                ((z.tall_slots, 8, LT), F32),
            ]
            + saved
        ),
        in_specs=[smem] * 2 + [vmem] * 8,
        out_specs=(anywhere,) * (5 + len(saved)),
        scratch_shapes=scratches(
            [((z.tall_slots, HALF, LT), F32), ((z.tall_slots, 8, LT), F32)]
            + saved
            + [
                ((3, flat, HALF), F32),
                ((3, flat, HALF), F32),
                (wide3, F32),
                (tall3, F32),
                ((TR, TC * B, D), BF16),
                (wide3, BF16),
                (tall3, BF16),
                (wide3, BF16),
                (tall3, BF16),
                (fold1, BF16),
                (tall1, BF16),
                (tall3, F32),
                (tall1, F32),
            ]
            + tall_scratch
            + [
                ((L, HALF), F32),
                ((L + 2 * PAD, HALF), F32),
                ((z.pair_rows, HALF), F32),
                ((2, HEAD_DIM + 16, L), BF16),
                ((HALF + 16, L), BF16),
                ((L, z.qb), F32),
                ((L, z.qb), F32),
                ((L + z.fold_rows, HALF), F32),
                ((L, HALF), F32),
            ]
        )
        + sems[:8]
        + [dma((18,))],
        compiler_params=pltpu.CompilerParams(
            collective_id=0, has_side_effects=True, vmem_limit_bytes=VMEM_LIMIT
        ),
        name="front",
    )(
        heights,
        widths,
        x,
        line(norm1_gain),
        line(norm1_shift),
        qkv_weight,
        line(query_bias),
        line(value_bias),
        lepe_weight,
        line(lepe_bias),
    )

    vec_rows = 8 + up(FF // D, 8)
    y, gres, gmix_wide, gmix_tall, dproj, dfc1, dfc2, vec_mid = local_call(
        dense_mid_kernel,
        z,
        "dense_mid",
        [
            ((TR, TC, B, D), BF16),
            ((TR, TC, B, D), F32),
            (wide1, BF16),
            (tall1, BF16),
            ((D, D), F32),
            ((D, FF), F32),
            ((FF, D), F32),
            ((vec_rows, D), F32),
        ],
        [((z.tokens, HALF), BF16)] * 2
        + [((z.tokens, HALF), F32)] * 2
        + [((B, z.wide_rows1, HALF), F32), (tall1, F32)]
        + [((z.tokens, D), F32)] * 2
        + [((z.tokens, HALF), F32)]
        + [((z.tokens, D), BF16)] * 3
        + [((TC * B, FF), F32)] * 4
        + [((TC * B, FF), BF16)] * 4,
        [heights, widths],
        [
            back_wide,
            back_tall,
            x,
            ct,
            proj_weight,
            line(proj_bias),
            line(norm2_gain),
            line(norm2_shift),
            fc1_weight,
            line(fc1_bias),
            fc2_weight,
            line(fc2_bias),
        ],
    )
    steps = ("core", "x", "row", "far")
    lanes = reduce_width(z, (dproj.size + dfc1.size + dfc2.size) // D, steps)
    plan = reduce_plan(z, lanes, steps)
    small = (16, D)
    late_steps = ("slab", "far_all")
    late_lanes = reduce_width(z, 3 * HALF, late_steps)
    late_plan = reduce_plan(z, late_lanes, late_steps)
    taps16 = ((16, HALF), F32)
    sums = [((D, lanes), BF16), ((vec_rows, D), F32)]
    arguments = [heights, widths, gmix_wide, gmix_tall, lepe_weight, vec_mid]
    arguments += [dproj, dfc1, dfc2, tall_qkv, tall_ot, tall_lse, *wide_saved]
    in_specs = [smem] * 2 + [vmem] * 4 + [anywhere] * (6 + len(saved))
    more = []
    last_scratch = []
    if z.merged:
        arguments += [line(norm1_gain), line(norm1_shift), x, qkv_weight, gres.reshape(-1, D)]
        in_specs += [vmem] * 2 + [anywhere] * 3
        outs = [((TR, TC, B, D), F32), ((D, 2 * late_lanes), BF16), (small, F32)] + sums
        out_specs = (vmem,) * 5
        more = [(wide3, BF16), (tall3, BF16), taps16, taps16, ((z.C, z.pair_rows, HALF), F32)]
        more += [((D, 3 * D), F32), ((8, D), F32), (small, F32)]
        more += [((TR, TC, B, D), BF16), ((D, 3 * D), BF16)]
        last_scratch = late_scratch(z, late_plan, late_lanes, small)
    else:
        outs = [(wide3, BF16), (tall3, BF16), taps16, taps16] + sums
        out_specs = (anywhere, anywhere) + (vmem,) * 4
    results = pl.pallas_call(
        functools.partial(back_kernel, z, plan, late_plan),
        out_shape=shapes(outs),
        in_specs=in_specs,
        out_specs=out_specs,
        scratch_shapes=scratches(
            [(dproj.shape, F32), (dfc1.shape, F32), (dfc2.shape, F32), (tall3, BF16)]
            + [((z.tall_slots, HALF, LT), F32), ((z.tall_slots, 8, LT), F32)]
            + saved
            + [
                (wide1, BF16),
                (tall1, BF16),
                (wide3, BF16),
                (tall3, BF16),
                (tall3, F32),
                (tall1, F32),
            ]
            + tall_scratch[:5]
            + [((z.tall_group, 3, LT + 16, HALF), F32), tall_scratch[5]]
            + [
                ((L + 2 * PAD, HALF), F32),
                ((L + 2 * PAD, HALF), F32),
                ((HALF, z.pairs * span), BF16),
                ((8, z.pairs * span), F32),
                ((L, HALF), F32),
                ((HALF // 2, per_head * z.qb), F32),
                ((HALF // 2, L), F32),
                ((HALF // 2, L), F32),
                ((z.pair_rows, HALF), F32),
            ]
            + [((L, z.qb), F32)] * 4
            + [((L, z.qb), BF16)] * 4
        )
        + [sems[8], sems[9], sems[2], sems[3], sems[0], sems[1], sems[6], sems[7]]
        + [dma((19,))]
        + scratches(more)
        + Reduction.scratch(z, plan, lanes, (vec_rows, D))
        + last_scratch,
        compiler_params=pltpu.CompilerParams(
            collective_id=1, has_side_effects=True, vmem_limit_bytes=VMEM_LIMIT
        ),
        name="back",
    )(*arguments)
    if z.merged:
        grad_in, late, vec_late, early, vec_mid = results
    else:
        got_wide, got_tall, dwide_taps, dtall_taps, early, vec_mid = results
        grad_in, dqkv, vec_out = local_call(
            dense_out_kernel,
            z,
            "dense_out",
            [((TR, TC, B, D), F32), ((D, 3 * D), F32), ((8, D), F32)],
            [((3, flat, HALF), F32), ((3, flat, HALF), F32), (wide3, F32), (tall3, F32)],
            [],
            [got_wide, got_tall, x, gres, line(norm1_gain), line(norm1_shift), qkv_weight],
        )
        late, vec_late = reduce_last(z, dqkv, vec_out, dwide_taps, dtall_taps, 2)
    dqkv, dproj, dfc1, dfc2, n1g, n1s, qb, vb, taps, lb, pb, n2g, n2s, b1, b2 = local_call(
        split_kernel,
        z,
        "split",
        [((D, 3 * D), F32), (dproj.shape, F32), (dfc1.shape, F32), (dfc2.shape, F32)]
        + [((1, D), F32)] * 4
        + [((9, D), F32)]
        + [((1, D), F32)] * 4
        + [((1, FF), F32), ((1, D), F32)],
        [],
        [],
        [late, vec_late, vec_mid, early],
    )
    flat_of = lambda v: v.reshape(-1)
    return (
        y.transpose(2, 0, 1, 3),
        grad_in.transpose(2, 0, 1, 3),
        flat_of(n1g),
        flat_of(n1s),
        dqkv,
        flat_of(qb),
        flat_of(vb),
        taps,
        flat_of(lb),
        dproj,
        flat_of(pb),
        flat_of(n2g),
        flat_of(n2s),
        dfc1,
        flat_of(b1),
        dfc2,
        flat_of(b2),
    )


def solution(mesh):
    image = P(None, "row", "col", None)
    return jax.shard_map(
        functools.partial(per_device, mesh),
        mesh=mesh,
        in_specs=(image,) + (P(),) * 17 + (image,),
        out_specs=(image, image) + (P(),) * 15,
        check_vma=False,
    )
```

```python
import functools
import math
import types

import jax
import jax.numpy as jnp
from jax import lax
from jax.experimental import pallas as pl
from jax.experimental.pallas import tpu as pltpu
from jax.sharding import PartitionSpec as P

HEADS = 8
SW = 7
BRANCH_HEADS = HEADS // 2
HALF = 128
HEAD_DIM = 32
NORM_EPSILON = 1e-05
MASKED = -1e30
LOG2E = math.log2(math.e)
PAD = 8
VMEM_LIMIT = 62 * 1024 * 1024
MESH = pl.DeviceIdType.MESH
F32 = jnp.float32
BF16 = jnp.bfloat16
NT = (((1,), (1,)), ((), ()))
TN = (((0,), (0,)), ((), ()))


def up(value, unit):
    return -(-value // unit) * unit


def mm(a, b):
    return jnp.dot(a, b, preferred_element_type=F32)


def mm_nt(a, b):
    return lax.dot_general(a, b, NT, preferred_element_type=F32)


def mm_tn(a, b):
    return lax.dot_general(a, b, TN, preferred_element_type=F32)


class Sizes:
    def __init__(self, mesh, shape):
        self.images, self.rows, self.cols, self.dim = shape
        self.R = mesh.shape["row"]
        self.C = mesh.shape["col"]
        self.pix = self.rows * self.cols
        self.tokens = self.pix * self.images
        self.stripes = self.cols // SW
        self.G = self.C // self.images
        self.wide_heads = BRANCH_HEADS // self.G
        self.hc = HALF // self.G
        self.tall_images = self.images // self.R
        self.wide_len = self.C * self.pix
        self.qb = 256 if self.wide_len <= 2048 else 128
        self.merged = self.G == 1 and self.wide_len <= 2048
        self.tall_own = self.rows * SW
        self.tall_len = self.R * self.tall_own
        self.tall_pad = up(self.tall_own, 8)
        self.pairs = self.wide_heads // 2
        self.fold = self.pix // 2
        self.pair_rows = up(self.pix + self.fold, 16)
        self.fold_rows = up(self.fold, 16)
        self.wide_rows1 = up(self.pix, 16)
        self.tall_slots = self.tall_images * self.stripes
        self.tall_group = 4 if self.tall_len <= 128 else 1
        heads = list(range(BRANCH_HEADS))
        self.tall_head_sets = [heads] if self.tall_group > 1 else [[h] for h in heads]
        self.tall_rows1 = self.tall_slots * self.tall_pad
        self.tall_rows3 = 3 * self.tall_rows1


def norm_parts(values):
    average = jnp.mean(values, -1, keepdims=True)
    centred = values - average
    spread = jnp.mean(centred * centred, -1, keepdims=True)
    inverse = lax.rsqrt(spread + NORM_EPSILON)
    return centred * inverse, inverse


def low_lanes(shape):
    return lax.broadcasted_iota(jnp.int32, shape, len(shape) - 1) < HALF // 2


def low_half(rows):
    return lax.broadcasted_iota(jnp.int32, (rows, HALF), 1) < HALF // 2


def turn(value):
    return jnp.concatenate([value[..., HALF // 2 :], value[..., : HALF // 2]], -1)


def dense_in_wide(z, x_ref, gain_ref, shift_ref, w_ref, bias, sw_ref, low_ref, pw, gw):
    B, D, TC, TR = z.images, z.dim, z.cols, z.rows

    def one_row(i, carry):
        x = x_ref[i].astype(F32).reshape(TC * B, D)
        normed, _ = norm_parts(x)
        low = (normed * gain_ref[...] + shift_ref[...]).astype(BF16)
        low_ref[i] = low
        proj = branch_projection(z, low, w_ref, bias, 0)
        for j in range(TC):
            at = pl.multiple_of((j * TR + i) * B, B)
            for n in range(3):
                pw[n, pl.ds(at, B), :] = proj[j, :, n * HALF : (n + 1) * HALF]
        return carry

    lax.fori_loop(0, TR, one_row, 0)
    rows = up(z.pix, 8)
    half = up(z.fold, 8)
    lo = low_half(rows)
    lo_half = low_half(half)
    gw[:, :, z.pix + z.fold :, :] = jnp.zeros_like(gw[:, :, z.pix + z.fold :, :])
    for b in range(B):
        q = pw[0, pl.ds(b, rows, stride=B), :]
        k = pw[1, pl.ds(b, rows, stride=B), :]
        v1 = pw[2, pl.ds(b, half, stride=B), :]
        v2 = pw[2, pl.ds(z.fold * B + b, half, stride=B), :]
        qk = (jnp.where(lo, q, turn(k)), jnp.where(lo, turn(q), k))
        vv = (jnp.where(lo_half, v1, turn(v2)), jnp.where(lo_half, turn(v1), v2))
        for u in range(2):
            d = b * z.G + u // z.pairs
            gw[d, u % z.pairs, :rows, :] = qk[u]
            gw[d, u % z.pairs, z.pix : z.pix + z.fold, :] = vv[u][: z.fold]
    for pair in range(z.pairs):
        sw_ref[:, pair] = gw[:, pair].astype(BF16)


def branch_projection(z, low, w_ref, bias, first):
    D = z.dim
    lanes = [slice(n * D + first, n * D + first + HALF) for n in range(3)]
    weight = jnp.concatenate([w_ref[:, own] for own in lanes], -1)
    own_bias = jnp.concatenate([bias[:, own] for own in lanes], -1)
    return (mm(low, weight) + own_bias).reshape(z.cols, z.images, 3 * HALF)


def dense_in_tall(z, w_ref, bias, st_ref, low_ref, pt, gt):
    B, TC, TR = z.images, z.cols, z.rows

    def one_row(i, carry):
        proj = branch_projection(z, low_ref[i], w_ref, bias, HALF)
        for j in range(TC):
            s, jj = divmod(j, SW)
            at = pl.multiple_of(((s * TR + i) * SW + jj) * B, B)
            for n in range(3):
                pt[n, pl.ds(at, B), :] = proj[j, :, n * HALF : (n + 1) * HALF]
        return carry

    lax.fori_loop(0, TR, one_row, 0)
    size = up(z.tall_own, 8)
    for b in range(B):
        for n in range(3):
            for s in range(z.stripes):
                part = pt[n, pl.ds(s * z.tall_own * B + b, size, stride=B), :]
                at = (((b % z.tall_images) * z.stripes + s) * 3 + n) * z.tall_pad
                gt[b // z.tall_images, at : at + size, :] = part
    st_ref[...] = gt[...].astype(BF16)


def erf_parts(values):
    cdf = 0.5 * (1.0 + lax.erf(values * (0.5**0.5)))
    density = jnp.exp(-0.5 * values * values) * (1.0 / math.sqrt(2.0 * math.pi))
    return cdf, density


def pack(full, pieces):
    D = full.shape[0]
    at = 0
    for ref in pieces:
        for k in range(ref.shape[0] // D):
            width = ref.shape[1]
            full[:, at : at + width] = ref[k * D : (k + 1) * D, :].astype(BF16)
            at += width
    if at < full.shape[1]:
        full[:, at:] = jnp.zeros((D, full.shape[1] - at), BF16)


def dense_mid_kernel(
    z,
    heights_ref,
    widths_ref,
    rw_ref,
    rt_ref,
    x_ref,
    ct_ref,
    pw_ref,
    pb_ref,
    gain_ref,
    shift_ref,
    w1_ref,
    b1_ref,
    w2_ref,
    b2_ref,
    y_ref,
    gres_ref,
    gw_ref,
    gt_ref,
    dsum_ref,
    vec_ref,
    dpw_ref,
    dw1_ref,
    dw2_ref,
    mw,
    mt,
    gmw,
    gmt,
    gws,
    gts,
    res,
    n2s,
    r2s,
    gys,
    acts,
    mixes,
    pre0,
    pre1,
    gh0,
    gh1,
    hid0,
    hid1,
    gpre0,
    gpre1,
):
    B, D, TC, TR = z.images, z.dim, z.cols, z.rows
    T = TC * B
    count = z.tall_own * B
    blocks = [rw_ref[:, u].astype(F32)[:, : z.fold, :] for u in range(z.pairs)]
    if z.G > 1:
        pairs = rw_ref[:, 0].astype(F32).reshape(B, z.G, z.fold_rows, HALF)
        blocks = [pairs[:, g, : z.fold, :] for g in range(2)]
    lo = low_lanes((B, z.fold, HALF))
    for half, value in enumerate(
        (jnp.where(lo, blocks[0], turn(blocks[1])), jnp.where(lo, turn(blocks[0]), blocks[1]))
    ):
        size = z.fold * B
        value = jnp.swapaxes(value, 0, 1).reshape(size, HALF)
        mw[half * size : (half + 1) * size, :] = value.astype(BF16)
    gts[...] = rt_ref[...].astype(F32)
    for s in range(z.stripes):
        rows = []
        for b in range(B):
            at = ((b % z.tall_images) * z.stripes + s) * z.tall_pad
            rows.append(gts[b // z.tall_images, at : at + z.tall_own, :])
        value = jnp.swapaxes(jnp.stack(rows), 0, 1).reshape(count, HALF)
        mt[s * count : (s + 1) * count, :] = value.astype(BF16)
    for ref in (dpw_ref, dw1_ref, dw2_ref, vec_ref):
        ref[...] = jnp.zeros_like(ref)
    row_start = lax.axis_index("row") * TR
    col_start = lax.axis_index("col") * TC
    image = lax.broadcasted_iota(jnp.int32, (B, D), 0)
    height = jnp.zeros((B, D), jnp.int32)
    width = jnp.zeros((B, D), jnp.int32)
    for b in range(B):
        height = jnp.where(image == b, heights_ref[b], height)
        width = jnp.where(image == b, widths_ref[b], width)
    below_cols = (lax.broadcasted_iota(jnp.int32, (TC, B, D), 0) + col_start) < width[None]
    slots = ((pre0, gh0, hid0, gpre0), (pre1, gh1, hid1, gpre1))

    def places(i, j):
        s, jj = divmod(j, SW)
        return (j * TR + i) * B, ((s * TR + i) * SW + jj) * B

    def first(i):
        pre, gh = slots[i % 2][:2]
        own = slice(i * T, (i + 1) * T)
        at = [places(i, j) for j in range(TC)]
        wide = jnp.concatenate([mw[w : w + B, :] for w, _ in at], 0)
        tall = jnp.concatenate([mt[t : t + B, :] for _, t in at], 0)
        mixture = jnp.concatenate([wide, tall], -1)
        mixes[own, :] = mixture
        x = x_ref[i].astype(F32).reshape(T, D)
        residual = x + (mm(mixture, pw_ref[...]) + pb_ref[...])
        res[own, :] = residual
        n2, r2 = norm_parts(residual)
        n2s[own, :] = n2
        r2s[own, :] = jnp.broadcast_to(r2, (T, HALF))
        act = (n2 * gain_ref[...] + shift_ref[...]).astype(BF16)
        acts[own, :] = act
        pre[...] = mm(act, w1_ref[...]) + b1_ref[...]
        below_rows = (i + row_start) < height[None]
        inside = jnp.logical_and(below_cols, below_rows)
        gy = jnp.where(inside, ct_ref[i].astype(F32), 0.0).reshape(T, D).astype(BF16)
        gys[own, :] = gy
        gh[...] = mm_nt(gy, w2_ref[...])

    def second(i):
        pre, gh, hid, gpre = slots[i % 2]
        FF = pre.shape[1]
        for at, size in key_tiles(FF, 256):
            lanes = slice(at, at + size)
            value = pre[:, lanes]
            cdf, density = erf_parts(value)
            hid[:, lanes] = (value * cdf).astype(BF16)
            low = (gh[:, lanes] * (cdf + value * density)).astype(BF16)
            gpre[:, lanes] = low
            total = jnp.sum(low.astype(F32), 0, keepdims=True)
            for k in range(size // D):
                row = 8 + at // D + k
                vec_ref[row : row + 1, :] += total[:, k * D : (k + 1) * D]

    def third(i):
        hid, gpre = slots[i % 2][2:]
        own = slice(i * T, (i + 1) * T)
        out = res[own, :] + (mm(hid[...], w2_ref[...]) + b2_ref[...])
        y_ref[i] = out.astype(BF16).reshape(TC, B, D)
        gy = gys[own, :]
        dw2_ref[...] += mm_tn(hid[...], gy)
        dw1_ref[...] += mm_tn(acts[own, :], gpre[...])
        gact = mm_nt(gpre[...], w1_ref[...])
        n2 = n2s[own, :]
        r2 = r2s[own, :1]
        gy = gy.astype(F32)
        g = gact * gain_ref[...]
        gres = gy + r2 * (
            g - jnp.mean(g, -1, keepdims=True) - n2 * jnp.mean(g * n2, -1, keepdims=True)
        )
        gres_ref[i] = gres.reshape(TC, B, D)
        gattn = gres.astype(BF16)
        dpw_ref[...] += mm_tn(mixes[own, :], gattn)
        gmix = mm_nt(gattn, pw_ref[...]).astype(BF16).astype(F32)
        vec_ref[0:1, :] += jnp.sum(gact * n2, 0, keepdims=True)
        vec_ref[1:2, :] += jnp.sum(gact, 0, keepdims=True)
        vec_ref[2:3, :] += jnp.sum(gattn.astype(F32), 0, keepdims=True)
        vec_ref[3:4, :] += jnp.sum(gy, 0, keepdims=True)
        vec_ref[4:5, :] += jnp.sum(gmix, 0, keepdims=True)
        gm3 = gmix.reshape(TC, B, D)
        for j in range(TC):
            wide_at, tall_at = places(i, j)
            gmw[wide_at : wide_at + B, :] = gm3[j, :, :HALF]
            gmt[tall_at : tall_at + B, :] = gm3[j, :, HALF:]

    for t in range(TR + 2):
        if t < TR:
            first(t)
        if 0 <= t - 1 < TR:
            second(t - 1)
        if t - 2 >= 0:
            third(t - 2)
    pack(dsum_ref, (dpw_ref, dw1_ref, dw2_ref))
    gws[:, : z.pix, :] = jnp.swapaxes(gmw[...].reshape(z.pix, B, HALF), 0, 1)
    if z.G == 1:
        gw_ref[...] = gws[...].astype(BF16)
    else:
        for b in range(B):
            for g in range(z.G):
                gw_ref[b * z.G + g] = gws[b, :, g * z.hc : (g + 1) * z.hc].astype(BF16)
    for s in range(z.stripes):
        value = gmt[s * count : (s + 1) * count, :].reshape(z.tall_own, B, HALF)
        value = jnp.swapaxes(value, 0, 1)
        for b in range(B):
            at = ((b % z.tall_images) * z.stripes + s) * z.tall_pad
            gts[b // z.tall_images, at : at + z.tall_own, :] = value[b]
    gt_ref[...] = gts[...].astype(BF16)


def dense_out_kernel(
    z,
    rw_ref,
    rt_ref,
    x_ref,
    gres_ref,
    gain_ref,
    shift_ref,
    w_ref,
    gin_ref,
    dw_ref,
    vec_ref,
    pw,
    pt,
    gw,
    gt,
):
    B, D, TC, TR = z.images, z.dim, z.cols, z.rows
    T = TC * B
    gw[...] = rw_ref[...].astype(F32)
    gt[...] = rt_ref[...].astype(F32)
    lo = low_half(z.pix)
    lo_half = low_half(z.fold)
    for b in range(B):
        qk = []
        vv = []
        for u in range(2):
            d = b * z.G + u // z.pairs
            qk.append(gw[d, u % z.pairs, : z.pix, :])
            vv.append(gw[d, u % z.pairs, z.pix : z.pix + z.fold, :])
        places = pl.ds(b, z.pix, stride=B)
        pw[0, places, :] = jnp.where(lo, qk[0], turn(qk[1]))
        pw[1, places, :] = jnp.where(lo, turn(qk[0]), qk[1])
        pw[2, pl.ds(b, z.fold, stride=B), :] = jnp.where(lo_half, vv[0], turn(vv[1]))
        pw[2, pl.ds(z.fold * B + b, z.fold, stride=B), :] = jnp.where(
            lo_half, turn(vv[0]), vv[1]
        )
        for n in range(3):
            for s in range(z.stripes):
                at = (((b % z.tall_images) * z.stripes + s) * 3 + n) * z.tall_pad
                pt[n, pl.ds(s * z.tall_own * B + b, z.tall_own, stride=B), :] = gt[
                    b // z.tall_images, at : at + z.tall_own, :
                ]
    dw_ref[...] = jnp.zeros_like(dw_ref)
    vec_ref[...] = jnp.zeros_like(vec_ref)

    def one_row(i, carry):
        x = x_ref[i].astype(F32).reshape(T, D)
        n1, r1 = norm_parts(x)
        low = (n1 * gain_ref[...] + shift_ref[...]).astype(BF16)
        lanes = []
        for n in range(3):
            wide = []
            tall = []
            for j in range(TC):
                s, jj = divmod(j, SW)
                wide_at = pl.multiple_of((j * TR + i) * B, B)
                tall_at = pl.multiple_of(((s * TR + i) * SW + jj) * B, B)
                wide.append(pw[n, pl.ds(wide_at, B), :])
                tall.append(pt[n, pl.ds(tall_at, B), :])
            lanes.append(jnp.concatenate(wide, 0))
            lanes.append(jnp.concatenate(tall, 0))
        gproj = jnp.concatenate(lanes, -1)
        vec_ref[2:3, :] += jnp.sum(gproj[:, :D], 0, keepdims=True)
        vec_ref[3:4, :] += jnp.sum(gproj[:, 2 * D :], 0, keepdims=True)
        gproj = gproj.astype(BF16)
        dw_ref[...] += mm_tn(low, gproj)
        gn = mm_nt(gproj, w_ref[...])
        vec_ref[0:1, :] += jnp.sum(gn * n1, 0, keepdims=True)
        vec_ref[1:2, :] += jnp.sum(gn, 0, keepdims=True)
        g = gn * gain_ref[...]
        gin = gres_ref[i].reshape(T, D) + r1 * (
            g - jnp.mean(g, -1, keepdims=True) - n1 * jnp.mean(g * n1, -1, keepdims=True)
        )
        gin_ref[i] = gin.reshape(TC, B, D)
        return carry

    lax.fori_loop(0, TR, one_row, 0)


def key_tiles(length, tile):
    return [(at, min(tile, length - at)) for at in range(0, length, tile)]


def token_places(start, count, lanes):
    token = (lax.broadcasted_iota(jnp.int32, (count, lanes), 0) + start).astype(F32)
    along = jnp.floor((token + 0.5) * (1.0 / SW))
    across = token - along * SW
    return along, across


def conv_forward(vpad, base, count, kernels, across):
    total = None
    for a in (-1, 0, 1):
        inner = None
        for l in (-1, 0, 1):
            term = kernels(a, l) * vpad[base + SW * l + a : base + SW * l + a + count, :]
            inner = term if inner is None else inner + term
        if a == -1:
            inner = jnp.where(across >= 1, inner, 0.0)
        if a == 1:
            inner = jnp.where(across <= SW - 2, inner, 0.0)
        total = inner if total is None else total + inner
    return total


def conv_backward(gpad, base, count, kernels, across):
    total = None
    for a in (-1, 0, 1):
        inner = None
        for l in (-1, 0, 1):
            at = base - SW * l - a
            term = kernels(a, l) * gpad[at : at + count, :]
            inner = term if inner is None else inner + term
        if a == -1:
            inner = jnp.where(across <= SW - 2, inner, 0.0)
        if a == 1:
            inner = jnp.where(across >= 1, inner, 0.0)
        total = inner if total is None else total + inner
    return total


def wide_tap(a, l):
    return 3 * (a + 1) + (l + 1)


def tall_tap(a, l):
    return 3 * (l + 1) + (a + 1)


def head_lanes(h, rows):
    lane = lax.broadcasted_iota(jnp.int32, (rows, HALF), 1)
    return jnp.logical_and(lane >= h * HEAD_DIM, lane < (h + 1) * HEAD_DIM)


def wide_plan(z):
    per_head = z.wide_len // z.qb
    tail = z.wide_len - per_head * z.qb
    blocks = 2 * per_head
    lanes = up(2 * tail, 128)
    return per_head, tail, blocks, lanes, blocks * z.qb + lanes


def diagonal(tail, first, lanes):
    channel = lax.broadcasted_iota(jnp.int32, (HALF, lanes), 0) - first * HEAD_DIM
    query = lax.broadcasted_iota(jnp.int32, (HALF, lanes), 1)
    keep = channel < -HALF
    for h in range(2):
        keep = jnp.logical_or(
            keep,
            jnp.logical_and(
                jnp.logical_and(channel >= h * HEAD_DIM, channel < (h + 1) * HEAD_DIM),
                jnp.logical_and(query >= h * tail, query < (h + 1) * tail),
            ),
        )
    return keep


def tail_columns(rows, tail, first, lanes):
    copies = [rows, rows]
    if lanes > 2 * tail:
        copies.append(jnp.zeros((lanes - 2 * tail, HALF), F32))
    return jnp.where(diagonal(tail, first, lanes), jnp.concatenate(copies, 0).T, 0.0)


def tail_rows(columns, tail):
    flat = columns.T
    return flat[:tail] + flat[tail : 2 * tail]


def head_rows_mask(h, value):
    row = lax.broadcasted_iota(jnp.int32, value.shape, 0)
    keep = jnp.logical_and(row >= h * HEAD_DIM, row < (h + 1) * HEAD_DIM)
    return jnp.where(keep, value, 0.0)


def between(value, high):
    return jnp.maximum(jnp.minimum(value, high), 0)


def wide_ends(z, heights_ref, widths_ref):
    image = lax.axis_index("col") // z.G
    start = lax.axis_index("row") * z.rows
    return (
        between(heights_ref[image] - start, z.rows),
        between(widths_ref[image], z.C * z.cols),
    )


def tall_ends(z, heights_ref, widths_ref):
    def ends(p):
        image = lax.axis_index("row") * z.tall_images + p // z.stripes
        start = lax.axis_index("col") * z.cols + lax.rem(p, z.stripes) * SW
        return (
            between(widths_ref[image] - start, SW),
            between(heights_ref[image], z.R * z.rows),
        )

    return ends


def own_lanes(z, value):
    if z.G == 1:
        return value
    turned = jnp.where(lax.rem(lax.axis_index("col"), z.G) == 0, value, turn(value))
    return jnp.where(low_half(value.shape[0]), turned, 0.0)


def wide_limits(lim_ref):
    across_limit, along_limit = lim_ref
    empty = across_limit * along_limit == 0
    scale = jnp.where(empty, 1e-20, LOG2E * HEAD_DIM**-0.5)
    return across_limit, along_limit, empty, scale


def wide_inside(lim_ref, at, size):
    along, across = token_places(at, size, HALF)
    return jnp.logical_and(across < lim_ref[0], along < lim_ref[1]), across


def wide_pair_prepare(
    z, pair, lim_ref, recv, kcat, qtb, kt, qk, vpad, stage, vt, vt_all, waits=()
):
    L = z.wide_len
    per_head, tail, blocks, tail_lanes, span = wide_plan(z)
    full = per_head * z.qb
    _, _, empty, _ = wide_limits(lim_ref)
    cut = up(z.pix, 16)
    if waits:
        waits[0].arrive()
        for later in waits[2:]:
            later.start()
    for c in range(z.C):
        stage[:cut, :] = recv[c, pair, :cut].astype(F32)
        qk[c * z.pix : (c + 1) * z.pix, :] = stage[: z.pix, :]
    ones = jnp.where(lax.broadcasted_iota(jnp.int32, (HALF, z.qb), 0) == 0, 1.0, 0.0).astype(BF16)

    def keys(at, size):
        rows = pl.ds(at, size)
        both = qk[rows, :]
        kcat[pair, rows, :HALF] = both.astype(BF16)
        inside, _ = wide_inside(lim_ref, at, size)
        allowed = jnp.logical_or(inside, empty)
        lane = lax.broadcasted_iota(jnp.int32, (size, HALF), 1) == 0
        bias = jnp.where(jnp.logical_and(lane, jnp.logical_not(allowed)), MASKED, 0.0)
        kcat[pair, rows, HALF:] = bias.astype(BF16)
        return both

    def flip(n, carry):
        at = pl.multiple_of(n * z.qb, z.qb)
        both = keys(at, z.qb).T
        kt[pair, :, pl.ds(at, z.qb)] = both[HALF // 2 :].astype(BF16)
        for h in range(2):
            cols = pl.ds(pl.multiple_of((h * per_head + n) * z.qb, z.qb), z.qb)
            parts = [jnp.zeros((HALF // 2, z.qb), F32)] + [jnp.zeros((HEAD_DIM, z.qb), F32)] * 2
            parts[1 + h] = both[h * HEAD_DIM : (h + 1) * HEAD_DIM]
            qtb[pair, :HALF, cols] = jnp.concatenate(parts, 0).astype(BF16)
            qtb[pair, HALF:, cols] = ones
        return carry

    lax.fori_loop(0, per_head, flip, 0)
    tail_cols = slice(blocks * z.qb, span)
    tail_both = keys(full, tail)
    kt[pair, :, full:L] = tail_both.T[HALF // 2 :].astype(BF16)
    qtb[pair, :HALF, tail_cols] = tail_columns(turn(tail_both), tail, 2, tail_lanes).astype(BF16)
    qtb[pair, HALF:, tail_cols] = ones[:, :tail_lanes]
    if waits:
        waits[1].arrive()
    lo = low_half(z.fold)
    start = z.pix // 16 * 16
    for c in range(z.C):
        stage[start:, :] = recv[c, pair, start:].astype(F32)
        v = stage[z.pix : z.pix + z.fold, :]
        at = c * z.pix
        one = slice(PAD + at, PAD + at + z.fold)
        two = slice(PAD + at + z.fold, PAD + at + z.pix)
        if pair == 0:
            vpad[one, :] = jnp.where(lo, v, 0.0)
            vpad[two, :] = jnp.where(lo, turn(v), 0.0)
        else:
            vpad[one, :] = jnp.where(lo, vpad[one, :], turn(v))
            vpad[two, :] = jnp.where(lo, vpad[two, :], v)

    def values(at, size):
        vt_full = vpad[pl.ds(pl.multiple_of(at + PAD, 8), size), :].T
        first = lax.broadcasted_iota(jnp.int32, (16, size), 0) == 0
        first = jnp.where(first, 1.0, 0.0)
        vt_all[:, pl.ds(at, size)] = jnp.concatenate([vt_full, first], 0).astype(BF16)
        for h in range(2):
            own = (2 * pair + h) * HEAD_DIM
            own = vt_full[own : own + HEAD_DIM]
            vt[h, :, pl.ds(at, size)] = jnp.concatenate([own, first], 0).astype(BF16)

    def flip_values(n, carry):
        values(pl.multiple_of(n * z.qb, z.qb), z.qb)
        return carry

    lax.fori_loop(0, per_head, flip_values, 0)
    values(full, tail)


def wide_pair_attend(z, pair, lim_ref, kcat, qtb, ot, lse, vt, vt_all, ss0, ss1):
    L = z.wide_len
    per_head, tail, blocks, tail_lanes, span = wide_plan(z)
    full = per_head * z.qb
    base = pair * span
    _, _, _, scale = wide_limits(lim_ref)
    tail_cols = slice(blocks * z.qb, span)

    def scores(cols, slot):
        s = mm(kcat[pair], qtb[pair, :, cols])
        slot[...] = s
        return jnp.max(jnp.max(s.reshape(L // 8, 8, s.shape[1]), 0), 0, keepdims=True)

    def block_scores(n, slot):
        return scores(pl.ds(pl.multiple_of(n * z.qb, z.qb), z.qb), slot)

    def weigh(values, slot, top):
        p = jnp.exp2((slot[...] - top) * scale).astype(BF16)
        acc = mm(values, p)
        at = acc.shape[0] - 16
        total = acc[at : at + 1]
        return acc[:at] * (1.0 / total), top * scale + jnp.log2(total)

    def block_rest(n, slot, top):
        h = n // per_head
        out, low = weigh(vt[h], slot, top)
        rows = pl.ds(pl.multiple_of((2 * pair + h) * HEAD_DIM, HEAD_DIM), HEAD_DIM)
        ot[rows, pl.ds(pl.multiple_of((n - h * per_head) * z.qb, z.qb), z.qb)] = out
        lse[0:1, pl.ds(pl.multiple_of(base + n * z.qb, 128), z.qb)] = low

    def two(m, top):
        n = 2 * m
        top_next = block_scores(n + 1, ss1)
        block_rest(n, ss0, top)
        top = block_scores(n + 2, ss0)
        block_rest(n + 1, ss1, top_next)
        return top

    top = lax.fori_loop(0, blocks // 2 - 1, two, block_scores(0, ss0))
    top_next = block_scores(blocks - 1, ss1)
    block_rest(blocks - 2, ss0, top)
    tail_slot = ss0.at[:, :tail_lanes]
    top = scores(tail_cols, tail_slot)
    block_rest(blocks - 1, ss1, top_next)
    out, low = weigh(vt_all[...], tail_slot, top)
    lse[0:1, base + blocks * z.qb : base + span] = low
    out = jnp.where(diagonal(tail, 2 * pair, tail_lanes), out, 0.0)
    ot[:, full + pair * tail_lanes : full + (pair + 1) * tail_lanes] = out


def wide_lepe(z, lim_ref, lw_ref, lb_ref, vpad, lepe):
    L = z.wide_len
    for at, size in key_tiles(L, z.qb):
        inside, _ = wide_inside(lim_ref, at, size)
        rows = slice(at + PAD, at + PAD + size)
        vpad[rows, :] = jnp.where(inside, vpad[rows, :], 0.0)

    def taps(a, l):
        t = wide_tap(a, l)
        return lw_ref[t : t + 1, :]

    for at, size in key_tiles(L, 224):
        along, across = token_places(at, size, HALF)
        lepe[at : at + size, :] = conv_forward(vpad, at + PAD, size, taps, across) + lb_ref


def wide_pair_mixture(z, pair, ot, lepe, osum, out_ref):
    L = z.wide_len
    per_head, tail, _, tail_lanes, _ = wide_plan(z)
    full = per_head * z.qb

    def doubled(value):
        lo = low_half(value.shape[0])
        return jnp.where(lo, value, turn(value)) if pair == 0 else jnp.where(lo, turn(value), value)

    def finish(n, carry):
        rows = pl.ds(pl.multiple_of(n * z.qb, z.qb), z.qb)
        osum[rows, :] = doubled(ot[:, rows].T + lepe[rows, :])
        return carry

    lax.fori_loop(0, per_head, finish, 0)
    last = tail_rows(ot[:, full + pair * tail_lanes : full + (pair + 1) * tail_lanes], tail)
    osum[full:L, :] = doubled(last + lepe[full:L, :])
    lo = low_half(z.fold_rows)
    for c in range(z.C):
        at = c * z.pix
        one = osum[at : at + z.fold_rows, :]
        two = osum[at + z.fold : at + z.fold + z.fold_rows, :]
        out_ref[c, pair] = jnp.where(lo, one, two).astype(BF16)


def wide_backward_start(z, lim_ref, recv, lw_ref, v_ref, ot, dlw_ref, gpad, vpad, dotb, delta, dvl, stage):
    L = z.wide_len
    per_head, tail, blocks, tail_lanes, span = wide_plan(z)
    full = per_head * z.qb
    gpad[...] = jnp.zeros_like(gpad)
    vpad[...] = jnp.zeros_like(vpad)
    stage[...] = jnp.zeros_like(stage)
    for c in range(z.C):
        stage[: z.wide_rows1, : z.hc] = recv[c].astype(F32)
        gpad[PAD + c * z.pix : PAD + (c + 1) * z.pix, :] = stage[: z.pix, :]

    def prepare(at, size):
        rows = pl.ds(at, size)
        padded = pl.ds(pl.multiple_of(at + PAD, 8), size)
        inside, _ = wide_inside(lim_ref, at, size)
        vpad[padded, :] = jnp.where(inside, v_ref[rows, :].astype(F32), 0.0)
        return gpad[padded, :]

    def flip(n, carry):
        at = pl.multiple_of(n * z.qb, z.qb)
        gt = prepare(at, z.qb).T
        prod = gt * ot[:, pl.ds(at, z.qb)]
        for h in range(z.wide_heads):
            first = (h // 2) * span + (h % 2) * full
            cols = pl.ds(pl.multiple_of(first + n * z.qb, 128), z.qb)
            dotb[:, cols] = head_rows_mask(h, gt).astype(BF16)
            delta[0:1, cols] = jnp.sum(
                prod[h * HEAD_DIM : (h + 1) * HEAD_DIM], 0, keepdims=True
            )
        return carry

    lax.fori_loop(0, per_head, flip, 0)
    last = prepare(full, tail)
    for pair in range(z.pairs):
        cols = slice(pair * span + blocks * z.qb, (pair + 1) * span)
        gt = tail_columns(last, tail, 2 * pair, tail_lanes)
        dotb[:, cols] = gt.astype(BF16)
        out = ot[:, full + pair * tail_lanes : full + (pair + 1) * tail_lanes]
        delta[0:1, cols] = jnp.sum(gt * out, 0, keepdims=True)

    def taps(a, l):
        t = wide_tap(a, l)
        return lw_ref[t : t + 1, :]

    sums_of = {}
    for at, size in key_tiles(L, 224):
        inside, across = wide_inside(lim_ref, at, size)
        lepe = conv_backward(gpad, at + PAD, size, taps, across)
        dvl[at : at + size, :] = jnp.where(inside, lepe, 0.0)
        add_kernel_sums(sums_of, gpad, vpad, at + PAD, size, across, wide_tap)
    dlw_ref[...] = jnp.zeros_like(dlw_ref)
    for t, value in sums_of.items():
        dlw_ref[t : t + 1, :] = jnp.sum(value, 0, keepdims=True)


def wide_pair_backward(
    z,
    pair,
    lim_ref,
    v_ref,
    kcat,
    qtb,
    kt,
    lse,
    dotb,
    delta,
    dvl,
    dqt,
    dkt,
    dvt,
    dqk,
    dvv,
    stage,
    slots,
    out_ref,
    midway,
    segments,
):
    L = z.wide_len
    per_head, tail, blocks, tail_lanes, span = wide_plan(z)
    full = per_head * z.qb
    base = pair * span
    _, _, _, scale = wide_limits(lim_ref)
    dkt[...] = jnp.zeros_like(dkt)
    dvt[...] = jnp.zeros_like(dvt)
    tail_cols = slice(blocks * z.qb, span)

    def shifted(cols):
        if isinstance(cols, slice):
            return slice(base + cols.start, base + cols.stop)
        return pl.ds(pl.multiple_of(base + cols.start, 128), cols.size)

    def products(cols, s_slot, dp_slot):
        s_slot[...] = mm(kcat[pair], qtb[pair, :, cols])
        dp_slot[...] = mm(v_ref[...], dotb[:, shifted(cols)])

    def weights(cols, s_slot, dp_slot, p_slot, ds_slot):
        low = lse[0:1, shifted(cols)]
        dlt = delta[0:1, shifted(cols)]
        for at, size in key_tiles(L, z.qb):
            rows = slice(at, at + size)
            p = jnp.exp2(s_slot[rows, :] * scale - low)
            p_slot[rows, :] = p.astype(BF16)
            ds_slot[rows, :] = (p * (dp_slot[rows, :] - dlt)).astype(BF16)

    def block_cols(n):
        return pl.ds(pl.multiple_of(n * z.qb, z.qb), z.qb)

    def first(n, k):
        products(block_cols(n), *slots[k][:2])

    def second(n, k):
        weights(block_cols(n), *slots[k])

    def third(n, k):
        h = n // per_head
        p_slot, ds_slot = slots[k][2:]
        cols = block_cols(n)
        rows = pl.ds(pl.multiple_of(h * HEAD_DIM, HEAD_DIM), HEAD_DIM)
        g_rows = pl.ds(pl.multiple_of((2 * pair + h) * HEAD_DIM, HEAD_DIM), HEAD_DIM)
        q_rows = pl.ds(pl.multiple_of(HALF // 2 + h * HEAD_DIM, HEAD_DIM), HEAD_DIM)
        dvt[rows, :] += mm_nt(dotb[g_rows, shifted(cols)], p_slot[...])
        dkt[rows, :] += mm_nt(qtb[pair, q_rows, cols], ds_slot[...])
        at = pl.ds(pl.multiple_of((n - h * per_head) * z.qb, z.qb), z.qb)
        dqt[rows, at] = mm(kt[pair, rows, :], ds_slot[...])

    first(0, 0)
    first(1, 1)
    second(0, 0)

    def two(m, carry):
        n = 2 * m
        first(n, 0)
        second(n - 1, 1)
        third(n - 2, 0)
        first(n + 1, 1)
        second(n, 0)
        third(n - 1, 1)
        return carry

    marks = [1 + (blocks // 2 - 1) * k // segments for k in range(segments + 1)]
    for k in range(segments):
        lax.fori_loop(marks[k], marks[k + 1], two, 0)
        if k + 1 < segments:
            midway()
    tail_slots = [ref.at[:, :tail_lanes] for ref in slots[0]]
    products(tail_cols, *tail_slots[:2])
    second(blocks - 1, 1)
    third(blocks - 2, 0)
    weights(tail_cols, *tail_slots)
    third(blocks - 1, 1)
    half = HALF // 2
    dvt[...] += mm_nt(dotb[pair * half : (pair + 1) * half, shifted(tail_cols)], tail_slots[2][...])
    dkt[...] += mm_nt(qtb[pair, half:HALF, tail_cols], tail_slots[3][...])
    last = mm(kt[pair], tail_slots[3][...])
    empty_half = jnp.zeros((half, tail_lanes), F32)
    last = jnp.concatenate([last, empty_half], 0)
    last = jnp.where(diagonal(tail, 0, tail_lanes), last, 0.0)
    norm = HEAD_DIM**-0.5
    dk_last = jnp.concatenate([jnp.zeros((half, tail), F32), dkt[:, full:L]], 0).T
    dqk[full:L, :] = (tail_rows(last, tail) + dk_last) * norm

    def doubled(value):
        lo = low_half(value.shape[0])
        return jnp.where(lo, value, turn(value)) if pair == 0 else jnp.where(lo, turn(value), value)

    def finish(n, carry):
        rows = pl.ds(pl.multiple_of(n * z.qb, z.qb), z.qb)
        dqk[rows, :] = jnp.concatenate([dqt[:, rows], dkt[:, rows]], 0).T * norm
        dv = dvt[:, rows]
        dvv[rows, :] = jnp.concatenate([dv, dv], 0).T + doubled(dvl[rows, :])
        return carry

    lax.fori_loop(0, per_head, finish, 0)
    dv = dvt[:, full:L]
    dvv[full:L, :] = jnp.concatenate([dv, dv], 0).T + doubled(dvl[full:L, :])
    lo = low_half(z.fold)
    for c in range(z.C):
        at = c * z.pix
        stage[: z.pix, :] = dqk[at : at + z.pix, :]
        stage[z.pix : z.pix + z.fold, :] = jnp.where(
            lo, dvv[at : at + z.fold, :], dvv[at + z.fold : at + z.pix, :]
        )
        out_ref[c, pair] = stage[...].astype(BF16)


def add_kernel_sums(sums, gpad, vpad, base, size, across, tap):
    g = gpad[base : base + size, :]
    for a in (-1, 0, 1):
        ga = g
        if a == -1:
            ga = jnp.where(across >= 1, g, 0.0)
        if a == 1:
            ga = jnp.where(across <= SW - 2, g, 0.0)
        for l in (-1, 0, 1):
            at = base + SW * l + a
            term = (ga * vpad[at : at + size, :]).reshape(size // 8, 8, HALF).sum(0)
            t = tap(a, l)
            sums[t] = sums[t] + term if t in sums else term


def tall_prepare(z, p, lim_ref, L):
    across_limit, along_limit = lim_ref(p)
    empty = across_limit * along_limit == 0
    scale = jnp.where(empty, 1e-20, LOG2E * HEAD_DIM**-0.5)
    along, across = token_places(0, L, HALF)
    inside = jnp.logical_and(across < across_limit, along < along_limit)
    allowed = jnp.logical_or(inside, empty)
    token = lax.broadcasted_iota(jnp.int32, (L, HALF), 0)
    allowed = jnp.logical_and(allowed, token < z.tall_len)
    lane = lax.broadcasted_iota(jnp.int32, (L, HALF), 1) == 0
    bias = jnp.where(jnp.logical_and(lane, jnp.logical_not(allowed)), MASKED, 0.0).astype(BF16)
    return inside, across, scale, bias


def tall_pull(z, source, p, per, n, target, base):
    for r in range(z.R):
        at = pl.multiple_of((p * per + n) * z.tall_pad, 8)
        block = source[r, pl.ds(at, z.tall_pad), :]
        target[base + r * z.tall_own : base + (r + 1) * z.tall_own, :] = block[: z.tall_own]


def tall_push(z, source, p, per, n, target, base=0):
    for r in range(z.R):
        at = pl.multiple_of((p * per + n) * z.tall_pad, 8)
        target[r, pl.ds(at, z.tall_pad), :] = source[
            base + r * z.tall_own : base + r * z.tall_own + z.tall_pad, :
        ]


def tall_operands(z, k, q, bias, kstack, L):
    for h in range(BRANCH_HEADS):
        kstack[h * L : (h + 1) * L, :HALF] = jnp.where(head_lanes(h, L), k, 0.0).astype(BF16)
        kstack[h * L : (h + 1) * L, HALF:] = bias
    first = lax.broadcasted_iota(jnp.int32, (HALF, L), 0) == 0
    return jnp.concatenate([q.T, jnp.where(first, 1.0, 0.0)], 0).astype(BF16)


def tall_forward(
    z, start, stop, lim_ref, lw_ref, lb_ref, ot_ref, lse_ref, src, dst, qs, ks, vs, vpad, osum, kstack
):
    L = qs.shape[1]

    def taps(a, l):
        t = tall_tap(a, l)
        return lw_ref[t : t + 1, :]

    def group(m, carry):
        each = range(z.tall_group)
        ps = [m * z.tall_group + u for u in each]
        for u in each:
            for n, target in enumerate((qs, ks, vs)):
                tall_pull(z, src, ps[u], 3, n, target.at[u], 0)
        made = [tall_prepare(z, ps[u], lim_ref, L) for u in each]
        qts = [tall_operands(z, ks[u], qs[u], made[u][3], kstack.at[u], L) for u in each]
        scores = [mm(kstack[u], qts[u]) for u in each]
        tail = lax.broadcasted_iota(jnp.int32, (16, L), 0) == 0
        tail = jnp.where(tail, 1.0, 0.0)
        vts = [vs[u].T for u in each]
        tops = [
            [jnp.max(scores[u][h * L : (h + 1) * L], 0, keepdims=True) for h in range(BRANCH_HEADS)]
            for u in each
        ]
        accs = []
        for u in each:
            row = []
            for h in range(BRANCH_HEADS):
                s = scores[u][h * L : (h + 1) * L]
                e = jnp.exp2((s - tops[u][h]) * made[u][2]).astype(BF16)
                vt = jnp.concatenate([vts[u][h * HEAD_DIM : (h + 1) * HEAD_DIM], tail], 0)
                row.append(mm(vt.astype(BF16), e))
            accs.append(row)
        for u in each:
            inside, across, scale, _ = made[u]
            outs = []
            for h in range(BRANCH_HEADS):
                total = accs[u][h][HEAD_DIM : HEAD_DIM + 1]
                outs.append(accs[u][h][:HEAD_DIM] * (1.0 / total))
                lse_ref[ps[u], h : h + 1, :] = tops[u][h] * scale + jnp.log2(total)
            ot = jnp.concatenate(outs, 0)
            ot_ref[ps[u]] = ot
            vpad[u, PAD : PAD + L, :] = jnp.where(inside, vs[u], 0.0)
            lepe = conv_forward(vpad.at[u], PAD, L, taps, across)
            osum[u, :L, :] = ot.T + lepe + lb_ref
        for u in each:
            tall_push(z, osum.at[u], ps[u], 1, 0, dst)
        return carry

    lax.fori_loop(start, stop, group, 0)


def tall_backward(
    z,
    start,
    stop,
    lim_ref,
    lw_ref,
    ot_ref,
    lse_ref,
    dlw_ref,
    src,
    gsrc,
    dst,
    qs,
    ks,
    vs,
    gpad,
    vpad,
    stage,
    kstack,
):
    L = qs.shape[1]
    norm = HEAD_DIM**-0.5

    def taps(a, l):
        t = tall_tap(a, l)
        return lw_ref[t : t + 1, :]

    def group(m, carry):
        each = range(z.tall_group)
        ps = [m * z.tall_group + u for u in each]
        for u in each:
            for n, target in enumerate((qs, ks, vs)):
                tall_pull(z, src, ps[u], 3, n, target.at[u], 0)
            tall_pull(z, gsrc, ps[u], 1, 0, gpad.at[u], PAD)
        made = [tall_prepare(z, ps[u], lim_ref, L) for u in each]
        gts = [gpad[u, PAD : PAD + L, :].T for u in each]
        qts = [tall_operands(z, ks[u], qs[u], made[u][3], kstack.at[u], L) for u in each]
        kts = [ks[u].T.astype(BF16) for u in each]
        dvs = [None] * len(ps)
        dks = [None] * len(ps)
        dqs = [[] for u in each]
        for some in z.tall_head_sets:
            scores = []
            dps = []
            for u in each:
                rows = slice(some[0] * L, (some[-1] + 1) * L)
                scores.append(mm(kstack[u, rows, :], qts[u]))
                v = vs[u]
                vstack = jnp.concatenate([jnp.where(head_lanes(h, L), v, 0.0) for h in some], 0)
                dps.append(mm(vstack.astype(BF16), gts[u].astype(BF16)))
            weights = []
            for u in each:
                prod = gts[u] * ot_ref[ps[u]]
                lse = lse_ref[ps[u]]
                row = []
                for i, h in enumerate(some):
                    rows = slice(i * L, (i + 1) * L)
                    delta = jnp.sum(prod[h * HEAD_DIM : (h + 1) * HEAD_DIM], 0, keepdims=True)
                    w = jnp.exp2(scores[u][rows] * made[u][2] - lse[h : h + 1])
                    ds = (w * (dps[u][rows] - delta)).astype(BF16)
                    row.append((w.astype(BF16), ds))
                weights.append(row)
            for u in each:
                for i, h in enumerate(some):
                    keep = head_lanes(h, L)
                    w, ds = weights[u][i]
                    dv_h = mm(w, jnp.where(keep, gpad[u, PAD : PAD + L, :], 0.0).astype(BF16))
                    dk_h = mm(ds, jnp.where(keep, qs[u], 0.0).astype(BF16))
                    dvs[u] = dv_h if dvs[u] is None else dvs[u] + dv_h
                    dks[u] = dk_h if dks[u] is None else dks[u] + dk_h
                    dqs[u].append(mm(kts[u][h * HEAD_DIM : (h + 1) * HEAD_DIM], ds))
        results = [(jnp.concatenate(dqs[u], 0), dks[u], dvs[u]) for u in each]
        sums = {}
        for u in each:
            inside, across = made[u][:2]
            vpad[u, PAD : PAD + L, :] = jnp.where(inside, vs[u], 0.0)
            lepe = conv_backward(gpad.at[u], PAD, L, taps, across)
            add_kernel_sums(sums, gpad.at[u], vpad.at[u], PAD, L, across, tall_tap)
            dqt, dk, dv = results[u]
            stage[u, 0, :L, :] = dqt.T * norm
            stage[u, 1, :L, :] = dk * norm
            stage[u, 2, :L, :] = dv + jnp.where(inside, lepe, 0.0)
        for t, value in sums.items():
            dlw_ref[t : t + 1, :] += jnp.sum(value, 0, keepdims=True)
        for u in each:
            for n in range(3):
                tall_push(z, stage.at[u, n], ps[u], 3, n, dst)
        return carry

    lax.fori_loop(start, stop, group, 0)


def partners(z):
    col = lax.axis_index("col")
    row = lax.axis_index("row")
    found = [(row, lax.rem(col + k, z.C)) for k in range(1, z.C)]
    found += [(lax.rem(row + k, z.R), col) for k in range(1, z.R)]
    first = col - lax.rem(col, 4)
    for r in range(1, z.R):
        for k in range(1, 4):
            found.append((lax.rem(row + r, z.R), first + lax.rem(col + k, 4)))
    return found


def greet(z):
    barrier = pltpu.get_barrier_semaphore()
    for device in partners(z):
        pl.semaphore_signal(barrier, inc=1, device_id=device, device_id_type=MESH)


def all_greeted(z):
    pl.semaphore_wait(pltpu.get_barrier_semaphore(), len(partners(z)))


class Exchange:
    def __init__(self, z, axis, source, target, sends, receives):
        self.axis = axis
        self.source, self.target = source, target
        self.me = lax.axis_index(axis)
        count = z.C if axis == "col" else z.R
        col = lax.axis_index("col")
        row = lax.axis_index("row")
        self.copies = []
        for k in range(1, count):
            other = lax.rem(self.me + k, count)
            self.copies.append(
                pltpu.make_async_remote_copy(
                    src_ref=source(other),
                    dst_ref=target(self.me),
                    send_sem=sends.at[k],
                    recv_sem=receives.at[k],
                    device_id=(row, other) if axis == "col" else (other, col),
                    device_id_type=MESH,
                )
            )

    def start(self):
        for copy in self.copies:
            copy.start()

    def keep_own(self):
        self.target(self.me)[...] = self.source(self.me)[...]

    def arrive(self):
        for copy in self.copies:
            copy.wait_recv()

    def sent(self):
        for copy in self.copies:
            copy.wait_send()


def split_of(rows, lanes, parts):
    for by_rows in range(parts, 0, -1):
        if parts % by_rows == 0:
            by_lanes = parts // by_rows
            if rows % (16 * by_rows) == 0 and lanes % (128 * by_lanes) == 0:
                return by_rows, by_lanes
    raise ValueError("no split")


def reduce_plan(z, lanes, steps):
    rows = z.dim
    plan = []
    for step in steps:
        members = {"core": 2, "x": 2, "row": z.R, "slab": 4 * z.R}.get(step, z.C // 4)
        a, b = (1, 1) if step == "far_all" else split_of(rows, lanes, members)
        rows, lanes = rows // a, lanes // b
        plan.append((members, step, a, b, rows, lanes))
    return plan


def reduce_width(z, lanes, steps):
    while True:
        try:
            reduce_plan(z, lanes, steps)
            return lanes
        except ValueError:
            lanes += 128


def place_of(step):
    col = lax.axis_index("col")
    row = lax.axis_index("row")
    if step == "row":
        return row
    if step == "slab":
        return row * 4 + lax.rem(col, 4)
    if step in ("far", "far_all"):
        return col // 4
    return lax.rem(col // {"core": 1, "x": 2}[step], 2)


def peer_of(step, members, k):
    col = lax.axis_index("col")
    row = lax.axis_index("row")
    me = place_of(step)
    at = lax.rem(me + k, members)
    if step == "row":
        return at, (at, col)
    if step == "slab":
        return at, (at // 4, col - lax.rem(col, 4) + lax.rem(at, 4))
    return at, (row, col + (at - me) * {"core": 1, "x": 2, "far": 4, "far_all": 4}[step])


class SmallSum:
    def __init__(self, plan, value, slots, sends, receives):
        self.plan, self.value, self.slots = plan, value, slots
        self.sends, self.receives = sends, receives

    def start(self, stage):
        members, step = self.plan[stage][:2]
        me = place_of(step)
        self.copies = []
        for k in range(1, members):
            self.copies.append(
                pltpu.make_async_remote_copy(
                    src_ref=self.value,
                    dst_ref=self.slots[stage].at[me],
                    send_sem=self.sends.at[stage, k],
                    recv_sem=self.receives.at[stage, k],
                    device_id=peer_of(step, members, k)[1],
                    device_id_type=MESH,
                )
            )
        for copy in self.copies:
            copy.start()
        self.slots[stage][me] = self.value[...]

    def end(self, stage, out):
        for copy in self.copies:
            copy.wait()
        total = self.slots[stage][0]
        for k in range(1, self.plan[stage][0]):
            total = total + self.slots[stage][k]
        out[...] = total
        self.value = out


class Reduction:
    def __init__(self, z, plan, refs, small=None):
        n = len(plan)
        self.z, self.plan, self.n = z, plan, n
        self.full, refs = refs[0], refs[1:]
        self.recvs, refs = refs[:n], refs[n:]
        self.held, refs = refs[:n], refs[n:]
        self.gathers, refs = refs[:n], refs[n:]
        self.ssem, self.rsem, self.gsem, self.hsem = refs[:4]
        self.small = small
        if small is not None:
            self.smalls = refs[4 : 4 + n]
            self.vsem, self.wsem = refs[4 + n :]
        self.current = self.full
        self.copies = None

    @staticmethod
    def scratch(z, plan, lanes, small_shape=None):
        dma = pltpu.SemaphoreType.DMA
        most = max(step[0] for step in plan)
        shapes = [pltpu.VMEM((z.dim, lanes), BF16)]
        shapes += [pltpu.VMEM((step[0], step[4], step[5]), BF16) for step in plan]
        shapes += [pltpu.VMEM((step[4], step[5]), BF16) for step in plan]
        shapes += [pltpu.VMEM((z.dim, lanes), BF16)]
        shapes += [pltpu.VMEM((step[4], step[5]), BF16) for step in plan[:-1]]
        shapes += [dma((len(plan), most)) for _ in range(4)]
        if small_shape is not None:
            shapes += [pltpu.VMEM((step[0],) + small_shape, F32) for step in plan]
            shapes += [dma((len(plan), most)) for _ in range(2)]
        return shapes

    def place(self, stage):
        return place_of(self.plan[stage][1])

    def peer(self, stage, k):
        members, step = self.plan[stage][:2]
        return peer_of(step, members, k)

    def window(self, ref, stage, index):
        members, step, a, b, rows, width = self.plan[stage]
        if a * b == 1:
            return ref
        r0 = pl.multiple_of((index // b) * rows, 16)
        l0 = pl.multiple_of(lax.rem(index, b) * width, 128)
        return ref.at[pl.ds(r0, rows), pl.ds(l0, width)]

    def fill(self, pieces):
        D = self.z.dim
        at = 0
        for ref in pieces:
            for k in range(ref.shape[0] // D):
                width = ref.shape[1]
                self.full[:, at : at + width] = ref[k * D : (k + 1) * D, :].astype(BF16)
                at += width
        if at < self.full.shape[1]:
            self.full[:, at:] = jnp.zeros((D, self.full.shape[1] - at), BF16)

    def scatter_start(self, stage):
        me = self.place(stage)
        self.copies = []
        for k in range(1, self.plan[stage][0]):
            index, device = self.peer(stage, k)
            self.copies.append(
                pltpu.make_async_remote_copy(
                    src_ref=self.window(self.current, stage, index),
                    dst_ref=self.recvs[stage].at[me],
                    send_sem=self.ssem.at[stage, k],
                    recv_sem=self.rsem.at[stage, k],
                    device_id=device,
                    device_id_type=MESH,
                )
            )
            if self.small is not None:
                self.copies.append(
                    pltpu.make_async_remote_copy(
                        src_ref=self.small,
                        dst_ref=self.smalls[stage].at[me],
                        send_sem=self.vsem.at[stage, k],
                        recv_sem=self.wsem.at[stage, k],
                        device_id=device,
                        device_id_type=MESH,
                    )
                )
        for copy in self.copies:
            copy.start()
        self.recvs[stage][me] = self.window(self.current, stage, me)[...]
        if self.small is not None:
            self.smalls[stage][me] = self.small[...]

    def scatter_end(self, stage, small_out=None):
        for copy in self.copies:
            copy.wait()
        members = self.plan[stage][0]
        rows, width = self.plan[stage][4:]
        for at, size in key_tiles(width, 512):
            lanes = slice(at, at + size)
            total = self.recvs[stage][0, :, lanes].astype(F32)
            for k in range(1, members):
                total = total + self.recvs[stage][k, :, lanes].astype(F32)
            self.held[stage][:, lanes] = total.astype(BF16)
        self.current = self.held[stage]
        if self.small is not None:
            small = self.smalls[stage][0]
            for k in range(1, members):
                small = small + self.smalls[stage][k]
            if stage + 1 < self.n:
                self.smalls[stage][0] = small
                self.small = self.smalls[stage].at[0]
            else:
                small_out[...] = small

    def gather_start(self, stage):
        me = self.place(stage)
        self.copies = []
        for k in range(1, self.plan[stage][0]):
            index, device = self.peer(stage, k)
            self.copies.append(
                pltpu.make_async_remote_copy(
                    src_ref=self.current,
                    dst_ref=self.window(self.gathers[stage], stage, me),
                    send_sem=self.gsem.at[stage, k],
                    recv_sem=self.hsem.at[stage, k],
                    device_id=device,
                    device_id_type=MESH,
                )
            )
        for copy in self.copies:
            copy.start()
        self.window(self.gathers[stage], stage, me)[...] = self.current[...]

    def gather_end(self, stage):
        for copy in self.copies:
            copy.wait()
        self.current = self.gathers[stage]

    def steps(self, small_out=None):
        n = self.n
        ends = [functools.partial(self.scatter_end, s, small_out) for s in range(n)]
        back = [s for s in range(n - 1, -1, -1) if self.plan[s][1] != "far_all"]
        ends += [functools.partial(self.gather_end, s) for s in back]
        starts = [functools.partial(self.scatter_start, s) for s in range(n)]
        starts += [functools.partial(self.gather_start, s) for s in back]
        return starts, ends


def spread(block, outs):
    D = block.shape[0]
    at = 0
    for ref in outs:
        for k in range(ref.shape[0] // D):
            width = ref.shape[1]
            ref[k * D : (k + 1) * D, :] = block[:, at : at + width].astype(F32)
            at += width


def reduce_kernel(z, plan, dqkv_ref, vec_ref, dwt_ref, dtt_ref, sum_ref, osmall, small, *refs):
    greet(z)
    small[:16, :HALF] = own_lanes_back(z, dwt_ref[...])
    small[:16, HALF:] = dtt_ref[...]
    small[9:13, :] = vec_ref[:4, :]
    work = Reduction(z, plan, refs, small)
    work.fill((dqkv_ref,))
    all_greeted(z)
    starts, ends = work.steps(osmall)
    for start, end in zip(starts, ends):
        start()
        end()
    sum_ref[...] = work.current[...]


def own_lanes_back(z, value):
    if z.G == 1:
        return value
    return jnp.where(lax.rem(lax.axis_index("col"), z.G) == 0, value, turn(value))


def reduce_last(z, dqkv, vec, dwt, dtt, collective_id):
    steps = ("slab", "far")
    lanes = reduce_width(z, dqkv.size // z.dim, steps)
    plan = reduce_plan(z, lanes, steps)
    vmem = pl.BlockSpec(memory_space=pltpu.VMEM)
    small = (16, z.dim)
    return pl.pallas_call(
        functools.partial(reduce_kernel, z, plan),
        out_shape=(
            jax.ShapeDtypeStruct((z.dim, lanes), BF16),
            jax.ShapeDtypeStruct(small, F32),
        ),
        in_specs=[vmem] * 4,
        out_specs=(vmem,) * 2,
        scratch_shapes=[pltpu.VMEM(small, F32)] + Reduction.scratch(z, plan, lanes, small),
        compiler_params=pltpu.CompilerParams(
            collective_id=collective_id, has_side_effects=True, vmem_limit_bytes=VMEM_LIMIT
        ),
        name="reduce_last",
    )(dqkv, vec, dwt, dtt)


def split_kernel(z, sum_ref, late_ref, early_ref, first_ref, dw_ref, dpw_ref, dw1_ref, dw2_ref, *outs):
    if z.merged:
        width = sum_ref.shape[1] // 2
        for n in range(3):
            own = slice(n * HALF, (n + 1) * HALF)
            dw_ref[:, n * z.dim + HALF : (n + 1) * z.dim] = sum_ref[:, own].astype(F32)
            own = slice(width + n * HALF, width + (n + 1) * HALF)
            dw_ref[:, n * z.dim : n * z.dim + HALF] = sum_ref[:, own].astype(F32)
    else:
        spread(sum_ref, (dw_ref,))
    spread(first_ref, (dpw_ref, dw1_ref, dw2_ref))
    n1g, n1s, qb, vb, taps, lb, pb, n2g, n2s, b1, b2 = outs
    taps[...] = late_ref[:9, :]
    for ref, row in ((n1g, 9), (n1s, 10), (qb, 11), (vb, 12)):
        ref[...] = late_ref[row : row + 1, :]
    for ref, row in ((n2g, 0), (n2s, 1), (pb, 2), (b2, 3), (lb, 4)):
        ref[...] = early_ref[row : row + 1, :]
    D = z.dim
    for k in range(b1.shape[1] // D):
        b1[:, k * D : (k + 1) * D] = early_ref[8 + k : 9 + k, :]


def front_kernel(
    z,
    heights_ref,
    widths_ref,
    x_ref,
    gain_ref,
    shift_ref,
    w_ref,
    qb_ref,
    vb_ref,
    tap_ref,
    tap_bias_ref,
    back_wide,
    back_tall,
    tq_out,
    tot_out,
    tlse_out,
    v_out,
    kcat_out,
    qtb_out,
    kt_out,
    ot_out,
    lse_out,
    tot_ref,
    tlse_ref,
    v_ref,
    kcat,
    qtb,
    kt,
    ot,
    lse,
    pw,
    pt,
    gw,
    gt,
    low,
    send_wide,
    send_tall,
    recv_wide,
    recv_tall,
    out_wide,
    out_tall,
    t_src,
    t_dst,
    t_q,
    t_k,
    t_v,
    t_vpad,
    t_osum,
    t_kstack,
    qk,
    vpad,
    stage,
    vt,
    vt_all,
    ss0,
    ss1,
    osum,
    lepe,
    wsend,
    wrecv,
    tsend,
    trecv,
    wsend1,
    wrecv1,
    tsend1,
    trecv1,
    local,
):
    greet(z)
    wlim_ref = wide_ends(z, heights_ref, widths_ref)
    tlim_ref = tall_ends(z, heights_ref, widths_ref)
    ttap_ref = tap_ref[:, HALF:]
    tbias_ref = tap_bias_ref[:, HALF:]
    wtap_ref = own_lanes(z, tap_ref[:, :HALF])
    wbias_ref = own_lanes(z, tap_bias_ref[:, :HALF])
    bias = jnp.concatenate([qb_ref[...], jnp.zeros_like(qb_ref), vb_ref[...]], -1)
    dense_in_wide(z, x_ref, gain_ref, shift_ref, w_ref, bias, send_wide, low, pw, gw)
    all_greeted(z)
    cut = up(z.pix, 16)
    parts = [(0, 0, cut), (0, cut, z.pair_rows)]
    parts += [(pair, 0, z.pair_rows) for pair in range(1, z.pairs)]
    wides = [
        Exchange(
            z,
            "col",
            lambda d, pair=pair, at=at, end=end: send_wide.at[d, pair, at:end],
            lambda d, pair=pair, at=at, end=end: recv_wide.at[d, pair, at:end],
            wsend.at[k],
            wrecv.at[k],
        )
        for k, (pair, at, end) in enumerate(parts)
    ]
    tall = Exchange(
        z, "row", lambda d: send_tall.at[d], lambda d: recv_tall.at[d], tsend, trecv
    )
    for wide in wides[:2]:
        wide.start()
    dense_in_tall(z, w_ref, bias, send_tall, low, pt, gt)
    tall.start()
    for wide in wides:
        wide.keep_own()
    tall.keep_own()
    for ref in (t_q, t_k, t_v, t_vpad, t_osum, vpad, qk):
        ref[...] = jnp.zeros_like(ref)
    groups = z.tall_slots // z.tall_group
    early = groups // 2
    half = z.tall_rows1 // 2
    col = lax.axis_index("col")
    row = lax.axis_index("row")
    jobs = []
    own = []

    def wide_back(pair):
        wide_pair_mixture(z, pair, ot, lepe, osum, out_wide)
        job = Exchange(
            z,
            "col",
            lambda d: out_wide.at[d, pair],
            lambda d: back_wide.at[d, pair],
            wsend1.at[pair],
            wrecv1.at[pair],
        )
        job.start()
        jobs.append(job)
        copy = pltpu.make_async_copy(
            out_wide.at[col, pair], back_wide.at[col, pair], local.at[pair]
        )
        copy.start()
        own.append(copy)

    def tall_part(k, start, stop):
        tall_forward(
            z, start, stop, tlim_ref, ttap_ref, tbias_ref, tot_ref, tlse_ref,
            t_src, t_dst, t_q, t_k, t_v, t_vpad, t_osum, t_kstack,
        )
        rows = pl.ds(k * half, half)
        out_tall[:, rows, :] = t_dst[:, rows, :].astype(BF16)
        job = Exchange(
            z,
            "row",
            lambda d: out_tall.at[d, rows],
            lambda d: back_tall.at[d, rows],
            tsend1.at[k],
            trecv1.at[k],
        )
        job.start()
        jobs.append(job)
        copy = pltpu.make_async_copy(
            out_tall.at[row, rows], back_tall.at[row, rows], local.at[2 + k]
        )
        copy.start()
        own.append(copy)

    def save(source, target):
        copy = pltpu.make_async_copy(source, target, local.at[4 + len(saves)])
        copy.start()
        saves.append(copy)

    saves = []
    for pair in range(z.pairs):
        if pair > 0:
            wides[pair + 1].arrive()
        wide_pair_prepare(
            z, pair, wlim_ref, recv_wide, kcat, qtb, kt, qk, vpad, stage, vt, vt_all,
            wides if pair == 0 else (),
        )
        save(kcat.at[pair], kcat_out.at[pair])
        save(qtb.at[pair], qtb_out.at[pair])
        save(kt.at[pair], kt_out.at[pair])
        if pair + 1 == z.pairs:
            v_ref[...] = vpad[PAD : PAD + z.wide_len, :].astype(BF16)
            save(v_ref, v_out)
            wide_lepe(z, wlim_ref, wtap_ref, wbias_ref, vpad, lepe)
            for done in range(pair):
                wide_back(done)
        wide_pair_attend(z, pair, wlim_ref, kcat, qtb, ot, lse, vt, vt_all, ss0, ss1)
        if pair == 0:
            tall.arrive()
            save(recv_tall, tq_out)
            t_src[...] = recv_tall[...].astype(F32)
            tall_part(0, 0, early)
    save(ot, ot_out)
    save(lse, lse_out)
    wide_back(z.pairs - 1)
    tall_part(1, early, groups)
    save(tot_ref, tot_out)
    save(tlse_ref, tlse_out)
    for copy in own + saves:
        copy.wait()
    for job in wides + [tall] + jobs:
        job.sent()
    for job in jobs:
        job.arrive()


def out_wide_planes(z, pair, got, wide, thirds):
    wide[...] = got[:, pair].astype(F32)

    def place(n, start, value):
        lo = low_lanes(value.shape)
        value = jnp.where(lo, value, 0.0) if pair == 0 else jnp.where(lo, 0.0, value)
        count = value.shape[1] * z.images
        value = jnp.swapaxes(value, 0, 1).reshape(count, HALF)
        thirds[n][start * z.images : start * z.images + count, :HALF] = value.astype(BF16)

    both = wide[:, : z.pix, :]
    folded = wide[:, z.pix : z.pix + z.fold, :]
    place(0, 0, both if pair == 0 else turn(both))
    place(1, 0, turn(both) if pair == 0 else both)
    place(2, 0, folded if pair == 0 else turn(folded))
    place(2, z.fold, turn(folded) if pair == 0 else folded)


def out_tall_planes(z, got, tall, thirds):
    tall[...] = got[...].astype(F32)
    count = z.tall_own * z.images
    for n in range(3):
        for s in range(z.stripes):
            blocks = []
            for b in range(z.images):
                at = (((b % z.tall_images) * z.stripes + s) * 3 + n) * z.tall_pad
                blocks.append(tall[b // z.tall_images, at : at + z.tall_own, :])
            value = jnp.swapaxes(jnp.stack(blocks), 0, 1).reshape(count, HALF)
            thirds[n][s * count : (s + 1) * count, HALF:] = value.astype(BF16)


def wide_rows_of(z, third, i):
    rows = []
    for j in range(z.cols):
        at = pl.multiple_of((j * z.rows + i) * z.images, z.images)
        rows.append(third[pl.ds(at, z.images), :HALF])
    return jnp.concatenate(rows, 0)


def tall_rows_of(z, third, i):
    rows = []
    for j in range(z.cols):
        s, jj = divmod(j, SW)
        at = pl.multiple_of(((s * z.rows + i) * SW + jj) * z.images, z.images)
        rows.append(third[pl.ds(at, z.images), HALF:])
    return jnp.concatenate(rows, 0)


def own_rows(z, i):
    T = z.cols * z.images
    return pl.ds(pl.multiple_of(i * T, 16), T)


def out_first(z, x_ref, gain_ref, shift_ref, w_ref, thirds, low, dw, gn, vec):
    T = z.cols * z.images
    D = z.dim
    dw[...] = jnp.zeros_like(dw)
    vec[...] = jnp.zeros_like(vec)

    def one_row(i, carry):
        normed, _ = norm_parts(x_ref[i].astype(F32).reshape(T, D))
        low_i = (normed * gain_ref[...] + shift_ref[...]).astype(BF16)
        for j in range(z.cols):
            at = pl.multiple_of((j * z.rows + i) * z.images, z.images)
            low[pl.ds(at, z.images), :] = low_i[j * z.images : (j + 1) * z.images]
        parts = []
        for third in thirds:
            parts += [wide_rows_of(z, third, i), tall_rows_of(z, third, i)]
        gproj = jnp.concatenate(parts, -1)
        vec[2:3, :] += jnp.sum(gproj[:, :D].astype(F32), 0, keepdims=True)
        vec[3:4, :] += jnp.sum(gproj[:, 2 * D :].astype(F32), 0, keepdims=True)
        dw[...] += mm_tn(low_i, gproj)
        gn[own_rows(z, i), :] = mm_nt(gproj, w_ref[...])
        return carry

    lax.fori_loop(0, z.rows, one_row, 0)


def out_second(z, thirds, low, dw, vec):
    D = z.dim
    for n, third in enumerate(thirds):
        own = third[:, :HALF]
        dw[:, n * D : n * D + HALF] += mm_tn(low[...], own)
        if n != 1:
            row = 2 if n == 0 else 3
            vec[row : row + 1, :HALF] += jnp.sum(own.astype(F32), 0, keepdims=True)


def out_third(z, x_ref, gain_ref, w_ref, thirds, gn, gres, gin_ref, vec):
    T = z.cols * z.images
    D = z.dim

    def one_row(i, carry):
        rows = own_rows(z, i)
        gproj = jnp.concatenate([wide_rows_of(z, third, i) for third in thirds], -1)
        weight = jnp.concatenate([w_ref[:, n * D : n * D + HALF] for n in range(3)], -1)
        gnorm = gn[rows, :] + mm_nt(gproj, weight)
        n1, r1 = norm_parts(x_ref[i].astype(F32).reshape(T, D))
        vec[0:1, :] += jnp.sum(gnorm * n1, 0, keepdims=True)
        vec[1:2, :] += jnp.sum(gnorm, 0, keepdims=True)
        g = gnorm * gain_ref[...]
        gin = gres[rows, :] + r1 * (
            g - jnp.mean(g, -1, keepdims=True) - n1 * jnp.mean(g * n1, -1, keepdims=True)
        )
        gin_ref[i] = gin.reshape(z.cols, z.images, D)
        return carry

    lax.fori_loop(0, z.rows, one_row, 0)


BACK_LOADS = ("dsum", "tq", "tot", "tlse", "v", "kcat", "qtb", "kt", "ot", "lse")


def back_names(z):
    names = ["heights", "widths", "gw", "gt", "tap", "vec"]
    names += [name + "_any" for name in BACK_LOADS]
    if z.merged:
        names += ["gain", "shift", "x_any", "w_any", "gres_any", "gin", "late", "late_small"]
    else:
        names += ["got_wide", "got_tall", "dwt", "dtt"]
    names += ["sums", "smalls", *BACK_LOADS[1:]]
    names += ["recv_wide", "recv_tall", "send_wide", "send_tall", "t_src", "t_gsrc"]
    names += ["t_q", "t_k", "t_v", "t_gpad", "t_vpad", "t_stage", "t_kstack"]
    names += ["gpad", "vpad", "dotb", "delta", "dvl", "dqt", "dkt", "dvt", "stage"]
    names += ["ss0", "ss1", "dp0", "dp1", "ps0", "ps1", "ds0", "ds1"]
    names += ["wsend", "wrecv", "tsend", "trecv", "wsend1", "wrecv1", "tsend1", "trecv1", "local"]
    if z.merged:
        names += ["got_wide", "got_tall", "dwt", "dtt", "wide_block", "dw", "last_vec", "small", "x", "w"]
    return names


def back_kernel(z, plan, late_plan, *refs):
    names = back_names(z)
    r = types.SimpleNamespace(**dict(zip(names, refs)))
    refs = refs[len(names) :]
    size = len(Reduction.scratch(z, plan, z.dim, (8, z.dim)))
    early_refs, late_refs = refs[:size], refs[size:]
    r.dsum = early_refs[0]
    greet(z)
    loads = {}
    for i, name in enumerate(BACK_LOADS + (("x", "w") if z.merged else ())):
        loads[name] = pltpu.make_async_copy(
            getattr(r, name + "_any"), getattr(r, name), r.local.at[5 + i]
        )
        loads[name].start()
    wlim = wide_ends(z, r.heights, r.widths)
    tlim = tall_ends(z, r.heights, r.widths)
    tall_taps = r.tap[:, HALF:]
    wide_taps = own_lanes(z, r.tap[:, :HALF])
    work = Reduction(z, plan, early_refs, r.vec)
    starts, ends = work.steps(r.smalls)
    all_greeted(z)
    tall = Exchange(z, "row", lambda d: r.gt.at[d], lambda d: r.recv_tall.at[d], r.tsend, r.trecv)
    wide = Exchange(z, "col", lambda d: r.gw.at[d], lambda d: r.recv_wide.at[d], r.wsend, r.wrecv)
    tall.start()
    wide.start()
    loads["dsum"].wait()
    starts[0]()
    tall.keep_own()
    wide.keep_own()
    for ref in (r.t_q, r.t_k, r.t_v, r.t_gpad, r.t_vpad, r.t_stage):
        ref[...] = jnp.zeros_like(ref)
    r.dtt[...] = jnp.zeros_like(r.dtt)
    loads["tq"].wait()
    r.t_src[...] = r.tq[...].astype(F32)
    loads["tot"].wait()
    loads["tlse"].wait()
    groups = z.tall_slots // z.tall_group
    early = groups // 2
    half = z.tall_rows3 // 2
    col = lax.axis_index("col")
    row = lax.axis_index("row")
    outs = []
    own = []

    def keep(source, target, k):
        copy = pltpu.make_async_copy(source, target, r.local.at[k])
        copy.start()
        own.append(copy)

    def tall_part(k, start, stop):
        tall_backward(
            z, start, stop, tlim, tall_taps, r.tot, r.tlse, r.dtt, r.t_src, r.t_gsrc, r.t_src,
            r.t_q, r.t_k, r.t_v, r.t_gpad, r.t_vpad, r.t_stage, r.t_kstack,
        )
        rows = pl.ds(k * half, half)
        r.send_tall[:, rows, :] = r.t_src[:, rows, :].astype(BF16)
        job = Exchange(
            z,
            "row",
            lambda d: r.send_tall.at[d, rows],
            lambda d: r.got_tall.at[d, rows],
            r.tsend1.at[k],
            r.trecv1.at[k],
        )
        job.start()
        keep(r.send_tall.at[row, rows], r.got_tall.at[row, rows], 2 + k)
        return job

    done = [0]

    def point():
        if done[0] < len(ends) - 1:
            ends[done[0]]()
            starts[done[0] + 1]()
            done[0] += 1

    tall.arrive()
    r.t_gsrc[...] = r.recv_tall[...].astype(F32)
    outs.append(tall_part(0, 0, early))
    point()
    for name in BACK_LOADS[4:]:
        loads[name].wait()
    wide.arrive()
    wide_backward_start(
        z, wlim, r.recv_wide, wide_taps, r.v, r.ot, r.dwt, r.gpad, r.vpad, r.dotb, r.delta, r.dvl,
        r.stage,
    )
    point()
    slots = ((r.ss0, r.dp0, r.ps0, r.ds0), (r.ss1, r.dp1, r.ps1, r.ds1))
    for pair in range(z.pairs):
        wide_pair_backward(
            z, pair, wlim, r.v, r.kcat, r.qtb, r.kt, r.lse, r.dotb, r.delta, r.dvl, r.dqt, r.dkt,
            r.dvt, r.gpad, r.vpad, r.stage, slots, r.send_wide, point, 3 if pair == 0 else 2,
        )
        job = Exchange(
            z,
            "col",
            lambda d, pair=pair: r.send_wide.at[d, pair],
            lambda d, pair=pair: r.got_wide.at[d, pair],
            r.wsend1.at[pair],
            r.wrecv1.at[pair],
        )
        point()
        job.start()
        keep(r.send_wide.at[col, pair], r.got_wide.at[col, pair], pair)
        outs.append(job)
        if pair == 0:
            outs.append(tall_part(1, early, groups))
    while done[0] < len(ends) - 1:
        point()
    if not z.merged:
        ends[-1]()
        r.sums[...] = work.current[...]
        for copy in own:
            copy.wait()
        tall.sent()
        wide.sent()
        for job in outs:
            job.sent()
            job.arrive()
        return
    loads["x"].wait()
    loads["w"].wait()
    back_finish(z, r, late_plan, late_refs, work, ends, outs, own)
    tall.sent()
    wide.sent()
    for job in outs:
        job.sent()


def late_scratch(z, late_plan, late_lanes, small):
    most = max(step[0] for step in late_plan)
    shapes = Reduction.scratch(z, late_plan, late_lanes) * 2
    shapes += [pltpu.VMEM((step[0],) + small, F32) for step in late_plan]
    shapes += [pltpu.SemaphoreType.DMA((len(late_plan), most))] * 2
    return shapes


def back_finish(z, r, late_plan, refs, work, ends, outs, own):
    size = len(Reduction.scratch(z, late_plan, z.dim))
    lates = [Reduction(z, late_plan, refs[:size]), Reduction(z, late_plan, refs[size : 2 * size])]
    (start_a, end_a), (start_b, end_b) = [late.steps() for late in lates]
    refs = refs[2 * size :]
    n = len(late_plan)
    small = SmallSum(late_plan, r.small, refs[:n], refs[n], refs[n + 1])
    low, gn, gres, thirds = r.ps0, r.ss0, r.ss1, (r.ps1, r.ds0, r.ds1)
    load = pltpu.make_async_copy(r.gres_any, gres, r.local.at[4])
    load.start()
    for copy in own:
        copy.wait()
    for job in outs[:-1]:
        job.arrive()
    out_wide_planes(z, 0, r.got_wide, r.wide_block, thirds)
    out_tall_planes(z, r.got_tall, r.t_src, thirds)
    out_first(z, r.x, r.gain, r.shift, r.w, thirds, low, r.dw, gn, r.last_vec)
    lates[0].fill([r.dw.at[:, n * z.dim + HALF : (n + 1) * z.dim] for n in range(3)])
    start_a[0]()
    ends[-1]()
    r.sums[...] = work.current[...]
    outs[-1].arrive()
    out_wide_planes(z, 1, r.got_wide, r.wide_block, thirds)
    out_second(z, thirds, low, r.dw, r.last_vec)
    lates[1].fill([r.dw.at[:, n * z.dim : n * z.dim + HALF] for n in range(3)])
    start_b[0]()
    end_a[0]()
    start_a[1]()
    load.wait()
    out_third(z, r.x, r.gain, r.w, thirds, gn, gres, r.gin, r.last_vec)
    r.small[:, :HALF] = r.dwt[...]
    r.small[:, HALF:] = r.dtt[...]
    r.small[9:13, :] = r.last_vec[:4, :]
    small.start(0)
    end_b[0]()
    start_b[1]()
    end_a[1]()
    start_a[2]()
    small.end(0, r.small)
    small.start(1)
    end_b[1]()
    start_b[2]()
    end_a[2]()
    width = lates[0].full.shape[1]
    r.late[:, :width] = lates[0].current[...]
    small.end(1, r.late_small)
    end_b[2]()
    r.late[:, width:] = lates[1].current[...]


def local_call(kernel, z, name, outs, scratch, scalars, arrays):
    vmem = pl.BlockSpec(memory_space=pltpu.VMEM)
    smem = pl.BlockSpec(memory_space=pltpu.SMEM)
    return pl.pallas_call(
        functools.partial(kernel, z),
        out_shape=tuple(jax.ShapeDtypeStruct(shape, kind) for shape, kind in outs),
        in_specs=[smem] * len(scalars) + [vmem] * len(arrays),
        out_specs=(vmem,) * len(outs),
        scratch_shapes=[pltpu.VMEM(shape, kind) for shape, kind in scratch],
        compiler_params=pltpu.CompilerParams(vmem_limit_bytes=VMEM_LIMIT),
        name=name,
    )(*scalars, *arrays)


def per_device(
    mesh,
    features,
    heights,
    widths,
    norm1_gain,
    norm1_shift,
    qkv_weight,
    query_bias,
    value_bias,
    lepe_weight,
    lepe_bias,
    proj_weight,
    proj_bias,
    norm2_gain,
    norm2_shift,
    fc1_weight,
    fc1_bias,
    fc2_weight,
    fc2_bias,
    cotangent,
):
    z = Sizes(mesh, features.shape)
    B, D, TC, TR = z.images, z.dim, z.cols, z.rows
    x = features.transpose(1, 2, 0, 3)
    ct = cotangent.transpose(1, 2, 0, 3)
    line = lambda v: v.reshape(1, -1)
    FF = fc1_weight.shape[1]
    wide3 = (z.C, z.pairs, z.pair_rows, HALF)
    wide1 = (z.C, z.wide_rows1, z.hc)
    fold1 = (z.C, z.pairs, z.fold_rows, HALF)
    tall3 = (z.R, z.tall_rows3, HALF)
    tall1 = (z.R, z.tall_rows1, HALF)
    flat = up(z.tokens, 16 * B) + 16 * B
    L = z.wide_len
    LT = up(z.tall_len, 128)
    per_head, tail, blocks, tail_lanes, span = wide_plan(z)
    vmem = pl.BlockSpec(memory_space=pltpu.VMEM)
    smem = pl.BlockSpec(memory_space=pltpu.SMEM)
    anywhere = pl.BlockSpec(memory_space=pl.ANY)
    dma = pltpu.SemaphoreType.DMA
    saved = [
        ((L, HALF), BF16),
        ((z.pairs, L, 2 * HALF), BF16),
        ((z.pairs, 2 * HALF, span), BF16),
        ((z.pairs, HALF // 2, L), BF16),
        ((HALF, per_head * z.qb + z.pairs * tail_lanes), F32),
        ((8, z.pairs * span), F32),
    ]
    tall_scratch = [
        ((z.tall_group, LT, HALF), F32),
        ((z.tall_group, LT, HALF), F32),
        ((z.tall_group, LT, HALF), F32),
        ((z.tall_group, LT + 16, HALF), F32),
        ((z.tall_group, LT + 16, HALF), F32),
        ((z.tall_group, BRANCH_HEADS * LT, 2 * HALF), BF16),
    ]
    sems = [
        dma((z.pairs + 1, z.C)),
        dma((z.pairs + 1, z.C)),
        dma((z.R,)),
        dma((z.R,)),
        dma((z.pairs, z.C)),
        dma((z.pairs, z.C)),
        dma((2, z.R)),
        dma((2, z.R)),
        dma((z.C,)),
        dma((z.C,)),
    ]
    shapes = lambda items: tuple(jax.ShapeDtypeStruct(s, k) for s, k in items)
    scratches = lambda items: [pltpu.VMEM(s, k) for s, k in items]

    back_wide, back_tall, tall_qkv, tall_ot, tall_lse, *wide_saved = pl.pallas_call(
        functools.partial(front_kernel, z),
        out_shape=shapes(
            [
                (fold1, BF16),
                (tall1, BF16),
                (tall3, BF16),
                ((z.tall_slots, HALF, LT), F32),
                ((z.tall_slots, 8, LT), F32),
            ]
            + saved
        ),
        in_specs=[smem] * 2 + [vmem] * 8,
        out_specs=(anywhere,) * (5 + len(saved)),
        scratch_shapes=scratches(
            [((z.tall_slots, HALF, LT), F32), ((z.tall_slots, 8, LT), F32)]
            + saved
            + [
                ((3, flat, HALF), F32),
                ((3, flat, HALF), F32),
                (wide3, F32),
                (tall3, F32),
                ((TR, TC * B, D), BF16),
                (wide3, BF16),
                (tall3, BF16),
                (wide3, BF16),
                (tall3, BF16),
                (fold1, BF16),
                (tall1, BF16),
                (tall3, F32),
                (tall1, F32),
            ]
            + tall_scratch
            + [
                ((L, HALF), F32),
                ((L + 2 * PAD, HALF), F32),
                ((z.pair_rows, HALF), F32),
                ((2, HEAD_DIM + 16, L), BF16),
                ((HALF + 16, L), BF16),
                ((L, z.qb), F32),
                ((L, z.qb), F32),
                ((L + z.fold_rows, HALF), F32),
                ((L, HALF), F32),
            ]
        )
        + sems[:8]
        + [dma((18,))],
        compiler_params=pltpu.CompilerParams(
            collective_id=0, has_side_effects=True, vmem_limit_bytes=VMEM_LIMIT
        ),
        name="front",
    )(
        heights,
        widths,
        x,
        line(norm1_gain),
        line(norm1_shift),
        qkv_weight,
        line(query_bias),
        line(value_bias),
        lepe_weight,
        line(lepe_bias),
    )

    vec_rows = 8 + up(FF // D, 8)
    steps = ("core", "x", "row", "far")
    lanes = reduce_width(z, D + 2 * FF, steps)
    plan = reduce_plan(z, lanes, steps)
    y, gres, gmix_wide, gmix_tall, dsum, vec_mid = local_call(
        dense_mid_kernel,
        z,
        "dense_mid",
        [
            ((TR, TC, B, D), BF16),
            ((TR, TC, B, D), F32),
            (wide1, BF16),
            (tall1, BF16),
            ((D, lanes), BF16),
            ((vec_rows, D), F32),
        ],
        [((D, D), F32), ((D, FF), F32), ((FF, D), F32)]
        + [((z.tokens, HALF), BF16)] * 2
        + [((z.tokens, HALF), F32)] * 2
        + [((B, z.wide_rows1, HALF), F32), (tall1, F32)]
        + [((z.tokens, D), F32)] * 2
        + [((z.tokens, HALF), F32)]
        + [((z.tokens, D), BF16)] * 3
        + [((TC * B, FF), F32)] * 4
        + [((TC * B, FF), BF16)] * 4,
        [heights, widths],
        [
            back_wide,
            back_tall,
            x,
            ct,
            proj_weight,
            line(proj_bias),
            line(norm2_gain),
            line(norm2_shift),
            fc1_weight,
            line(fc1_bias),
            fc2_weight,
            line(fc2_bias),
        ],
    )
    small = (16, D)
    late_steps = ("slab", "far_all")
    late_lanes = reduce_width(z, 3 * HALF, late_steps)
    late_plan = reduce_plan(z, late_lanes, late_steps)
    taps16 = ((16, HALF), F32)
    sums = [((D, lanes), BF16), ((vec_rows, D), F32)]
    arguments = [heights, widths, gmix_wide, gmix_tall, lepe_weight, vec_mid]
    arguments += [dsum, tall_qkv, tall_ot, tall_lse, *wide_saved]
    in_specs = [smem] * 2 + [vmem] * 4 + [anywhere] * (4 + len(saved))
    more = []
    last_scratch = []
    if z.merged:
        arguments += [line(norm1_gain), line(norm1_shift), x, qkv_weight, gres.reshape(-1, D)]
        in_specs += [vmem] * 2 + [anywhere] * 3
        outs = [((TR, TC, B, D), F32), ((D, 2 * late_lanes), BF16), (small, F32)] + sums
        out_specs = (vmem,) * 5
        more = [(wide3, BF16), (tall3, BF16), taps16, taps16, ((z.C, z.pair_rows, HALF), F32)]
        more += [((D, 3 * D), F32), ((8, D), F32), (small, F32)]
        more += [((TR, TC, B, D), BF16), ((D, 3 * D), BF16)]
        last_scratch = late_scratch(z, late_plan, late_lanes, small)
    else:
        outs = [(wide3, BF16), (tall3, BF16), taps16, taps16] + sums
        out_specs = (anywhere, anywhere) + (vmem,) * 4
    results = pl.pallas_call(
        functools.partial(back_kernel, z, plan, late_plan),
        out_shape=shapes(outs),
        in_specs=in_specs,
        out_specs=out_specs,
        scratch_shapes=scratches(
            [(tall3, BF16)]
            + [((z.tall_slots, HALF, LT), F32), ((z.tall_slots, 8, LT), F32)]
            + saved
            + [
                (wide1, BF16),
                (tall1, BF16),
                (wide3, BF16),
                (tall3, BF16),
                (tall3, F32),
                (tall1, F32),
            ]
            + tall_scratch[:5]
            + [((z.tall_group, 3, LT + 16, HALF), F32), tall_scratch[5]]
            + [
                ((L + 2 * PAD, HALF), F32),
                ((L + 2 * PAD, HALF), F32),
                ((HALF, z.pairs * span), BF16),
                ((8, z.pairs * span), F32),
                ((L, HALF), F32),
                ((HALF // 2, per_head * z.qb), F32),
                ((HALF // 2, L), F32),
                ((HALF // 2, L), F32),
                ((z.pair_rows, HALF), F32),
            ]
            + [((L, z.qb), F32)] * 4
            + [((L, z.qb), BF16)] * 4
        )
        + [sems[8], sems[9], sems[2], sems[3], sems[0], sems[1], sems[6], sems[7]]
        + [dma((19,))]
        + scratches(more)
        + Reduction.scratch(z, plan, lanes, (vec_rows, D))
        + last_scratch,
        compiler_params=pltpu.CompilerParams(
            collective_id=1, has_side_effects=True, vmem_limit_bytes=VMEM_LIMIT
        ),
        name="back",
    )(*arguments)
    if z.merged:
        grad_in, late, vec_late, early, vec_mid = results
    else:
        got_wide, got_tall, dwide_taps, dtall_taps, early, vec_mid = results
        grad_in, dqkv, vec_out = local_call(
            dense_out_kernel,
            z,
            "dense_out",
            [((TR, TC, B, D), F32), ((D, 3 * D), F32), ((8, D), F32)],
            [((3, flat, HALF), F32), ((3, flat, HALF), F32), (wide3, F32), (tall3, F32)],
            [],
            [got_wide, got_tall, x, gres, line(norm1_gain), line(norm1_shift), qkv_weight],
        )
        late, vec_late = reduce_last(z, dqkv, vec_out, dwide_taps, dtall_taps, 2)
    dqkv, dproj, dfc1, dfc2, n1g, n1s, qb, vb, taps, lb, pb, n2g, n2s, b1, b2 = local_call(
        split_kernel,
        z,
        "split",
        [((D, 3 * D), F32), ((D, D), F32), ((D, FF), F32), ((FF, D), F32)]
        + [((1, D), F32)] * 4
        + [((9, D), F32)]
        + [((1, D), F32)] * 4
        + [((1, FF), F32), ((1, D), F32)],
        [],
        [],
        [late, vec_late, vec_mid, early],
    )
    flat_of = lambda v: v.reshape(-1)
    return (
        y.transpose(2, 0, 1, 3),
        grad_in.transpose(2, 0, 1, 3),
        flat_of(n1g),
        flat_of(n1s),
        dqkv,
        flat_of(qb),
        flat_of(vb),
        taps,
        flat_of(lb),
        dproj,
        flat_of(pb),
        flat_of(n2g),
        flat_of(n2s),
        dfc1,
        flat_of(b1),
        dfc2,
        flat_of(b2),
    )


def solution(mesh):
    image = P(None, "row", "col", None)
    return jax.shard_map(
        functools.partial(per_device, mesh),
        mesh=mesh,
        in_specs=(image,) + (P(),) * 17 + (image,),
        out_specs=(image, image) + (P(),) * 15,
        check_vma=False,
    )
```
